32 devices in a mesh: gx: 4 (over z), gy: 4 (over y, x), gz: 2 (over core).
Axes of the slice: x: 2, y: 2, z: 4, core: 2. Of those that a mesh axis runs over, the one named last changes fastest.
Arguments:
- orbitals: float32 [32, 32, 32, 256], P(None, 'gx', 'gy', 'gz'), may hold values from -6 to 6
- potential: float32 [32, 32, 256], P('gx', 'gy', 'gz'), may hold values from -2 to 0
- projectors: float32 [256, 4, 512], P(('gx', 'gy', 'gz')), may hold values from -0.5 to 0.5
- owner_rank: int32 [256], replicated, may hold values from 0 to 31, as said below
- box_anchor: int32 [3, 256], replicated, may hold values from 0 to 120, as said below
- box_extent: int32 [256], replicated, may hold values from 4 to 8
- coupling: float32 [256, 4], replicated, may hold values from 0.5 to 3
Outputs:
- filtered: float32 [32, 32, 32, 256], P(None, 'gx', 'gy', 'gz')
- intersection: float32 [32, 32], replicated
The draws below stay inside these ranges and needn't reach their ends.
Inputs may be any that keep to these rules, and one draw needn't show every extreme that they name: owner_rank[a] is (ix * 4 + iy) * 2 + iz for the domain (ix, iy, iz) that holds all of atom a's box; every device holds at most 24 atoms, an eighth of the devices exactly 24. box_anchor[0, a] is at most 0, box_anchor[1, a] at most 0, box_anchor[2, a] at most 120, so each box lies inside its owner's domain.
All inputs are finite; a program needn't handle non-finite values.
Results may differ from the reference program's by a relative error of at most 0.00013.
Values sent between devices are 32-bit elements; how exact they have to be, the bound alone decides.
No kernel may reach another device: no remote copies, remote signals or barrier semaphores. Data moves between devices by JAX's collectives and lax.ppermute only.
A program may use at most 128 MiB of HBM per device.

```python
import math
import jax
import jax.numpy as jnp
from jax import lax

S = 32
NPROJ = 4
B = 8
DEGREE = 4
CX = 8
CY = 8
CZ = 128
ATOM_DEV = 8
NX = 32
NY = 32
NZ = 256
ATOMS = 256
N_GY = 4
N_GZ = 2


def owner_table(key):
    devices_all = ATOMS // ATOM_DEV
    eighth = devices_all // 8
    base_loads = jnp.concatenate([jnp.full((eighth,), 3 * ATOM_DEV, jnp.int32), jnp.full((3 * eighth,), ATOM_DEV, jnp.int32), jnp.full((4 * eighth,), ATOM_DEV // 2, jnp.int32)])
    device_order = jax.random.permutation(jax.random.fold_in(key, 11), devices_all)
    device_loads = jnp.zeros((devices_all,), jnp.int32).at[device_order].set(base_loads)
    sorted_owner = jnp.repeat(jnp.arange(devices_all, dtype=jnp.int32), device_loads, total_repeat_length=ATOMS)
    shuffle = jax.random.permutation(jax.random.fold_in(key, 12), ATOMS)
    return sorted_owner[shuffle]


def draw_owner_rank(key, part):
    return owner_table(key)


def draw_box_anchor(key, part):
    upper_ends = jnp.array([[CX - B + 1], [CY - B + 1], [CZ - B + 1]], jnp.int32)
    jitter = jax.random.randint(jax.random.fold_in(key, 13), (3, ATOMS), 0, upper_ends, dtype=jnp.int32)
    jitter = jitter.at[2, 0].set(CZ - B)
    jitter = jitter.at[0, 1].set(0)
    return jitter.astype(jnp.int32)


def plant(entries, own_key, low, largest):
    index_at = [jax.random.randint(jax.random.fold_in(own_key, axis), (), 0, length) for axis, length in enumerate(entries.shape)]
    main_axis = entries.shape.index(max(entries.shape))
    neighbour = index_at[:main_axis] + [(index_at[main_axis] + 1) % entries.shape[main_axis]] + index_at[main_axis + 1:]
    return entries.at[tuple(index_at)].set(low).at[tuple(neighbour)].set(largest)


def levels(key, extent, cuts, least, high):
    factor_of, own = 1.0, jax.random.fold_in(key, 6)
    for axis_at, blocks in cuts:
        steps = jnp.exp(jax.random.uniform(jax.random.fold_in(own, axis_at), (blocks,), jnp.float32, least / len(cuts), high / len(cuts)))
        factor_of = factor_of * jnp.repeat(steps, extent[axis_at] // blocks).reshape([-1 if axis == axis_at else 1 for axis in range(len(extent))])
    return factor_of


def bell_draw(key, shape, width, most, cuts=(), kind=jnp.bfloat16):
    values = width * jax.random.normal(key, shape, jnp.float32)
    if cuts:
        values = values * levels(key, shape, cuts, -0.22, 0.18)
    return jnp.clip(values, -most, most).astype(kind)


def setup_inputs(seed: int = 0) -> dict:
    seeds = jax.random.split(jax.random.key(seed), 8)
    return {
        "orbitals": bell_draw(seeds[0], (S, NX, NY, NZ), 1.0, 6.0, ((1, 4), (2, 4), (3, 2)), jnp.float32),
        "potential": jnp.clip(-2.0 + 2.0 * jax.random.uniform(seeds[1], (NX, NY, NZ), jnp.float32) ** levels(seeds[1], (NX, NY, NZ), ((0, 4), (1, 4), (2, 2)), -0.2, 0.2), -2.0, 0.0),
        "projectors": bell_draw(seeds[2], (ATOMS, NPROJ, B * B * B), 0.08, 0.5, ((0, 32),), jnp.float32),
        "owner_rank": draw_owner_rank(jax.random.fold_in(seeds[7], 71), 0),
        "box_anchor": draw_box_anchor(jax.random.fold_in(seeds[7], 71), 0),
        "box_extent": plant(jax.random.randint(seeds[5], (ATOMS,), B // 2, B + 1), jax.random.fold_in(seeds[5], 1), B // 2, B).astype(jnp.int32),
        "coupling": jnp.clip(jnp.exp(jax.random.uniform(seeds[6], (ATOMS, NPROJ), jnp.float32, math.log(0.5), math.log(3.0))), 0.5, 3.0),
    }


STENCIL = (-5369.0 / 1800.0, 12.0 / 7.0, -15.0 / 56.0, 10.0 / 189.0, -1.0 / 112.0, 2.0 / 1925.0, -1.0 / 16632.0)
SPACING = 0.5
LOW_EDGE = -2.5
CUTOFF = 4.0
UPPER = 60.0


def laplace_wrap(field):
    padded = jnp.pad(field, 6, mode="wrap")
    span_x, span_y, span_z = field.shape
    summed = 3.0 * STENCIL[0] * field
    for offset in range(1, 7):
        weight = STENCIL[offset]
        summed = summed + weight * (padded[6 + offset:6 + offset + span_x, 6:6 + span_y, 6:6 + span_z] + padded[6 - offset:6 - offset + span_x, 6:6 + span_y, 6:6 + span_z])
        summed = summed + weight * (padded[6:6 + span_x, 6 + offset:6 + offset + span_y, 6:6 + span_z] + padded[6:6 + span_x, 6 - offset:6 - offset + span_y, 6:6 + span_z])
        summed = summed + weight * (padded[6:6 + span_x, 6:6 + span_y, 6 + offset:6 + offset + span_z] + padded[6:6 + span_x, 6:6 + span_y, 6 - offset:6 - offset + span_z])
    return summed / (SPACING * SPACING)


def box_masks(box_extent):
    cell_offsets = jnp.arange(B, dtype=jnp.int32)
    limit = box_extent[:, None, None, None]
    inside = (cell_offsets[None, :, None, None] < limit) & (cell_offsets[None, None, :, None] < limit) & (cell_offsets[None, None, None, :] < limit)
    return inside.reshape(box_extent.shape[0], B * B * B).astype(jnp.float32)


def nonlocal_one(field, masked, corners, coupling):
    def add_atom(atom_index, nonlocal_sum):
        corner = (corners[0, atom_index].astype(jnp.int32), corners[1, atom_index].astype(jnp.int32), corners[2, atom_index].astype(jnp.int32))
        box_cells = lax.dynamic_slice(field, corner, (B, B, B)).reshape(B * B * B)
        coeffs = jnp.dot(masked[atom_index], box_cells, precision=lax.Precision.HIGHEST) * coupling[atom_index]
        addition = jnp.dot(coeffs, masked[atom_index], precision=lax.Precision.HIGHEST).reshape(B, B, B)
        current = lax.dynamic_slice(nonlocal_sum, corner, (B, B, B))
        return lax.dynamic_update_slice(nonlocal_sum, current + addition, corner)
    return lax.fori_loop(0, ATOMS, add_atom, jnp.zeros_like(field))


def reference(orbitals, potential, projectors, owner_rank, box_anchor, box_extent, coupling):
    masked = projectors * box_masks(box_extent)[:, None, :]
    own_x = owner_rank // (N_GY * N_GZ)
    own_y = (owner_rank // N_GZ) % N_GY
    own_z = owner_rank % N_GZ
    corners = (jnp.stack([own_x * CX, own_y * CY, own_z * CZ]) + box_anchor).astype(jnp.int32)

    def apply_h(field):
        return -0.5 * laplace_wrap(field) + potential * field + nonlocal_one(field, masked, corners, coupling)

    def filter_one(field):
        half_width = (UPPER - CUTOFF) / 2.0
        middle = (UPPER + CUTOFF) / 2.0
        sigma_one = half_width / (LOW_EDGE - middle)
        sigma_now = sigma_one
        result = (apply_h(field) - middle * field) * (sigma_one / half_width)
        previous = field
        for degree_step in range(1, DEGREE):
            sigma_next = 1.0 / (2.0 / sigma_one - sigma_now)
            next_state = (apply_h(result) - middle * result) * (2.0 * sigma_next / half_width) - (sigma_now * sigma_next) * previous
            previous = result
            result = next_state
            sigma_now = sigma_next
        return result

    filtered = lax.map(filter_one, orbitals)
    flattened = filtered.reshape(filtered.shape[0], -1)
    intersection = jnp.dot(flattened, flattened.T, precision=lax.Precision.HIGHEST) / (NX * NY * NZ)
    return filtered, intersection
```

```python
import functools
import jax
import jax.numpy as jnp
from jax import lax
from jax.experimental import pallas as pl
from jax.experimental.pallas import tpu as pltpu
import ml_dtypes
import numpy as np
from jax.sharding import PartitionSpec as P

B = 8
DEGREE = 4
ATOM_DEV = 8


STENCIL = (
    -5369.0 / 1800.0,
    12.0 / 7.0,
    -15.0 / 56.0,
    10.0 / 189.0,
    -1.0 / 112.0,
    2.0 / 1925.0,
    -1.0 / 16632.0,
)
SPACING = 0.5
LOW_EDGE = -2.5
CUTOFF = 4.0
UPPER = 60.0


def extended(cells, sides, width):
    for axis, dim in sides:
        count = lax.axis_size(axis)
        head = lax.slice_in_dim(cells, 0, width, axis=dim)
        tail = lax.slice_in_dim(cells, cells.shape[dim] - width, cells.shape[dim], axis=dim)
        cells = jnp.concatenate(
            [
                lax.ppermute(tail, axis, [(i, (i + 1) % count) for i in range(count)]),
                cells,
                lax.ppermute(head, axis, [((i + 1) % count, i) for i in range(count)]),
            ],
            axis=dim,
        )
    return cells


def laplace_padded(padded, shape):
    span_x, span_y, span_z = (shape[1], shape[2], shape[3])
    summed = 3.0 * STENCIL[0] * padded[:, 6 : 6 + span_x, 6 : 6 + span_y, 6 : 6 + span_z]
    for offset in range(1, 7):
        weight = STENCIL[offset]
        summed = summed + weight * (
            padded[:, 6 + offset : 6 + offset + span_x, 6 : 6 + span_y, 6 : 6 + span_z]
            + padded[:, 6 - offset : 6 - offset + span_x, 6 : 6 + span_y, 6 : 6 + span_z]
        )
        summed = summed + weight * (
            padded[:, 6 : 6 + span_x, 6 + offset : 6 + offset + span_y, 6 : 6 + span_z]
            + padded[:, 6 : 6 + span_x, 6 - offset : 6 - offset + span_y, 6 : 6 + span_z]
        )
        summed = summed + weight * (
            padded[:, 6 : 6 + span_x, 6 : 6 + span_y, 6 + offset : 6 + offset + span_z]
            + padded[:, 6 : 6 + span_x, 6 : 6 + span_y, 6 - offset : 6 - offset + span_z]
        )
    return summed / (SPACING * SPACING)


def collect_boxes(projectors, member, box_anchor, box_extent, coupling, capacity):
    member_int = member.astype(jnp.int32)
    slot_all = jnp.cumsum(member_int) - 1
    count = jnp.sum(member_int)
    slot_ids = jnp.arange(capacity, dtype=jnp.int32)
    onehot = ((slot_all[None, :] == slot_ids[:, None]) & member[None, :]).astype(jnp.float32)
    buffer = jnp.einsum(
        "cp,pkf->ckf",
        onehot,
        lax.all_gather(projectors, ("gx", "gy", "gz"), axis=0, tiled=True),
        precision=lax.Precision.HIGHEST,
    )
    hot_all = (slot_all[None, :] == slot_ids[:, None]) & member[None, :]
    slot_anchor = jnp.sum(jnp.where(hot_all[None, :, :], box_anchor[:, None, :], 0), axis=2)
    slot_extent = jnp.sum(jnp.where(hot_all, box_extent[None, :], 0), axis=1)
    slot_coupling = jnp.sum(jnp.where(hot_all[:, :, None], coupling[None, :, :], 0.0), axis=1)
    cell_offsets = jnp.arange(B, dtype=jnp.int32)
    limit = slot_extent[:, None, None, None]
    inside = (
        (cell_offsets[None, :, None, None] < limit)
        & (cell_offsets[None, None, :, None] < limit)
        & (cell_offsets[None, None, None, :] < limit)
    )
    buffer = buffer * inside.reshape(capacity, 1, B * B * B).astype(jnp.float32)
    return (buffer, slot_anchor, slot_coupling, count)


def nonlocal_term(field, buffer, slot_anchor, slot_coupling, count, domain_start):
    states = field.shape[0]

    def add_slot(slot_index, nonlocal_sum):
        corner = slot_anchor[:, slot_index] - domain_start
        start_cell = (0, corner[0], corner[1], corner[2])
        box_cells = lax.dynamic_slice(field, start_cell, (states, B, B, B)).reshape(
            states, B * B * B
        )
        proj_box = buffer[slot_index]
        coeffs = (
            jnp.dot(box_cells, proj_box.T, precision=lax.Precision.HIGHEST)
            * slot_coupling[slot_index][None, :]
        )
        addition = jnp.dot(coeffs, proj_box, precision=lax.Precision.HIGHEST).reshape(
            states, B, B, B
        )
        current = lax.dynamic_slice(nonlocal_sum, start_cell, (states, B, B, B))
        return lax.dynamic_update_slice(nonlocal_sum, current + addition, start_cell)

    return lax.fori_loop(0, count, add_slot, jnp.zeros_like(field))


def run_filter(field, apply_h):
    half_width = (UPPER - CUTOFF) / 2.0
    middle = (UPPER + CUTOFF) / 2.0
    sigma_one = half_width / (LOW_EDGE - middle)
    sigma_now = sigma_one
    result = (apply_h(field) - middle * field) * (sigma_one / half_width)
    previous = field
    for degree_step in range(1, DEGREE):
        sigma_next = 1.0 / (2.0 / sigma_one - sigma_now)
        next_state = (apply_h(result) - middle * result) * (
            2.0 * sigma_next / half_width
        ) - sigma_now * sigma_next * previous
        previous = result
        result = next_state
        sigma_now = sigma_next
    return result


def domain_body(orbitals, potential, projectors, owner_rank, box_anchor, box_extent, coupling):
    groups_y = lax.axis_size("gy")
    groups_z = lax.axis_size("gz")
    own_x = owner_rank // (groups_y * groups_z)
    own_y = owner_rank // groups_z % groups_y
    own_z = owner_rank % groups_z
    index_x = lax.axis_index("gx")
    index_y = lax.axis_index("gy")
    index_z = lax.axis_index("gz")
    span_x, span_y, span_z = (orbitals.shape[1], orbitals.shape[2], orbitals.shape[3])
    grid_anchor = jnp.stack([own_x * span_x, own_y * span_y, own_z * span_z]) + box_anchor
    member = (own_x == index_x) & (own_y == index_y) & (own_z == index_z)
    buffer, slot_anchor, slot_coupling, count = collect_boxes(
        projectors, member, grid_anchor, box_extent, coupling, 3 * ATOM_DEV
    )
    domain_start = jnp.stack([index_x * span_x, index_y * span_y, index_z * span_z])

    def apply_cube(field):
        padded = extended(field, (("gx", 1), ("gy", 2), ("gz", 3)), 6)
        return (
            -0.5 * laplace_padded(padded, field.shape)
            + potential[None] * field
            + nonlocal_term(field, buffer, slot_anchor, slot_coupling, count, domain_start)
        )

    filtered = run_filter(orbitals, apply_cube)
    flattened = filtered.reshape(filtered.shape[0], -1)
    partial_value = jnp.dot(flattened, flattened.T, precision=lax.Precision.HIGHEST)
    cells_total = span_x * span_y * span_z * lax.axis_size("gx") * groups_y * groups_z
    intersection = lax.psum(partial_value, ("gx", "gy", "gz")) / cells_total
    return (filtered, intersection)


SUB = 8
LANE = 128
NPROJ = 4


def split_terms(matrix):
    high = matrix.astype(ml_dtypes.bfloat16)
    low = (matrix - high.astype(np.float64)).astype(ml_dtypes.bfloat16)
    return np.concatenate([high, low], axis=0)


def ring_matrix(length):
    matrix = np.zeros((length, length))
    for offset in range(1, 7):
        weight = -0.5 * STENCIL[offset] / (SPACING * SPACING)
        for row in range(length):
            matrix[row, (row + offset) % length] += weight
            matrix[row, (row - offset) % length] += weight
    return matrix


def z_weights(groups_z):
    return split_terms(ring_matrix(groups_z * LANE))


def y_weights(groups_y):
    ring = ring_matrix(groups_y * SUB).reshape(groups_y, SUB, groups_y, SUB)
    full = np.einsum("aibj,xy->axibyj", ring, np.eye(SUB))
    return split_terms(full.reshape(groups_y * SUB * SUB, groups_y * SUB * SUB))


def split_pair(value):
    high = value.astype(jnp.bfloat16)
    low = (value - high.astype(jnp.float32)).astype(jnp.bfloat16)
    return high, low


def mxu(left, right):
    return jnp.dot(left, right, preferred_element_type=jnp.float32)


def box_window(anchor):
    lane = lax.broadcasted_iota(jnp.int32, (SUB, LANE), 1)
    return (lane - anchor) & (LANE - 1)


def filter_kernel(
    groups,
    owner,
    anchor,
    start,
    pack,
    coupling,
    zmat,
    ymat,
    out,
    state_a,
    state_b,
    rolled,
    added,
    boxes,
    coeffs,
    high_buf,
    low_buf,
    near,
):
    groups_x, groups_y, groups_z = groups
    domains = groups_x * groups_y * groups_z
    plane = groups_y * groups_z
    atom_groups = coupling.shape[0] // (2 * SUB)
    per_domain = atom_groups // domains
    half_width = (UPPER - CUTOFF) / 2.0
    middle = (UPPER + CUTOFF) / 2.0
    edge_z = groups_z * LANE
    edge_y = groups_y * SUB * SUB
    weights = [-0.5 * value / (SPACING * SPACING) for value in STENCIL]

    def proj_at(group, kp, row):
        return pack[group // per_domain, SUB + (group % per_domain) * 2 * SUB + kp * SUB + row]

    def apply_step(cur, prev, new, alpha, beta):
        def spread(dom, carry):
            for x in range(SUB):
                value = cur[dom, x]
                rolled[dom, x] = value if x == 0 else pltpu.roll(value, SUB * x, 1)
                added[dom, x] = jnp.zeros((SUB, LANE), jnp.float32)
            return carry

        lax.fori_loop(0, domains, spread, 0)

        lane = lax.broadcasted_iota(jnp.int32, (SUB, LANE), 1)
        lower = lane < LANE // 2

        def gather(group, carry):
            for pair in range(4):
                halves = []
                for par in range(2):
                    atom = group * SUB + pair * 2 + par
                    dom = owner[atom]
                    at = anchor[atom]
                    window = box_window(at)
                    parts = [rolled[dom, x] for x in range(SUB)]
                    for bit in (SUB, 2 * SUB, 4 * SUB):
                        odd = (window & bit) != 0
                        parts = [
                            jnp.where(odd, parts[i + 1], parts[i])
                            for i in range(0, len(parts), 2)
                        ]
                    turn = (LANE - at + (LANE // 2) * par) & (LANE - 1)
                    halves.append(pltpu.roll(parts[0], turn, 1))
                both = jnp.where(lower, halves[0], halves[1])
                for kpar in range(2):
                    boxes[pl.ds(group * SUB * SUB + kpar * 4 + pair, SUB, stride=SUB), :] = both
            return carry

        lax.fori_loop(0, atom_groups, gather, 0)

        def project(group, carry):
            base = group * SUB * SUB
            for kp in range(2):
                total = boxes[pl.ds(base, SUB), :] * proj_at(group, kp, 0)
                for row in range(1, SUB):
                    total = total + boxes[pl.ds(base + row * SUB, SUB), :] * proj_at(group, kp, row)
                coeffs[pl.ds(group * 2 * SUB + kp * SUB, SUB), :] = total
            return carry

        lax.fori_loop(0, atom_groups, project, 0)

        same = (
            lax.broadcasted_iota(jnp.int32, (LANE, LANE), 0) // (LANE // 2)
            == lax.broadcasted_iota(jnp.int32, (LANE, LANE), 1) // (LANE // 2)
        ).astype(jnp.float32).astype(jnp.bfloat16)
        high, low = split_pair(coeffs[...])
        coeffs[...] = (mxu(high, same) + mxu(low, same)) * coupling[...]

        def expand(group, carry):
            base = group * SUB * SUB
            first = coeffs[pl.ds(group * 2 * SUB, SUB), :]
            second = coeffs[pl.ds(group * 2 * SUB + SUB, SUB), :]
            for row in range(SUB):
                boxes[pl.ds(base + row * SUB, SUB), :] = first * proj_at(
                    group, 0, row
                ) + second * proj_at(group, 1, row)
            return carry

        lax.fori_loop(0, atom_groups, expand, 0)

        def scatter(group, carry):
            for pair in range(4):
                base = group * SUB * SUB + pair
                both = (
                    boxes[pl.ds(base, SUB, stride=SUB), :]
                    + boxes[pl.ds(base + 4, SUB, stride=SUB), :]
                )
                for par in range(2):
                    atom = group * SUB + pair * 2 + par
                    dom = owner[atom]
                    at = anchor[atom]
                    turned = pltpu.roll(both, (at + (LANE // 2) * par) & (LANE - 1), 1)
                    slot = box_window(at) >> 3
                    for x in range(SUB):
                        added[dom, x] = added[dom, x] + jnp.where(slot == x, turned, 0.0)
            return carry

        lax.fori_loop(0, atom_groups, scatter, 0)

        def combine(gx, carry):
            for gy in range(groups_y):
                for gz in range(groups_z):
                    dom = gx * plane + gy * groups_z + gz
                    high, low = split_pair(cur[dom].reshape(SUB * SUB, LANE))
                    rows = slice(gy * SUB * SUB, (gy + 1) * SUB * SUB)
                    lanes = slice(gz * LANE, (gz + 1) * LANE)
                    high_buf[rows, lanes] = high
                    low_buf[rows, lanes] = low
            high = high_buf[...]
            low = low_buf[...]
            near[...] = (
                mxu(high, zmat[:edge_z])
                + mxu(low, zmat[:edge_z])
                + mxu(high, zmat[edge_z:])
                + mxu(ymat[:edge_y], high)
                + mxu(ymat[:edge_y], low)
                + mxu(ymat[edge_y:], high)
            )
            for gy in range(groups_y):
                for gz in range(groups_z):
                    column = {}
                    for t in range(-6, SUB + 6):
                        away = gx + t // SUB
                        away = lax.rem(away + groups_x, groups_x)
                        column[t] = cur[away * plane + gy * groups_z + gz, t % SUB]
                    dom = gx * plane + gy * groups_z + gz
                    for x in range(SUB):
                        value = column[x]
                        total = near[
                            pl.ds(gy * SUB * SUB + x * SUB, SUB), pl.ds(gz * LANE, LANE)
                        ]
                        extra = added[dom, x]
                        total = total + (
                            extra if x == 0 else pltpu.roll(extra, LANE - SUB * x, 1)
                        )
                        for offset in range(1, 7):
                            total = total + weights[offset] * (
                                column[x + offset] + column[x - offset]
                            )
                        total = total + (pack[dom, x] + (3.0 * weights[0] - middle)) * value
                        total = total * alpha
                        if beta is not None:
                            total = total + beta * prev[dom, x]
                        new[dom, x] = total
            return carry

        lax.fori_loop(0, groups_x, combine, 0)

    sigma_one = half_width / (LOW_EDGE - middle)
    sigma_now = sigma_one
    apply_step(start, None, state_a, sigma_one / half_width, None)
    prev, cur = start, state_a
    for degree_step in range(1, DEGREE):
        sigma_next = 1.0 / (2.0 / sigma_one - sigma_now)
        if degree_step == DEGREE - 1:
            new = out
        else:
            new = state_b if cur is state_a else state_a
        apply_step(
            cur, prev, new, 2.0 * sigma_next / half_width, -sigma_now * sigma_next
        )
        prev, cur = cur, new
        sigma_now = sigma_next


def packed_projectors(projectors, extent):
    atoms = projectors.shape[0]
    cells = jnp.arange(B, dtype=jnp.int32)
    limit = extent[:, None, None, None]
    inside = (
        (cells[None, :, None, None] < limit)
        & (cells[None, None, :, None] < limit)
        & (cells[None, None, None, :] < limit)
    )
    masked = jnp.where(inside[:, None], projectors.reshape(atoms, NPROJ, B, B, B), 0.0)
    masked = masked.reshape(atoms // SUB, 4, 2, 2, 2, B, B, B)
    return masked.transpose(0, 3, 6, 4, 1, 2, 5, 7).reshape(atoms // SUB * 2 * B, SUB, LANE)


def packed_coupling(coupling):
    atoms = coupling.shape[0]
    parts = coupling.reshape(atoms // SUB, 4, 2, 2, 2).transpose(0, 3, 4, 1, 2)
    wide = jnp.broadcast_to(parts[..., None], parts.shape + (LANE // 2,))
    return wide.reshape(atoms * 2, LANE)


def filter_call(groups, owner, anchor, field, pack, coupling, interpret=False):
    groups_x, groups_y, groups_z = groups
    domains = groups_x * groups_y * groups_z
    atoms = owner.shape[0]
    shape = (domains, SUB, SUB, LANE)
    rows, lanes = groups_y * SUB * SUB, groups_z * LANE
    vmem = pl.BlockSpec(memory_space=pltpu.VMEM)
    smem = pl.BlockSpec(memory_space=pltpu.SMEM)
    return pl.pallas_call(
        functools.partial(filter_kernel, groups),
        out_shape=jax.ShapeDtypeStruct(shape, jnp.float32),
        in_specs=[smem, smem, vmem, vmem, vmem, vmem, vmem],
        out_specs=vmem,
        scratch_shapes=[
            pltpu.VMEM(shape, jnp.float32),
            pltpu.VMEM(shape, jnp.float32),
            pltpu.VMEM(shape, jnp.float32),
            pltpu.VMEM(shape, jnp.float32),
            pltpu.VMEM((atoms * SUB, LANE), jnp.float32),
            pltpu.VMEM((atoms * 2, LANE), jnp.float32),
            pltpu.VMEM((rows, lanes), jnp.bfloat16),
            pltpu.VMEM((rows, lanes), jnp.bfloat16),
            pltpu.VMEM((rows, lanes), jnp.float32),
        ],
        compiler_params=pltpu.CompilerParams(vmem_limit_bytes=48 * 1024 * 1024),
        interpret=interpret,
    )(
        owner,
        anchor,
        field,
        pack,
        coupling,
        jnp.asarray(z_weights(groups_z)),
        jnp.asarray(y_weights(groups_y)),
    )


def state_body(orbitals, potential, projectors, owner_rank, box_anchor, box_extent, coupling):
    axes = ("gx", "gy", "gz")
    groups = tuple(lax.axis_size(axis) for axis in axes)
    domains = groups[0] * groups[1] * groups[2]
    atoms_own = projectors.shape[0]
    me = (lax.axis_index("gx") * groups[1] + lax.axis_index("gy")) * groups[2] + lax.axis_index("gz")
    extent = lax.dynamic_slice(box_extent, (me * atoms_own,), (atoms_own,))
    pack = jnp.concatenate([potential, packed_projectors(projectors, extent)], axis=0)
    pack = lax.all_gather(pack, axes, axis=0, tiled=False)
    field = lax.all_to_all(orbitals, axes, split_axis=0, concat_axis=0, tiled=True)
    result = filter_call(
        groups, owner_rank, box_anchor[2], field, pack, packed_coupling(coupling)
    )
    filtered = lax.all_to_all(result, axes, split_axis=0, concat_axis=0, tiled=True)
    flattened = filtered.reshape(filtered.shape[0], -1)
    partial_value = jnp.dot(flattened, flattened.T, precision=lax.Precision.HIGHEST)
    cells_total = orbitals.shape[1] * orbitals.shape[2] * orbitals.shape[3] * domains
    intersection = lax.psum(partial_value, axes) / cells_total
    return (filtered, intersection)


def body(orbitals, potential, projectors, owner_rank, box_anchor, box_extent, coupling):
    domains = lax.axis_size("gx") * lax.axis_size("gy") * lax.axis_size("gz")
    whole_states = (
        orbitals.shape == (domains, SUB, SUB, LANE)
        and projectors.shape[0] % SUB == 0
        and projectors.shape[1] == NPROJ
    )
    chosen = state_body if whole_states else domain_body
    return chosen(
        orbitals, potential, projectors, owner_rank, box_anchor, box_extent, coupling
    )


def solution(mesh):
    return jax.shard_map(
        body,
        mesh=mesh,
        in_specs=(
            P(None, "gx", "gy", "gz"),
            P("gx", "gy", "gz"),
            P(("gx", "gy", "gz"), None, None),
            P(),
            P(),
            P(),
            P(),
        ),
        out_specs=(P(None, "gx", "gy", "gz"), P()),
        check_vma=False,
    )
```

```python
import functools
import jax
import jax.numpy as jnp
from jax import lax
from jax.experimental import pallas as pl
from jax.experimental.pallas import tpu as pltpu
import ml_dtypes
import numpy as np
from jax.sharding import PartitionSpec as P

B = 8
DEGREE = 4
ATOM_DEV = 8


STENCIL = (
    -5369.0 / 1800.0,
    12.0 / 7.0,
    -15.0 / 56.0,
    10.0 / 189.0,
    -1.0 / 112.0,
    2.0 / 1925.0,
    -1.0 / 16632.0,
)
SPACING = 0.5
LOW_EDGE = -2.5
CUTOFF = 4.0
UPPER = 60.0


def extended(cells, sides, width):
    for axis, dim in sides:
        count = lax.axis_size(axis)
        head = lax.slice_in_dim(cells, 0, width, axis=dim)
        tail = lax.slice_in_dim(cells, cells.shape[dim] - width, cells.shape[dim], axis=dim)
        cells = jnp.concatenate(
            [
                lax.ppermute(tail, axis, [(i, (i + 1) % count) for i in range(count)]),
                cells,
                lax.ppermute(head, axis, [((i + 1) % count, i) for i in range(count)]),
            ],
            axis=dim,
        )
    return cells


def laplace_padded(padded, shape):
    span_x, span_y, span_z = (shape[1], shape[2], shape[3])
    summed = 3.0 * STENCIL[0] * padded[:, 6 : 6 + span_x, 6 : 6 + span_y, 6 : 6 + span_z]
    for offset in range(1, 7):
        weight = STENCIL[offset]
        summed = summed + weight * (
            padded[:, 6 + offset : 6 + offset + span_x, 6 : 6 + span_y, 6 : 6 + span_z]
            + padded[:, 6 - offset : 6 - offset + span_x, 6 : 6 + span_y, 6 : 6 + span_z]
        )
        summed = summed + weight * (
            padded[:, 6 : 6 + span_x, 6 + offset : 6 + offset + span_y, 6 : 6 + span_z]
            + padded[:, 6 : 6 + span_x, 6 - offset : 6 - offset + span_y, 6 : 6 + span_z]
        )
        summed = summed + weight * (
            padded[:, 6 : 6 + span_x, 6 : 6 + span_y, 6 + offset : 6 + offset + span_z]
            + padded[:, 6 : 6 + span_x, 6 : 6 + span_y, 6 - offset : 6 - offset + span_z]
        )
    return summed / (SPACING * SPACING)


def collect_boxes(projectors, member, box_anchor, box_extent, coupling, capacity):
    member_int = member.astype(jnp.int32)
    slot_all = jnp.cumsum(member_int) - 1
    count = jnp.sum(member_int)
    slot_ids = jnp.arange(capacity, dtype=jnp.int32)
    onehot = ((slot_all[None, :] == slot_ids[:, None]) & member[None, :]).astype(jnp.float32)
    buffer = jnp.einsum(
        "cp,pkf->ckf",
        onehot,
        lax.all_gather(projectors, ("gx", "gy", "gz"), axis=0, tiled=True),
        precision=lax.Precision.HIGHEST,
    )
    hot_all = (slot_all[None, :] == slot_ids[:, None]) & member[None, :]
    slot_anchor = jnp.sum(jnp.where(hot_all[None, :, :], box_anchor[:, None, :], 0), axis=2)
    slot_extent = jnp.sum(jnp.where(hot_all, box_extent[None, :], 0), axis=1)
    slot_coupling = jnp.sum(jnp.where(hot_all[:, :, None], coupling[None, :, :], 0.0), axis=1)
    cell_offsets = jnp.arange(B, dtype=jnp.int32)
    limit = slot_extent[:, None, None, None]
    inside = (
        (cell_offsets[None, :, None, None] < limit)
        & (cell_offsets[None, None, :, None] < limit)
        & (cell_offsets[None, None, None, :] < limit)
    )
    buffer = buffer * inside.reshape(capacity, 1, B * B * B).astype(jnp.float32)
    return (buffer, slot_anchor, slot_coupling, count)


def nonlocal_term(field, buffer, slot_anchor, slot_coupling, count, domain_start):
    states = field.shape[0]

    def add_slot(slot_index, nonlocal_sum):
        corner = slot_anchor[:, slot_index] - domain_start
        start_cell = (0, corner[0], corner[1], corner[2])
        box_cells = lax.dynamic_slice(field, start_cell, (states, B, B, B)).reshape(
            states, B * B * B
        )
        proj_box = buffer[slot_index]
        coeffs = (
            jnp.dot(box_cells, proj_box.T, precision=lax.Precision.HIGHEST)
            * slot_coupling[slot_index][None, :]
        )
        addition = jnp.dot(coeffs, proj_box, precision=lax.Precision.HIGHEST).reshape(
            states, B, B, B
        )
        current = lax.dynamic_slice(nonlocal_sum, start_cell, (states, B, B, B))
        return lax.dynamic_update_slice(nonlocal_sum, current + addition, start_cell)

    return lax.fori_loop(0, count, add_slot, jnp.zeros_like(field))


def run_filter(field, apply_h):
    half_width = (UPPER - CUTOFF) / 2.0
    middle = (UPPER + CUTOFF) / 2.0
    sigma_one = half_width / (LOW_EDGE - middle)
    sigma_now = sigma_one
    result = (apply_h(field) - middle * field) * (sigma_one / half_width)
    previous = field
    for degree_step in range(1, DEGREE):
        sigma_next = 1.0 / (2.0 / sigma_one - sigma_now)
        next_state = (apply_h(result) - middle * result) * (
            2.0 * sigma_next / half_width
        ) - sigma_now * sigma_next * previous
        previous = result
        result = next_state
        sigma_now = sigma_next
    return result


def domain_body(orbitals, potential, projectors, owner_rank, box_anchor, box_extent, coupling):
    groups_y = lax.axis_size("gy")
    groups_z = lax.axis_size("gz")
    own_x = owner_rank // (groups_y * groups_z)
    own_y = owner_rank // groups_z % groups_y
    own_z = owner_rank % groups_z
    index_x = lax.axis_index("gx")
    index_y = lax.axis_index("gy")
    index_z = lax.axis_index("gz")
    span_x, span_y, span_z = (orbitals.shape[1], orbitals.shape[2], orbitals.shape[3])
    grid_anchor = jnp.stack([own_x * span_x, own_y * span_y, own_z * span_z]) + box_anchor
    member = (own_x == index_x) & (own_y == index_y) & (own_z == index_z)
    buffer, slot_anchor, slot_coupling, count = collect_boxes(
        projectors, member, grid_anchor, box_extent, coupling, 3 * ATOM_DEV
    )
    domain_start = jnp.stack([index_x * span_x, index_y * span_y, index_z * span_z])

    def apply_cube(field):
        padded = extended(field, (("gx", 1), ("gy", 2), ("gz", 3)), 6)
        return (
            -0.5 * laplace_padded(padded, field.shape)
            + potential[None] * field
            + nonlocal_term(field, buffer, slot_anchor, slot_coupling, count, domain_start)
        )

    filtered = run_filter(orbitals, apply_cube)
    flattened = filtered.reshape(filtered.shape[0], -1)
    partial_value = jnp.dot(flattened, flattened.T, precision=lax.Precision.HIGHEST)
    cells_total = span_x * span_y * span_z * lax.axis_size("gx") * groups_y * groups_z
    intersection = lax.psum(partial_value, ("gx", "gy", "gz")) / cells_total
    return (filtered, intersection)


SUB = 8
LANE = 128
HALF = LANE // 2
NPROJ = 4


def split_terms(matrix):
    high = matrix.astype(ml_dtypes.bfloat16)
    low = (matrix - high.astype(np.float64)).astype(ml_dtypes.bfloat16)
    return high, low


def stencil_weight(distance):
    if distance == 0 or abs(distance) > 6:
        return 0.0
    return -0.5 * STENCIL[abs(distance)] / (SPACING * SPACING)


def ring_matrix(length):
    matrix = np.zeros((length, length))
    for offset in range(-6, 7):
        for row in range(length):
            matrix[row, (row + offset) % length] += stencil_weight(offset)
    return matrix


def plane_weights(groups_y):
    slab = groups_y * HALF
    ring = ring_matrix(groups_y * SUB).reshape(groups_y, SUB, groups_y, SUB)
    blocks = []
    for shift in (-SUB, 0, SUB):
        along_x = np.array(
            [[stencil_weight(shift + i - o) for o in range(SUB)] for i in range(SUB)]
        )
        block = np.einsum("ab,io,jp->aijbop", np.eye(groups_y), along_x, np.eye(SUB))
        if shift == 0:
            block = block + np.einsum("ajbp,io->aijbop", ring, np.eye(SUB))
        blocks.append(block.reshape(slab, slab))
    high, low = split_terms(np.concatenate(blocks, axis=0))
    return np.concatenate([high, high, low], axis=0)


def depth_weights(groups_z):
    high, low = split_terms(ring_matrix(groups_z * LANE))
    return np.concatenate([high, low, high], axis=1)


def split_pair(value):
    high = value.astype(jnp.bfloat16)
    low = (value - high.astype(jnp.float32)).astype(jnp.bfloat16)
    return high, low


def mxu(left, right):
    return jnp.dot(left, right, preferred_element_type=jnp.float32)


def filter_kernel(groups, atoms, place, half, my_z, start, *refs):
    groups_x, groups_y, groups_z = groups
    packs = refs[:groups_z]
    coupling, plane, depth, out = refs[groups_z : groups_z + 4]
    field_a, field_b, field_c, local, added, boxes, coeffs, high_buf, low_buf, near = refs[
        groups_z + 4 :
    ]
    columns = groups_x * groups_y
    domains = columns * groups_z
    pairs = columns // 2
    span = groups_z * LANE
    slab = groups_y * HALF
    pairs_slab = groups_y // 2
    per_device = atoms // domains // SUB
    half_width = (UPPER - CUTOFF) / 2.0
    middle = (UPPER + CUTOFF) / 2.0
    diagonal = -0.5 * 3.0 * STENCIL[0] / (SPACING * SPACING) - middle
    lane = lax.broadcasted_iota(jnp.int32, (SUB, LANE), 1)
    lower = lane < HALF
    side = lane // HALF
    f32 = jnp.float32

    def depth_of(hop):
        return lax.rem(my_z[0] + (groups_z - hop), groups_z)

    for hop in range(groups_z):
        base = depth_of(hop) * LANE

        def lay_potential(pair, carry):
            for row in range(SUB):
                first = packs[hop][2 * pair, row]
                second = packs[hop][2 * pair + 1, row]
                at = pl.multiple_of(pair * span + base + row * SUB, SUB)
                local[pl.ds(at, SUB), :] = diagonal + jnp.where(
                    lower, first, pltpu.roll(second, HALF, 1)
                )
                at = pl.multiple_of(pair * span + base + HALF + row * SUB, SUB)
                local[pl.ds(at, SUB), :] = diagonal + jnp.where(
                    lower, pltpu.roll(first, HALF, 1), second
                )
            return carry

        lax.fori_loop(0, pairs, lay_potential, 0)

    def lay_field(pair, carry):
        for depth_at in range(groups_z):
            first = start[2 * pair * groups_z + depth_at].reshape(HALF, LANE)
            second = start[(2 * pair + 1) * groups_z + depth_at].reshape(HALF, LANE)
            turned = jnp.concatenate([first, second], axis=0).T
            at = pl.multiple_of(pair * span + depth_at * LANE, LANE)
            field_a[pl.ds(at, LANE), :] = turned
            high, low = split_pair(turned)
            cols = pl.ds(pl.multiple_of(pair * LANE, LANE), LANE)
            high_buf[depth_at * LANE : (depth_at + 1) * LANE, cols] = high
            low_buf[depth_at * LANE : (depth_at + 1) * LANE, cols] = low
            for spare in range(2):
                added[spare, pl.ds(at, LANE), :] = jnp.zeros((LANE, LANE), f32)
        return carry

    lax.fori_loop(0, pairs, lay_field, 0)

    ones = (
        (
            lax.broadcasted_iota(jnp.int32, (LANE, LANE), 0) // HALF
            == lax.broadcasted_iota(jnp.int32, (LANE, LANE), 1) // HALF
        )
        .astype(f32)
        .astype(jnp.bfloat16)
    )

    def each_group(visit):
        for hop in range(groups_z):
            depth_at = depth_of(hop)

            def step(column, carry):
                device = column * groups_z + depth_at
                for inner in range(per_device):
                    stored = (hop * columns + column) * per_device + inner
                    visit(
                        stored,
                        device * per_device + inner,
                        lambda kp, row: packs[hop][column, SUB + (inner * 2 + kp) * SUB + row],
                    )
                return carry

            lax.fori_loop(0, columns, step, 0)

    def apply_step(cur, prev, new, alpha, beta, last):
        def gather(stored, group, proj):
            for j in range(SUB):
                atom = group * SUB + j
                value = cur[pl.ds(place[atom], SUB), :]
                both = jnp.where(side == half[atom], value, pltpu.roll(value, HALF, 1))
                boxes[pl.ds(stored * SUB * SUB + j, SUB, stride=SUB), :] = both

        each_group(gather)

        def project(stored, group, proj):
            base = pl.multiple_of(stored * SUB * SUB, SUB * SUB)
            values = [boxes[pl.ds(base + row * SUB, SUB), :] for row in range(SUB)]
            for kp in range(2):
                terms = [values[row] * proj(kp, row) for row in range(SUB)]
                while len(terms) > 1:
                    terms = [terms[i] + terms[i + 1] for i in range(0, len(terms), 2)]
                at = pl.multiple_of(stored * 2 * SUB + kp * SUB, SUB)
                coeffs[pl.ds(at, SUB), :] = terms[0]

        each_group(project)

        high, low = split_pair(coeffs[...])
        coeffs[...] = mxu(high, ones) + mxu(low, ones)

        def expand(stored, group, proj):
            base = pl.multiple_of(stored * SUB * SUB, SUB * SUB)
            at = pl.multiple_of(stored * 2 * SUB, 2 * SUB)
            by = pl.multiple_of(group * 2 * SUB, 2 * SUB)
            first = coeffs[pl.ds(at, SUB), :] * coupling[pl.ds(by, SUB), :]
            second = coeffs[pl.ds(at + SUB, SUB), :] * coupling[pl.ds(by + SUB, SUB), :]
            for row in range(SUB):
                value = first * proj(0, row) + second * proj(1, row)
                boxes[pl.ds(base + row * SUB, SUB), :] = value + pltpu.roll(value, HALF, 1)

        each_group(expand)

        def scatter(stored, group, proj):
            for j in range(SUB):
                atom = group * SUB + j
                value = boxes[pl.ds(stored * SUB * SUB + j, SUB, stride=SUB), :]
                value = jnp.where(side == half[atom], value, 0.0)
                at = pl.ds(place[atom], SUB)
                added[j % 2, at, :] = added[j % 2, at, :] + value

        each_group(scatter)

        def product(slab_at, carry):
            def around(buf, shift):
                other = lax.rem(slab_at + shift + groups_x, groups_x)
                return buf[:, pl.ds(pl.multiple_of(other * slab, slab), slab)]

            high = [around(high_buf, shift) for shift in (-1, 0, 1)]
            low = [around(low_buf, shift) for shift in (-1, 0, 1)]
            left = jnp.concatenate(high + low + high + [depth[...]], axis=1)
            right = jnp.concatenate([plane[...], high[1], high[1], low[1]], axis=0)
            near[:, pl.ds(pl.multiple_of(slab_at * slab, slab), slab)] = mxu(left, right)
            return carry

        lax.fori_loop(0, groups_x, product, 0)

        def combine(pair, carry):
            for at_row in range(0, span, SUB):
                at = pl.multiple_of(pair * span + at_row, SUB)
                rows = pl.ds(at, SUB)
                cols = pl.ds(pl.multiple_of(pair * LANE, LANE), LANE)
                total = near[at_row : at_row + SUB, cols] + local[rows, :] * cur[rows, :]
                total = (total + (added[0, rows, :] + added[1, rows, :])) * alpha
                if beta is not None:
                    total = total + beta * prev[rows, :]
                new[rows, :] = total
                if not last:
                    for spare in range(2):
                        added[spare, rows, :] = jnp.zeros((SUB, LANE), f32)
            if not last:
                for at_row in range(0, span, 2 * SUB):
                    at = pl.multiple_of(pair * span + at_row, 2 * SUB)
                    cols = pl.ds(pl.multiple_of(pair * LANE, LANE), LANE)
                    high, low = split_pair(new[pl.ds(at, 2 * SUB), :])
                    high_buf[at_row : at_row + 2 * SUB, cols] = high
                    low_buf[at_row : at_row + 2 * SUB, cols] = low
            return carry

        lax.fori_loop(0, pairs, combine, 0)

    sigma_one = half_width / (LOW_EDGE - middle)
    sigma_now = sigma_one
    apply_step(field_a, None, field_b, sigma_one / half_width, None, DEGREE == 1)
    prev, cur, new = field_a, field_b, field_c
    for degree_step in range(1, DEGREE):
        sigma_next = 1.0 / (2.0 / sigma_one - sigma_now)
        apply_step(
            cur,
            prev,
            new,
            2.0 * sigma_next / half_width,
            -sigma_now * sigma_next,
            degree_step == DEGREE - 1,
        )
        prev, cur, new = cur, new, prev
        sigma_now = sigma_next

    def hand_back(pair, carry):
        for depth_at in range(groups_z):
            at = pl.multiple_of(pair * span + depth_at * LANE, LANE)
            turned = cur[pl.ds(at, LANE), :].T
            out[2 * pair * groups_z + depth_at] = turned[:HALF].reshape(SUB, SUB, LANE)
            out[(2 * pair + 1) * groups_z + depth_at] = turned[HALF:].reshape(SUB, SUB, LANE)
        return carry

    lax.fori_loop(0, pairs, hand_back, 0)


def packed_inputs(potential, projectors, extent):
    atoms = projectors.shape[0]
    cells = jnp.arange(B, dtype=jnp.int32)
    limit = extent[:, None, None, None]
    inside = (
        (cells[None, :, None, None] < limit)
        & (cells[None, None, :, None] < limit)
        & (cells[None, None, None, :] < limit)
    )
    masked = jnp.where(
        inside.reshape(atoms, 1, B * B * B), projectors, 0.0
    ).reshape(atoms // SUB, SUB, 2, 2, B * B, B)
    masked = masked.transpose(0, 2, 5, 1, 3, 4).reshape(atoms // SUB * 2 * B, SUB, LANE)
    shaped = potential.reshape(HALF, 2, HALF).transpose(2, 1, 0).reshape(SUB, SUB, LANE)
    return jnp.concatenate([shaped, masked], axis=0)


def packed_coupling(coupling):
    atoms = coupling.shape[0]
    parts = coupling.reshape(atoms // SUB, SUB, 2, 2).transpose(0, 2, 1, 3)
    wide = jnp.broadcast_to(parts[..., None], parts.shape + (HALF,))
    return wide.reshape(atoms * 2, LANE)


def box_places(groups, owner, anchor):
    groups_z = groups[2]
    column = owner // groups_z
    place = (column // 2 * groups_z + owner % groups_z) * LANE + anchor
    return place, column % 2


def filter_call(groups, place, half, my_z, field, packs, coupling, interpret=False):
    groups_x, groups_y, groups_z = groups
    columns = groups_x * groups_y
    atoms = place.shape[0]
    shape = (columns * groups_z, SUB, SUB, LANE)
    span = groups_z * LANE
    width = columns * HALF
    cells = (columns // 2 * span, LANE)
    vmem = pl.BlockSpec(memory_space=pltpu.VMEM)
    smem = pl.BlockSpec(memory_space=pltpu.SMEM)
    return pl.pallas_call(
        functools.partial(filter_kernel, groups, atoms),
        out_shape=jax.ShapeDtypeStruct(shape, jnp.float32),
        in_specs=[smem] * 3 + [vmem] * (groups_z + 4),
        out_specs=vmem,
        scratch_shapes=[
            pltpu.VMEM(cells, jnp.float32),
            pltpu.VMEM(cells, jnp.float32),
            pltpu.VMEM(cells, jnp.float32),
            pltpu.VMEM(cells, jnp.float32),
            pltpu.VMEM((2,) + cells, jnp.float32),
            pltpu.VMEM((atoms * SUB, LANE), jnp.float32),
            pltpu.VMEM((atoms * 2, LANE), jnp.float32),
            pltpu.VMEM((span, width), jnp.bfloat16),
            pltpu.VMEM((span, width), jnp.bfloat16),
            pltpu.VMEM((span, width), jnp.float32),
        ],
        compiler_params=pltpu.CompilerParams(vmem_limit_bytes=48 * 1024 * 1024),
        interpret=interpret,
    )(
        place,
        half,
        my_z,
        field,
        *packs,
        coupling,
        jnp.asarray(plane_weights(groups_y)),
        jnp.asarray(depth_weights(groups_z)),
    )


def state_body(orbitals, potential, projectors, owner_rank, box_anchor, box_extent, coupling):
    axes = ("gx", "gy", "gz")
    groups = tuple(lax.axis_size(axis) for axis in axes)
    groups_z = groups[2]
    domains = groups[0] * groups[1] * groups_z
    atoms_own = projectors.shape[0]
    my_z = lax.axis_index("gz")
    me = (lax.axis_index("gx") * groups[1] + lax.axis_index("gy")) * groups_z + my_z
    extent = lax.dynamic_slice(box_extent, (me * atoms_own,), (atoms_own,))
    pack = packed_inputs(potential, projectors, extent)
    pack = lax.all_gather(pack, ("gx", "gy"), axis=0, tiled=False)
    packs = [pack] + [
        lax.ppermute(pack, "gz", [(i, (i + hop) % groups_z) for i in range(groups_z)])
        for hop in range(1, groups_z)
    ]
    field = lax.all_to_all(orbitals, axes, split_axis=0, concat_axis=0, tiled=True)
    place, half = box_places(groups, owner_rank, box_anchor[2])
    result = filter_call(
        groups, place, half, my_z[None], field, packs, packed_coupling(coupling)
    )
    filtered = lax.all_to_all(result, axes, split_axis=0, concat_axis=0, tiled=True)
    states = filtered.shape[0]
    flattened = filtered.reshape(states, -1)
    partial_value = jnp.dot(flattened, flattened.T, precision=lax.Precision.HIGHEST)
    quarter = partial_value.reshape(-1, SUB, states).transpose(1, 0, 2).reshape(SUB, -1)
    parts = lax.all_to_all(
        jnp.broadcast_to(quarter[None], (domains,) + quarter.shape),
        axes,
        split_axis=0,
        concat_axis=0,
        tiled=True,
    )
    summed = jnp.sum(parts, axis=0).reshape(SUB, -1, states).transpose(1, 0, 2)
    cells_total = orbitals.shape[1] * orbitals.shape[2] * orbitals.shape[3] * domains
    intersection = summed.reshape(states, states) / cells_total
    return (filtered, intersection)


def body(orbitals, potential, projectors, owner_rank, box_anchor, box_extent, coupling):
    domains = lax.axis_size("gx") * lax.axis_size("gy") * lax.axis_size("gz")
    whole_states = (
        orbitals.shape == (domains, SUB, SUB, LANE)
        and projectors.shape[0] % SUB == 0
        and projectors.shape[1] == NPROJ
        and lax.axis_size("gy") % 2 == 0
    )
    chosen = state_body if whole_states else domain_body
    return chosen(
        orbitals, potential, projectors, owner_rank, box_anchor, box_extent, coupling
    )


def solution(mesh):
    return jax.shard_map(
        body,
        mesh=mesh,
        in_specs=(
            P(None, "gx", "gy", "gz"),
            P("gx", "gy", "gz"),
            P(("gx", "gy", "gz"), None, None),
            P(),
            P(),
            P(),
            P(),
        ),
        out_specs=(P(None, "gx", "gy", "gz"), P()),
        check_vma=False,
    )
```

```python
import functools
import jax
import jax.numpy as jnp
from jax import lax
from jax.experimental import pallas as pl
from jax.experimental.pallas import tpu as pltpu
import ml_dtypes
import numpy as np
from jax.sharding import PartitionSpec as P

B = 8
DEGREE = 4
ATOM_DEV = 8


STENCIL = (
    -5369.0 / 1800.0,
    12.0 / 7.0,
    -15.0 / 56.0,
    10.0 / 189.0,
    -1.0 / 112.0,
    2.0 / 1925.0,
    -1.0 / 16632.0,
)
SPACING = 0.5
LOW_EDGE = -2.5
CUTOFF = 4.0
UPPER = 60.0


def extended(cells, sides, width):
    for axis, dim in sides:
        count = lax.axis_size(axis)
        head = lax.slice_in_dim(cells, 0, width, axis=dim)
        tail = lax.slice_in_dim(cells, cells.shape[dim] - width, cells.shape[dim], axis=dim)
        cells = jnp.concatenate(
            [
                lax.ppermute(tail, axis, [(i, (i + 1) % count) for i in range(count)]),
                cells,
                lax.ppermute(head, axis, [((i + 1) % count, i) for i in range(count)]),
            ],
            axis=dim,
        )
    return cells


def laplace_padded(padded, shape):
    span_x, span_y, span_z = (shape[1], shape[2], shape[3])
    summed = 3.0 * STENCIL[0] * padded[:, 6 : 6 + span_x, 6 : 6 + span_y, 6 : 6 + span_z]
    for offset in range(1, 7):
        weight = STENCIL[offset]
        summed = summed + weight * (
            padded[:, 6 + offset : 6 + offset + span_x, 6 : 6 + span_y, 6 : 6 + span_z]
            + padded[:, 6 - offset : 6 - offset + span_x, 6 : 6 + span_y, 6 : 6 + span_z]
        )
        summed = summed + weight * (
            padded[:, 6 : 6 + span_x, 6 + offset : 6 + offset + span_y, 6 : 6 + span_z]
            + padded[:, 6 : 6 + span_x, 6 - offset : 6 - offset + span_y, 6 : 6 + span_z]
        )
        summed = summed + weight * (
            padded[:, 6 : 6 + span_x, 6 : 6 + span_y, 6 + offset : 6 + offset + span_z]
            + padded[:, 6 : 6 + span_x, 6 : 6 + span_y, 6 - offset : 6 - offset + span_z]
        )
    return summed / (SPACING * SPACING)


def collect_boxes(projectors, member, box_anchor, box_extent, coupling, capacity):
    member_int = member.astype(jnp.int32)
    slot_all = jnp.cumsum(member_int) - 1
    count = jnp.sum(member_int)
    slot_ids = jnp.arange(capacity, dtype=jnp.int32)
    onehot = ((slot_all[None, :] == slot_ids[:, None]) & member[None, :]).astype(jnp.float32)
    buffer = jnp.einsum(
        "cp,pkf->ckf",
        onehot,
        lax.all_gather(projectors, ("gx", "gy", "gz"), axis=0, tiled=True),
        precision=lax.Precision.HIGHEST,
    )
    hot_all = (slot_all[None, :] == slot_ids[:, None]) & member[None, :]
    slot_anchor = jnp.sum(jnp.where(hot_all[None, :, :], box_anchor[:, None, :], 0), axis=2)
    slot_extent = jnp.sum(jnp.where(hot_all, box_extent[None, :], 0), axis=1)
    slot_coupling = jnp.sum(jnp.where(hot_all[:, :, None], coupling[None, :, :], 0.0), axis=1)
    cell_offsets = jnp.arange(B, dtype=jnp.int32)
    limit = slot_extent[:, None, None, None]
    inside = (
        (cell_offsets[None, :, None, None] < limit)
        & (cell_offsets[None, None, :, None] < limit)
        & (cell_offsets[None, None, None, :] < limit)
    )
    buffer = buffer * inside.reshape(capacity, 1, B * B * B).astype(jnp.float32)
    return (buffer, slot_anchor, slot_coupling, count)


def nonlocal_term(field, buffer, slot_anchor, slot_coupling, count, domain_start):
    states = field.shape[0]

    def add_slot(slot_index, nonlocal_sum):
        corner = slot_anchor[:, slot_index] - domain_start
        start_cell = (0, corner[0], corner[1], corner[2])
        box_cells = lax.dynamic_slice(field, start_cell, (states, B, B, B)).reshape(
            states, B * B * B
        )
        proj_box = buffer[slot_index]
        coeffs = (
            jnp.dot(box_cells, proj_box.T, precision=lax.Precision.HIGHEST)
            * slot_coupling[slot_index][None, :]
        )
        addition = jnp.dot(coeffs, proj_box, precision=lax.Precision.HIGHEST).reshape(
            states, B, B, B
        )
        current = lax.dynamic_slice(nonlocal_sum, start_cell, (states, B, B, B))
        return lax.dynamic_update_slice(nonlocal_sum, current + addition, start_cell)

    return lax.fori_loop(0, count, add_slot, jnp.zeros_like(field))


def run_filter(field, apply_h):
    half_width = (UPPER - CUTOFF) / 2.0
    middle = (UPPER + CUTOFF) / 2.0
    sigma_one = half_width / (LOW_EDGE - middle)
    sigma_now = sigma_one
    result = (apply_h(field) - middle * field) * (sigma_one / half_width)
    previous = field
    for degree_step in range(1, DEGREE):
        sigma_next = 1.0 / (2.0 / sigma_one - sigma_now)
        next_state = (apply_h(result) - middle * result) * (
            2.0 * sigma_next / half_width
        ) - sigma_now * sigma_next * previous
        previous = result
        result = next_state
        sigma_now = sigma_next
    return result


def domain_body(orbitals, potential, projectors, owner_rank, box_anchor, box_extent, coupling):
    groups_y = lax.axis_size("gy")
    groups_z = lax.axis_size("gz")
    own_x = owner_rank // (groups_y * groups_z)
    own_y = owner_rank // groups_z % groups_y
    own_z = owner_rank % groups_z
    index_x = lax.axis_index("gx")
    index_y = lax.axis_index("gy")
    index_z = lax.axis_index("gz")
    span_x, span_y, span_z = (orbitals.shape[1], orbitals.shape[2], orbitals.shape[3])
    grid_anchor = jnp.stack([own_x * span_x, own_y * span_y, own_z * span_z]) + box_anchor
    member = (own_x == index_x) & (own_y == index_y) & (own_z == index_z)
    buffer, slot_anchor, slot_coupling, count = collect_boxes(
        projectors, member, grid_anchor, box_extent, coupling, 3 * ATOM_DEV
    )
    domain_start = jnp.stack([index_x * span_x, index_y * span_y, index_z * span_z])

    def apply_cube(field):
        padded = extended(field, (("gx", 1), ("gy", 2), ("gz", 3)), 6)
        return (
            -0.5 * laplace_padded(padded, field.shape)
            + potential[None] * field
            + nonlocal_term(field, buffer, slot_anchor, slot_coupling, count, domain_start)
        )

    filtered = run_filter(orbitals, apply_cube)
    flattened = filtered.reshape(filtered.shape[0], -1)
    partial_value = jnp.dot(flattened, flattened.T, precision=lax.Precision.HIGHEST)
    cells_total = span_x * span_y * span_z * lax.axis_size("gx") * groups_y * groups_z
    intersection = lax.psum(partial_value, ("gx", "gy", "gz")) / cells_total
    return (filtered, intersection)


SUB = 8
LANE = 128
HALF = LANE // 2
NPROJ = 4


def split_terms(matrix):
    high = matrix.astype(ml_dtypes.bfloat16)
    low = (matrix - high.astype(np.float64)).astype(ml_dtypes.bfloat16)
    return high, low


def stencil_weight(distance):
    if distance == 0 or abs(distance) > 6:
        return 0.0
    return -0.5 * STENCIL[abs(distance)] / (SPACING * SPACING)


def ring_matrix(length):
    matrix = np.zeros((length, length))
    for offset in range(-6, 7):
        for row in range(length):
            matrix[row, (row + offset) % length] += stencil_weight(offset)
    return matrix


def plane_weights(groups_y):
    slab = groups_y * HALF
    ring = ring_matrix(groups_y * SUB).reshape(groups_y, SUB, groups_y, SUB)
    blocks = []
    for shift in (-SUB, 0, SUB):
        along_x = np.array(
            [[stencil_weight(shift + i - o) for o in range(SUB)] for i in range(SUB)]
        )
        block = np.einsum("ab,io,jp->aijbop", np.eye(groups_y), along_x, np.eye(SUB))
        if shift == 0:
            block = block + np.einsum("ajbp,io->aijbop", ring, np.eye(SUB))
        blocks.append(block.reshape(slab, slab))
    high, low = split_terms(np.concatenate(blocks, axis=0))
    return np.concatenate([high, high, low], axis=0)


def depth_weights(groups_z):
    high, low = split_terms(ring_matrix(groups_z * LANE))
    return np.concatenate([high, low, high], axis=1)


def split_pair(value):
    high = value.astype(jnp.bfloat16)
    low = (value - high.astype(jnp.float32)).astype(jnp.bfloat16)
    return high, low


def mxu(left, right):
    return jnp.dot(left, right, preferred_element_type=jnp.float32)


def row_sums(values):
    row = lax.broadcasted_iota(jnp.int32, (SUB, LANE), 0)
    for stride in (1, 2, 4):
        keep = (row & stride) == 0
        values = [
            jnp.where(keep, one, two) + pltpu.roll(jnp.where(keep, two, one), stride, 0)
            for one, two in zip(values[0::2], values[1::2])
        ]
    return values[0]


SPARES = 2


def filter_kernel(groups, atoms, place, half, my_place, *refs):
    groups_x, groups_y, groups_z = groups
    pieces = groups_y * groups_z
    field_in = refs[0]
    packs_in = refs[1 : 1 + pieces]
    coupling_in, plane_in, depth_in, out = refs[1 + pieces : 5 + pieces]
    (
        field_a,
        field_b,
        field_c,
        local,
        added,
        coeffs,
        high_buf,
        low_buf,
        near,
        packs,
        coupling,
        plane,
        depth,
        in_sems,
        pack_sems,
        out_sems,
    ) = refs[5 + pieces :]
    columns = groups_x * groups_y
    domains = columns * groups_z
    pairs = columns // 2
    span = groups_z * LANE
    slab = groups_y * HALF
    per_device = atoms // domains // SUB
    half_width = (UPPER - CUTOFF) / 2.0
    middle = (UPPER + CUTOFF) / 2.0
    diagonal = -0.5 * 3.0 * STENCIL[0] / (SPACING * SPACING) - middle
    lane = lax.broadcasted_iota(jnp.int32, (SUB, LANE), 1)
    lower = lane < HALF
    side = lane // HALF
    f32 = jnp.float32

    loads = [
        pltpu.make_async_copy(source, target, in_sems.at[number])
        for number, (source, target) in enumerate(
            ((field_in, field_b), (plane_in, plane), (depth_in, depth), (coupling_in, coupling))
        )
    ]
    for load in loads:
        load.start()
    pack_loads = []
    for hop_z in range(groups_z):
        for hop_y in range(groups_y):
            source = packs_in[hop_z * groups_y + hop_y]
            for hop_x in range(groups_x):
                from_x = lax.rem(my_place[0] + (groups_x - hop_x), groups_x)
                from_y = lax.rem(my_place[1] + (groups_y - hop_y), groups_y)
                from_z = lax.rem(my_place[2] + (groups_z - hop_z), groups_z)
                device = (from_x * groups_y + from_y) * groups_z + from_z
                number = (hop_z * groups_y + hop_y) * groups_x + hop_x
                pack_loads.append(
                    pltpu.make_async_copy(
                        source.at[hop_x], packs.at[device], pack_sems.at[number]
                    )
                )
    for load in pack_loads:
        load.start()
    loads[0].wait()

    def split_rows(source, pair, first_row, rows):
        cols = pl.ds(pl.multiple_of(pair * LANE, LANE), LANE)
        for at_row in range(first_row, first_row + rows, 2 * SUB):
            at = pl.multiple_of(pair * span + at_row, 2 * SUB)
            high, low = split_pair(source[pl.ds(at, 2 * SUB), :])
            high_buf[at_row : at_row + 2 * SUB, cols] = high
            low_buf[at_row : at_row + 2 * SUB, cols] = low

    def block_rows(pair, parity, depth_at):
        return pl.multiple_of(((2 * pair + parity) * groups_z + depth_at) * HALF, HALF)

    def lay_field(pair, carry):
        for depth_at in range(groups_z):
            first = field_b[pl.ds(block_rows(pair, 0, depth_at), HALF), :]
            second = field_b[pl.ds(block_rows(pair, 1, depth_at), HALF), :]
            at = pl.multiple_of(pair * span + depth_at * LANE, LANE)
            field_a[pl.ds(at, LANE), :] = jnp.concatenate([first, second], axis=0).T
            for spare in range(SPARES):
                added[spare, pl.ds(at, LANE), :] = jnp.zeros((LANE, LANE), f32)
        split_rows(field_a, pair, 0, span)
        return carry

    lax.fori_loop(0, pairs, lay_field, 0)

    for load in loads[1:] + pack_loads:
        load.wait()

    def lay_potential(pair, carry):
        for depth_at in range(groups_z):
            for row in range(SUB):
                first = packs[2 * pair * groups_z + depth_at, row]
                second = packs[(2 * pair + 1) * groups_z + depth_at, row]
                at = pl.multiple_of(pair * span + depth_at * LANE + row * SUB, SUB)
                local[pl.ds(at, SUB), :] = diagonal + jnp.where(
                    lower, first, pltpu.roll(second, HALF, 1)
                )
                at = pl.multiple_of(at + HALF, SUB)
                local[pl.ds(at, SUB), :] = diagonal + jnp.where(
                    lower, pltpu.roll(first, HALF, 1), second
                )
        return carry

    lax.fori_loop(0, pairs, lay_potential, 0)

    ones = (
        (
            lax.broadcasted_iota(jnp.int32, (LANE, LANE), 0) // HALF
            == lax.broadcasted_iota(jnp.int32, (LANE, LANE), 1) // HALF
        )
        .astype(f32)
        .astype(jnp.bfloat16)
    )

    def slab_groups(slab_at):
        for number in range(groups_y * groups_z):
            device = slab_at * (groups_y * groups_z) + number
            for inner in range(per_device):
                yield device, inner

    def apply_step(cur, prev, new, alpha, beta, spill):
        last = spill is not None

        def product(slab_at, carry):
            def around(buf, shift):
                other = lax.rem(slab_at + shift + groups_x, groups_x)
                return buf[:, pl.ds(pl.multiple_of(other * slab, slab), slab)]

            high = [around(high_buf, shift) for shift in (-1, 0, 1)]
            low = [around(low_buf, shift) for shift in (-1, 0, 1)]
            left = jnp.concatenate(high + low + high + [depth[...]], axis=1)
            right = jnp.concatenate([plane[...], high[1], high[1], low[1]], axis=0)
            near[:, pl.ds(pl.multiple_of(slab_at * slab, slab), slab)] = mxu(left, right)

            for device, inner in slab_groups(slab_at):
                group = device * per_device + inner
                terms = ([], [])
                for j in range(SUB):
                    atom = group * SUB + j
                    value = cur[pl.ds(place[atom], SUB), :]
                    both = jnp.where(side == half[atom], value, pltpu.roll(value, HALF, 1))
                    for kp in range(2):
                        at = SUB + (inner * 2 + kp) * SUB + j
                        terms[kp].append(both * packs[device, at])
                for kp in range(2):
                    at = pl.multiple_of((group * 2 + kp) * SUB, SUB)
                    coeffs[pl.ds(at, SUB), :] = row_sums(terms[kp])
            return carry

        lax.fori_loop(0, groups_x, product, 0)

        high, low = split_pair(coeffs[...])
        coeffs[...] = (mxu(high, ones) + mxu(low, ones)) * coupling[...]

        def scatter(slab_at, carry):
            for device, inner in slab_groups(slab_at):
                group = device * per_device + inner
                for j in range(SUB):
                    atom = group * SUB + j
                    value = 0.0
                    for kp in range(2):
                        at = SUB + (inner * 2 + kp) * SUB + j
                        row = coeffs[pl.ds((group * 2 + kp) * SUB + j, 1), :]
                        value = value + jnp.broadcast_to(row, (SUB, LANE)) * packs[device, at]
                    value = value + pltpu.roll(value, HALF, 1)
                    value = jnp.where(side == half[atom], value, 0.0)
                    rows = pl.ds(place[atom], SUB)
                    added[j % SPARES, rows, :] = added[j % SPARES, rows, :] + value
            return carry

        lax.fori_loop(0, groups_x, scatter, 0)

        def combine(pair, carry):
            for at_row in range(0, span, SUB):
                at = pl.multiple_of(pair * span + at_row, SUB)
                rows = pl.ds(at, SUB)
                cols = pl.ds(pl.multiple_of(pair * LANE, LANE), LANE)
                total = near[at_row : at_row + SUB, cols] + local[rows, :] * cur[rows, :]
                for spare in range(SPARES):
                    total = total + added[spare, rows, :]
                    if not last:
                        added[spare, rows, :] = jnp.zeros((SUB, LANE), f32)
                total = total * alpha
                if beta is not None:
                    total = total + beta * prev[rows, :]
                new[rows, :] = total
            if not last:
                split_rows(new, pair, 0, span)
            else:
                for depth_at in range(groups_z):
                    at = pl.multiple_of(pair * span + depth_at * LANE, LANE)
                    turned = new[pl.ds(at, LANE), :].T
                    spill[pl.ds(block_rows(pair, 0, depth_at), HALF), :] = turned[:HALF]
                    spill[pl.ds(block_rows(pair, 1, depth_at), HALF), :] = turned[HALF:]
                rows = pl.ds(pl.multiple_of(pair * span, span), span)
                pltpu.make_async_copy(spill.at[rows], out.at[rows], out_sems.at[pair]).start()
            return carry

        lax.fori_loop(0, pairs, combine, 0)

    sigma_one = half_width / (LOW_EDGE - middle)
    sigma_now = sigma_one
    apply_step(field_a, None, field_b, sigma_one / half_width, None, None)
    prev, cur, new = field_a, field_b, field_c
    for degree_step in range(1, DEGREE):
        sigma_next = 1.0 / (2.0 / sigma_one - sigma_now)
        last = degree_step == DEGREE - 1
        target = prev if degree_step > 1 else new
        spare = new if degree_step > 1 else prev
        apply_step(
            cur,
            prev,
            target,
            2.0 * sigma_next / half_width,
            -sigma_now * sigma_next,
            spare if last else None,
        )
        prev, cur, new = cur, target, spare
        sigma_now = sigma_next

    def finish(pair, carry):
        rows = pl.ds(pl.multiple_of(pair * span, span), span)
        pltpu.make_async_copy(prev.at[rows], out.at[rows], out_sems.at[pair]).wait()
        return carry

    lax.fori_loop(0, pairs, finish, 0)


def packed_inputs(potential, projectors, extent):
    atoms = projectors.shape[0]
    cells = jnp.arange(B, dtype=jnp.int32)
    limit = extent[:, None, None, None]
    inside = (
        (cells[None, :, None, None] < limit)
        & (cells[None, None, :, None] < limit)
        & (cells[None, None, None, :] < limit)
    )
    masked = jnp.where(
        inside.reshape(atoms, 1, B * B * B), projectors, 0.0
    ).reshape(atoms // SUB, SUB, 2, 2, B * B, B)
    masked = masked.transpose(0, 2, 1, 5, 3, 4).reshape(atoms // SUB * 2 * B, SUB, LANE)
    shaped = potential.reshape(HALF, 2, HALF).transpose(2, 1, 0).reshape(SUB, SUB, LANE)
    return jnp.concatenate([shaped, masked], axis=0)


def packed_coupling(coupling):
    atoms = coupling.shape[0]
    parts = coupling.reshape(atoms // SUB, SUB, 2, 2).transpose(0, 2, 1, 3)
    wide = jnp.broadcast_to(parts[..., None], parts.shape + (HALF,))
    return wide.reshape(atoms * 2, LANE)


def box_places(groups, owner, anchor):
    groups_z = groups[2]
    column = owner // groups_z
    place = (column // 2 * groups_z + owner % groups_z) * LANE + anchor
    return place, column % 2


def filter_call(groups, place, half, my_place, field, packs, coupling, interpret=False):
    groups_x, groups_y, groups_z = groups
    columns = groups_x * groups_y
    atoms = place.shape[0]
    span = groups_z * LANE
    width = columns * HALF
    cells = (columns // 2 * span, LANE)
    plane = jnp.asarray(plane_weights(groups_y))
    depth = jnp.asarray(depth_weights(groups_z))
    anywhere = pl.BlockSpec(memory_space=pl.ANY)
    smem = pl.BlockSpec(memory_space=pltpu.SMEM)
    out = pl.pallas_call(
        functools.partial(filter_kernel, groups, atoms),
        out_shape=jax.ShapeDtypeStruct(cells, jnp.float32),
        in_specs=[smem] * 3 + [anywhere] * (len(packs) + 4),
        out_specs=anywhere,
        scratch_shapes=[
            pltpu.VMEM(cells, jnp.float32),
            pltpu.VMEM(cells, jnp.float32),
            pltpu.VMEM(cells, jnp.float32),
            pltpu.VMEM(cells, jnp.float32),
            pltpu.VMEM((SPARES,) + cells, jnp.float32),
            pltpu.VMEM((atoms * 2, LANE), jnp.float32),
            pltpu.VMEM((span, width), jnp.bfloat16),
            pltpu.VMEM((span, width), jnp.bfloat16),
            pltpu.VMEM((span, width), jnp.float32),
            pltpu.VMEM((columns * groups_z,) + packs[0].shape[1:], jnp.float32),
            pltpu.VMEM(coupling.shape, jnp.float32),
            pltpu.VMEM(plane.shape, plane.dtype),
            pltpu.VMEM(depth.shape, depth.dtype),
            pltpu.SemaphoreType.DMA((4,)),
            pltpu.SemaphoreType.DMA((columns * groups_z,)),
            pltpu.SemaphoreType.DMA((columns // 2,)),
        ],
        compiler_params=pltpu.CompilerParams(vmem_limit_bytes=48 * 1024 * 1024),
        interpret=interpret,
    )(place, half, my_place, field.reshape(cells), *packs, coupling, plane, depth)
    return out.reshape(field.shape)


def hops(value, axis):
    count = lax.axis_size(axis)
    return [value] + [
        lax.ppermute(value, axis, [(i, (i + hop) % count) for i in range(count)])
        for hop in range(1, count)
    ]


def state_body(orbitals, potential, projectors, owner_rank, box_anchor, box_extent, coupling):
    axes = ("gx", "gy", "gz")
    groups = tuple(lax.axis_size(axis) for axis in axes)
    groups_z = groups[2]
    domains = groups[0] * groups[1] * groups_z
    atoms_own = projectors.shape[0]
    my_place = jnp.stack([lax.axis_index(axis) for axis in axes])
    me = (my_place[0] * groups[1] + my_place[1]) * groups_z + my_place[2]
    extent = lax.dynamic_slice(box_extent, (me * atoms_own,), (atoms_own,))
    pack = packed_inputs(potential, projectors, extent)
    line = jnp.stack(hops(pack, "gx"))
    plane = hops(line, "gy")
    crossed = [hops(piece, "gz") for piece in plane]
    packs = [crossed[hop_y][hop_z] for hop_z in range(groups_z) for hop_y in range(groups[1])]
    field = lax.all_to_all(orbitals, axes, split_axis=0, concat_axis=0, tiled=True)
    place, half = box_places(groups, owner_rank, box_anchor[2])
    result = filter_call(
        groups, place, half, my_place, field, packs, packed_coupling(coupling)
    )
    filtered = lax.all_to_all(result, axes, split_axis=0, concat_axis=0, tiled=True)
    states = filtered.shape[0]
    flattened = filtered.reshape(states, -1)
    partial_value = jnp.dot(flattened, flattened.T, precision=lax.Precision.HIGHEST)
    quarter = partial_value.reshape(-1, SUB, states).transpose(1, 0, 2).reshape(SUB, -1)
    parts = lax.all_to_all(
        jnp.broadcast_to(quarter[None], (domains,) + quarter.shape),
        axes,
        split_axis=0,
        concat_axis=0,
        tiled=True,
    )
    summed = jnp.sum(parts, axis=0).reshape(SUB, -1, states).transpose(1, 0, 2)
    cells_total = orbitals.shape[1] * orbitals.shape[2] * orbitals.shape[3] * domains
    intersection = summed.reshape(states, states) / cells_total
    return (filtered, intersection)


def body(orbitals, potential, projectors, owner_rank, box_anchor, box_extent, coupling):
    domains = lax.axis_size("gx") * lax.axis_size("gy") * lax.axis_size("gz")
    whole_states = (
        orbitals.shape == (domains, SUB, SUB, LANE)
        and projectors.shape[0] % SUB == 0
        and projectors.shape[1] == NPROJ
        and lax.axis_size("gy") % 2 == 0
    )
    chosen = state_body if whole_states else domain_body
    return chosen(
        orbitals, potential, projectors, owner_rank, box_anchor, box_extent, coupling
    )


def solution(mesh):
    return jax.shard_map(
        body,
        mesh=mesh,
        in_specs=(
            P(None, "gx", "gy", "gz"),
            P("gx", "gy", "gz"),
            P(("gx", "gy", "gz"), None, None),
            P(),
            P(),
            P(),
            P(),
        ),
        out_specs=(P(None, "gx", "gy", "gz"), P()),
        check_vma=False,
    )
```

```python
import functools
import jax
import jax.numpy as jnp
from jax import lax
from jax.experimental import pallas as pl
from jax.experimental.pallas import tpu as pltpu
import ml_dtypes
import numpy as np
from jax.sharding import PartitionSpec as P

B = 8
DEGREE = 4
ATOM_DEV = 8


STENCIL = (
    -5369.0 / 1800.0,
    12.0 / 7.0,
    -15.0 / 56.0,
    10.0 / 189.0,
    -1.0 / 112.0,
    2.0 / 1925.0,
    -1.0 / 16632.0,
)
SPACING = 0.5
LOW_EDGE = -2.5
CUTOFF = 4.0
UPPER = 60.0


def extended(cells, sides, width):
    for axis, dim in sides:
        count = lax.axis_size(axis)
        head = lax.slice_in_dim(cells, 0, width, axis=dim)
        tail = lax.slice_in_dim(cells, cells.shape[dim] - width, cells.shape[dim], axis=dim)
        cells = jnp.concatenate(
            [
                lax.ppermute(tail, axis, [(i, (i + 1) % count) for i in range(count)]),
                cells,
                lax.ppermute(head, axis, [((i + 1) % count, i) for i in range(count)]),
            ],
            axis=dim,
        )
    return cells


def laplace_padded(padded, shape):
    span_x, span_y, span_z = (shape[1], shape[2], shape[3])
    summed = 3.0 * STENCIL[0] * padded[:, 6 : 6 + span_x, 6 : 6 + span_y, 6 : 6 + span_z]
    for offset in range(1, 7):
        weight = STENCIL[offset]
        summed = summed + weight * (
            padded[:, 6 + offset : 6 + offset + span_x, 6 : 6 + span_y, 6 : 6 + span_z]
            + padded[:, 6 - offset : 6 - offset + span_x, 6 : 6 + span_y, 6 : 6 + span_z]
        )
        summed = summed + weight * (
            padded[:, 6 : 6 + span_x, 6 + offset : 6 + offset + span_y, 6 : 6 + span_z]
            + padded[:, 6 : 6 + span_x, 6 - offset : 6 - offset + span_y, 6 : 6 + span_z]
        )
        summed = summed + weight * (
            padded[:, 6 : 6 + span_x, 6 : 6 + span_y, 6 + offset : 6 + offset + span_z]
            + padded[:, 6 : 6 + span_x, 6 : 6 + span_y, 6 - offset : 6 - offset + span_z]
        )
    return summed / (SPACING * SPACING)


def collect_boxes(projectors, member, box_anchor, box_extent, coupling, capacity):
    member_int = member.astype(jnp.int32)
    slot_all = jnp.cumsum(member_int) - 1
    count = jnp.sum(member_int)
    slot_ids = jnp.arange(capacity, dtype=jnp.int32)
    onehot = ((slot_all[None, :] == slot_ids[:, None]) & member[None, :]).astype(jnp.float32)
    buffer = jnp.einsum(
        "cp,pkf->ckf",
        onehot,
        lax.all_gather(projectors, ("gx", "gy", "gz"), axis=0, tiled=True),
        precision=lax.Precision.HIGHEST,
    )
    hot_all = (slot_all[None, :] == slot_ids[:, None]) & member[None, :]
    slot_anchor = jnp.sum(jnp.where(hot_all[None, :, :], box_anchor[:, None, :], 0), axis=2)
    slot_extent = jnp.sum(jnp.where(hot_all, box_extent[None, :], 0), axis=1)
    slot_coupling = jnp.sum(jnp.where(hot_all[:, :, None], coupling[None, :, :], 0.0), axis=1)
    cell_offsets = jnp.arange(B, dtype=jnp.int32)
    limit = slot_extent[:, None, None, None]
    inside = (
        (cell_offsets[None, :, None, None] < limit)
        & (cell_offsets[None, None, :, None] < limit)
        & (cell_offsets[None, None, None, :] < limit)
    )
    buffer = buffer * inside.reshape(capacity, 1, B * B * B).astype(jnp.float32)
    return (buffer, slot_anchor, slot_coupling, count)


def nonlocal_term(field, buffer, slot_anchor, slot_coupling, count, domain_start):
    states = field.shape[0]

    def add_slot(slot_index, nonlocal_sum):
        corner = slot_anchor[:, slot_index] - domain_start
        start_cell = (0, corner[0], corner[1], corner[2])
        box_cells = lax.dynamic_slice(field, start_cell, (states, B, B, B)).reshape(
            states, B * B * B
        )
        proj_box = buffer[slot_index]
        coeffs = (
            jnp.dot(box_cells, proj_box.T, precision=lax.Precision.HIGHEST)
            * slot_coupling[slot_index][None, :]
        )
        addition = jnp.dot(coeffs, proj_box, precision=lax.Precision.HIGHEST).reshape(
            states, B, B, B
        )
        current = lax.dynamic_slice(nonlocal_sum, start_cell, (states, B, B, B))
        return lax.dynamic_update_slice(nonlocal_sum, current + addition, start_cell)

    return lax.fori_loop(0, count, add_slot, jnp.zeros_like(field))


def run_filter(field, apply_h):
    half_width = (UPPER - CUTOFF) / 2.0
    middle = (UPPER + CUTOFF) / 2.0
    sigma_one = half_width / (LOW_EDGE - middle)
    sigma_now = sigma_one
    result = (apply_h(field) - middle * field) * (sigma_one / half_width)
    previous = field
    for degree_step in range(1, DEGREE):
        sigma_next = 1.0 / (2.0 / sigma_one - sigma_now)
        next_state = (apply_h(result) - middle * result) * (
            2.0 * sigma_next / half_width
        ) - sigma_now * sigma_next * previous
        previous = result
        result = next_state
        sigma_now = sigma_next
    return result


def domain_body(orbitals, potential, projectors, owner_rank, box_anchor, box_extent, coupling):
    groups_y = lax.axis_size("gy")
    groups_z = lax.axis_size("gz")
    own_x = owner_rank // (groups_y * groups_z)
    own_y = owner_rank // groups_z % groups_y
    own_z = owner_rank % groups_z
    index_x = lax.axis_index("gx")
    index_y = lax.axis_index("gy")
    index_z = lax.axis_index("gz")
    span_x, span_y, span_z = (orbitals.shape[1], orbitals.shape[2], orbitals.shape[3])
    grid_anchor = jnp.stack([own_x * span_x, own_y * span_y, own_z * span_z]) + box_anchor
    member = (own_x == index_x) & (own_y == index_y) & (own_z == index_z)
    buffer, slot_anchor, slot_coupling, count = collect_boxes(
        projectors, member, grid_anchor, box_extent, coupling, 3 * ATOM_DEV
    )
    domain_start = jnp.stack([index_x * span_x, index_y * span_y, index_z * span_z])

    def apply_cube(field):
        padded = extended(field, (("gx", 1), ("gy", 2), ("gz", 3)), 6)
        return (
            -0.5 * laplace_padded(padded, field.shape)
            + potential[None] * field
            + nonlocal_term(field, buffer, slot_anchor, slot_coupling, count, domain_start)
        )

    filtered = run_filter(orbitals, apply_cube)
    flattened = filtered.reshape(filtered.shape[0], -1)
    partial_value = jnp.dot(flattened, flattened.T, precision=lax.Precision.HIGHEST)
    cells_total = span_x * span_y * span_z * lax.axis_size("gx") * groups_y * groups_z
    intersection = lax.psum(partial_value, ("gx", "gy", "gz")) / cells_total
    return (filtered, intersection)


SUB = 8
LANE = 128
HALF = LANE // 2
NPROJ = 4


def split_terms(matrix):
    high = matrix.astype(ml_dtypes.bfloat16)
    low = (matrix - high.astype(np.float64)).astype(ml_dtypes.bfloat16)
    return high, low


def stencil_weight(distance):
    if distance == 0 or abs(distance) > 6:
        return 0.0
    return -0.5 * STENCIL[abs(distance)] / (SPACING * SPACING)


def ring_matrix(length):
    matrix = np.zeros((length, length))
    for offset in range(-6, 7):
        for row in range(length):
            matrix[row, (row + offset) % length] += stencil_weight(offset)
    return matrix


def plane_weights(groups_y):
    slab = groups_y * HALF
    ring = ring_matrix(groups_y * SUB).reshape(groups_y, SUB, groups_y, SUB)
    blocks = []
    for shift in (-SUB, 0, SUB):
        along_x = np.array(
            [[stencil_weight(shift + i - o) for o in range(SUB)] for i in range(SUB)]
        )
        block = np.einsum("ab,io,jp->aijbop", np.eye(groups_y), along_x, np.eye(SUB))
        if shift == 0:
            block = block + np.einsum("ajbp,io->aijbop", ring, np.eye(SUB))
        blocks.append(block.reshape(slab, slab))
    high, low = split_terms(np.concatenate(blocks, axis=0))
    return np.concatenate([high, low], axis=0)


def depth_weights(groups_z):
    high, low = split_terms(ring_matrix(groups_z * LANE))
    return np.concatenate([high, low, high], axis=1)


def split_pair(value):
    high = value.astype(jnp.bfloat16)
    low = (value - high.astype(jnp.float32)).astype(jnp.bfloat16)
    return high, low


def mxu(left, right):
    return jnp.dot(left, right, preferred_element_type=jnp.float32)


def row_sums(values):
    row = lax.broadcasted_iota(jnp.int32, (SUB, LANE), 0)
    for stride in (1, 2, 4):
        keep = (row & stride) == 0
        values = [
            jnp.where(keep, one, two) + pltpu.roll(jnp.where(keep, two, one), stride, 0)
            for one, two in zip(values[0::2], values[1::2])
        ]
    return values[0]


SPARES = 2


def filter_kernel(groups, atoms, place, half, my_place, *refs):
    groups_x, groups_y, groups_z = groups
    pieces = groups_y * groups_z
    field_in = refs[0]
    packs_in = refs[1 : 1 + pieces]
    coupling_in, plane_in, depth_in, out = refs[1 + pieces : 5 + pieces]
    (
        field_a,
        field_b,
        field_c,
        local,
        added,
        coeffs,
        high_buf,
        low_buf,
        near,
        packs,
        coupling,
        plane,
        depth,
        in_sems,
        pack_sems,
        out_sems,
    ) = refs[5 + pieces :]
    columns = groups_x * groups_y
    domains = columns * groups_z
    pairs = columns // 2
    span = groups_z * LANE
    slab = groups_y * HALF
    per_device = atoms // domains // SUB
    half_width = (UPPER - CUTOFF) / 2.0
    middle = (UPPER + CUTOFF) / 2.0
    diagonal = -0.5 * 3.0 * STENCIL[0] / (SPACING * SPACING) - middle
    lane = lax.broadcasted_iota(jnp.int32, (SUB, LANE), 1)
    lower = lane < HALF
    side = lane // HALF
    f32 = jnp.float32

    loads = [
        pltpu.make_async_copy(source, target, in_sems.at[number])
        for number, (source, target) in enumerate(
            ((field_in, field_b), (plane_in, plane), (depth_in, depth), (coupling_in, coupling))
        )
    ]
    for load in loads:
        load.start()
    pack_loads = []
    for hop_z in range(groups_z):
        for hop_y in range(groups_y):
            source = packs_in[hop_z * groups_y + hop_y]
            for hop_x in range(groups_x):
                from_x = lax.rem(my_place[0] + (groups_x - hop_x), groups_x)
                from_y = lax.rem(my_place[1] + (groups_y - hop_y), groups_y)
                from_z = lax.rem(my_place[2] + (groups_z - hop_z), groups_z)
                device = (from_x * groups_y + from_y) * groups_z + from_z
                number = (hop_z * groups_y + hop_y) * groups_x + hop_x
                pack_loads.append(
                    pltpu.make_async_copy(
                        source.at[hop_x], packs.at[device], pack_sems.at[number]
                    )
                )
    for load in pack_loads:
        load.start()
    loads[0].wait()

    def split_rows(source, pair, first_row, rows):
        cols = pl.ds(pl.multiple_of(pair * LANE, LANE), LANE)
        for at_row in range(first_row, first_row + rows, 2 * SUB):
            at = pl.multiple_of(pair * span + at_row, 2 * SUB)
            high, low = split_pair(source[pl.ds(at, 2 * SUB), :])
            high_buf[at_row : at_row + 2 * SUB, cols] = high
            low_buf[at_row : at_row + 2 * SUB, cols] = low

    def block_rows(pair, parity, depth_at):
        return pl.multiple_of(((2 * pair + parity) * groups_z + depth_at) * HALF, HALF)

    def lay_field(pair, carry):
        for depth_at in range(groups_z):
            first = field_b[pl.ds(block_rows(pair, 0, depth_at), HALF), :]
            second = field_b[pl.ds(block_rows(pair, 1, depth_at), HALF), :]
            at = pl.multiple_of(pair * span + depth_at * LANE, LANE)
            field_a[pl.ds(at, LANE), :] = jnp.concatenate([first, second], axis=0).T
            for spare in range(SPARES):
                added[spare, pl.ds(at, LANE), :] = jnp.zeros((LANE, LANE), f32)
        split_rows(field_a, pair, 0, span)
        return carry

    lax.fori_loop(0, pairs, lay_field, 0)

    for load in loads[1:] + pack_loads:
        load.wait()

    def lay_potential(pair, carry):
        for depth_at in range(groups_z):
            for row in range(SUB):
                first = packs[2 * pair * groups_z + depth_at, row]
                second = packs[(2 * pair + 1) * groups_z + depth_at, row]
                at = pl.multiple_of(pair * span + depth_at * LANE + row * SUB, SUB)
                local[pl.ds(at, SUB), :] = diagonal + jnp.where(
                    lower, first, pltpu.roll(second, HALF, 1)
                )
                at = pl.multiple_of(at + HALF, SUB)
                local[pl.ds(at, SUB), :] = diagonal + jnp.where(
                    lower, pltpu.roll(first, HALF, 1), second
                )
        return carry

    lax.fori_loop(0, pairs, lay_potential, 0)

    ones = (
        (
            lax.broadcasted_iota(jnp.int32, (LANE, LANE), 0) // HALF
            == lax.broadcasted_iota(jnp.int32, (LANE, LANE), 1) // HALF
        )
        .astype(f32)
        .astype(jnp.bfloat16)
    )

    def slab_groups(slab_at):
        for number in range(groups_y * groups_z):
            device = slab_at * (groups_y * groups_z) + number
            for inner in range(per_device):
                yield device, inner

    def slab_of(buf, slab_at):
        return buf[:, pl.ds(pl.multiple_of(slab_at * slab, slab), slab)]

    def apply_step(cur, prev, new, alpha, beta, spill):
        last = spill is not None

        def product(slab_at, carry):
            def around(buf, shift):
                return slab_of(buf, lax.rem(slab_at + shift + groups_x, groups_x))

            high = [around(high_buf, shift) for shift in (-1, 0, 1)]
            low = [around(low_buf, shift) for shift in (-1, 0, 1)]
            left = jnp.concatenate(high + low, axis=1)
            right = jnp.concatenate([plane[: 3 * slab], plane[: 3 * slab]], axis=0)
            near[:, pl.ds(pl.multiple_of(slab_at * slab, slab), slab)] = mxu(left, right)

            for device, inner in slab_groups(slab_at):
                group = device * per_device + inner
                terms = ([], [])
                for j in range(SUB):
                    atom = group * SUB + j
                    value = cur[pl.ds(place[atom], SUB), :]
                    both = jnp.where(side == half[atom], value, pltpu.roll(value, HALF, 1))
                    for kp in range(2):
                        at = SUB + (inner * 2 + kp) * SUB + j
                        terms[kp].append(both * packs[device, at])
                for kp in range(2):
                    at = pl.multiple_of((group * 2 + kp) * SUB, SUB)
                    coeffs[pl.ds(at, SUB), :] = row_sums(terms[kp])
            return carry

        lax.fori_loop(0, groups_x, product, 0)

        high, low = split_pair(coeffs[...])
        coeffs[...] = (mxu(high, ones) + mxu(low, ones)) * coupling[...]

        def scatter(slab_at, carry):
            high = [
                slab_of(high_buf, lax.rem(slab_at + shift + groups_x, groups_x))
                for shift in (-1, 0, 1)
            ]
            left = jnp.concatenate(high + [depth[...]], axis=1)
            right = jnp.concatenate(
                [plane[3 * slab :], high[1], high[1], slab_of(low_buf, slab_at)], axis=0
            )
            at = pl.ds(pl.multiple_of(slab_at * slab, slab), slab)
            near[:, at] = near[:, at] + mxu(left, right)

            for device, inner in slab_groups(slab_at):
                group = device * per_device + inner
                for j in range(SUB):
                    atom = group * SUB + j
                    value = 0.0
                    for kp in range(2):
                        at = SUB + (inner * 2 + kp) * SUB + j
                        row = coeffs[pl.ds((group * 2 + kp) * SUB + j, 1), :]
                        value = value + jnp.broadcast_to(row, (SUB, LANE)) * packs[device, at]
                    value = value + pltpu.roll(value, HALF, 1)
                    value = jnp.where(side == half[atom], value, 0.0)
                    rows = pl.ds(place[atom], SUB)
                    added[j % SPARES, rows, :] = added[j % SPARES, rows, :] + value
            return carry

        lax.fori_loop(0, groups_x, scatter, 0)

        def combine(pair, carry):
            for at_row in range(0, span, SUB):
                at = pl.multiple_of(pair * span + at_row, SUB)
                rows = pl.ds(at, SUB)
                cols = pl.ds(pl.multiple_of(pair * LANE, LANE), LANE)
                total = near[at_row : at_row + SUB, cols] + local[rows, :] * cur[rows, :]
                for spare in range(SPARES):
                    total = total + added[spare, rows, :]
                    if not last:
                        added[spare, rows, :] = jnp.zeros((SUB, LANE), f32)
                total = total * alpha
                if beta is not None:
                    total = total + beta * prev[rows, :]
                new[rows, :] = total
            if not last:
                split_rows(new, pair, 0, span)
            else:
                for depth_at in range(groups_z):
                    at = pl.multiple_of(pair * span + depth_at * LANE, LANE)
                    turned = new[pl.ds(at, LANE), :].T
                    spill[pl.ds(block_rows(pair, 0, depth_at), HALF), :] = turned[:HALF]
                    spill[pl.ds(block_rows(pair, 1, depth_at), HALF), :] = turned[HALF:]
                rows = pl.ds(pl.multiple_of(pair * span, span), span)
                pltpu.make_async_copy(spill.at[rows], out.at[rows], out_sems.at[pair]).start()
            return carry

        lax.fori_loop(0, pairs, combine, 0)

    sigma_one = half_width / (LOW_EDGE - middle)
    sigma_now = sigma_one
    apply_step(field_a, None, field_b, sigma_one / half_width, None, None)
    prev, cur, new = field_a, field_b, field_c
    for degree_step in range(1, DEGREE):
        sigma_next = 1.0 / (2.0 / sigma_one - sigma_now)
        last = degree_step == DEGREE - 1
        target = prev if degree_step > 1 else new
        spare = new if degree_step > 1 else prev
        apply_step(
            cur,
            prev,
            target,
            2.0 * sigma_next / half_width,
            -sigma_now * sigma_next,
            spare if last else None,
        )
        prev, cur, new = cur, target, spare
        sigma_now = sigma_next

    def finish(pair, carry):
        rows = pl.ds(pl.multiple_of(pair * span, span), span)
        pltpu.make_async_copy(prev.at[rows], out.at[rows], out_sems.at[pair]).wait()
        return carry

    lax.fori_loop(0, pairs, finish, 0)


def packed_inputs(potential, projectors, extent):
    atoms = projectors.shape[0]
    cells = jnp.arange(B, dtype=jnp.int32)
    limit = extent[:, None, None, None]
    inside = (
        (cells[None, :, None, None] < limit)
        & (cells[None, None, :, None] < limit)
        & (cells[None, None, None, :] < limit)
    )
    masked = jnp.where(
        inside.reshape(atoms, 1, B * B * B), projectors, 0.0
    ).reshape(atoms // SUB, SUB, 2, 2, B * B, B)
    masked = masked.transpose(0, 2, 1, 5, 3, 4).reshape(atoms // SUB * 2 * B, SUB, LANE)
    shaped = potential.reshape(HALF, 2, HALF).transpose(2, 1, 0).reshape(SUB, SUB, LANE)
    return jnp.concatenate([shaped, masked], axis=0)


def packed_coupling(coupling):
    atoms = coupling.shape[0]
    parts = coupling.reshape(atoms // SUB, SUB, 2, 2).transpose(0, 2, 1, 3)
    wide = jnp.broadcast_to(parts[..., None], parts.shape + (HALF,))
    return wide.reshape(atoms * 2, LANE)


def box_places(groups, owner, anchor):
    groups_z = groups[2]
    column = owner // groups_z
    place = (column // 2 * groups_z + owner % groups_z) * LANE + anchor
    return place, column % 2


def filter_call(groups, place, half, my_place, field, packs, coupling, interpret=False):
    groups_x, groups_y, groups_z = groups
    columns = groups_x * groups_y
    atoms = place.shape[0]
    span = groups_z * LANE
    width = columns * HALF
    cells = (columns // 2 * span, LANE)
    plane = jnp.asarray(plane_weights(groups_y))
    depth = jnp.asarray(depth_weights(groups_z))
    anywhere = pl.BlockSpec(memory_space=pl.ANY)
    smem = pl.BlockSpec(memory_space=pltpu.SMEM)
    out = pl.pallas_call(
        functools.partial(filter_kernel, groups, atoms),
        out_shape=jax.ShapeDtypeStruct(cells, jnp.float32),
        in_specs=[smem] * 3 + [anywhere] * (len(packs) + 4),
        out_specs=anywhere,
        scratch_shapes=[
            pltpu.VMEM(cells, jnp.float32),
            pltpu.VMEM(cells, jnp.float32),
            pltpu.VMEM(cells, jnp.float32),
            pltpu.VMEM(cells, jnp.float32),
            pltpu.VMEM((SPARES,) + cells, jnp.float32),
            pltpu.VMEM((atoms * 2, LANE), jnp.float32),
            pltpu.VMEM((span, width), jnp.bfloat16),
            pltpu.VMEM((span, width), jnp.bfloat16),
            pltpu.VMEM((span, width), jnp.float32),
            pltpu.VMEM((columns * groups_z,) + packs[0].shape[1:], jnp.float32),
            pltpu.VMEM(coupling.shape, jnp.float32),
            pltpu.VMEM(plane.shape, plane.dtype),
            pltpu.VMEM(depth.shape, depth.dtype),
            pltpu.SemaphoreType.DMA((4,)),
            pltpu.SemaphoreType.DMA((columns * groups_z,)),
            pltpu.SemaphoreType.DMA((columns // 2,)),
        ],
        compiler_params=pltpu.CompilerParams(vmem_limit_bytes=20 * 1024 * 1024),
        interpret=interpret,
    )(place, half, my_place, field.reshape(cells), *packs, coupling, plane, depth)
    return out.reshape(field.shape)


def hops(value, axis):
    count = lax.axis_size(axis)
    return [value] + [
        lax.ppermute(value, axis, [(i, (i + hop) % count) for i in range(count)])
        for hop in range(1, count)
    ]


def state_body(orbitals, potential, projectors, owner_rank, box_anchor, box_extent, coupling):
    axes = ("gx", "gy", "gz")
    groups = tuple(lax.axis_size(axis) for axis in axes)
    groups_z = groups[2]
    domains = groups[0] * groups[1] * groups_z
    atoms_own = projectors.shape[0]
    my_place = jnp.stack([lax.axis_index(axis) for axis in axes])
    me = (my_place[0] * groups[1] + my_place[1]) * groups_z + my_place[2]
    extent = lax.dynamic_slice(box_extent, (me * atoms_own,), (atoms_own,))
    pack = packed_inputs(potential, projectors, extent)
    line = jnp.stack(hops(pack, "gx"))
    plane = hops(line, "gy")
    swapped = hops(line, "gz")
    orbitals, swapped = lax.optimization_barrier((orbitals, swapped))
    crossed = [swapped] + [hops(piece, "gz") for piece in plane[1:]]
    packs = [crossed[hop_y][hop_z] for hop_z in range(groups_z) for hop_y in range(groups[1])]
    field = lax.all_to_all(orbitals, axes, split_axis=0, concat_axis=0, tiled=True)
    place, half = box_places(groups, owner_rank, box_anchor[2])
    result = filter_call(
        groups, place, half, my_place, field, packs, packed_coupling(coupling)
    )
    filtered = lax.all_to_all(result, axes, split_axis=0, concat_axis=0, tiled=True)
    states = filtered.shape[0]
    flattened = filtered.reshape(states, -1)
    partial_value = jnp.dot(flattened, flattened.T, precision=lax.Precision.HIGHEST)
    quarter = partial_value.reshape(-1, SUB, states).transpose(1, 0, 2).reshape(SUB, -1)
    parts = lax.all_to_all(
        jnp.broadcast_to(quarter[None], (domains,) + quarter.shape),
        axes,
        split_axis=0,
        concat_axis=0,
        tiled=True,
    )
    summed = jnp.sum(parts, axis=0).reshape(SUB, -1, states).transpose(1, 0, 2)
    cells_total = orbitals.shape[1] * orbitals.shape[2] * orbitals.shape[3] * domains
    intersection = summed.reshape(states, states) / cells_total
    return (filtered, intersection)


def body(orbitals, potential, projectors, owner_rank, box_anchor, box_extent, coupling):
    domains = lax.axis_size("gx") * lax.axis_size("gy") * lax.axis_size("gz")
    whole_states = (
        orbitals.shape == (domains, SUB, SUB, LANE)
        and projectors.shape[0] % SUB == 0
        and projectors.shape[1] == NPROJ
        and lax.axis_size("gy") % 2 == 0
    )
    chosen = state_body if whole_states else domain_body
    return chosen(
        orbitals, potential, projectors, owner_rank, box_anchor, box_extent, coupling
    )


def solution(mesh):
    return jax.shard_map(
        body,
        mesh=mesh,
        in_specs=(
            P(None, "gx", "gy", "gz"),
            P("gx", "gy", "gz"),
            P(("gx", "gy", "gz"), None, None),
            P(),
            P(),
            P(),
            P(),
        ),
        out_specs=(P(None, "gx", "gy", "gz"), P()),
        check_vma=False,
    )
```

```python
import functools
import math
import jax
import jax.numpy as jnp
from jax import lax
from jax.experimental import pallas as pl
from jax.experimental.pallas import tpu as pltpu
import ml_dtypes
import numpy as np
from jax.sharding import PartitionSpec as P

B = 8
DEGREE = 4
ATOM_DEV = 8


STENCIL = (
    -5369.0 / 1800.0,
    12.0 / 7.0,
    -15.0 / 56.0,
    10.0 / 189.0,
    -1.0 / 112.0,
    2.0 / 1925.0,
    -1.0 / 16632.0,
)
SPACING = 0.5
LOW_EDGE = -2.5
CUTOFF = 4.0
UPPER = 60.0


def extended(cells, sides, width):
    for axis, dim in sides:
        count = lax.axis_size(axis)
        head = lax.slice_in_dim(cells, 0, width, axis=dim)
        tail = lax.slice_in_dim(cells, cells.shape[dim] - width, cells.shape[dim], axis=dim)
        cells = jnp.concatenate(
            [
                lax.ppermute(tail, axis, [(i, (i + 1) % count) for i in range(count)]),
                cells,
                lax.ppermute(head, axis, [((i + 1) % count, i) for i in range(count)]),
            ],
            axis=dim,
        )
    return cells


def laplace_padded(padded, shape):
    span_x, span_y, span_z = (shape[1], shape[2], shape[3])
    summed = 3.0 * STENCIL[0] * padded[:, 6 : 6 + span_x, 6 : 6 + span_y, 6 : 6 + span_z]
    for offset in range(1, 7):
        weight = STENCIL[offset]
        summed = summed + weight * (
            padded[:, 6 + offset : 6 + offset + span_x, 6 : 6 + span_y, 6 : 6 + span_z]
            + padded[:, 6 - offset : 6 - offset + span_x, 6 : 6 + span_y, 6 : 6 + span_z]
        )
        summed = summed + weight * (
            padded[:, 6 : 6 + span_x, 6 + offset : 6 + offset + span_y, 6 : 6 + span_z]
            + padded[:, 6 : 6 + span_x, 6 - offset : 6 - offset + span_y, 6 : 6 + span_z]
        )
        summed = summed + weight * (
            padded[:, 6 : 6 + span_x, 6 : 6 + span_y, 6 + offset : 6 + offset + span_z]
            + padded[:, 6 : 6 + span_x, 6 : 6 + span_y, 6 - offset : 6 - offset + span_z]
        )
    return summed / (SPACING * SPACING)


def collect_boxes(projectors, member, box_anchor, box_extent, coupling, capacity):
    member_int = member.astype(jnp.int32)
    slot_all = jnp.cumsum(member_int) - 1
    count = jnp.sum(member_int)
    slot_ids = jnp.arange(capacity, dtype=jnp.int32)
    onehot = ((slot_all[None, :] == slot_ids[:, None]) & member[None, :]).astype(jnp.float32)
    buffer = jnp.einsum(
        "cp,pkf->ckf",
        onehot,
        lax.all_gather(projectors, ("gx", "gy", "gz"), axis=0, tiled=True),
        precision=lax.Precision.HIGHEST,
    )
    hot_all = (slot_all[None, :] == slot_ids[:, None]) & member[None, :]
    slot_anchor = jnp.sum(jnp.where(hot_all[None, :, :], box_anchor[:, None, :], 0), axis=2)
    slot_extent = jnp.sum(jnp.where(hot_all, box_extent[None, :], 0), axis=1)
    slot_coupling = jnp.sum(jnp.where(hot_all[:, :, None], coupling[None, :, :], 0.0), axis=1)
    cell_offsets = jnp.arange(B, dtype=jnp.int32)
    limit = slot_extent[:, None, None, None]
    inside = (
        (cell_offsets[None, :, None, None] < limit)
        & (cell_offsets[None, None, :, None] < limit)
        & (cell_offsets[None, None, None, :] < limit)
    )
    buffer = buffer * inside.reshape(capacity, 1, B * B * B).astype(jnp.float32)
    return (buffer, slot_anchor, slot_coupling, count)


def nonlocal_term(field, buffer, slot_anchor, slot_coupling, count, domain_start):
    states = field.shape[0]

    def add_slot(slot_index, nonlocal_sum):
        corner = slot_anchor[:, slot_index] - domain_start
        start_cell = (0, corner[0], corner[1], corner[2])
        box_cells = lax.dynamic_slice(field, start_cell, (states, B, B, B)).reshape(
            states, B * B * B
        )
        proj_box = buffer[slot_index]
        coeffs = (
            jnp.dot(box_cells, proj_box.T, precision=lax.Precision.HIGHEST)
            * slot_coupling[slot_index][None, :]
        )
        addition = jnp.dot(coeffs, proj_box, precision=lax.Precision.HIGHEST).reshape(
            states, B, B, B
        )
        current = lax.dynamic_slice(nonlocal_sum, start_cell, (states, B, B, B))
        return lax.dynamic_update_slice(nonlocal_sum, current + addition, start_cell)

    return lax.fori_loop(0, count, add_slot, jnp.zeros_like(field))


def run_filter(field, apply_h):
    half_width = (UPPER - CUTOFF) / 2.0
    middle = (UPPER + CUTOFF) / 2.0
    sigma_one = half_width / (LOW_EDGE - middle)
    sigma_now = sigma_one
    result = (apply_h(field) - middle * field) * (sigma_one / half_width)
    previous = field
    for degree_step in range(1, DEGREE):
        sigma_next = 1.0 / (2.0 / sigma_one - sigma_now)
        next_state = (apply_h(result) - middle * result) * (
            2.0 * sigma_next / half_width
        ) - sigma_now * sigma_next * previous
        previous = result
        result = next_state
        sigma_now = sigma_next
    return result


def domain_body(orbitals, potential, projectors, owner_rank, box_anchor, box_extent, coupling):
    groups_y = lax.axis_size("gy")
    groups_z = lax.axis_size("gz")
    own_x = owner_rank // (groups_y * groups_z)
    own_y = owner_rank // groups_z % groups_y
    own_z = owner_rank % groups_z
    index_x = lax.axis_index("gx")
    index_y = lax.axis_index("gy")
    index_z = lax.axis_index("gz")
    span_x, span_y, span_z = (orbitals.shape[1], orbitals.shape[2], orbitals.shape[3])
    grid_anchor = jnp.stack([own_x * span_x, own_y * span_y, own_z * span_z]) + box_anchor
    member = (own_x == index_x) & (own_y == index_y) & (own_z == index_z)
    buffer, slot_anchor, slot_coupling, count = collect_boxes(
        projectors, member, grid_anchor, box_extent, coupling, 3 * ATOM_DEV
    )
    domain_start = jnp.stack([index_x * span_x, index_y * span_y, index_z * span_z])

    def apply_cube(field):
        padded = extended(field, (("gx", 1), ("gy", 2), ("gz", 3)), 6)
        return (
            -0.5 * laplace_padded(padded, field.shape)
            + potential[None] * field
            + nonlocal_term(field, buffer, slot_anchor, slot_coupling, count, domain_start)
        )

    filtered = run_filter(orbitals, apply_cube)
    flattened = filtered.reshape(filtered.shape[0], -1)
    partial_value = jnp.dot(flattened, flattened.T, precision=lax.Precision.HIGHEST)
    cells_total = span_x * span_y * span_z * lax.axis_size("gx") * groups_y * groups_z
    intersection = lax.psum(partial_value, ("gx", "gy", "gz")) / cells_total
    return (filtered, intersection)


SUB = 8
LANE = 128
HALF = LANE // 2
NPROJ = 4


def split_terms(matrix):
    high = matrix.astype(ml_dtypes.bfloat16)
    low = (matrix - high.astype(np.float64)).astype(ml_dtypes.bfloat16)
    return high, low


def stencil_weight(distance):
    if distance == 0 or abs(distance) > 6:
        return 0.0
    return -0.5 * STENCIL[abs(distance)] / (SPACING * SPACING)


def ring_matrix(length):
    matrix = np.zeros((length, length))
    for offset in range(-6, 7):
        for row in range(length):
            matrix[row, (row + offset) % length] += stencil_weight(offset)
    return matrix


def plane_weights(groups_y):
    slab = groups_y * HALF
    ring = ring_matrix(groups_y * SUB).reshape(groups_y, SUB, groups_y, SUB)
    blocks = []
    for shift in (-SUB, 0, SUB):
        along_x = np.array(
            [[stencil_weight(shift + i - o) for o in range(SUB)] for i in range(SUB)]
        )
        block = np.einsum("ab,io,jp->aijbop", np.eye(groups_y), along_x, np.eye(SUB))
        if shift == 0:
            block = block + np.einsum("ajbp,io->aijbop", ring, np.eye(SUB))
        blocks.append(block.reshape(slab, slab))
    high, low = split_terms(np.concatenate(blocks, axis=0))
    return np.concatenate([high, low], axis=0)


def depth_weights(groups_z):
    high, low = split_terms(ring_matrix(groups_z * LANE))
    return np.concatenate([high, low, high], axis=1)


def split_pair(value):
    high = value.astype(jnp.bfloat16)
    low = (value - high.astype(jnp.float32)).astype(jnp.bfloat16)
    return high, low


def mxu(left, right):
    return jnp.dot(left, right, preferred_element_type=jnp.float32)


def row_sums(values):
    row = lax.broadcasted_iota(jnp.int32, (SUB, LANE), 0)
    for stride in (1, 2, 4):
        keep = (row & stride) == 0
        values = [
            jnp.where(keep, one, two) + pltpu.roll(jnp.where(keep, two, one), stride, 0)
            for one, two in zip(values[0::2], values[1::2])
        ]
    return values[0]


SPARES = 2


def filter_kernel(groups, atoms, place, half, my_place, *refs):
    groups_x, groups_y, groups_z = groups
    pieces = groups_y * groups_z
    field_in = refs[0]
    packs_in = refs[1 : 1 + pieces]
    coupling_in, plane_in, depth_in, out = refs[1 + pieces : 5 + pieces]
    (
        field_a,
        field_b,
        field_c,
        local,
        added,
        coeffs,
        high_buf,
        low_buf,
        near,
        packs,
        coupling,
        plane,
        depth,
        in_sems,
        pack_sems,
        out_sems,
    ) = refs[5 + pieces :]
    columns = groups_x * groups_y
    domains = columns * groups_z
    pairs = columns // 2
    span = groups_z * LANE
    slab = groups_y * HALF
    per_device = atoms // domains // SUB
    half_width = (UPPER - CUTOFF) / 2.0
    middle = (UPPER + CUTOFF) / 2.0
    diagonal = -0.5 * 3.0 * STENCIL[0] / (SPACING * SPACING) - middle
    lane = lax.broadcasted_iota(jnp.int32, (SUB, LANE), 1)
    lower = lane < HALF
    side = lane // HALF
    f32 = jnp.float32

    loads = [
        pltpu.make_async_copy(source, target, in_sems.at[number])
        for number, (source, target) in enumerate(
            ((field_in, field_b), (plane_in, plane), (depth_in, depth), (coupling_in, coupling))
        )
    ]
    for load in loads:
        load.start()
    pack_loads = []
    for hop_z in range(groups_z):
        for hop_y in range(groups_y):
            source = packs_in[hop_z * groups_y + hop_y]
            for hop_x in range(groups_x):
                from_x = lax.rem(my_place[0] + (groups_x - hop_x), groups_x)
                from_y = lax.rem(my_place[1] + (groups_y - hop_y), groups_y)
                from_z = lax.rem(my_place[2] + (groups_z - hop_z), groups_z)
                device = (from_x * groups_y + from_y) * groups_z + from_z
                number = (hop_z * groups_y + hop_y) * groups_x + hop_x
                pack_loads.append(
                    pltpu.make_async_copy(
                        source.at[hop_x], packs.at[device], pack_sems.at[number]
                    )
                )
    for load in pack_loads:
        load.start()
    loads[0].wait()

    def split_rows(source, pair, first_row, rows):
        cols = pl.ds(pl.multiple_of(pair * LANE, LANE), LANE)
        for at_row in range(first_row, first_row + rows, 2 * SUB):
            at = pl.multiple_of(pair * span + at_row, 2 * SUB)
            high, low = split_pair(source[pl.ds(at, 2 * SUB), :])
            high_buf[at_row : at_row + 2 * SUB, cols] = high
            low_buf[at_row : at_row + 2 * SUB, cols] = low

    def block_rows(pair, parity, depth_at):
        return pl.multiple_of(((2 * pair + parity) * groups_z + depth_at) * HALF, HALF)

    def lay_field(pair, carry):
        for depth_at in range(groups_z):
            first = field_b[pl.ds(block_rows(pair, 0, depth_at), HALF), :]
            second = field_b[pl.ds(block_rows(pair, 1, depth_at), HALF), :]
            at = pl.multiple_of(pair * span + depth_at * LANE, LANE)
            field_a[pl.ds(at, LANE), :] = jnp.concatenate([first, second], axis=0).T
            for spare in range(SPARES):
                added[spare, pl.ds(at, LANE), :] = jnp.zeros((LANE, LANE), f32)
        split_rows(field_a, pair, 0, span)
        return carry

    lax.fori_loop(0, pairs, lay_field, 0)

    for load in loads[1:] + pack_loads:
        load.wait()

    def lay_potential(pair, carry):
        for depth_at in range(groups_z):
            for row in range(SUB):
                first = packs[2 * pair * groups_z + depth_at, row]
                second = packs[(2 * pair + 1) * groups_z + depth_at, row]
                at = pl.multiple_of(pair * span + depth_at * LANE + row * SUB, SUB)
                local[pl.ds(at, SUB), :] = diagonal + jnp.where(
                    lower, first, pltpu.roll(second, HALF, 1)
                )
                at = pl.multiple_of(at + HALF, SUB)
                local[pl.ds(at, SUB), :] = diagonal + jnp.where(
                    lower, pltpu.roll(first, HALF, 1), second
                )
        return carry

    lax.fori_loop(0, pairs, lay_potential, 0)

    ones = (
        (
            lax.broadcasted_iota(jnp.int32, (LANE, LANE), 0) // HALF
            == lax.broadcasted_iota(jnp.int32, (LANE, LANE), 1) // HALF
        )
        .astype(f32)
        .astype(jnp.bfloat16)
    )

    def slab_groups(slab_at):
        for number in range(groups_y * groups_z):
            device = slab_at * (groups_y * groups_z) + number
            for inner in range(per_device):
                yield device, inner

    def slab_of(buf, slab_at):
        return buf[:, pl.ds(pl.multiple_of(slab_at * slab, slab), slab)]

    def apply_step(cur, prev, new, alpha, beta, spill):
        last = spill is not None

        def product(slab_at, carry):
            def around(buf, shift):
                return slab_of(buf, lax.rem(slab_at + shift + groups_x, groups_x))

            high = [around(high_buf, shift) for shift in (-1, 0, 1)]
            low = [around(low_buf, shift) for shift in (-1, 0, 1)]
            left = jnp.concatenate(high + low, axis=1)
            right = jnp.concatenate([plane[: 3 * slab], plane[: 3 * slab]], axis=0)
            near[:, pl.ds(pl.multiple_of(slab_at * slab, slab), slab)] = mxu(left, right)

            for device, inner in slab_groups(slab_at):
                group = device * per_device + inner
                terms = ([], [])
                for j in range(SUB):
                    atom = group * SUB + j
                    value = cur[pl.ds(place[atom], SUB), :]
                    both = jnp.where(side == half[atom], value, pltpu.roll(value, HALF, 1))
                    for kp in range(2):
                        at = SUB + (inner * 2 + kp) * SUB + j
                        terms[kp].append(both * packs[device, at])
                for kp in range(2):
                    at = pl.multiple_of((group * 2 + kp) * SUB, SUB)
                    coeffs[pl.ds(at, SUB), :] = row_sums(terms[kp])
            return carry

        lax.fori_loop(0, groups_x, product, 0)

        high, low = split_pair(coeffs[...])
        coeffs[...] = (mxu(high, ones) + mxu(low, ones)) * coupling[...]

        def scatter(slab_at, carry):
            high = [
                slab_of(high_buf, lax.rem(slab_at + shift + groups_x, groups_x))
                for shift in (-1, 0, 1)
            ]
            left = jnp.concatenate(high + [depth[...]], axis=1)
            right = jnp.concatenate(
                [plane[3 * slab :], high[1], high[1], slab_of(low_buf, slab_at)], axis=0
            )
            at = pl.ds(pl.multiple_of(slab_at * slab, slab), slab)
            near[:, at] = near[:, at] + mxu(left, right)

            for device, inner in slab_groups(slab_at):
                group = device * per_device + inner
                for j in range(SUB):
                    atom = group * SUB + j
                    value = 0.0
                    for kp in range(2):
                        at = SUB + (inner * 2 + kp) * SUB + j
                        row = coeffs[pl.ds((group * 2 + kp) * SUB + j, 1), :]
                        value = value + jnp.broadcast_to(row, (SUB, LANE)) * packs[device, at]
                    value = value + pltpu.roll(value, HALF, 1)
                    value = jnp.where(side == half[atom], value, 0.0)
                    rows = pl.ds(place[atom], SUB)
                    added[j % SPARES, rows, :] = added[j % SPARES, rows, :] + value
            return carry

        lax.fori_loop(0, groups_x, scatter, 0)

        def combine(pair, carry):
            for at_row in range(0, span, SUB):
                at = pl.multiple_of(pair * span + at_row, SUB)
                rows = pl.ds(at, SUB)
                cols = pl.ds(pl.multiple_of(pair * LANE, LANE), LANE)
                total = near[at_row : at_row + SUB, cols] + local[rows, :] * cur[rows, :]
                for spare in range(SPARES):
                    total = total + added[spare, rows, :]
                    if not last:
                        added[spare, rows, :] = jnp.zeros((SUB, LANE), f32)
                total = total * alpha
                if beta is not None:
                    total = total + beta * prev[rows, :]
                new[rows, :] = total
            if not last:
                split_rows(new, pair, 0, span)
            else:
                for depth_at in range(groups_z):
                    at = pl.multiple_of(pair * span + depth_at * LANE, LANE)
                    turned = new[pl.ds(at, LANE), :].T
                    spill[pl.ds(block_rows(pair, 0, depth_at), HALF), :] = turned[:HALF]
                    spill[pl.ds(block_rows(pair, 1, depth_at), HALF), :] = turned[HALF:]
                rows = pl.ds(pl.multiple_of(pair * span, span), span)
                pltpu.make_async_copy(spill.at[rows], out.at[rows], out_sems.at[pair]).start()
            return carry

        lax.fori_loop(0, pairs, combine, 0)

    sigma_one = half_width / (LOW_EDGE - middle)
    sigma_now = sigma_one
    apply_step(field_a, None, field_b, sigma_one / half_width, None, None)
    prev, cur, new = field_a, field_b, field_c
    for degree_step in range(1, DEGREE):
        sigma_next = 1.0 / (2.0 / sigma_one - sigma_now)
        last = degree_step == DEGREE - 1
        target = prev if degree_step > 1 else new
        spare = new if degree_step > 1 else prev
        apply_step(
            cur,
            prev,
            target,
            2.0 * sigma_next / half_width,
            -sigma_now * sigma_next,
            spare if last else None,
        )
        prev, cur, new = cur, target, spare
        sigma_now = sigma_next

    def finish(pair, carry):
        rows = pl.ds(pl.multiple_of(pair * span, span), span)
        pltpu.make_async_copy(prev.at[rows], out.at[rows], out_sems.at[pair]).wait()
        return carry

    lax.fori_loop(0, pairs, finish, 0)


def packed_inputs(potential, projectors, extent):
    atoms = projectors.shape[0]
    cells = jnp.arange(B, dtype=jnp.int32)
    limit = extent[:, None, None, None]
    inside = (
        (cells[None, :, None, None] < limit)
        & (cells[None, None, :, None] < limit)
        & (cells[None, None, None, :] < limit)
    )
    masked = jnp.where(
        inside.reshape(atoms, 1, B * B * B), projectors, 0.0
    ).reshape(atoms // SUB, SUB, 2, 2, B * B, B)
    masked = masked.transpose(0, 2, 1, 5, 3, 4).reshape(atoms // SUB * 2 * B, SUB, LANE)
    shaped = potential.reshape(HALF, 2, HALF).transpose(2, 1, 0).reshape(SUB, SUB, LANE)
    return jnp.concatenate([shaped, masked], axis=0)


def packed_coupling(coupling):
    atoms = coupling.shape[0]
    parts = coupling.reshape(atoms // SUB, SUB, 2, 2).transpose(0, 2, 1, 3)
    wide = jnp.broadcast_to(parts[..., None], parts.shape + (HALF,))
    return wide.reshape(atoms * 2, LANE)


def box_places(groups, owner, anchor):
    groups_z = groups[2]
    column = owner // groups_z
    place = (column // 2 * groups_z + owner % groups_z) * LANE + anchor
    return place, column % 2


def filter_call(groups, place, half, my_place, field, packs, coupling, interpret=False):
    groups_x, groups_y, groups_z = groups
    columns = groups_x * groups_y
    atoms = place.shape[0]
    span = groups_z * LANE
    width = columns * HALF
    cells = (columns // 2 * span, LANE)
    plane = jnp.asarray(plane_weights(groups_y))
    depth = jnp.asarray(depth_weights(groups_z))
    anywhere = pl.BlockSpec(memory_space=pltpu.HBM)
    smem = pl.BlockSpec(memory_space=pltpu.SMEM)
    out = pl.pallas_call(
        functools.partial(filter_kernel, groups, atoms),
        out_shape=jax.ShapeDtypeStruct(cells, jnp.float32),
        in_specs=[smem] * 3 + [anywhere] * (len(packs) + 4),
        out_specs=anywhere,
        scratch_shapes=[
            pltpu.VMEM(cells, jnp.float32),
            pltpu.VMEM(cells, jnp.float32),
            pltpu.VMEM(cells, jnp.float32),
            pltpu.VMEM(cells, jnp.float32),
            pltpu.VMEM((SPARES,) + cells, jnp.float32),
            pltpu.VMEM((atoms * 2, LANE), jnp.float32),
            pltpu.VMEM((span, width), jnp.bfloat16),
            pltpu.VMEM((span, width), jnp.bfloat16),
            pltpu.VMEM((span, width), jnp.float32),
            pltpu.VMEM((columns * groups_z,) + packs[0].shape[1:], jnp.float32),
            pltpu.VMEM(coupling.shape, jnp.float32),
            pltpu.VMEM(plane.shape, plane.dtype),
            pltpu.VMEM(depth.shape, depth.dtype),
            pltpu.SemaphoreType.DMA((4,)),
            pltpu.SemaphoreType.DMA((columns * groups_z,)),
            pltpu.SemaphoreType.DMA((columns // 2,)),
        ],
        compiler_params=pltpu.CompilerParams(vmem_limit_bytes=20 * 1024 * 1024),
        interpret=interpret,
    )(place, half, my_place, field.reshape(cells), *packs, coupling, plane, depth)
    return out.reshape(field.shape)


def hops(value, axis):
    count = lax.axis_size(axis)
    return [value] + [
        lax.ppermute(value, axis, [(i, (i + hop) % count) for i in range(count)])
        for hop in range(1, count)
    ]


def state_body(orbitals, potential, projectors, owner_rank, box_anchor, box_extent, coupling):
    axes = ("gx", "gy", "gz")
    groups = tuple(lax.axis_size(axis) for axis in axes)
    groups_z = groups[2]
    domains = groups[0] * groups[1] * groups_z
    atoms_own = projectors.shape[0]
    my_place = jnp.stack([lax.axis_index(axis) for axis in axes])
    me = (my_place[0] * groups[1] + my_place[1]) * groups_z + my_place[2]
    extent = lax.dynamic_slice(box_extent, (me * atoms_own,), (atoms_own,))
    pack = packed_inputs(potential, projectors, extent)
    line = hops(pack, "gx")
    if len(line) > 1:
        orbitals, line[1] = lax.optimization_barrier((orbitals, line[1]))
    spread = [hops(piece, "gy") for piece in line]
    packs = []
    for hop_y in range(groups[1]):
        packs.append(hops(jnp.stack([pieces[hop_y] for pieces in spread]), "gz"))
    packs = [packs[hop_y][hop_z] for hop_z in range(groups_z) for hop_y in range(groups[1])]
    field = lax.all_to_all(orbitals, axes, split_axis=0, concat_axis=0, tiled=True)
    place, half = box_places(groups, owner_rank, box_anchor[2])
    result = filter_call(
        groups, place, half, my_place, field, packs, packed_coupling(coupling)
    )
    filtered = lax.all_to_all(result, axes, split_axis=0, concat_axis=0, tiled=True)
    flattened = filtered.reshape(filtered.shape[0], -1)
    intersection = jnp.dot(flattened, flattened.T, precision=lax.Precision.HIGHEST)
    for stage in (("gy", "gz"), ("gx",)):
        sharers = math.prod(lax.axis_size(axis) for axis in stage)
        copies = jnp.broadcast_to(intersection[None], (sharers,) + intersection.shape)
        copies = lax.all_to_all(copies, stage, split_axis=0, concat_axis=0, tiled=True)
        intersection = jnp.sum(copies, axis=0)
    cells_total = orbitals.shape[1] * orbitals.shape[2] * orbitals.shape[3] * domains
    return (filtered, intersection / cells_total)


def body(orbitals, potential, projectors, owner_rank, box_anchor, box_extent, coupling):
    domains = lax.axis_size("gx") * lax.axis_size("gy") * lax.axis_size("gz")
    whole_states = (
        orbitals.shape == (domains, SUB, SUB, LANE)
        and projectors.shape[0] % SUB == 0
        and projectors.shape[1] == NPROJ
        and lax.axis_size("gy") % 2 == 0
    )
    chosen = state_body if whole_states else domain_body
    return chosen(
        orbitals, potential, projectors, owner_rank, box_anchor, box_extent, coupling
    )


def solution(mesh):
    return jax.shard_map(
        body,
        mesh=mesh,
        in_specs=(
            P(None, "gx", "gy", "gz"),
            P("gx", "gy", "gz"),
            P(("gx", "gy", "gz"), None, None),
            P(),
            P(),
            P(),
            P(),
        ),
        out_specs=(P(None, "gx", "gy", "gz"), P()),
        check_vma=False,
    )
```

```python
import functools
import math
import jax
import jax.numpy as jnp
from jax import lax
from jax.experimental import pallas as pl
from jax.experimental.pallas import tpu as pltpu
import ml_dtypes
import numpy as np
from jax.sharding import PartitionSpec as P

B = 8
DEGREE = 4
ATOM_DEV = 8


STENCIL = (
    -5369.0 / 1800.0,
    12.0 / 7.0,
    -15.0 / 56.0,
    10.0 / 189.0,
    -1.0 / 112.0,
    2.0 / 1925.0,
    -1.0 / 16632.0,
)
SPACING = 0.5
LOW_EDGE = -2.5
CUTOFF = 4.0
UPPER = 60.0


def extended(cells, sides, width):
    for axis, dim in sides:
        count = lax.axis_size(axis)
        head = lax.slice_in_dim(cells, 0, width, axis=dim)
        tail = lax.slice_in_dim(cells, cells.shape[dim] - width, cells.shape[dim], axis=dim)
        cells = jnp.concatenate(
            [
                lax.ppermute(tail, axis, [(i, (i + 1) % count) for i in range(count)]),
                cells,
                lax.ppermute(head, axis, [((i + 1) % count, i) for i in range(count)]),
            ],
            axis=dim,
        )
    return cells


def laplace_padded(padded, shape):
    span_x, span_y, span_z = (shape[1], shape[2], shape[3])
    summed = 3.0 * STENCIL[0] * padded[:, 6 : 6 + span_x, 6 : 6 + span_y, 6 : 6 + span_z]
    for offset in range(1, 7):
        weight = STENCIL[offset]
        summed = summed + weight * (
            padded[:, 6 + offset : 6 + offset + span_x, 6 : 6 + span_y, 6 : 6 + span_z]
            + padded[:, 6 - offset : 6 - offset + span_x, 6 : 6 + span_y, 6 : 6 + span_z]
        )
        summed = summed + weight * (
            padded[:, 6 : 6 + span_x, 6 + offset : 6 + offset + span_y, 6 : 6 + span_z]
            + padded[:, 6 : 6 + span_x, 6 - offset : 6 - offset + span_y, 6 : 6 + span_z]
        )
        summed = summed + weight * (
            padded[:, 6 : 6 + span_x, 6 : 6 + span_y, 6 + offset : 6 + offset + span_z]
            + padded[:, 6 : 6 + span_x, 6 : 6 + span_y, 6 - offset : 6 - offset + span_z]
        )
    return summed / (SPACING * SPACING)


def collect_boxes(projectors, member, box_anchor, box_extent, coupling, capacity):
    member_int = member.astype(jnp.int32)
    slot_all = jnp.cumsum(member_int) - 1
    count = jnp.sum(member_int)
    slot_ids = jnp.arange(capacity, dtype=jnp.int32)
    onehot = ((slot_all[None, :] == slot_ids[:, None]) & member[None, :]).astype(jnp.float32)
    buffer = jnp.einsum(
        "cp,pkf->ckf",
        onehot,
        lax.all_gather(projectors, ("gx", "gy", "gz"), axis=0, tiled=True),
        precision=lax.Precision.HIGHEST,
    )
    hot_all = (slot_all[None, :] == slot_ids[:, None]) & member[None, :]
    slot_anchor = jnp.sum(jnp.where(hot_all[None, :, :], box_anchor[:, None, :], 0), axis=2)
    slot_extent = jnp.sum(jnp.where(hot_all, box_extent[None, :], 0), axis=1)
    slot_coupling = jnp.sum(jnp.where(hot_all[:, :, None], coupling[None, :, :], 0.0), axis=1)
    cell_offsets = jnp.arange(B, dtype=jnp.int32)
    limit = slot_extent[:, None, None, None]
    inside = (
        (cell_offsets[None, :, None, None] < limit)
        & (cell_offsets[None, None, :, None] < limit)
        & (cell_offsets[None, None, None, :] < limit)
    )
    buffer = buffer * inside.reshape(capacity, 1, B * B * B).astype(jnp.float32)
    return (buffer, slot_anchor, slot_coupling, count)


def nonlocal_term(field, buffer, slot_anchor, slot_coupling, count, domain_start):
    states = field.shape[0]

    def add_slot(slot_index, nonlocal_sum):
        corner = slot_anchor[:, slot_index] - domain_start
        start_cell = (0, corner[0], corner[1], corner[2])
        box_cells = lax.dynamic_slice(field, start_cell, (states, B, B, B)).reshape(
            states, B * B * B
        )
        proj_box = buffer[slot_index]
        coeffs = (
            jnp.dot(box_cells, proj_box.T, precision=lax.Precision.HIGHEST)
            * slot_coupling[slot_index][None, :]
        )
        addition = jnp.dot(coeffs, proj_box, precision=lax.Precision.HIGHEST).reshape(
            states, B, B, B
        )
        current = lax.dynamic_slice(nonlocal_sum, start_cell, (states, B, B, B))
        return lax.dynamic_update_slice(nonlocal_sum, current + addition, start_cell)

    return lax.fori_loop(0, count, add_slot, jnp.zeros_like(field))


def run_filter(field, apply_h):
    half_width = (UPPER - CUTOFF) / 2.0
    middle = (UPPER + CUTOFF) / 2.0
    sigma_one = half_width / (LOW_EDGE - middle)
    sigma_now = sigma_one
    result = (apply_h(field) - middle * field) * (sigma_one / half_width)
    previous = field
    for degree_step in range(1, DEGREE):
        sigma_next = 1.0 / (2.0 / sigma_one - sigma_now)
        next_state = (apply_h(result) - middle * result) * (
            2.0 * sigma_next / half_width
        ) - sigma_now * sigma_next * previous
        previous = result
        result = next_state
        sigma_now = sigma_next
    return result


def domain_body(orbitals, potential, projectors, owner_rank, box_anchor, box_extent, coupling):
    groups_y = lax.axis_size("gy")
    groups_z = lax.axis_size("gz")
    own_x = owner_rank // (groups_y * groups_z)
    own_y = owner_rank // groups_z % groups_y
    own_z = owner_rank % groups_z
    index_x = lax.axis_index("gx")
    index_y = lax.axis_index("gy")
    index_z = lax.axis_index("gz")
    span_x, span_y, span_z = (orbitals.shape[1], orbitals.shape[2], orbitals.shape[3])
    grid_anchor = jnp.stack([own_x * span_x, own_y * span_y, own_z * span_z]) + box_anchor
    member = (own_x == index_x) & (own_y == index_y) & (own_z == index_z)
    buffer, slot_anchor, slot_coupling, count = collect_boxes(
        projectors, member, grid_anchor, box_extent, coupling, 3 * ATOM_DEV
    )
    domain_start = jnp.stack([index_x * span_x, index_y * span_y, index_z * span_z])

    def apply_cube(field):
        padded = extended(field, (("gx", 1), ("gy", 2), ("gz", 3)), 6)
        return (
            -0.5 * laplace_padded(padded, field.shape)
            + potential[None] * field
            + nonlocal_term(field, buffer, slot_anchor, slot_coupling, count, domain_start)
        )

    filtered = run_filter(orbitals, apply_cube)
    flattened = filtered.reshape(filtered.shape[0], -1)
    partial_value = jnp.dot(flattened, flattened.T, precision=lax.Precision.HIGHEST)
    cells_total = span_x * span_y * span_z * lax.axis_size("gx") * groups_y * groups_z
    intersection = lax.psum(partial_value, ("gx", "gy", "gz")) / cells_total
    return (filtered, intersection)


SUB = 8
LANE = 128
HALF = LANE // 2
NPROJ = 4


def split_terms(matrix):
    high = matrix.astype(ml_dtypes.bfloat16)
    low = (matrix - high.astype(np.float64)).astype(ml_dtypes.bfloat16)
    return high, low


def stencil_weight(distance):
    if distance == 0 or abs(distance) > 6:
        return 0.0
    return -0.5 * STENCIL[abs(distance)] / (SPACING * SPACING)


def ring_matrix(length):
    matrix = np.zeros((length, length))
    for offset in range(-6, 7):
        for row in range(length):
            matrix[row, (row + offset) % length] += stencil_weight(offset)
    return matrix


def plane_weights(groups_y):
    slab = groups_y * HALF
    ring = ring_matrix(groups_y * SUB).reshape(groups_y, SUB, groups_y, SUB)
    blocks = []
    for shift in (-SUB, 0, SUB):
        along_x = np.array(
            [[stencil_weight(shift + i - o) for o in range(SUB)] for i in range(SUB)]
        )
        block = np.einsum("ab,io,jp->aijbop", np.eye(groups_y), along_x, np.eye(SUB))
        if shift == 0:
            block = block + np.einsum("ajbp,io->aijbop", ring, np.eye(SUB))
        blocks.append(block.reshape(slab, slab))
    high, low = split_terms(np.concatenate(blocks, axis=0))
    return np.concatenate([high, low], axis=0)


def depth_weights(groups_z):
    high, low = split_terms(ring_matrix(groups_z * LANE))
    return np.concatenate([high, low, high], axis=1)


def split_pair(value):
    high = value.astype(jnp.bfloat16)
    low = (value - high.astype(jnp.float32)).astype(jnp.bfloat16)
    return high, low


def mxu(left, right):
    return jnp.dot(left, right, preferred_element_type=jnp.float32)


def row_sums(values):
    row = lax.broadcasted_iota(jnp.int32, (SUB, LANE), 0)
    for stride in (1, 2, 4):
        keep = (row & stride) == 0
        values = [
            jnp.where(keep, one, two) + pltpu.roll(jnp.where(keep, two, one), stride, 0)
            for one, two in zip(values[0::2], values[1::2])
        ]
    return values[0]


SPARES = 2
TALL = 2 * SUB


def split_store(high_buf, low_buf, rows, cols, value):
    high, low = split_pair(value)
    high_buf[rows, cols] = high
    low_buf[rows, cols] = low


def slab_rows(slab_at, span):
    return pl.ds(pl.multiple_of(slab_at * span, span), span)


def plane_product(groups_x, span, high_buf, low_buf, plane, slabs):
    width = plane.shape[1]

    def around(buf, shift):
        parts = [
            buf[slab_rows(lax.rem(at + shift + groups_x, groups_x), span), :] for at in slabs
        ]
        return jnp.concatenate(parts, axis=0)

    high = [around(high_buf, shift) for shift in (-1, 0, 1)]
    low = [around(low_buf, shift) for shift in (-1, 0, 1)]
    left = jnp.concatenate(high + low + high, axis=1)
    right = jnp.concatenate([plane[: 3 * width], plane[: 3 * width], plane[3 * width :]], axis=0)
    return mxu(left, right)


def depth_product(span, high_buf, low_buf, depth, slab_at):
    high = high_buf[slab_rows(slab_at, span), :]
    low = low_buf[slab_rows(slab_at, span), :]
    return mxu(depth[...], jnp.concatenate([high, high, low], axis=0))


def chunk_of(groups_x):
    return 2 if groups_x % 2 == 0 else 1


def block_rows(groups_z, pair, parity, depth_at):
    return pl.ds(pl.multiple_of(((2 * pair + parity) * groups_z + depth_at) * HALF, HALF), HALF)


def first_kernel(groups, *refs):
    field_in, plane_in, depth_in, field, near = refs[:5]
    raw, high_buf, low_buf, plane, depth, sems = refs[5:]
    groups_x, groups_y, groups_z = groups
    span = groups_z * LANE
    pairs_slab = groups_y // 2
    loads = [
        pltpu.make_async_copy(source, target, sems.at[number])
        for number, (source, target) in enumerate(
            ((field_in, raw), (plane_in, plane), (depth_in, depth))
        )
    ]
    for load in loads:
        load.start()
    loads[0].wait()

    def lay_field(slab_at, carry):
        for tile in range(pairs_slab):
            pair = slab_at * pairs_slab + tile
            cols = slice(tile * LANE, (tile + 1) * LANE)
            for depth_at in range(groups_z):
                first = raw[block_rows(groups_z, pair, 0, depth_at), :]
                second = raw[block_rows(groups_z, pair, 1, depth_at), :]
                turned = jnp.concatenate([first, second], axis=0).T
                at = pl.multiple_of(pair * span + depth_at * LANE, LANE)
                field[pl.ds(at, LANE), :] = turned
                at = pl.multiple_of(slab_at * span + depth_at * LANE, LANE)
                split_store(high_buf, low_buf, pl.ds(at, LANE), cols, turned)
        return carry

    lax.fori_loop(0, groups_x, lay_field, 0)
    for load in loads[1:]:
        load.wait()
    chunk = chunk_of(groups_x)

    def product(chunk_at, carry):
        slabs = [chunk_at * chunk + number for number in range(chunk)]
        total = plane_product(groups_x, span, high_buf, low_buf, plane, slabs)
        near[slab_rows(chunk_at, chunk * span), :] = total
        for slab_at in slabs:
            rows = slab_rows(slab_at, span)
            near[rows, :] += depth_product(span, high_buf, low_buf, depth, slab_at)
        return carry

    lax.fori_loop(0, groups_x // chunk, product, 0)


def filter_kernel(groups, atoms, place, half, my_place, *refs):
    groups_x, groups_y, groups_z = groups
    pieces = groups_y * groups_z
    field_a, near_a = refs[:2]
    packs_in = refs[2 : 2 + pieces]
    coupling_in, plane_in, depth_in, out = refs[2 + pieces : 6 + pieces]
    (
        field_b,
        field_c,
        turned_out,
        local,
        added,
        coeffs,
        high_buf,
        low_buf,
        near,
        packs,
        coupling,
        plane,
        depth,
        in_sems,
        pack_sems,
        out_sems,
    ) = refs[6 + pieces :]
    columns = groups_x * groups_y
    domains = columns * groups_z
    pairs = columns // 2
    span = groups_z * LANE
    pairs_slab = groups_y // 2
    per_device = atoms // domains // SUB
    chunk = chunk_of(groups_x)
    half_width = (UPPER - CUTOFF) / 2.0
    middle = (UPPER + CUTOFF) / 2.0
    diagonal = -0.5 * 3.0 * STENCIL[0] / (SPACING * SPACING) - middle
    lane = lax.broadcasted_iota(jnp.int32, (SUB, LANE), 1)
    lower = lane < HALF
    side = lane // HALF
    f32 = jnp.float32

    loads = [
        pltpu.make_async_copy(source, target, in_sems.at[number])
        for number, (source, target) in enumerate(
            ((coupling_in, coupling), (plane_in, plane), (depth_in, depth))
        )
    ]
    pack_loads = []
    for hop_z in range(groups_z):
        for hop_y in range(groups_y):
            source = packs_in[hop_z * groups_y + hop_y]
            for hop_x in range(groups_x):
                from_x = lax.rem(my_place[0] + (groups_x - hop_x), groups_x)
                from_y = lax.rem(my_place[1] + (groups_y - hop_y), groups_y)
                from_z = lax.rem(my_place[2] + (groups_z - hop_z), groups_z)
                device = (from_x * groups_y + from_y) * groups_z + from_z
                number = (hop_z * groups_y + hop_y) * groups_x + hop_x
                pack_loads.append(
                    pltpu.make_async_copy(
                        source.at[hop_x], packs.at[device], pack_sems.at[number]
                    )
                )
    for load in pack_loads + loads:
        load.start()
    added[...] = jnp.zeros(added.shape, f32)
    for load in pack_loads + loads:
        load.wait()

    def lay_potential(pair, carry):
        for depth_at in range(groups_z):
            for row in range(SUB):
                first = packs[2 * pair * groups_z + depth_at, row]
                second = packs[(2 * pair + 1) * groups_z + depth_at, row]
                at = pl.multiple_of(pair * span + depth_at * LANE + row * SUB, SUB)
                local[pl.ds(at, SUB), :] = diagonal + jnp.where(
                    lower, first, pltpu.roll(second, HALF, 1)
                )
                at = pl.multiple_of(at + HALF, SUB)
                local[pl.ds(at, SUB), :] = diagonal + jnp.where(
                    lower, pltpu.roll(first, HALF, 1), second
                )
        return carry

    lax.fori_loop(0, pairs, lay_potential, 0)

    ones = (
        (
            lax.broadcasted_iota(jnp.int32, (LANE, LANE), 0) // HALF
            == lax.broadcasted_iota(jnp.int32, (LANE, LANE), 1) // HALF
        )
        .astype(f32)
        .astype(jnp.bfloat16)
    )

    def slab_groups(slab_at):
        for number in range(groups_y * groups_z):
            device = slab_at * (groups_y * groups_z) + number
            for inner in range(per_device):
                yield device, inner

    def apply_step(cur, prev, new, alpha, beta, first, last):
        def project(chunk_at, carry):
            slabs = [chunk_at * chunk + number for number in range(chunk)]
            if not first:
                total = plane_product(groups_x, span, high_buf, low_buf, plane, slabs)
                near[slab_rows(chunk_at, chunk * span), :] = total
            for slab_at in slabs:
                for device, inner in slab_groups(slab_at):
                    group = device * per_device + inner
                    terms = ([], [])
                    for j in range(SUB):
                        atom = group * SUB + j
                        value = cur[pl.ds(place[atom], SUB), :]
                        both = jnp.where(side == half[atom], value, pltpu.roll(value, HALF, 1))
                        for kp in range(2):
                            at = SUB + (inner * 2 + kp) * SUB + j
                            terms[kp].append(both * packs[device, at])
                    for kp in range(2):
                        at = pl.multiple_of((group * 2 + kp) * SUB, SUB)
                        coeffs[pl.ds(at, SUB), :] = row_sums(terms[kp])
            return carry

        lax.fori_loop(0, groups_x // chunk, project, 0)

        high, low = split_pair(coeffs[...])
        coeffs[...] = (mxu(high, ones) + mxu(low, ones)) * coupling[...]

        def scatter(slab_at, carry):
            if not first:
                rows = slab_rows(slab_at, span)
                near[rows, :] += depth_product(span, high_buf, low_buf, depth, slab_at)
            for device, inner in slab_groups(slab_at):
                group = device * per_device + inner
                for j in range(SUB):
                    atom = group * SUB + j
                    value = 0.0
                    for kp in range(2):
                        at = SUB + (inner * 2 + kp) * SUB + j
                        row = coeffs[pl.ds((group * 2 + kp) * SUB + j, 1), :]
                        value = value + jnp.broadcast_to(row, (SUB, LANE)) * packs[device, at]
                    value = value + pltpu.roll(value, HALF, 1)
                    value = jnp.where(side == half[atom], value, 0.0)
                    rows = pl.ds(place[atom], SUB)
                    added[j % SPARES, rows, :] = added[j % SPARES, rows, :] + value
            return carry

        lax.fori_loop(0, groups_x, scatter, 0)

        kinetic = near_a if first else near

        def combine(slab_at, carry):
            for tile in range(pairs_slab):
                pair = slab_at * pairs_slab + tile
                cols = slice(tile * LANE, (tile + 1) * LANE)
                for at_row in range(0, span, TALL):
                    rows = pl.ds(pl.multiple_of(pair * span + at_row, TALL), TALL)
                    slab_at_row = pl.ds(pl.multiple_of(slab_at * span + at_row, TALL), TALL)
                    total = kinetic[slab_at_row, cols] + local[rows, :] * cur[rows, :]
                    for spare in range(SPARES):
                        total = total + added[spare, rows, :]
                        if not last:
                            added[spare, rows, :] = jnp.zeros((TALL, LANE), f32)
                    total = total * alpha
                    if beta is not None:
                        total = total + beta * prev[rows, :]
                    new[rows, :] = total
                    if not last:
                        split_store(high_buf, low_buf, slab_at_row, cols, total)
                if last:
                    for depth_at in range(groups_z):
                        at = pl.multiple_of(pair * span + depth_at * LANE, LANE)
                        turned = new[pl.ds(at, LANE), :].T
                        turned_out[block_rows(groups_z, pair, 0, depth_at), :] = turned[:HALF]
                        turned_out[block_rows(groups_z, pair, 1, depth_at), :] = turned[HALF:]
                    rows = pl.ds(pl.multiple_of(pair * span, span), span)
                    pltpu.make_async_copy(
                        turned_out.at[rows], out.at[rows], out_sems.at[pair]
                    ).start()
            return carry

        lax.fori_loop(0, groups_x, combine, 0)

    sigma_one = half_width / (LOW_EDGE - middle)
    sigma_now = sigma_one
    apply_step(field_a, None, field_b, sigma_one / half_width, None, True, DEGREE == 1)
    prev, cur, new = field_a, field_b, field_c
    for degree_step in range(1, DEGREE):
        sigma_next = 1.0 / (2.0 / sigma_one - sigma_now)
        last = degree_step == DEGREE - 1
        target = prev if degree_step > 1 else new
        apply_step(
            cur,
            prev,
            target,
            2.0 * sigma_next / half_width,
            -sigma_now * sigma_next,
            False,
            last,
        )
        prev, cur = cur, target
        sigma_now = sigma_next

    def finish(pair, carry):
        rows = pl.ds(pl.multiple_of(pair * span, span), span)
        pltpu.make_async_copy(turned_out.at[rows], out.at[rows], out_sems.at[pair]).wait()
        return carry

    lax.fori_loop(0, pairs, finish, 0)


def packed_inputs(potential, projectors, extent):
    atoms = projectors.shape[0]
    cells = jnp.arange(B, dtype=jnp.int32)
    limit = extent[:, None, None, None]
    inside = (
        (cells[None, :, None, None] < limit)
        & (cells[None, None, :, None] < limit)
        & (cells[None, None, None, :] < limit)
    )
    masked = jnp.where(
        inside.reshape(atoms, 1, B * B * B), projectors, 0.0
    ).reshape(atoms // SUB, SUB, 2, 2, B * B, B)
    masked = masked.transpose(0, 2, 1, 5, 3, 4).reshape(atoms // SUB * 2 * B, SUB, LANE)
    shaped = potential.reshape(HALF, 2, HALF).transpose(2, 1, 0).reshape(SUB, SUB, LANE)
    return jnp.concatenate([shaped, masked], axis=0)


def packed_coupling(coupling):
    atoms = coupling.shape[0]
    parts = coupling.reshape(atoms // SUB, SUB, 2, 2).transpose(0, 2, 1, 3)
    wide = jnp.broadcast_to(parts[..., None], parts.shape + (HALF,))
    return wide.reshape(atoms * 2, LANE)


def box_places(groups, owner, anchor):
    groups_z = groups[2]
    column = owner // groups_z
    place = (column // 2 * groups_z + owner % groups_z) * LANE + anchor
    return place, column % 2


def weights_of(groups):
    return jnp.asarray(plane_weights(groups[1])), jnp.asarray(depth_weights(groups[2]))


def first_call(groups, field, interpret=False):
    groups_x, groups_y, groups_z = groups
    span = groups_z * LANE
    cells = (groups_x * groups_y // 2 * span, LANE)
    slabs = (groups_x * span, groups_y * HALF)
    plane, depth = weights_of(groups)
    vmem = pl.BlockSpec(memory_space=pltpu.VMEM)
    anywhere = pl.BlockSpec(memory_space=pl.ANY)
    work = 2 * slabs[0] * slabs[1] * (9 * slabs[1] + 3 * span)
    return pl.pallas_call(
        functools.partial(first_kernel, groups),
        out_shape=[
            jax.ShapeDtypeStruct(cells, jnp.float32),
            jax.ShapeDtypeStruct(slabs, jnp.float32),
        ],
        in_specs=[anywhere] * 3,
        out_specs=[vmem] * 2,
        scratch_shapes=[
            pltpu.VMEM(cells, jnp.float32),
            pltpu.VMEM(slabs, jnp.bfloat16),
            pltpu.VMEM(slabs, jnp.bfloat16),
            pltpu.VMEM(plane.shape, plane.dtype),
            pltpu.VMEM(depth.shape, depth.dtype),
            pltpu.SemaphoreType.DMA((3,)),
        ],
        compiler_params=pltpu.CompilerParams(vmem_limit_bytes=16 * 1024 * 1024),
        cost_estimate=pl.CostEstimate(
            flops=work, bytes_accessed=4 * field.size * 4, transcendentals=0
        ),
        interpret=interpret,
    )(field.reshape(cells), plane, depth)


def filter_call(groups, place, half, my_place, field, near, packs, coupling, interpret=False):
    groups_x, groups_y, groups_z = groups
    columns = groups_x * groups_y
    atoms = place.shape[0]
    plane, depth = weights_of(groups)
    vmem = pl.BlockSpec(memory_space=pltpu.VMEM)
    anywhere = pl.BlockSpec(memory_space=pl.ANY)
    smem = pl.BlockSpec(memory_space=pltpu.SMEM)
    work = 2 * near.shape[0] * near.shape[1] * (9 * near.shape[1] + 3 * groups_z * LANE)
    out = pl.pallas_call(
        functools.partial(filter_kernel, groups, atoms),
        out_shape=jax.ShapeDtypeStruct(field.shape, jnp.float32),
        in_specs=[smem] * 3 + [vmem] * 2 + [anywhere] * (len(packs) + 3),
        out_specs=anywhere,
        scratch_shapes=[
            pltpu.VMEM(field.shape, jnp.float32),
            pltpu.VMEM(field.shape, jnp.float32),
            pltpu.VMEM(field.shape, jnp.float32),
            pltpu.VMEM(field.shape, jnp.float32),
            pltpu.VMEM((SPARES,) + field.shape, jnp.float32),
            pltpu.VMEM((atoms * 2, LANE), jnp.float32),
            pltpu.VMEM(near.shape, jnp.bfloat16),
            pltpu.VMEM(near.shape, jnp.bfloat16),
            pltpu.VMEM(near.shape, jnp.float32),
            pltpu.VMEM((columns * groups_z,) + packs[0].shape[1:], jnp.float32),
            pltpu.VMEM(coupling.shape, jnp.float32),
            pltpu.VMEM(plane.shape, plane.dtype),
            pltpu.VMEM(depth.shape, depth.dtype),
            pltpu.SemaphoreType.DMA((3,)),
            pltpu.SemaphoreType.DMA((columns * groups_z,)),
            pltpu.SemaphoreType.DMA((columns // 2,)),
        ],
        compiler_params=pltpu.CompilerParams(vmem_limit_bytes=20 * 1024 * 1024),
        cost_estimate=pl.CostEstimate(
            flops=3 * work, bytes_accessed=8 * field.size * 4, transcendentals=0
        ),
        interpret=interpret,
    )(place, half, my_place, field, near, *packs, coupling, plane, depth)
    return out.reshape(columns * groups_z, SUB, SUB, LANE)


def hops(value, axis):
    count = lax.axis_size(axis)
    return [value] + [
        lax.ppermute(value, axis, [(i, (i + hop) % count) for i in range(count)])
        for hop in range(1, count)
    ]


def state_body(orbitals, potential, projectors, owner_rank, box_anchor, box_extent, coupling):
    axes = ("gx", "gy", "gz")
    groups = tuple(lax.axis_size(axis) for axis in axes)
    groups_z = groups[2]
    domains = groups[0] * groups[1] * groups_z
    atoms_own = projectors.shape[0]
    my_place = jnp.stack([lax.axis_index(axis) for axis in axes])
    me = (my_place[0] * groups[1] + my_place[1]) * groups_z + my_place[2]
    extent = lax.dynamic_slice(box_extent, (me * atoms_own,), (atoms_own,))
    pack = packed_inputs(potential, projectors, extent)
    line = jnp.stack(hops(pack, "gx"))
    orbitals, line = lax.optimization_barrier((orbitals, line))
    crossed = [hops(piece, "gz") for piece in hops(line, "gy")]
    packs = [crossed[hop_y][hop_z] for hop_z in range(groups_z) for hop_y in range(groups[1])]
    field = lax.all_to_all(orbitals, axes, split_axis=0, concat_axis=0, tiled=True)
    field, near = first_call(groups, field)
    place, half = box_places(groups, owner_rank, box_anchor[2])
    result = filter_call(
        groups, place, half, my_place, field, near, packs, packed_coupling(coupling)
    )
    filtered = lax.all_to_all(result, axes, split_axis=0, concat_axis=0, tiled=True)
    states = filtered.shape[0]
    flattened = filtered.reshape(states, -1)
    partial_value = jnp.dot(flattened, flattened.T, precision=lax.Precision.HIGHEST)
    quarter = partial_value.reshape(-1, SUB, states).transpose(1, 0, 2).reshape(SUB, -1)
    parts = lax.all_to_all(
        jnp.broadcast_to(quarter[None], (domains,) + quarter.shape),
        axes,
        split_axis=0,
        concat_axis=0,
        tiled=True,
    )
    summed = jnp.sum(parts, axis=0).reshape(SUB, -1, states).transpose(1, 0, 2)
    cells_total = orbitals.shape[1] * orbitals.shape[2] * orbitals.shape[3] * domains
    intersection = summed.reshape(states, states) / cells_total
    return (filtered, intersection)


def body(orbitals, potential, projectors, owner_rank, box_anchor, box_extent, coupling):
    domains = lax.axis_size("gx") * lax.axis_size("gy") * lax.axis_size("gz")
    whole_states = (
        orbitals.shape == (domains, SUB, SUB, LANE)
        and projectors.shape[0] % SUB == 0
        and projectors.shape[1] == NPROJ
        and lax.axis_size("gy") % 2 == 0
    )
    chosen = state_body if whole_states else domain_body
    return chosen(
        orbitals, potential, projectors, owner_rank, box_anchor, box_extent, coupling
    )


def solution(mesh):
    return jax.shard_map(
        body,
        mesh=mesh,
        in_specs=(
            P(None, "gx", "gy", "gz"),
            P("gx", "gy", "gz"),
            P(("gx", "gy", "gz"), None, None),
            P(),
            P(),
            P(),
            P(),
        ),
        out_specs=(P(None, "gx", "gy", "gz"), P()),
        check_vma=False,
    )
```

```python
import functools
import math
import jax
import jax.numpy as jnp
from jax import lax
from jax.experimental import pallas as pl
from jax.experimental.pallas import tpu as pltpu
import ml_dtypes
import numpy as np
from jax.sharding import PartitionSpec as P

B = 8
DEGREE = 4
ATOM_DEV = 8


STENCIL = (
    -5369.0 / 1800.0,
    12.0 / 7.0,
    -15.0 / 56.0,
    10.0 / 189.0,
    -1.0 / 112.0,
    2.0 / 1925.0,
    -1.0 / 16632.0,
)
SPACING = 0.5
LOW_EDGE = -2.5
CUTOFF = 4.0
UPPER = 60.0


def extended(cells, sides, width):
    for axis, dim in sides:
        count = lax.axis_size(axis)
        head = lax.slice_in_dim(cells, 0, width, axis=dim)
        tail = lax.slice_in_dim(cells, cells.shape[dim] - width, cells.shape[dim], axis=dim)
        cells = jnp.concatenate(
            [
                lax.ppermute(tail, axis, [(i, (i + 1) % count) for i in range(count)]),
                cells,
                lax.ppermute(head, axis, [((i + 1) % count, i) for i in range(count)]),
            ],
            axis=dim,
        )
    return cells


def laplace_padded(padded, shape):
    span_x, span_y, span_z = (shape[1], shape[2], shape[3])
    summed = 3.0 * STENCIL[0] * padded[:, 6 : 6 + span_x, 6 : 6 + span_y, 6 : 6 + span_z]
    for offset in range(1, 7):
        weight = STENCIL[offset]
        summed = summed + weight * (
            padded[:, 6 + offset : 6 + offset + span_x, 6 : 6 + span_y, 6 : 6 + span_z]
            + padded[:, 6 - offset : 6 - offset + span_x, 6 : 6 + span_y, 6 : 6 + span_z]
        )
        summed = summed + weight * (
            padded[:, 6 : 6 + span_x, 6 + offset : 6 + offset + span_y, 6 : 6 + span_z]
            + padded[:, 6 : 6 + span_x, 6 - offset : 6 - offset + span_y, 6 : 6 + span_z]
        )
        summed = summed + weight * (
            padded[:, 6 : 6 + span_x, 6 : 6 + span_y, 6 + offset : 6 + offset + span_z]
            + padded[:, 6 : 6 + span_x, 6 : 6 + span_y, 6 - offset : 6 - offset + span_z]
        )
    return summed / (SPACING * SPACING)


def collect_boxes(projectors, member, box_anchor, box_extent, coupling, capacity):
    member_int = member.astype(jnp.int32)
    slot_all = jnp.cumsum(member_int) - 1
    count = jnp.sum(member_int)
    slot_ids = jnp.arange(capacity, dtype=jnp.int32)
    onehot = ((slot_all[None, :] == slot_ids[:, None]) & member[None, :]).astype(jnp.float32)
    buffer = jnp.einsum(
        "cp,pkf->ckf",
        onehot,
        lax.all_gather(projectors, ("gx", "gy", "gz"), axis=0, tiled=True),
        precision=lax.Precision.HIGHEST,
    )
    hot_all = (slot_all[None, :] == slot_ids[:, None]) & member[None, :]
    slot_anchor = jnp.sum(jnp.where(hot_all[None, :, :], box_anchor[:, None, :], 0), axis=2)
    slot_extent = jnp.sum(jnp.where(hot_all, box_extent[None, :], 0), axis=1)
    slot_coupling = jnp.sum(jnp.where(hot_all[:, :, None], coupling[None, :, :], 0.0), axis=1)
    cell_offsets = jnp.arange(B, dtype=jnp.int32)
    limit = slot_extent[:, None, None, None]
    inside = (
        (cell_offsets[None, :, None, None] < limit)
        & (cell_offsets[None, None, :, None] < limit)
        & (cell_offsets[None, None, None, :] < limit)
    )
    buffer = buffer * inside.reshape(capacity, 1, B * B * B).astype(jnp.float32)
    return (buffer, slot_anchor, slot_coupling, count)


def nonlocal_term(field, buffer, slot_anchor, slot_coupling, count, domain_start):
    states = field.shape[0]

    def add_slot(slot_index, nonlocal_sum):
        corner = slot_anchor[:, slot_index] - domain_start
        start_cell = (0, corner[0], corner[1], corner[2])
        box_cells = lax.dynamic_slice(field, start_cell, (states, B, B, B)).reshape(
            states, B * B * B
        )
        proj_box = buffer[slot_index]
        coeffs = (
            jnp.dot(box_cells, proj_box.T, precision=lax.Precision.HIGHEST)
            * slot_coupling[slot_index][None, :]
        )
        addition = jnp.dot(coeffs, proj_box, precision=lax.Precision.HIGHEST).reshape(
            states, B, B, B
        )
        current = lax.dynamic_slice(nonlocal_sum, start_cell, (states, B, B, B))
        return lax.dynamic_update_slice(nonlocal_sum, current + addition, start_cell)

    return lax.fori_loop(0, count, add_slot, jnp.zeros_like(field))


def run_filter(field, apply_h):
    half_width = (UPPER - CUTOFF) / 2.0
    middle = (UPPER + CUTOFF) / 2.0
    sigma_one = half_width / (LOW_EDGE - middle)
    sigma_now = sigma_one
    result = (apply_h(field) - middle * field) * (sigma_one / half_width)
    previous = field
    for degree_step in range(1, DEGREE):
        sigma_next = 1.0 / (2.0 / sigma_one - sigma_now)
        next_state = (apply_h(result) - middle * result) * (
            2.0 * sigma_next / half_width
        ) - sigma_now * sigma_next * previous
        previous = result
        result = next_state
        sigma_now = sigma_next
    return result


def domain_body(orbitals, potential, projectors, owner_rank, box_anchor, box_extent, coupling):
    groups_y = lax.axis_size("gy")
    groups_z = lax.axis_size("gz")
    own_x = owner_rank // (groups_y * groups_z)
    own_y = owner_rank // groups_z % groups_y
    own_z = owner_rank % groups_z
    index_x = lax.axis_index("gx")
    index_y = lax.axis_index("gy")
    index_z = lax.axis_index("gz")
    span_x, span_y, span_z = (orbitals.shape[1], orbitals.shape[2], orbitals.shape[3])
    grid_anchor = jnp.stack([own_x * span_x, own_y * span_y, own_z * span_z]) + box_anchor
    member = (own_x == index_x) & (own_y == index_y) & (own_z == index_z)
    buffer, slot_anchor, slot_coupling, count = collect_boxes(
        projectors, member, grid_anchor, box_extent, coupling, 3 * ATOM_DEV
    )
    domain_start = jnp.stack([index_x * span_x, index_y * span_y, index_z * span_z])

    def apply_cube(field):
        padded = extended(field, (("gx", 1), ("gy", 2), ("gz", 3)), 6)
        return (
            -0.5 * laplace_padded(padded, field.shape)
            + potential[None] * field
            + nonlocal_term(field, buffer, slot_anchor, slot_coupling, count, domain_start)
        )

    filtered = run_filter(orbitals, apply_cube)
    flattened = filtered.reshape(filtered.shape[0], -1)
    partial_value = jnp.dot(flattened, flattened.T, precision=lax.Precision.HIGHEST)
    cells_total = span_x * span_y * span_z * lax.axis_size("gx") * groups_y * groups_z
    intersection = lax.psum(partial_value, ("gx", "gy", "gz")) / cells_total
    return (filtered, intersection)


SUB = 8
LANE = 128
HALF = LANE // 2
NPROJ = 4


def split_terms(matrix):
    high = matrix.astype(ml_dtypes.bfloat16)
    low = (matrix - high.astype(np.float64)).astype(ml_dtypes.bfloat16)
    return high, low


def stencil_weight(distance):
    if distance == 0 or abs(distance) > 6:
        return 0.0
    return -0.5 * STENCIL[abs(distance)] / (SPACING * SPACING)


def ring_matrix(length):
    matrix = np.zeros((length, length))
    for offset in range(-6, 7):
        for row in range(length):
            matrix[row, (row + offset) % length] += stencil_weight(offset)
    return matrix


def plane_weights(groups_y):
    slab = groups_y * HALF
    ring = ring_matrix(groups_y * SUB).reshape(groups_y, SUB, groups_y, SUB)
    blocks = []
    for shift in (-SUB, 0, SUB):
        along_x = np.array(
            [[stencil_weight(shift + i - o) for o in range(SUB)] for i in range(SUB)]
        )
        block = np.einsum("ab,io,jp->aijbop", np.eye(groups_y), along_x, np.eye(SUB))
        if shift == 0:
            block = block + np.einsum("ajbp,io->aijbop", ring, np.eye(SUB))
        blocks.append(block.reshape(slab, slab))
    high, low = split_terms(np.concatenate(blocks, axis=0))
    return np.concatenate([high, low], axis=0)


def depth_weights(groups_z):
    high, low = split_terms(ring_matrix(groups_z * LANE))
    return np.concatenate([high, low, high], axis=1)


def split_pair(value):
    high = value.astype(jnp.bfloat16)
    low = (value - high.astype(jnp.float32)).astype(jnp.bfloat16)
    return high, low


def mxu(left, right):
    return jnp.dot(left, right, preferred_element_type=jnp.float32)


def row_sums(values):
    row = lax.broadcasted_iota(jnp.int32, (SUB, LANE), 0)
    for stride in (1, 2, 4):
        keep = (row & stride) == 0
        values = [
            jnp.where(keep, one, two) + pltpu.roll(jnp.where(keep, two, one), stride, 0)
            for one, two in zip(values[0::2], values[1::2])
        ]
    return values[0]


SPARES = 3
TALL = 2 * SUB


def split_store(high_buf, low_buf, rows, cols, value):
    high, low = split_pair(value)
    high_buf[rows, cols] = high
    low_buf[rows, cols] = low


def slab_rows(slab_at, span):
    return pl.ds(pl.multiple_of(slab_at * span, span), span)


def plane_product(groups_x, span, high_buf, low_buf, plane, slabs):
    width = plane.shape[1]

    def around(buf, shift):
        parts = [
            buf[slab_rows(lax.rem(at + shift + groups_x, groups_x), span), :] for at in slabs
        ]
        return jnp.concatenate(parts, axis=0)

    high = [around(high_buf, shift) for shift in (-1, 0, 1)]
    low = [around(low_buf, shift) for shift in (-1, 0, 1)]
    left = jnp.concatenate(high + low + high, axis=1)
    right = jnp.concatenate([plane[: 3 * width], plane[: 3 * width], plane[3 * width :]], axis=0)
    return mxu(left, right)


def depth_product(span, high_buf, low_buf, depth, slab_at):
    high = high_buf[slab_rows(slab_at, span), :]
    low = low_buf[slab_rows(slab_at, span), :]
    return mxu(depth[...], jnp.concatenate([high, high, low], axis=0))


def lay_products(groups, high_buf, low_buf, plane, depth, slabs, near):
    groups_x, groups_y, groups_z = groups
    span = groups_z * LANE
    pairs_slab = groups_y // 2
    total = plane_product(groups_x, span, high_buf, low_buf, plane, slabs)
    for number, slab_at in enumerate(slabs):
        deep = depth_product(span, high_buf, low_buf, depth, slab_at)
        part = total[number * span : (number + 1) * span] + deep
        for tile in range(pairs_slab):
            cols = part[:, tile * LANE : (tile + 1) * LANE]
            near[slab_rows(slab_at * pairs_slab + tile, span), :] = cols


def chunk_of(groups_x):
    return 2 if groups_x % 2 == 0 else 1


def block_rows(groups_z, pair, parity, depth_at):
    return pl.ds(pl.multiple_of(((2 * pair + parity) * groups_z + depth_at) * HALF, HALF), HALF)


def first_kernel(groups, *refs):
    field_in, plane_in, depth_in, field, near = refs[:5]
    raw, high_buf, low_buf, plane, depth, sems = refs[5:]
    groups_x, groups_y, groups_z = groups
    span = groups_z * LANE
    pairs_slab = groups_y // 2
    loads = [
        pltpu.make_async_copy(source, target, sems.at[number])
        for number, (source, target) in enumerate(
            ((field_in, raw), (plane_in, plane), (depth_in, depth))
        )
    ]
    for load in loads:
        load.start()
    loads[0].wait()

    def lay_field(slab_at, carry):
        for tile in range(pairs_slab):
            pair = slab_at * pairs_slab + tile
            cols = slice(tile * LANE, (tile + 1) * LANE)
            for depth_at in range(groups_z):
                first = raw[block_rows(groups_z, pair, 0, depth_at), :]
                second = raw[block_rows(groups_z, pair, 1, depth_at), :]
                turned = jnp.concatenate([first, second], axis=0).T
                at = pl.multiple_of(pair * span + depth_at * LANE, LANE)
                field[pl.ds(at, LANE), :] = turned
                at = pl.multiple_of(slab_at * span + depth_at * LANE, LANE)
                split_store(high_buf, low_buf, pl.ds(at, LANE), cols, turned)
        return carry

    lax.fori_loop(0, groups_x, lay_field, 0)
    for load in loads[1:]:
        load.wait()
    chunk = chunk_of(groups_x)

    def product(chunk_at, carry):
        slabs = [chunk_at * chunk + number for number in range(chunk)]
        lay_products(groups, high_buf, low_buf, plane, depth, slabs, near)
        return carry

    lax.fori_loop(0, groups_x // chunk, product, 0)


def filter_kernel(groups, atoms, place, half, my_place, *refs):
    groups_x, groups_y, groups_z = groups
    pieces = groups_y * groups_z
    field_a, near_a = refs[:2]
    packs_in = refs[2 : 2 + pieces]
    plane_in, depth_in, out = refs[2 + pieces : 5 + pieces]
    (
        field_b,
        field_c,
        turned_out,
        local,
        coeffs,
        high_buf,
        low_buf,
        near,
        packs,
        plane,
        depth,
        in_sems,
        pack_sems,
        out_sems,
    ) = refs[5 + pieces : 5 + pieces + 14]
    spares = refs[5 + pieces + 14 :]
    targets = (near,) + tuple(spares)
    columns = groups_x * groups_y
    domains = columns * groups_z
    pairs = columns // 2
    span = groups_z * LANE
    pairs_slab = groups_y // 2
    per_device = atoms // domains // SUB
    chunk = chunk_of(groups_x)
    half_width = (UPPER - CUTOFF) / 2.0
    middle = (UPPER + CUTOFF) / 2.0
    diagonal = -0.5 * 3.0 * STENCIL[0] / (SPACING * SPACING) - middle
    lane = lax.broadcasted_iota(jnp.int32, (SUB, LANE), 1)
    lower = lane < HALF
    side = lane // HALF
    f32 = jnp.float32

    loads = [
        pltpu.make_async_copy(source, target, in_sems.at[number])
        for number, (source, target) in enumerate(
            ((near_a, near), (plane_in, plane), (depth_in, depth))
        )
    ]
    pack_loads = []
    for hop_z in range(groups_z):
        for hop_y in range(groups_y):
            source = packs_in[hop_z * groups_y + hop_y]
            for hop_x in range(groups_x):
                from_x = lax.rem(my_place[0] + (groups_x - hop_x), groups_x)
                from_y = lax.rem(my_place[1] + (groups_y - hop_y), groups_y)
                from_z = lax.rem(my_place[2] + (groups_z - hop_z), groups_z)
                device = (from_x * groups_y + from_y) * groups_z + from_z
                number = (hop_z * groups_y + hop_y) * groups_x + hop_x
                pack_loads.append(
                    pltpu.make_async_copy(
                        source.at[hop_x], packs.at[device], pack_sems.at[number]
                    )
                )
    for load in pack_loads + loads:
        load.start()
    for spare in spares:
        spare[...] = jnp.zeros(spare.shape, f32)
    for load in pack_loads + loads:
        load.wait()

    def lay_potential(pair, carry):
        for depth_at in range(groups_z):
            for row in range(SUB):
                first = packs[2 * pair * groups_z + depth_at, row]
                second = packs[(2 * pair + 1) * groups_z + depth_at, row]
                at = pl.multiple_of(pair * span + depth_at * LANE + row * SUB, SUB)
                local[pl.ds(at, SUB), :] = diagonal + jnp.where(
                    lower, first, pltpu.roll(second, HALF, 1)
                )
                at = pl.multiple_of(at + HALF, SUB)
                local[pl.ds(at, SUB), :] = diagonal + jnp.where(
                    lower, pltpu.roll(first, HALF, 1), second
                )
        return carry

    lax.fori_loop(0, pairs, lay_potential, 0)

    ones = (
        (
            lax.broadcasted_iota(jnp.int32, (LANE, LANE), 0) // HALF
            == lax.broadcasted_iota(jnp.int32, (LANE, LANE), 1) // HALF
        )
        .astype(f32)
        .astype(jnp.bfloat16)
    )

    def slab_groups(slab_at):
        for number in range(groups_y * groups_z):
            device = slab_at * (groups_y * groups_z) + number
            for inner in range(per_device):
                yield device, inner

    def apply_step(cur, prev, new, alpha, beta, first, last):
        def project(chunk_at, carry):
            slabs = [chunk_at * chunk + number for number in range(chunk)]
            if not first:
                lay_products(groups, high_buf, low_buf, plane, depth, slabs, near)
            for slab_at in slabs:
                for device, inner in slab_groups(slab_at):
                    group = device * per_device + inner
                    terms = ([], [])
                    for j in range(SUB):
                        atom = group * SUB + j
                        value = cur[pl.ds(place[atom], SUB), :]
                        both = jnp.where(side == half[atom], value, pltpu.roll(value, HALF, 1))
                        for kp in range(2):
                            at = SUB + (inner * 2 + kp) * SUB + j
                            terms[kp].append(both * packs[device, at])
                    for kp in range(2):
                        at = pl.multiple_of((group * 2 + kp) * SUB, SUB)
                        coeffs[pl.ds(at, SUB), :] = row_sums(terms[kp])
            return carry

        lax.fori_loop(0, groups_x // chunk, project, 0)

        high, low = split_pair(coeffs[...])
        coeffs[...] = mxu(high, ones) + mxu(low, ones)

        def scatter(slab_at, carry):
            for device, inner in slab_groups(slab_at):
                group = device * per_device + inner
                weights = [
                    coeffs[pl.ds(pl.multiple_of((group * 2 + kp) * SUB, SUB), SUB), :]
                    for kp in range(2)
                ]
                for j in range(SUB):
                    atom = group * SUB + j
                    parts = [
                        jnp.broadcast_to(weights[kp][j : j + 1], (SUB, LANE))
                        * packs[device, SUB + (inner * 2 + kp) * SUB + j]
                        for kp in range(2)
                    ]
                    value = parts[0] + parts[1]
                    value = value + pltpu.roll(value, HALF, 1)
                    value = jnp.where(side == half[atom], value, 0.0)
                    rows = pl.ds(place[atom], SUB)
                    target = targets[j % len(targets)]
                    target[rows, :] = target[rows, :] + value
            return carry

        lax.fori_loop(0, groups_x, scatter, 0)

        def combine(slab_at, carry):
            for tile in range(pairs_slab):
                pair = slab_at * pairs_slab + tile
                cols = slice(tile * LANE, (tile + 1) * LANE)
                for at_row in range(0, span, TALL):
                    rows = pl.ds(pl.multiple_of(pair * span + at_row, TALL), TALL)
                    slab_at_row = pl.ds(pl.multiple_of(slab_at * span + at_row, TALL), TALL)
                    total = local[rows, :] * cur[rows, :]
                    for target in targets:
                        total = total + target[rows, :]
                    if not last:
                        for target in targets[1:]:
                            target[rows, :] = jnp.zeros((TALL, LANE), f32)
                    total = total * alpha
                    if beta is not None:
                        total = total + beta * prev[rows, :]
                    new[rows, :] = total
                    if not last:
                        split_store(high_buf, low_buf, slab_at_row, cols, total)
                if last:
                    for depth_at in range(groups_z):
                        at = pl.multiple_of(pair * span + depth_at * LANE, LANE)
                        turned = new[pl.ds(at, LANE), :].T
                        turned_out[block_rows(groups_z, pair, 0, depth_at), :] = turned[:HALF]
                        turned_out[block_rows(groups_z, pair, 1, depth_at), :] = turned[HALF:]
                    rows = pl.ds(pl.multiple_of(pair * span, span), span)
                    pltpu.make_async_copy(
                        turned_out.at[rows], out.at[rows], out_sems.at[pair]
                    ).start()
            return carry

        lax.fori_loop(0, groups_x, combine, 0)

    sigma_one = half_width / (LOW_EDGE - middle)
    sigma_now = sigma_one
    apply_step(field_a, None, field_b, sigma_one / half_width, None, True, DEGREE == 1)
    prev, cur, new = field_a, field_b, field_c
    for degree_step in range(1, DEGREE):
        sigma_next = 1.0 / (2.0 / sigma_one - sigma_now)
        last = degree_step == DEGREE - 1
        target = prev if degree_step > 1 else new
        apply_step(
            cur,
            prev,
            target,
            2.0 * sigma_next / half_width,
            -sigma_now * sigma_next,
            False,
            last,
        )
        prev, cur = cur, target
        sigma_now = sigma_next

    def finish(pair, carry):
        rows = pl.ds(pl.multiple_of(pair * span, span), span)
        pltpu.make_async_copy(turned_out.at[rows], out.at[rows], out_sems.at[pair]).wait()
        return carry

    lax.fori_loop(0, pairs, finish, 0)


def packed_inputs(potential, projectors, extent, coupling):
    atoms = projectors.shape[0]
    cells = jnp.arange(B, dtype=jnp.int32)
    limit = extent[:, None, None, None]
    inside = (
        (cells[None, :, None, None] < limit)
        & (cells[None, None, :, None] < limit)
        & (cells[None, None, None, :] < limit)
    )
    masked = jnp.where(
        inside.reshape(atoms, 1, B * B * B), projectors * jnp.sqrt(coupling)[:, :, None], 0.0
    ).reshape(atoms // SUB, SUB, 2, 2, B * B, B)
    masked = masked.transpose(0, 2, 1, 5, 3, 4).reshape(atoms // SUB * 2 * B, SUB, LANE)
    shaped = potential.reshape(HALF, 2, HALF).transpose(2, 1, 0).reshape(SUB, SUB, LANE)
    return jnp.concatenate([shaped, masked], axis=0)


def box_places(groups, owner, anchor):
    groups_z = groups[2]
    column = owner // groups_z
    place = (column // 2 * groups_z + owner % groups_z) * LANE + anchor
    return place, column % 2


def weights_of(groups):
    return jnp.asarray(plane_weights(groups[1])), jnp.asarray(depth_weights(groups[2]))


def first_call(groups, field, interpret=False):
    groups_x, groups_y, groups_z = groups
    span = groups_z * LANE
    cells = (groups_x * groups_y // 2 * span, LANE)
    slabs = (groups_x * span, groups_y * HALF)
    plane, depth = weights_of(groups)
    vmem = pl.BlockSpec(memory_space=pltpu.VMEM)
    anywhere = pl.BlockSpec(memory_space=pl.ANY)
    in_hbm = pl.BlockSpec(memory_space=pltpu.HBM)
    work = 2 * slabs[0] * slabs[1] * (9 * slabs[1] + 3 * span)
    return pl.pallas_call(
        functools.partial(first_kernel, groups),
        out_shape=[
            jax.ShapeDtypeStruct(cells, jnp.float32),
            jax.ShapeDtypeStruct(cells, jnp.float32),
        ],
        in_specs=[anywhere, in_hbm, in_hbm],
        out_specs=[vmem] * 2,
        scratch_shapes=[
            pltpu.VMEM(cells, jnp.float32),
            pltpu.VMEM(slabs, jnp.bfloat16),
            pltpu.VMEM(slabs, jnp.bfloat16),
            pltpu.VMEM(plane.shape, plane.dtype),
            pltpu.VMEM(depth.shape, depth.dtype),
            pltpu.SemaphoreType.DMA((3,)),
        ],
        compiler_params=pltpu.CompilerParams(vmem_limit_bytes=16 * 1024 * 1024),
        cost_estimate=pl.CostEstimate(
            flops=work, bytes_accessed=4 * field.size * 4, transcendentals=0
        ),
        interpret=interpret,
    )(field.reshape(cells), plane, depth)


def filter_call(groups, place, half, my_place, field, near, packs, interpret=False):
    groups_x, groups_y, groups_z = groups
    columns = groups_x * groups_y
    atoms = place.shape[0]
    plane, depth = weights_of(groups)
    vmem = pl.BlockSpec(memory_space=pltpu.VMEM)
    anywhere = pl.BlockSpec(memory_space=pl.ANY)
    smem = pl.BlockSpec(memory_space=pltpu.SMEM)
    slabs = (groups_x * groups_z * LANE, groups_y * HALF)
    work = 2 * slabs[0] * slabs[1] * (9 * slabs[1] + 3 * groups_z * LANE)
    in_hbm = pl.BlockSpec(memory_space=pltpu.HBM)
    out = pl.pallas_call(
        functools.partial(filter_kernel, groups, atoms),
        out_shape=jax.ShapeDtypeStruct(field.shape, jnp.float32),
        in_specs=[smem] * 3 + [vmem] * 2 + [anywhere] * len(packs) + [in_hbm] * 2,
        out_specs=anywhere,
        scratch_shapes=[
            pltpu.VMEM(field.shape, jnp.float32),
            pltpu.VMEM(field.shape, jnp.float32),
            pltpu.VMEM(field.shape, jnp.float32),
            pltpu.VMEM(field.shape, jnp.float32),
            pltpu.VMEM((atoms * 2, LANE), jnp.float32),
            pltpu.VMEM(slabs, jnp.bfloat16),
            pltpu.VMEM(slabs, jnp.bfloat16),
            pltpu.VMEM(near.shape, jnp.float32),
            pltpu.VMEM((columns * groups_z,) + packs[0].shape[1:], jnp.float32),
            pltpu.VMEM(plane.shape, plane.dtype),
            pltpu.VMEM(depth.shape, depth.dtype),
            pltpu.SemaphoreType.DMA((3,)),
            pltpu.SemaphoreType.DMA((columns * groups_z,)),
            pltpu.SemaphoreType.DMA((columns // 2,)),
        ]
        + [pltpu.VMEM(field.shape, jnp.float32) for _ in range(SPARES)],
        compiler_params=pltpu.CompilerParams(vmem_limit_bytes=22 * 1024 * 1024),
        cost_estimate=pl.CostEstimate(
            flops=3 * work, bytes_accessed=8 * field.size * 4, transcendentals=0
        ),
        interpret=interpret,
    )(place, half, my_place, field, near, *packs, plane, depth)
    return out.reshape(columns * groups_z, SUB, SUB, LANE)


def hops(value, axis):
    count = lax.axis_size(axis)
    return [value] + [
        lax.ppermute(value, axis, [(i, (i + hop) % count) for i in range(count)])
        for hop in range(1, count)
    ]


def state_body(orbitals, potential, projectors, owner_rank, box_anchor, box_extent, coupling):
    axes = ("gx", "gy", "gz")
    groups = tuple(lax.axis_size(axis) for axis in axes)
    groups_z = groups[2]
    domains = groups[0] * groups[1] * groups_z
    atoms_own = projectors.shape[0]
    my_place = jnp.stack([lax.axis_index(axis) for axis in axes])
    me = (my_place[0] * groups[1] + my_place[1]) * groups_z + my_place[2]
    extent = lax.dynamic_slice(box_extent, (me * atoms_own,), (atoms_own,))
    own = lax.dynamic_slice(coupling, (me * atoms_own, 0), (atoms_own, NPROJ))
    pack = packed_inputs(potential, projectors, extent, own)
    line = jnp.stack(hops(pack, "gx"))
    orbitals, line = lax.optimization_barrier((orbitals, line))
    crossed = [hops(piece, "gz") for piece in hops(line, "gy")]
    packs = [crossed[hop_y][hop_z] for hop_z in range(groups_z) for hop_y in range(groups[1])]
    field = lax.all_to_all(orbitals, axes, split_axis=0, concat_axis=0, tiled=True)
    field, near = first_call(groups, field)
    place, half = box_places(groups, owner_rank, box_anchor[2])
    result = filter_call(groups, place, half, my_place, field, near, packs)
    filtered = lax.all_to_all(result, axes, split_axis=0, concat_axis=0, tiled=True)
    states = filtered.shape[0]
    flattened = filtered.reshape(states, -1)
    partial_value = jnp.dot(flattened, flattened.T, precision=lax.Precision.HIGHEST)
    quarter = partial_value.reshape(-1, SUB, states).transpose(1, 0, 2).reshape(SUB, -1)
    parts = lax.all_to_all(
        jnp.broadcast_to(quarter[None], (domains,) + quarter.shape),
        axes,
        split_axis=0,
        concat_axis=0,
        tiled=True,
    )
    summed = jnp.sum(parts, axis=0).reshape(SUB, -1, states).transpose(1, 0, 2)
    cells_total = orbitals.shape[1] * orbitals.shape[2] * orbitals.shape[3] * domains
    intersection = summed.reshape(states, states) / cells_total
    return (filtered, intersection)


def body(orbitals, potential, projectors, owner_rank, box_anchor, box_extent, coupling):
    domains = lax.axis_size("gx") * lax.axis_size("gy") * lax.axis_size("gz")
    whole_states = (
        orbitals.shape == (domains, SUB, SUB, LANE)
        and projectors.shape[0] % SUB == 0
        and projectors.shape[1] == NPROJ
        and lax.axis_size("gy") % 2 == 0
    )
    chosen = state_body if whole_states else domain_body
    return chosen(
        orbitals, potential, projectors, owner_rank, box_anchor, box_extent, coupling
    )


def solution(mesh):
    return jax.shard_map(
        body,
        mesh=mesh,
        in_specs=(
            P(None, "gx", "gy", "gz"),
            P("gx", "gy", "gz"),
            P(("gx", "gy", "gz"), None, None),
            P(),
            P(),
            P(),
            P(),
        ),
        out_specs=(P(None, "gx", "gy", "gz"), P()),
        check_vma=False,
    )
```

```python
import functools
import math
import jax
import jax.numpy as jnp
from jax import lax
from jax.experimental import pallas as pl
from jax.experimental.pallas import tpu as pltpu
import ml_dtypes
import numpy as np
from jax.sharding import PartitionSpec as P

B = 8
DEGREE = 4
ATOM_DEV = 8


STENCIL = (
    -5369.0 / 1800.0,
    12.0 / 7.0,
    -15.0 / 56.0,
    10.0 / 189.0,
    -1.0 / 112.0,
    2.0 / 1925.0,
    -1.0 / 16632.0,
)
SPACING = 0.5
LOW_EDGE = -2.5
CUTOFF = 4.0
UPPER = 60.0


def extended(cells, sides, width):
    for axis, dim in sides:
        count = lax.axis_size(axis)
        head = lax.slice_in_dim(cells, 0, width, axis=dim)
        tail = lax.slice_in_dim(cells, cells.shape[dim] - width, cells.shape[dim], axis=dim)
        cells = jnp.concatenate(
            [
                lax.ppermute(tail, axis, [(i, (i + 1) % count) for i in range(count)]),
                cells,
                lax.ppermute(head, axis, [((i + 1) % count, i) for i in range(count)]),
            ],
            axis=dim,
        )
    return cells


def laplace_padded(padded, shape):
    span_x, span_y, span_z = (shape[1], shape[2], shape[3])
    summed = 3.0 * STENCIL[0] * padded[:, 6 : 6 + span_x, 6 : 6 + span_y, 6 : 6 + span_z]
    for offset in range(1, 7):
        weight = STENCIL[offset]
        summed = summed + weight * (
            padded[:, 6 + offset : 6 + offset + span_x, 6 : 6 + span_y, 6 : 6 + span_z]
            + padded[:, 6 - offset : 6 - offset + span_x, 6 : 6 + span_y, 6 : 6 + span_z]
        )
        summed = summed + weight * (
            padded[:, 6 : 6 + span_x, 6 + offset : 6 + offset + span_y, 6 : 6 + span_z]
            + padded[:, 6 : 6 + span_x, 6 - offset : 6 - offset + span_y, 6 : 6 + span_z]
        )
        summed = summed + weight * (
            padded[:, 6 : 6 + span_x, 6 : 6 + span_y, 6 + offset : 6 + offset + span_z]
            + padded[:, 6 : 6 + span_x, 6 : 6 + span_y, 6 - offset : 6 - offset + span_z]
        )
    return summed / (SPACING * SPACING)


def collect_boxes(projectors, member, box_anchor, box_extent, coupling, capacity):
    member_int = member.astype(jnp.int32)
    slot_all = jnp.cumsum(member_int) - 1
    count = jnp.sum(member_int)
    slot_ids = jnp.arange(capacity, dtype=jnp.int32)
    onehot = ((slot_all[None, :] == slot_ids[:, None]) & member[None, :]).astype(jnp.float32)
    buffer = jnp.einsum(
        "cp,pkf->ckf",
        onehot,
        lax.all_gather(projectors, ("gx", "gy", "gz"), axis=0, tiled=True),
        precision=lax.Precision.HIGHEST,
    )
    hot_all = (slot_all[None, :] == slot_ids[:, None]) & member[None, :]
    slot_anchor = jnp.sum(jnp.where(hot_all[None, :, :], box_anchor[:, None, :], 0), axis=2)
    slot_extent = jnp.sum(jnp.where(hot_all, box_extent[None, :], 0), axis=1)
    slot_coupling = jnp.sum(jnp.where(hot_all[:, :, None], coupling[None, :, :], 0.0), axis=1)
    cell_offsets = jnp.arange(B, dtype=jnp.int32)
    limit = slot_extent[:, None, None, None]
    inside = (
        (cell_offsets[None, :, None, None] < limit)
        & (cell_offsets[None, None, :, None] < limit)
        & (cell_offsets[None, None, None, :] < limit)
    )
    buffer = buffer * inside.reshape(capacity, 1, B * B * B).astype(jnp.float32)
    return (buffer, slot_anchor, slot_coupling, count)


def nonlocal_term(field, buffer, slot_anchor, slot_coupling, count, domain_start):
    states = field.shape[0]

    def add_slot(slot_index, nonlocal_sum):
        corner = slot_anchor[:, slot_index] - domain_start
        start_cell = (0, corner[0], corner[1], corner[2])
        box_cells = lax.dynamic_slice(field, start_cell, (states, B, B, B)).reshape(
            states, B * B * B
        )
        proj_box = buffer[slot_index]
        coeffs = (
            jnp.dot(box_cells, proj_box.T, precision=lax.Precision.HIGHEST)
            * slot_coupling[slot_index][None, :]
        )
        addition = jnp.dot(coeffs, proj_box, precision=lax.Precision.HIGHEST).reshape(
            states, B, B, B
        )
        current = lax.dynamic_slice(nonlocal_sum, start_cell, (states, B, B, B))
        return lax.dynamic_update_slice(nonlocal_sum, current + addition, start_cell)

    return lax.fori_loop(0, count, add_slot, jnp.zeros_like(field))


def run_filter(field, apply_h):
    half_width = (UPPER - CUTOFF) / 2.0
    middle = (UPPER + CUTOFF) / 2.0
    sigma_one = half_width / (LOW_EDGE - middle)
    sigma_now = sigma_one
    result = (apply_h(field) - middle * field) * (sigma_one / half_width)
    previous = field
    for degree_step in range(1, DEGREE):
        sigma_next = 1.0 / (2.0 / sigma_one - sigma_now)
        next_state = (apply_h(result) - middle * result) * (
            2.0 * sigma_next / half_width
        ) - sigma_now * sigma_next * previous
        previous = result
        result = next_state
        sigma_now = sigma_next
    return result


def domain_body(orbitals, potential, projectors, owner_rank, box_anchor, box_extent, coupling):
    groups_y = lax.axis_size("gy")
    groups_z = lax.axis_size("gz")
    own_x = owner_rank // (groups_y * groups_z)
    own_y = owner_rank // groups_z % groups_y
    own_z = owner_rank % groups_z
    index_x = lax.axis_index("gx")
    index_y = lax.axis_index("gy")
    index_z = lax.axis_index("gz")
    span_x, span_y, span_z = (orbitals.shape[1], orbitals.shape[2], orbitals.shape[3])
    grid_anchor = jnp.stack([own_x * span_x, own_y * span_y, own_z * span_z]) + box_anchor
    member = (own_x == index_x) & (own_y == index_y) & (own_z == index_z)
    buffer, slot_anchor, slot_coupling, count = collect_boxes(
        projectors, member, grid_anchor, box_extent, coupling, 3 * ATOM_DEV
    )
    domain_start = jnp.stack([index_x * span_x, index_y * span_y, index_z * span_z])

    def apply_cube(field):
        padded = extended(field, (("gx", 1), ("gy", 2), ("gz", 3)), 6)
        return (
            -0.5 * laplace_padded(padded, field.shape)
            + potential[None] * field
            + nonlocal_term(field, buffer, slot_anchor, slot_coupling, count, domain_start)
        )

    filtered = run_filter(orbitals, apply_cube)
    flattened = filtered.reshape(filtered.shape[0], -1)
    partial_value = jnp.dot(flattened, flattened.T, precision=lax.Precision.HIGHEST)
    cells_total = span_x * span_y * span_z * lax.axis_size("gx") * groups_y * groups_z
    intersection = lax.psum(partial_value, ("gx", "gy", "gz")) / cells_total
    return (filtered, intersection)


SUB = 8
LANE = 128
HALF = LANE // 2
NPROJ = 4


def split_terms(matrix):
    high = matrix.astype(ml_dtypes.bfloat16)
    low = (matrix - high.astype(np.float64)).astype(ml_dtypes.bfloat16)
    return high, low


def stencil_weight(distance):
    if distance == 0 or abs(distance) > 6:
        return 0.0
    return -0.5 * STENCIL[abs(distance)] / (SPACING * SPACING)


def ring_matrix(length):
    matrix = np.zeros((length, length))
    for offset in range(-6, 7):
        for row in range(length):
            matrix[row, (row + offset) % length] += stencil_weight(offset)
    return matrix


def plane_weights(groups_y):
    slab = groups_y * HALF
    ring = ring_matrix(groups_y * SUB).reshape(groups_y, SUB, groups_y, SUB)
    blocks = []
    for shift in (-SUB, 0, SUB):
        along_x = np.array(
            [[stencil_weight(shift + i - o) for o in range(SUB)] for i in range(SUB)]
        )
        block = np.einsum("ab,io,jp->aijbop", np.eye(groups_y), along_x, np.eye(SUB))
        if shift == 0:
            block = block + np.einsum("ajbp,io->aijbop", ring, np.eye(SUB))
        blocks.append(block.reshape(slab, slab))
    high, low = split_terms(np.concatenate(blocks, axis=0))
    return np.concatenate([high, low], axis=0)


def depth_weights(groups_z):
    high, low = split_terms(ring_matrix(groups_z * LANE))
    return np.concatenate([high, low, high], axis=1)


def split_pair(value):
    high = value.astype(jnp.bfloat16)
    low = (value - high.astype(jnp.float32)).astype(jnp.bfloat16)
    return high, low


def mxu(left, right):
    return jnp.dot(left, right, preferred_element_type=jnp.float32)


def row_sums(values):
    row = lax.broadcasted_iota(jnp.int32, (SUB, LANE), 0)
    for stride in (1, 2, 4):
        keep = (row & stride) == 0
        values = [
            jnp.where(keep, one, two) + pltpu.roll(jnp.where(keep, two, one), stride, 0)
            for one, two in zip(values[0::2], values[1::2])
        ]
    return values[0]


SPARES = 3
TALL = 2 * SUB


def split_store(high_buf, low_buf, rows, cols, value):
    high, low = split_pair(value)
    high_buf[rows, cols] = high
    low_buf[rows, cols] = low


def slab_rows(slab_at, span):
    return pl.ds(pl.multiple_of(slab_at * span, span), span)


def plane_product(groups_x, span, high_buf, low_buf, plane, slabs):
    width = plane.shape[1]

    def around(buf, shift):
        parts = [
            buf[slab_rows(lax.rem(at + shift + groups_x, groups_x), span), :] for at in slabs
        ]
        return jnp.concatenate(parts, axis=0)

    high = [around(high_buf, shift) for shift in (-1, 0, 1)]
    low = [around(low_buf, shift) for shift in (-1, 0, 1)]
    left = jnp.concatenate(high + low + high, axis=1)
    right = jnp.concatenate([plane[: 3 * width], plane[: 3 * width], plane[3 * width :]], axis=0)
    return mxu(left, right)


def depth_product(span, high_buf, low_buf, depth, slab_at):
    high = high_buf[slab_rows(slab_at, span), :]
    low = low_buf[slab_rows(slab_at, span), :]
    return mxu(depth[...], jnp.concatenate([high, high, low], axis=0))


def lay_products(groups, high_buf, low_buf, plane, depth, slabs, near):
    groups_x, groups_y, groups_z = groups
    span = groups_z * LANE
    pairs_slab = groups_y // 2
    total = plane_product(groups_x, span, high_buf, low_buf, plane, slabs)
    for number, slab_at in enumerate(slabs):
        deep = depth_product(span, high_buf, low_buf, depth, slab_at)
        part = total[number * span : (number + 1) * span] + deep
        for tile in range(pairs_slab):
            cols = part[:, tile * LANE : (tile + 1) * LANE]
            near[slab_rows(slab_at * pairs_slab + tile, span), :] = cols


def chunk_of(groups_x):
    return 2 if groups_x % 2 == 0 else 1


def block_rows(groups_z, pair, parity, depth_at):
    return pl.ds(pl.multiple_of(((2 * pair + parity) * groups_z + depth_at) * HALF, HALF), HALF)


def first_kernel(groups, *refs):
    field_in, plane_in, depth_in, field, near = refs[:5]
    raw, high_buf, low_buf, plane, depth, sems = refs[5:]
    groups_x, groups_y, groups_z = groups
    span = groups_z * LANE
    pairs_slab = groups_y // 2
    loads = [
        pltpu.make_async_copy(source, target, sems.at[number])
        for number, (source, target) in enumerate(
            ((field_in, raw), (plane_in, plane), (depth_in, depth))
        )
    ]
    for load in loads:
        load.start()
    loads[0].wait()

    def lay_field(slab_at, carry):
        for tile in range(pairs_slab):
            pair = slab_at * pairs_slab + tile
            cols = slice(tile * LANE, (tile + 1) * LANE)
            for depth_at in range(groups_z):
                first = raw[block_rows(groups_z, pair, 0, depth_at), :]
                second = raw[block_rows(groups_z, pair, 1, depth_at), :]
                turned = jnp.concatenate([first, second], axis=0).T
                at = pl.multiple_of(pair * span + depth_at * LANE, LANE)
                field[pl.ds(at, LANE), :] = turned
                at = pl.multiple_of(slab_at * span + depth_at * LANE, LANE)
                split_store(high_buf, low_buf, pl.ds(at, LANE), cols, turned)
        return carry

    lax.fori_loop(0, groups_x, lay_field, 0)
    for load in loads[1:]:
        load.wait()
    chunk = chunk_of(groups_x)

    def product(chunk_at, carry):
        slabs = [chunk_at * chunk + number for number in range(chunk)]
        lay_products(groups, high_buf, low_buf, plane, depth, slabs, near)
        return carry

    lax.fori_loop(0, groups_x // chunk, product, 0)


def filter_kernel(groups, atoms, place, half, my_place, *refs):
    groups_x, groups_y, groups_z = groups
    pieces = groups_y * groups_z
    field_a, near_a = refs[:2]
    packs_in = refs[2 : 2 + pieces]
    plane_in, depth_in, out = refs[2 + pieces : 5 + pieces]
    (
        field_b,
        field_c,
        turned_out,
        local,
        coeffs,
        high_buf,
        low_buf,
        near,
        packs,
        plane,
        depth,
        in_sems,
        pack_sems,
        out_sems,
    ) = refs[5 + pieces : 5 + pieces + 14]
    spares = refs[5 + pieces + 14 :]
    targets = (near,) + tuple(spares)
    columns = groups_x * groups_y
    domains = columns * groups_z
    pairs = columns // 2
    span = groups_z * LANE
    pairs_slab = groups_y // 2
    per_device = atoms // domains // SUB
    chunk = chunk_of(groups_x)
    half_width = (UPPER - CUTOFF) / 2.0
    middle = (UPPER + CUTOFF) / 2.0
    diagonal = -0.5 * 3.0 * STENCIL[0] / (SPACING * SPACING) - middle
    lane = lax.broadcasted_iota(jnp.int32, (SUB, LANE), 1)
    lower = lane < HALF
    side = lane // HALF
    row = lax.broadcasted_iota(jnp.int32, (SUB, LANE), 0)
    f32 = jnp.float32

    loads = [
        pltpu.make_async_copy(source, target, in_sems.at[number])
        for number, (source, target) in enumerate(
            ((near_a, near), (plane_in, plane), (depth_in, depth))
        )
    ]
    pack_loads = []
    for hop_z in range(groups_z):
        for hop_y in range(groups_y):
            source = packs_in[hop_z * groups_y + hop_y]
            for hop_x in range(groups_x):
                from_x = lax.rem(my_place[0] + (groups_x - hop_x), groups_x)
                from_y = lax.rem(my_place[1] + (groups_y - hop_y), groups_y)
                from_z = lax.rem(my_place[2] + (groups_z - hop_z), groups_z)
                device = (from_x * groups_y + from_y) * groups_z + from_z
                number = (hop_z * groups_y + hop_y) * groups_x + hop_x
                pack_loads.append(
                    pltpu.make_async_copy(
                        source.at[hop_x], packs.at[device], pack_sems.at[number]
                    )
                )
    for load in pack_loads + loads:
        load.start()
    for spare in spares:
        spare[...] = jnp.zeros(spare.shape, f32)
    for load in pack_loads + loads:
        load.wait()

    def lay_potential(pair, carry):
        for depth_at in range(groups_z):
            for tile in range(SUB):
                first = packs[2 * pair * groups_z + depth_at, tile]
                second = packs[(2 * pair + 1) * groups_z + depth_at, tile]
                at = pl.multiple_of(pair * span + depth_at * LANE + tile * SUB, SUB)
                local[pl.ds(at, SUB), :] = diagonal + jnp.where(
                    lower, first, pltpu.roll(second, HALF, 1)
                )
                at = pl.multiple_of(at + HALF, SUB)
                local[pl.ds(at, SUB), :] = diagonal + jnp.where(
                    lower, pltpu.roll(first, HALF, 1), second
                )
        return carry

    lax.fori_loop(0, pairs, lay_potential, 0)

    ones = (
        (
            lax.broadcasted_iota(jnp.int32, (LANE, LANE), 0) // HALF
            == lax.broadcasted_iota(jnp.int32, (LANE, LANE), 1) // HALF
        )
        .astype(f32)
        .astype(jnp.bfloat16)
    )

    def slab_groups(slab_at):
        for number in range(groups_y * groups_z):
            device = slab_at * (groups_y * groups_z) + number
            for inner in range(per_device):
                yield device, inner

    def box_tiles(atom):
        at = place[atom]
        turn = at & (SUB - 1)
        base = pl.multiple_of(at - turn, SUB)
        after = pl.multiple_of(base + jnp.where(turn > 0, SUB, 0), SUB)
        return turn, pl.ds(base, SUB), pl.ds(after, SUB)

    def turn_projectors(device, carry):
        for inner in range(per_device):
            for j in range(SUB):
                turn = place[(device * per_device + inner) * SUB + j] & (SUB - 1)
                for kp in range(2):
                    at = SUB + (inner * 2 + kp) * SUB + j
                    packs[device, at] = pltpu.roll(packs[device, at], turn, 0)
        return carry

    lax.fori_loop(0, domains, turn_projectors, 0)

    def apply_step(cur, prev, new, alpha, beta, first, last):
        def project(chunk_at, carry):
            slabs = [chunk_at * chunk + number for number in range(chunk)]
            if not first:
                lay_products(groups, high_buf, low_buf, plane, depth, slabs, near)
            for slab_at in slabs:
                for device, inner in slab_groups(slab_at):
                    group = device * per_device + inner
                    terms = ([], [])
                    for j in range(SUB):
                        atom = group * SUB + j
                        turn, rows, rows_after = box_tiles(atom)
                        value = jnp.where(row >= turn, cur[rows, :], cur[rows_after, :])
                        both = jnp.where(side == half[atom], value, pltpu.roll(value, HALF, 1))
                        for kp in range(2):
                            at = SUB + (inner * 2 + kp) * SUB + j
                            terms[kp].append(both * packs[device, at])
                    for kp in range(2):
                        at = pl.multiple_of((group * 2 + kp) * SUB, SUB)
                        coeffs[pl.ds(at, SUB), :] = row_sums(terms[kp])
            return carry

        lax.fori_loop(0, groups_x // chunk, project, 0)

        high, low = split_pair(coeffs[...])
        coeffs[...] = mxu(high, ones) + mxu(low, ones)

        def scatter(slab_at, carry):
            for device, inner in slab_groups(slab_at):
                group = device * per_device + inner
                weights = [
                    coeffs[pl.ds(pl.multiple_of((group * 2 + kp) * SUB, SUB), SUB), :]
                    for kp in range(2)
                ]
                for j in range(SUB):
                    atom = group * SUB + j
                    parts = [
                        jnp.broadcast_to(weights[kp][j : j + 1], (SUB, LANE))
                        * packs[device, SUB + (inner * 2 + kp) * SUB + j]
                        for kp in range(2)
                    ]
                    value = parts[0] + parts[1]
                    value = value + pltpu.roll(value, HALF, 1)
                    value = jnp.where(side == half[atom], value, 0.0)
                    turn, rows, rows_after = box_tiles(atom)
                    target = targets[j % len(targets)]
                    target[rows, :] = target[rows, :] + jnp.where(row >= turn, value, 0.0)
                    target[rows_after, :] = target[rows_after, :] + jnp.where(
                        row >= turn, 0.0, value
                    )
            return carry

        lax.fori_loop(0, groups_x, scatter, 0)

        def combine(slab_at, carry):
            for tile in range(pairs_slab):
                pair = slab_at * pairs_slab + tile
                cols = slice(tile * LANE, (tile + 1) * LANE)
                for at_row in range(0, span, TALL):
                    rows = pl.ds(pl.multiple_of(pair * span + at_row, TALL), TALL)
                    slab_at_row = pl.ds(pl.multiple_of(slab_at * span + at_row, TALL), TALL)
                    total = local[rows, :] * cur[rows, :]
                    for target in targets:
                        total = total + target[rows, :]
                    if not last:
                        for target in targets[1:]:
                            target[rows, :] = jnp.zeros((TALL, LANE), f32)
                    total = total * alpha
                    if beta is not None:
                        total = total + beta * prev[rows, :]
                    new[rows, :] = total
                    if not last:
                        split_store(high_buf, low_buf, slab_at_row, cols, total)
                if last:
                    for depth_at in range(groups_z):
                        at = pl.multiple_of(pair * span + depth_at * LANE, LANE)
                        turned = new[pl.ds(at, LANE), :].T
                        turned_out[block_rows(groups_z, pair, 0, depth_at), :] = turned[:HALF]
                        turned_out[block_rows(groups_z, pair, 1, depth_at), :] = turned[HALF:]
                    rows = pl.ds(pl.multiple_of(pair * span, span), span)
                    pltpu.make_async_copy(
                        turned_out.at[rows], out.at[rows], out_sems.at[pair]
                    ).start()
            return carry

        lax.fori_loop(0, groups_x, combine, 0)

    sigma_one = half_width / (LOW_EDGE - middle)
    sigma_now = sigma_one
    apply_step(field_a, None, field_b, sigma_one / half_width, None, True, DEGREE == 1)
    prev, cur, new = field_a, field_b, field_c
    for degree_step in range(1, DEGREE):
        sigma_next = 1.0 / (2.0 / sigma_one - sigma_now)
        last = degree_step == DEGREE - 1
        target = prev if degree_step > 1 else new
        apply_step(
            cur,
            prev,
            target,
            2.0 * sigma_next / half_width,
            -sigma_now * sigma_next,
            False,
            last,
        )
        prev, cur = cur, target
        sigma_now = sigma_next

    def finish(pair, carry):
        rows = pl.ds(pl.multiple_of(pair * span, span), span)
        pltpu.make_async_copy(turned_out.at[rows], out.at[rows], out_sems.at[pair]).wait()
        return carry

    lax.fori_loop(0, pairs, finish, 0)


def packed_inputs(potential, projectors, extent, coupling):
    atoms = projectors.shape[0]
    cells = jnp.arange(B, dtype=jnp.int32)
    limit = extent[:, None, None, None]
    inside = (
        (cells[None, :, None, None] < limit)
        & (cells[None, None, :, None] < limit)
        & (cells[None, None, None, :] < limit)
    )
    masked = jnp.where(
        inside.reshape(atoms, 1, B * B * B), projectors * jnp.sqrt(coupling)[:, :, None], 0.0
    ).reshape(atoms // SUB, SUB, 2, 2, B * B, B)
    masked = masked.transpose(0, 2, 1, 5, 3, 4).reshape(atoms // SUB * 2 * B, SUB, LANE)
    shaped = potential.reshape(HALF, 2, HALF).transpose(2, 1, 0).reshape(SUB, SUB, LANE)
    return jnp.concatenate([shaped, masked], axis=0)


def box_places(groups, owner, anchor):
    groups_z = groups[2]
    column = owner // groups_z
    place = (column // 2 * groups_z + owner % groups_z) * LANE + anchor
    return place, column % 2


def weights_of(groups):
    return jnp.asarray(plane_weights(groups[1])), jnp.asarray(depth_weights(groups[2]))


def first_call(groups, field, interpret=False):
    groups_x, groups_y, groups_z = groups
    span = groups_z * LANE
    cells = (groups_x * groups_y // 2 * span, LANE)
    slabs = (groups_x * span, groups_y * HALF)
    plane, depth = weights_of(groups)
    vmem = pl.BlockSpec(memory_space=pltpu.VMEM)
    anywhere = pl.BlockSpec(memory_space=pl.ANY)
    in_hbm = pl.BlockSpec(memory_space=pltpu.HBM)
    work = 2 * slabs[0] * slabs[1] * (9 * slabs[1] + 3 * span)
    return pl.pallas_call(
        functools.partial(first_kernel, groups),
        out_shape=[
            jax.ShapeDtypeStruct(cells, jnp.float32),
            jax.ShapeDtypeStruct(cells, jnp.float32),
        ],
        in_specs=[anywhere, in_hbm, in_hbm],
        out_specs=[vmem] * 2,
        scratch_shapes=[
            pltpu.VMEM(cells, jnp.float32),
            pltpu.VMEM(slabs, jnp.bfloat16),
            pltpu.VMEM(slabs, jnp.bfloat16),
            pltpu.VMEM(plane.shape, plane.dtype),
            pltpu.VMEM(depth.shape, depth.dtype),
            pltpu.SemaphoreType.DMA((3,)),
        ],
        compiler_params=pltpu.CompilerParams(vmem_limit_bytes=16 * 1024 * 1024),
        cost_estimate=pl.CostEstimate(
            flops=work, bytes_accessed=4 * field.size * 4, transcendentals=0
        ),
        interpret=interpret,
    )(field.reshape(cells), plane, depth)


def filter_call(groups, place, half, my_place, field, near, packs, interpret=False):
    groups_x, groups_y, groups_z = groups
    columns = groups_x * groups_y
    atoms = place.shape[0]
    plane, depth = weights_of(groups)
    vmem = pl.BlockSpec(memory_space=pltpu.VMEM)
    anywhere = pl.BlockSpec(memory_space=pl.ANY)
    smem = pl.BlockSpec(memory_space=pltpu.SMEM)
    slabs = (groups_x * groups_z * LANE, groups_y * HALF)
    work = 2 * slabs[0] * slabs[1] * (9 * slabs[1] + 3 * groups_z * LANE)
    in_hbm = pl.BlockSpec(memory_space=pltpu.HBM)
    out = pl.pallas_call(
        functools.partial(filter_kernel, groups, atoms),
        out_shape=jax.ShapeDtypeStruct(field.shape, jnp.float32),
        in_specs=[smem] * 3 + [vmem] * 2 + [anywhere] * len(packs) + [in_hbm] * 2,
        out_specs=anywhere,
        scratch_shapes=[
            pltpu.VMEM(field.shape, jnp.float32),
            pltpu.VMEM(field.shape, jnp.float32),
            pltpu.VMEM(field.shape, jnp.float32),
            pltpu.VMEM(field.shape, jnp.float32),
            pltpu.VMEM((atoms * 2, LANE), jnp.float32),
            pltpu.VMEM(slabs, jnp.bfloat16),
            pltpu.VMEM(slabs, jnp.bfloat16),
            pltpu.VMEM(near.shape, jnp.float32),
            pltpu.VMEM((columns * groups_z,) + packs[0].shape[1:], jnp.float32),
            pltpu.VMEM(plane.shape, plane.dtype),
            pltpu.VMEM(depth.shape, depth.dtype),
            pltpu.SemaphoreType.DMA((3,)),
            pltpu.SemaphoreType.DMA((columns * groups_z,)),
            pltpu.SemaphoreType.DMA((columns // 2,)),
        ]
        + [pltpu.VMEM(field.shape, jnp.float32) for _ in range(SPARES)],
        compiler_params=pltpu.CompilerParams(vmem_limit_bytes=22 * 1024 * 1024),
        cost_estimate=pl.CostEstimate(
            flops=3 * work, bytes_accessed=8 * field.size * 4, transcendentals=0
        ),
        interpret=interpret,
    )(place, half, my_place, field, near, *packs, plane, depth)
    return out.reshape(columns * groups_z, SUB, SUB, LANE)


def hops(value, axis):
    count = lax.axis_size(axis)
    return [value] + [
        lax.ppermute(value, axis, [(i, (i + hop) % count) for i in range(count)])
        for hop in range(1, count)
    ]


def state_body(orbitals, potential, projectors, owner_rank, box_anchor, box_extent, coupling):
    axes = ("gx", "gy", "gz")
    groups = tuple(lax.axis_size(axis) for axis in axes)
    groups_z = groups[2]
    domains = groups[0] * groups[1] * groups_z
    atoms_own = projectors.shape[0]
    my_place = jnp.stack([lax.axis_index(axis) for axis in axes])
    me = (my_place[0] * groups[1] + my_place[1]) * groups_z + my_place[2]
    extent = lax.dynamic_slice(box_extent, (me * atoms_own,), (atoms_own,))
    own = lax.dynamic_slice(coupling, (me * atoms_own, 0), (atoms_own, NPROJ))
    pack = packed_inputs(potential, projectors, extent, own)
    line = jnp.stack(hops(pack, "gx"))
    place, half = box_places(groups, owner_rank, box_anchor[2])
    orbitals, line, place, half = lax.optimization_barrier((orbitals, line, place, half))
    crossed = [hops(piece, "gz") for piece in hops(line, "gy")]
    packs = [crossed[hop_y][hop_z] for hop_z in range(groups_z) for hop_y in range(groups[1])]
    field = lax.all_to_all(orbitals, axes, split_axis=0, concat_axis=0, tiled=True)
    field, near = first_call(groups, field)
    result = filter_call(groups, place, half, my_place, field, near, packs)
    filtered = lax.all_to_all(result, axes, split_axis=0, concat_axis=0, tiled=True)
    states = filtered.shape[0]
    flattened = filtered.reshape(states, -1)
    partial_value = jnp.dot(flattened, flattened.T, precision=lax.Precision.HIGHEST)
    quarter = partial_value.reshape(-1, SUB, states).transpose(1, 0, 2).reshape(SUB, -1)
    parts = lax.all_to_all(
        jnp.broadcast_to(quarter[None], (domains,) + quarter.shape),
        axes,
        split_axis=0,
        concat_axis=0,
        tiled=True,
    )
    summed = jnp.sum(parts, axis=0).reshape(SUB, -1, states).transpose(1, 0, 2)
    cells_total = orbitals.shape[1] * orbitals.shape[2] * orbitals.shape[3] * domains
    intersection = summed.reshape(states, states) / cells_total
    return (filtered, intersection)


def body(orbitals, potential, projectors, owner_rank, box_anchor, box_extent, coupling):
    domains = lax.axis_size("gx") * lax.axis_size("gy") * lax.axis_size("gz")
    whole_states = (
        orbitals.shape == (domains, SUB, SUB, LANE)
        and projectors.shape[0] % SUB == 0
        and projectors.shape[1] == NPROJ
        and lax.axis_size("gy") % 2 == 0
    )
    chosen = state_body if whole_states else domain_body
    return chosen(
        orbitals, potential, projectors, owner_rank, box_anchor, box_extent, coupling
    )


def solution(mesh):
    return jax.shard_map(
        body,
        mesh=mesh,
        in_specs=(
            P(None, "gx", "gy", "gz"),
            P("gx", "gy", "gz"),
            P(("gx", "gy", "gz"), None, None),
            P(),
            P(),
            P(),
            P(),
        ),
        out_specs=(P(None, "gx", "gy", "gz"), P()),
        check_vma=False,
    )
```

```python
import functools
import math
import jax
import jax.numpy as jnp
from jax import lax
from jax.experimental import pallas as pl
from jax.experimental.pallas import tpu as pltpu
import ml_dtypes
import numpy as np
from jax.sharding import PartitionSpec as P

B = 8
DEGREE = 4
ATOM_DEV = 8


STENCIL = (
    -5369.0 / 1800.0,
    12.0 / 7.0,
    -15.0 / 56.0,
    10.0 / 189.0,
    -1.0 / 112.0,
    2.0 / 1925.0,
    -1.0 / 16632.0,
)
SPACING = 0.5
LOW_EDGE = -2.5
CUTOFF = 4.0
UPPER = 60.0


def extended(cells, sides, width):
    for axis, dim in sides:
        count = lax.axis_size(axis)
        head = lax.slice_in_dim(cells, 0, width, axis=dim)
        tail = lax.slice_in_dim(cells, cells.shape[dim] - width, cells.shape[dim], axis=dim)
        cells = jnp.concatenate(
            [
                lax.ppermute(tail, axis, [(i, (i + 1) % count) for i in range(count)]),
                cells,
                lax.ppermute(head, axis, [((i + 1) % count, i) for i in range(count)]),
            ],
            axis=dim,
        )
    return cells


def laplace_padded(padded, shape):
    span_x, span_y, span_z = (shape[1], shape[2], shape[3])
    summed = 3.0 * STENCIL[0] * padded[:, 6 : 6 + span_x, 6 : 6 + span_y, 6 : 6 + span_z]
    for offset in range(1, 7):
        weight = STENCIL[offset]
        summed = summed + weight * (
            padded[:, 6 + offset : 6 + offset + span_x, 6 : 6 + span_y, 6 : 6 + span_z]
            + padded[:, 6 - offset : 6 - offset + span_x, 6 : 6 + span_y, 6 : 6 + span_z]
        )
        summed = summed + weight * (
            padded[:, 6 : 6 + span_x, 6 + offset : 6 + offset + span_y, 6 : 6 + span_z]
            + padded[:, 6 : 6 + span_x, 6 - offset : 6 - offset + span_y, 6 : 6 + span_z]
        )
        summed = summed + weight * (
            padded[:, 6 : 6 + span_x, 6 : 6 + span_y, 6 + offset : 6 + offset + span_z]
            + padded[:, 6 : 6 + span_x, 6 : 6 + span_y, 6 - offset : 6 - offset + span_z]
        )
    return summed / (SPACING * SPACING)


def collect_boxes(projectors, member, box_anchor, box_extent, coupling, capacity):
    member_int = member.astype(jnp.int32)
    slot_all = jnp.cumsum(member_int) - 1
    count = jnp.sum(member_int)
    slot_ids = jnp.arange(capacity, dtype=jnp.int32)
    onehot = ((slot_all[None, :] == slot_ids[:, None]) & member[None, :]).astype(jnp.float32)
    buffer = jnp.einsum(
        "cp,pkf->ckf",
        onehot,
        lax.all_gather(projectors, ("gx", "gy", "gz"), axis=0, tiled=True),
        precision=lax.Precision.HIGHEST,
    )
    hot_all = (slot_all[None, :] == slot_ids[:, None]) & member[None, :]
    slot_anchor = jnp.sum(jnp.where(hot_all[None, :, :], box_anchor[:, None, :], 0), axis=2)
    slot_extent = jnp.sum(jnp.where(hot_all, box_extent[None, :], 0), axis=1)
    slot_coupling = jnp.sum(jnp.where(hot_all[:, :, None], coupling[None, :, :], 0.0), axis=1)
    cell_offsets = jnp.arange(B, dtype=jnp.int32)
    limit = slot_extent[:, None, None, None]
    inside = (
        (cell_offsets[None, :, None, None] < limit)
        & (cell_offsets[None, None, :, None] < limit)
        & (cell_offsets[None, None, None, :] < limit)
    )
    buffer = buffer * inside.reshape(capacity, 1, B * B * B).astype(jnp.float32)
    return (buffer, slot_anchor, slot_coupling, count)


def nonlocal_term(field, buffer, slot_anchor, slot_coupling, count, domain_start):
    states = field.shape[0]

    def add_slot(slot_index, nonlocal_sum):
        corner = slot_anchor[:, slot_index] - domain_start
        start_cell = (0, corner[0], corner[1], corner[2])
        box_cells = lax.dynamic_slice(field, start_cell, (states, B, B, B)).reshape(
            states, B * B * B
        )
        proj_box = buffer[slot_index]
        coeffs = (
            jnp.dot(box_cells, proj_box.T, precision=lax.Precision.HIGHEST)
            * slot_coupling[slot_index][None, :]
        )
        addition = jnp.dot(coeffs, proj_box, precision=lax.Precision.HIGHEST).reshape(
            states, B, B, B
        )
        current = lax.dynamic_slice(nonlocal_sum, start_cell, (states, B, B, B))
        return lax.dynamic_update_slice(nonlocal_sum, current + addition, start_cell)

    return lax.fori_loop(0, count, add_slot, jnp.zeros_like(field))


def run_filter(field, apply_h):
    half_width = (UPPER - CUTOFF) / 2.0
    middle = (UPPER + CUTOFF) / 2.0
    sigma_one = half_width / (LOW_EDGE - middle)
    sigma_now = sigma_one
    result = (apply_h(field) - middle * field) * (sigma_one / half_width)
    previous = field
    for degree_step in range(1, DEGREE):
        sigma_next = 1.0 / (2.0 / sigma_one - sigma_now)
        next_state = (apply_h(result) - middle * result) * (
            2.0 * sigma_next / half_width
        ) - sigma_now * sigma_next * previous
        previous = result
        result = next_state
        sigma_now = sigma_next
    return result


def domain_body(orbitals, potential, projectors, owner_rank, box_anchor, box_extent, coupling):
    groups_y = lax.axis_size("gy")
    groups_z = lax.axis_size("gz")
    own_x = owner_rank // (groups_y * groups_z)
    own_y = owner_rank // groups_z % groups_y
    own_z = owner_rank % groups_z
    index_x = lax.axis_index("gx")
    index_y = lax.axis_index("gy")
    index_z = lax.axis_index("gz")
    span_x, span_y, span_z = (orbitals.shape[1], orbitals.shape[2], orbitals.shape[3])
    grid_anchor = jnp.stack([own_x * span_x, own_y * span_y, own_z * span_z]) + box_anchor
    member = (own_x == index_x) & (own_y == index_y) & (own_z == index_z)
    buffer, slot_anchor, slot_coupling, count = collect_boxes(
        projectors, member, grid_anchor, box_extent, coupling, 3 * ATOM_DEV
    )
    domain_start = jnp.stack([index_x * span_x, index_y * span_y, index_z * span_z])

    def apply_cube(field):
        padded = extended(field, (("gx", 1), ("gy", 2), ("gz", 3)), 6)
        return (
            -0.5 * laplace_padded(padded, field.shape)
            + potential[None] * field
            + nonlocal_term(field, buffer, slot_anchor, slot_coupling, count, domain_start)
        )

    filtered = run_filter(orbitals, apply_cube)
    flattened = filtered.reshape(filtered.shape[0], -1)
    partial_value = jnp.dot(flattened, flattened.T, precision=lax.Precision.HIGHEST)
    cells_total = span_x * span_y * span_z * lax.axis_size("gx") * groups_y * groups_z
    intersection = lax.psum(partial_value, ("gx", "gy", "gz")) / cells_total
    return (filtered, intersection)


SUB = 8
LANE = 128
HALF = LANE // 2
NPROJ = 4


def split_terms(matrix):
    high = matrix.astype(ml_dtypes.bfloat16)
    low = (matrix - high.astype(np.float64)).astype(ml_dtypes.bfloat16)
    return high, low


def stencil_weight(distance):
    if distance == 0 or abs(distance) > 6:
        return 0.0
    return -0.5 * STENCIL[abs(distance)] / (SPACING * SPACING)


def ring_matrix(length):
    matrix = np.zeros((length, length))
    for offset in range(-6, 7):
        for row in range(length):
            matrix[row, (row + offset) % length] += stencil_weight(offset)
    return matrix


def plane_weights(groups_y):
    slab = groups_y * HALF
    ring = ring_matrix(groups_y * SUB).reshape(groups_y, SUB, groups_y, SUB)
    blocks = []
    for shift in (-SUB, 0, SUB):
        along_x = np.array(
            [[stencil_weight(shift + i - o) for o in range(SUB)] for i in range(SUB)]
        )
        block = np.einsum("ab,io,jp->aijbop", np.eye(groups_y), along_x, np.eye(SUB))
        if shift == 0:
            block = block + np.einsum("ajbp,io->aijbop", ring, np.eye(SUB))
        blocks.append(block.reshape(slab, slab))
    high, low = split_terms(np.concatenate(blocks, axis=0))
    return np.concatenate([high, low], axis=0)


def depth_weights(groups_z):
    high, low = split_terms(ring_matrix(groups_z * LANE))
    return np.concatenate([high, low, high], axis=1)


def split_pair(value):
    high = value.astype(jnp.bfloat16)
    low = (value - high.astype(jnp.float32)).astype(jnp.bfloat16)
    return high, low


def mxu(left, right):
    return jnp.dot(left, right, preferred_element_type=jnp.float32)


def row_sums(values):
    row = lax.broadcasted_iota(jnp.int32, (SUB, LANE), 0)
    for stride in (1, 2, 4):
        keep = (row & stride) == 0
        values = [
            jnp.where(keep, one, two) + pltpu.roll(jnp.where(keep, two, one), stride, 0)
            for one, two in zip(values[0::2], values[1::2])
        ]
    return values[0]


def spread_row(ref, at):
    return ref[pl.ds(at, SUB, stride=0), :]


SPARES = 3
TALL = 2 * SUB


def split_store(high_buf, low_buf, rows, cols, value):
    high, low = split_pair(value)
    high_buf[rows, cols] = high
    low_buf[rows, cols] = low


def slab_rows(slab_at, span):
    return pl.ds(pl.multiple_of(slab_at * span, span), span)


def plane_product(groups_x, span, high_buf, low_buf, plane, slabs):
    width = plane.shape[1]

    def around(buf, shift):
        parts = [
            buf[slab_rows(lax.rem(at + shift + groups_x, groups_x), span), :] for at in slabs
        ]
        return jnp.concatenate(parts, axis=0)

    high = [around(high_buf, shift) for shift in (-1, 0, 1)]
    low = [around(low_buf, shift) for shift in (-1, 0, 1)]
    left = jnp.concatenate(high + low + high, axis=1)
    right = jnp.concatenate([plane[: 3 * width], plane[: 3 * width], plane[3 * width :]], axis=0)
    return mxu(left, right)


def depth_product(span, high_buf, low_buf, depth, slab_at):
    high = high_buf[slab_rows(slab_at, span), :]
    low = low_buf[slab_rows(slab_at, span), :]
    return mxu(depth[...], jnp.concatenate([high, high, low], axis=0))


def lay_products(groups, high_buf, low_buf, plane, depth, slabs, near):
    groups_x, groups_y, groups_z = groups
    span = groups_z * LANE
    pairs_slab = groups_y // 2
    total = plane_product(groups_x, span, high_buf, low_buf, plane, slabs)
    for number, slab_at in enumerate(slabs):
        deep = depth_product(span, high_buf, low_buf, depth, slab_at)
        part = total[number * span : (number + 1) * span] + deep
        for tile in range(pairs_slab):
            cols = part[:, tile * LANE : (tile + 1) * LANE]
            near[slab_rows(slab_at * pairs_slab + tile, span), :] = cols


def chunk_of(groups_x):
    return 2 if groups_x % 2 == 0 else 1


def block_rows(groups_z, pair, parity, depth_at):
    return pl.ds(pl.multiple_of(((2 * pair + parity) * groups_z + depth_at) * HALF, HALF), HALF)


def first_kernel(groups, *refs):
    field_in, plane, depth, field, near, raw, high_buf, low_buf, sems = refs
    groups_x, groups_y, groups_z = groups
    span = groups_z * LANE
    pairs_slab = groups_y // 2
    load = pltpu.make_async_copy(field_in, raw, sems.at[0])
    load.start()
    load.wait()

    def lay_field(slab_at, carry):
        for tile in range(pairs_slab):
            pair = slab_at * pairs_slab + tile
            cols = slice(tile * LANE, (tile + 1) * LANE)
            for depth_at in range(groups_z):
                first = raw[block_rows(groups_z, pair, 0, depth_at), :]
                second = raw[block_rows(groups_z, pair, 1, depth_at), :]
                turned = jnp.concatenate([first, second], axis=0).T
                at = pl.multiple_of(pair * span + depth_at * LANE, LANE)
                field[pl.ds(at, LANE), :] = turned
                at = pl.multiple_of(slab_at * span + depth_at * LANE, LANE)
                split_store(high_buf, low_buf, pl.ds(at, LANE), cols, turned)
        return carry

    lax.fori_loop(0, groups_x, lay_field, 0)
    chunk = chunk_of(groups_x)

    def product(chunk_at, carry):
        slabs = [chunk_at * chunk + number for number in range(chunk)]
        lay_products(groups, high_buf, low_buf, plane, depth, slabs, near)
        return carry

    lax.fori_loop(0, groups_x // chunk, product, 0)


def filter_kernel(groups, atoms, place, half, my_place, *refs):
    groups_x, groups_y, groups_z = groups
    pieces = groups_y * groups_z
    field_a, near_a = refs[:2]
    packs_in = refs[2 : 2 + pieces]
    plane, depth, out = refs[2 + pieces : 5 + pieces]
    (
        field_b,
        field_c,
        turned_out,
        local,
        coeffs,
        high_buf,
        low_buf,
        near,
        packs,
        in_sems,
        pack_sems,
        out_sems,
    ) = refs[5 + pieces : 5 + pieces + 12]
    spares = refs[5 + pieces + 12 :]
    targets = (near,) + tuple(spares)
    columns = groups_x * groups_y
    domains = columns * groups_z
    pairs = columns // 2
    span = groups_z * LANE
    pairs_slab = groups_y // 2
    per_device = atoms // domains // SUB
    chunk = chunk_of(groups_x)
    half_width = (UPPER - CUTOFF) / 2.0
    middle = (UPPER + CUTOFF) / 2.0
    diagonal = -0.5 * 3.0 * STENCIL[0] / (SPACING * SPACING) - middle
    lane = lax.broadcasted_iota(jnp.int32, (SUB, LANE), 1)
    lower = lane < HALF
    side = lane // HALF
    f32 = jnp.float32

    loads = [pltpu.make_async_copy(near_a, near, in_sems.at[0])]
    pack_loads = []
    for hop_z in range(groups_z):
        for hop_y in range(groups_y):
            source = packs_in[hop_z * groups_y + hop_y]
            for hop_x in range(groups_x):
                from_x = lax.rem(my_place[0] + (groups_x - hop_x), groups_x)
                from_y = lax.rem(my_place[1] + (groups_y - hop_y), groups_y)
                from_z = lax.rem(my_place[2] + (groups_z - hop_z), groups_z)
                device = (from_x * groups_y + from_y) * groups_z + from_z
                number = (hop_z * groups_y + hop_y) * groups_x + hop_x
                pack_loads.append(
                    pltpu.make_async_copy(
                        source.at[hop_x], packs.at[device], pack_sems.at[number]
                    )
                )
    for load in pack_loads + loads:
        load.start()
    for spare in spares:
        spare[...] = jnp.zeros(spare.shape, f32)
    for load in pack_loads + loads:
        load.wait()

    def lay_potential(pair, carry):
        for depth_at in range(groups_z):
            for row in range(SUB):
                first = packs[2 * pair * groups_z + depth_at, row]
                second = packs[(2 * pair + 1) * groups_z + depth_at, row]
                at = pl.multiple_of(pair * span + depth_at * LANE + row * SUB, SUB)
                local[pl.ds(at, SUB), :] = diagonal + jnp.where(
                    lower, first, pltpu.roll(second, HALF, 1)
                )
                at = pl.multiple_of(at + HALF, SUB)
                local[pl.ds(at, SUB), :] = diagonal + jnp.where(
                    lower, pltpu.roll(first, HALF, 1), second
                )
        return carry

    lax.fori_loop(0, pairs, lay_potential, 0)

    ones = (
        (
            lax.broadcasted_iota(jnp.int32, (LANE, LANE), 0) // HALF
            == lax.broadcasted_iota(jnp.int32, (LANE, LANE), 1) // HALF
        )
        .astype(f32)
        .astype(jnp.bfloat16)
    )

    share = 4 if domains % 4 == 0 else 1
    parts = domains // share

    def part_groups(part):
        for number in range(share):
            for inner in range(per_device):
                yield part * share + number, inner

    def apply_step(cur, prev, new, alpha, beta, first, last):
        def product(chunk_at, carry):
            slabs = [chunk_at * chunk + number for number in range(chunk)]
            lay_products(groups, high_buf, low_buf, plane, depth, slabs, near)
            return carry

        if not first:
            lax.fori_loop(0, groups_x // chunk, product, 0)

        def project(part, carry):
            for device, inner in part_groups(part):
                group = device * per_device + inner
                terms = ([], [])
                for j in range(SUB):
                    atom = group * SUB + j
                    value = cur[pl.ds(place[atom], SUB), :]
                    both = jnp.where(side == half[atom], value, pltpu.roll(value, HALF, 1))
                    for kp in range(2):
                        at = SUB + (inner * 2 + kp) * SUB + j
                        terms[kp].append(both * packs[device, at])
                for kp in range(2):
                    at = pl.multiple_of((group * 2 + kp) * SUB, SUB)
                    coeffs[pl.ds(at, SUB), :] = row_sums(terms[kp])
            return carry

        lax.fori_loop(0, parts, project, 0)

        high, low = split_pair(coeffs[: 2 * atoms, :])
        coeffs[: 2 * atoms, :] = mxu(high, ones) + mxu(low, ones)

        def scatter(part, carry):
            for device, inner in part_groups(part):
                group = device * per_device + inner
                bases = [pl.multiple_of((group * 2 + kp) * SUB, SUB) for kp in range(2)]
                for j in range(SUB):
                    atom = group * SUB + j
                    parts = [
                        spread_row(coeffs, bases[kp] + j)
                        * packs[device, SUB + (inner * 2 + kp) * SUB + j]
                        for kp in range(2)
                    ]
                    value = parts[0] + parts[1]
                    value = value + pltpu.roll(value, HALF, 1)
                    value = jnp.where(side == half[atom], value, 0.0)
                    rows = pl.ds(place[atom], SUB)
                    target = targets[j % len(targets)]
                    target[rows, :] = target[rows, :] + value
            return carry

        lax.fori_loop(0, parts, scatter, 0)

        def combine(slab_at, carry):
            for tile in range(pairs_slab):
                pair = slab_at * pairs_slab + tile
                cols = slice(tile * LANE, (tile + 1) * LANE)
                for at_row in range(0, span, TALL):
                    rows = pl.ds(pl.multiple_of(pair * span + at_row, TALL), TALL)
                    slab_at_row = pl.ds(pl.multiple_of(slab_at * span + at_row, TALL), TALL)
                    total = local[rows, :] * cur[rows, :]
                    for target in targets:
                        total = total + target[rows, :]
                    if not last:
                        for target in targets[1:]:
                            target[rows, :] = jnp.zeros((TALL, LANE), f32)
                    total = total * alpha
                    if beta is not None:
                        total = total + beta * prev[rows, :]
                    new[rows, :] = total
                    if not last:
                        split_store(high_buf, low_buf, slab_at_row, cols, total)
                if last:
                    for depth_at in range(groups_z):
                        at = pl.multiple_of(pair * span + depth_at * LANE, LANE)
                        turned = new[pl.ds(at, LANE), :].T
                        turned_out[block_rows(groups_z, pair, 0, depth_at), :] = turned[:HALF]
                        turned_out[block_rows(groups_z, pair, 1, depth_at), :] = turned[HALF:]
                    rows = pl.ds(pl.multiple_of(pair * span, span), span)
                    pltpu.make_async_copy(
                        turned_out.at[rows], out.at[rows], out_sems.at[pair]
                    ).start()
            return carry

        lax.fori_loop(0, groups_x, combine, 0)

    sigma_one = half_width / (LOW_EDGE - middle)
    sigma_now = sigma_one
    apply_step(field_a, None, field_b, sigma_one / half_width, None, True, DEGREE == 1)
    prev, cur, new = field_a, field_b, field_c
    for degree_step in range(1, DEGREE):
        sigma_next = 1.0 / (2.0 / sigma_one - sigma_now)
        last = degree_step == DEGREE - 1
        target = prev if degree_step > 1 else new
        apply_step(
            cur,
            prev,
            target,
            2.0 * sigma_next / half_width,
            -sigma_now * sigma_next,
            False,
            last,
        )
        prev, cur = cur, target
        sigma_now = sigma_next

    def finish(pair, carry):
        rows = pl.ds(pl.multiple_of(pair * span, span), span)
        pltpu.make_async_copy(turned_out.at[rows], out.at[rows], out_sems.at[pair]).wait()
        return carry

    lax.fori_loop(0, pairs, finish, 0)


def pack_kernel(my_first, extent, coupling, potential, projectors, out):
    atoms = projectors.shape[0]
    f32, bf16 = jnp.float32, jnp.bfloat16
    lane = lax.broadcasted_iota(jnp.int32, (SUB, LANE), 1)
    row = lax.broadcasted_iota(jnp.int32, (SUB, LANE), 0)
    lower = lane < HALF

    flat = potential[...].reshape(HALF, LANE)
    turned = jnp.concatenate([flat, flat], axis=0).T
    low = lax.broadcasted_iota(jnp.int32, (HALF, LANE), 1) < HALF
    out[:SUB] = jnp.where(low, turned[:HALF], turned[HALF:]).reshape(SUB, SUB, LANE)

    cells = projectors.shape[2]
    own_row = lax.broadcasted_iota(jnp.int32, (SUB, cells), 1) % B
    own_row = own_row == lax.broadcasted_iota(jnp.int32, (SUB, cells), 0)
    sides = []
    for kh in range(2):
        parts = []
        for kp in range(2):
            for atom in range(atoms):
                line = projectors[atom, 2 * kp + kh : 2 * kp + kh + 1, :]
                parts.append(jnp.where(own_row, jnp.broadcast_to(line, (SUB, cells)), 0.0))
        sides.append(jnp.concatenate(parts, axis=0))
    value = jnp.concatenate(sides, axis=1)
    source = lax.broadcasted_iota(jnp.int32, (2 * cells, LANE), 0) // B
    hot = source == lax.broadcasted_iota(jnp.int32, (2 * cells, LANE), 1)
    hot = hot.astype(f32).astype(bf16)
    high = value.astype(bf16)
    rest = value - high.astype(f32)
    mid = rest.astype(bf16)
    small = (rest - mid.astype(f32)).astype(bf16)
    moved = (mxu(high, hot) + mxu(mid, hot)) + mxu(small, hot)

    reach = jnp.maximum(jnp.maximum((lane >> 3) & (B - 1), lane & (B - 1)), row)
    for kp in range(2):
        for atom in range(atoms):
            at = my_first[0] + atom
            scale = jnp.sqrt(
                jnp.where(lower, coupling[2 * kp, at], coupling[2 * kp + 1, at])
            )
            number = kp * atoms + atom
            part = moved[number * SUB : (number + 1) * SUB]
            group, j = atom // SUB, atom % SUB
            out[SUB + (group * 2 + kp) * SUB + j] = jnp.where(
                reach < extent[at], part * scale, 0.0
            )


def packed_inputs(my_first, extent, coupling, potential, projectors, interpret=False):
    vmem = pl.BlockSpec(memory_space=pltpu.VMEM)
    smem = pl.BlockSpec(memory_space=pltpu.SMEM)
    atoms = projectors.shape[0]
    return pl.pallas_call(
        pack_kernel,
        out_shape=jax.ShapeDtypeStruct((SUB + 2 * atoms, SUB, LANE), jnp.float32),
        in_specs=[smem] * 3 + [vmem] * 2,
        out_specs=vmem,
        compiler_params=pltpu.CompilerParams(vmem_limit_bytes=8 * 1024 * 1024),
        interpret=interpret,
    )(my_first, extent, coupling.T, potential, projectors)


def weights_kernel(plane_in, depth_in, plane, depth, sems):
    loads = [
        pltpu.make_async_copy(plane_in, plane, sems.at[0]),
        pltpu.make_async_copy(depth_in, depth, sems.at[1]),
    ]
    for load in loads:
        load.start()
    for load in loads:
        load.wait()


def weights_call(groups, interpret=False):
    plane = jnp.asarray(plane_weights(groups[1]))
    depth = jnp.asarray(depth_weights(groups[2]))
    return pl.pallas_call(
        weights_kernel,
        out_shape=[jax.ShapeDtypeStruct(part.shape, part.dtype) for part in (plane, depth)],
        in_specs=[pl.BlockSpec(memory_space=pl.ANY)] * 2,
        out_specs=[pl.BlockSpec(memory_space=pltpu.VMEM)] * 2,
        scratch_shapes=[pltpu.SemaphoreType.DMA((2,))],
        compiler_params=pltpu.CompilerParams(vmem_limit_bytes=4 * 1024 * 1024),
        interpret=interpret,
    )(plane, depth)


def box_places(groups, owner, anchor):
    groups_z = groups[2]
    column = owner // groups_z
    place = (column // 2 * groups_z + owner % groups_z) * LANE + anchor
    return place, column % 2


def first_call(groups, field, plane, depth, interpret=False):
    groups_x, groups_y, groups_z = groups
    span = groups_z * LANE
    cells = (groups_x * groups_y // 2 * span, LANE)
    slabs = (groups_x * span, groups_y * HALF)
    vmem = pl.BlockSpec(memory_space=pltpu.VMEM)
    anywhere = pl.BlockSpec(memory_space=pl.ANY)
    work = 2 * slabs[0] * slabs[1] * (9 * slabs[1] + 3 * span)
    return pl.pallas_call(
        functools.partial(first_kernel, groups),
        out_shape=[
            jax.ShapeDtypeStruct(cells, jnp.float32),
            jax.ShapeDtypeStruct(cells, jnp.float32),
        ],
        in_specs=[anywhere, vmem, vmem],
        out_specs=[vmem] * 2,
        scratch_shapes=[
            pltpu.VMEM(cells, jnp.float32),
            pltpu.VMEM(slabs, jnp.bfloat16),
            pltpu.VMEM(slabs, jnp.bfloat16),
            pltpu.SemaphoreType.DMA((1,)),
        ],
        compiler_params=pltpu.CompilerParams(vmem_limit_bytes=12 * 1024 * 1024),
        cost_estimate=pl.CostEstimate(
            flops=work, bytes_accessed=4 * field.size * 4, transcendentals=0
        ),
        interpret=interpret,
    )(field.reshape(cells), plane, depth)


def filter_call(
    groups, place, half, my_place, field, near, packs, plane, depth, interpret=False
):
    groups_x, groups_y, groups_z = groups
    columns = groups_x * groups_y
    atoms = place.shape[0]
    vmem = pl.BlockSpec(memory_space=pltpu.VMEM)
    anywhere = pl.BlockSpec(memory_space=pl.ANY)
    smem = pl.BlockSpec(memory_space=pltpu.SMEM)
    slabs = (groups_x * groups_z * LANE, groups_y * HALF)
    work = 2 * slabs[0] * slabs[1] * (9 * slabs[1] + 3 * groups_z * LANE)
    out = pl.pallas_call(
        functools.partial(filter_kernel, groups, atoms),
        out_shape=jax.ShapeDtypeStruct(field.shape, jnp.float32),
        in_specs=[smem] * 3 + [vmem] * 2 + [anywhere] * len(packs) + [vmem] * 2,
        out_specs=anywhere,
        scratch_shapes=[
            pltpu.VMEM(field.shape, jnp.float32),
            pltpu.VMEM(field.shape, jnp.float32),
            pltpu.VMEM(field.shape, jnp.float32),
            pltpu.VMEM(field.shape, jnp.float32),
            pltpu.VMEM((atoms * 2 + SUB, LANE), jnp.float32),
            pltpu.VMEM(slabs, jnp.bfloat16),
            pltpu.VMEM(slabs, jnp.bfloat16),
            pltpu.VMEM(near.shape, jnp.float32),
            pltpu.VMEM((columns * groups_z,) + packs[0].shape[1:], jnp.float32),
            pltpu.SemaphoreType.DMA((1,)),
            pltpu.SemaphoreType.DMA((columns * groups_z,)),
            pltpu.SemaphoreType.DMA((columns // 2,)),
        ]
        + [pltpu.VMEM(field.shape, jnp.float32) for _ in range(SPARES)],
        compiler_params=pltpu.CompilerParams(vmem_limit_bytes=20 * 1024 * 1024),
        cost_estimate=pl.CostEstimate(
            flops=3 * work, bytes_accessed=8 * field.size * 4, transcendentals=0
        ),
        interpret=interpret,
    )(place, half, my_place, field, near, *packs, plane, depth)
    return out.reshape(columns * groups_z, SUB, SUB, LANE)


def hops(value, axis):
    count = lax.axis_size(axis)
    return [value] + [
        lax.ppermute(value, axis, [(i, (i + hop) % count) for i in range(count)])
        for hop in range(1, count)
    ]


def state_body(orbitals, potential, projectors, owner_rank, box_anchor, box_extent, coupling):
    axes = ("gx", "gy", "gz")
    groups = tuple(lax.axis_size(axis) for axis in axes)
    groups_z = groups[2]
    domains = groups[0] * groups[1] * groups_z
    atoms_own = projectors.shape[0]
    my_place = jnp.stack([lax.axis_index(axis) for axis in axes])
    me = (my_place[0] * groups[1] + my_place[1]) * groups_z + my_place[2]
    pack = packed_inputs((me * atoms_own)[None], box_extent, coupling, potential, projectors)
    line = jnp.stack(hops(pack, "gx"))
    place, half = box_places(groups, owner_rank, box_anchor[2])
    plane, depth = weights_call(groups)
    orbitals, line, place, half, plane, depth = lax.optimization_barrier(
        (orbitals, line, place, half, plane, depth)
    )
    crossed = [hops(piece, "gz") for piece in hops(line, "gy")]
    packs = [crossed[hop_y][hop_z] for hop_z in range(groups_z) for hop_y in range(groups[1])]
    field = lax.all_to_all(orbitals, axes, split_axis=0, concat_axis=0, tiled=True)
    field, near = first_call(groups, field, plane, depth)
    result = filter_call(groups, place, half, my_place, field, near, packs, plane, depth)
    filtered = lax.all_to_all(result, axes, split_axis=0, concat_axis=0, tiled=True)
    states = filtered.shape[0]
    flattened = filtered.reshape(states, -1)
    partial_value = jnp.dot(flattened, flattened.T, precision=lax.Precision.HIGHEST)
    quarter = partial_value.reshape(-1, SUB, states).transpose(1, 0, 2).reshape(SUB, -1)
    parts = lax.all_to_all(
        jnp.broadcast_to(quarter[None], (domains,) + quarter.shape),
        axes,
        split_axis=0,
        concat_axis=0,
        tiled=True,
    )
    summed = jnp.sum(parts, axis=0).reshape(SUB, -1, states).transpose(1, 0, 2)
    cells_total = orbitals.shape[1] * orbitals.shape[2] * orbitals.shape[3] * domains
    intersection = summed.reshape(states, states) / cells_total
    return (filtered, intersection)


def body(orbitals, potential, projectors, owner_rank, box_anchor, box_extent, coupling):
    domains = lax.axis_size("gx") * lax.axis_size("gy") * lax.axis_size("gz")
    whole_states = (
        orbitals.shape == (domains, SUB, SUB, LANE)
        and projectors.shape[0] % SUB == 0
        and projectors.shape[1] == NPROJ
        and lax.axis_size("gy") % 2 == 0
    )
    chosen = state_body if whole_states else domain_body
    return chosen(
        orbitals, potential, projectors, owner_rank, box_anchor, box_extent, coupling
    )


def solution(mesh):
    return jax.shard_map(
        body,
        mesh=mesh,
        in_specs=(
            P(None, "gx", "gy", "gz"),
            P("gx", "gy", "gz"),
            P(("gx", "gy", "gz"), None, None),
            P(),
            P(),
            P(),
            P(),
        ),
        out_specs=(P(None, "gx", "gy", "gz"), P()),
        check_vma=False,
    )
```

```python
import functools
import math
import jax
import jax.numpy as jnp
from jax import lax
from jax.experimental import pallas as pl
from jax.experimental.pallas import tpu as pltpu
import ml_dtypes
import numpy as np
from jax.sharding import PartitionSpec as P

B = 8
DEGREE = 4
ATOM_DEV = 8


STENCIL = (
    -5369.0 / 1800.0,
    12.0 / 7.0,
    -15.0 / 56.0,
    10.0 / 189.0,
    -1.0 / 112.0,
    2.0 / 1925.0,
    -1.0 / 16632.0,
)
SPACING = 0.5
LOW_EDGE = -2.5
CUTOFF = 4.0
UPPER = 60.0


def extended(cells, sides, width):
    for axis, dim in sides:
        count = lax.axis_size(axis)
        head = lax.slice_in_dim(cells, 0, width, axis=dim)
        tail = lax.slice_in_dim(cells, cells.shape[dim] - width, cells.shape[dim], axis=dim)
        cells = jnp.concatenate(
            [
                lax.ppermute(tail, axis, [(i, (i + 1) % count) for i in range(count)]),
                cells,
                lax.ppermute(head, axis, [((i + 1) % count, i) for i in range(count)]),
            ],
            axis=dim,
        )
    return cells


def laplace_padded(padded, shape):
    span_x, span_y, span_z = (shape[1], shape[2], shape[3])
    summed = 3.0 * STENCIL[0] * padded[:, 6 : 6 + span_x, 6 : 6 + span_y, 6 : 6 + span_z]
    for offset in range(1, 7):
        weight = STENCIL[offset]
        summed = summed + weight * (
            padded[:, 6 + offset : 6 + offset + span_x, 6 : 6 + span_y, 6 : 6 + span_z]
            + padded[:, 6 - offset : 6 - offset + span_x, 6 : 6 + span_y, 6 : 6 + span_z]
        )
        summed = summed + weight * (
            padded[:, 6 : 6 + span_x, 6 + offset : 6 + offset + span_y, 6 : 6 + span_z]
            + padded[:, 6 : 6 + span_x, 6 - offset : 6 - offset + span_y, 6 : 6 + span_z]
        )
        summed = summed + weight * (
            padded[:, 6 : 6 + span_x, 6 : 6 + span_y, 6 + offset : 6 + offset + span_z]
            + padded[:, 6 : 6 + span_x, 6 : 6 + span_y, 6 - offset : 6 - offset + span_z]
        )
    return summed / (SPACING * SPACING)


def collect_boxes(projectors, member, box_anchor, box_extent, coupling, capacity):
    member_int = member.astype(jnp.int32)
    slot_all = jnp.cumsum(member_int) - 1
    count = jnp.sum(member_int)
    slot_ids = jnp.arange(capacity, dtype=jnp.int32)
    onehot = ((slot_all[None, :] == slot_ids[:, None]) & member[None, :]).astype(jnp.float32)
    buffer = jnp.einsum(
        "cp,pkf->ckf",
        onehot,
        lax.all_gather(projectors, ("gx", "gy", "gz"), axis=0, tiled=True),
        precision=lax.Precision.HIGHEST,
    )
    hot_all = (slot_all[None, :] == slot_ids[:, None]) & member[None, :]
    slot_anchor = jnp.sum(jnp.where(hot_all[None, :, :], box_anchor[:, None, :], 0), axis=2)
    slot_extent = jnp.sum(jnp.where(hot_all, box_extent[None, :], 0), axis=1)
    slot_coupling = jnp.sum(jnp.where(hot_all[:, :, None], coupling[None, :, :], 0.0), axis=1)
    cell_offsets = jnp.arange(B, dtype=jnp.int32)
    limit = slot_extent[:, None, None, None]
    inside = (
        (cell_offsets[None, :, None, None] < limit)
        & (cell_offsets[None, None, :, None] < limit)
        & (cell_offsets[None, None, None, :] < limit)
    )
    buffer = buffer * inside.reshape(capacity, 1, B * B * B).astype(jnp.float32)
    return (buffer, slot_anchor, slot_coupling, count)


def nonlocal_term(field, buffer, slot_anchor, slot_coupling, count, domain_start):
    states = field.shape[0]

    def add_slot(slot_index, nonlocal_sum):
        corner = slot_anchor[:, slot_index] - domain_start
        start_cell = (0, corner[0], corner[1], corner[2])
        box_cells = lax.dynamic_slice(field, start_cell, (states, B, B, B)).reshape(
            states, B * B * B
        )
        proj_box = buffer[slot_index]
        coeffs = (
            jnp.dot(box_cells, proj_box.T, precision=lax.Precision.HIGHEST)
            * slot_coupling[slot_index][None, :]
        )
        addition = jnp.dot(coeffs, proj_box, precision=lax.Precision.HIGHEST).reshape(
            states, B, B, B
        )
        current = lax.dynamic_slice(nonlocal_sum, start_cell, (states, B, B, B))
        return lax.dynamic_update_slice(nonlocal_sum, current + addition, start_cell)

    return lax.fori_loop(0, count, add_slot, jnp.zeros_like(field))


def run_filter(field, apply_h):
    half_width = (UPPER - CUTOFF) / 2.0
    middle = (UPPER + CUTOFF) / 2.0
    sigma_one = half_width / (LOW_EDGE - middle)
    sigma_now = sigma_one
    result = (apply_h(field) - middle * field) * (sigma_one / half_width)
    previous = field
    for degree_step in range(1, DEGREE):
        sigma_next = 1.0 / (2.0 / sigma_one - sigma_now)
        next_state = (apply_h(result) - middle * result) * (
            2.0 * sigma_next / half_width
        ) - sigma_now * sigma_next * previous
        previous = result
        result = next_state
        sigma_now = sigma_next
    return result


def domain_body(orbitals, potential, projectors, owner_rank, box_anchor, box_extent, coupling):
    groups_y = lax.axis_size("gy")
    groups_z = lax.axis_size("gz")
    own_x = owner_rank // (groups_y * groups_z)
    own_y = owner_rank // groups_z % groups_y
    own_z = owner_rank % groups_z
    index_x = lax.axis_index("gx")
    index_y = lax.axis_index("gy")
    index_z = lax.axis_index("gz")
    span_x, span_y, span_z = (orbitals.shape[1], orbitals.shape[2], orbitals.shape[3])
    grid_anchor = jnp.stack([own_x * span_x, own_y * span_y, own_z * span_z]) + box_anchor
    member = (own_x == index_x) & (own_y == index_y) & (own_z == index_z)
    buffer, slot_anchor, slot_coupling, count = collect_boxes(
        projectors, member, grid_anchor, box_extent, coupling, 3 * ATOM_DEV
    )
    domain_start = jnp.stack([index_x * span_x, index_y * span_y, index_z * span_z])

    def apply_cube(field):
        padded = extended(field, (("gx", 1), ("gy", 2), ("gz", 3)), 6)
        return (
            -0.5 * laplace_padded(padded, field.shape)
            + potential[None] * field
            + nonlocal_term(field, buffer, slot_anchor, slot_coupling, count, domain_start)
        )

    filtered = run_filter(orbitals, apply_cube)
    flattened = filtered.reshape(filtered.shape[0], -1)
    partial_value = jnp.dot(flattened, flattened.T, precision=lax.Precision.HIGHEST)
    cells_total = span_x * span_y * span_z * lax.axis_size("gx") * groups_y * groups_z
    intersection = lax.psum(partial_value, ("gx", "gy", "gz")) / cells_total
    return (filtered, intersection)


SUB = 8
LANE = 128
HALF = LANE // 2
NPROJ = 4


def split_terms(matrix):
    high = matrix.astype(ml_dtypes.bfloat16)
    low = (matrix - high.astype(np.float64)).astype(ml_dtypes.bfloat16)
    return high, low


def stencil_weight(distance):
    if distance == 0 or abs(distance) > 6:
        return 0.0
    return -0.5 * STENCIL[abs(distance)] / (SPACING * SPACING)


def ring_matrix(length):
    matrix = np.zeros((length, length))
    for offset in range(-6, 7):
        for row in range(length):
            matrix[row, (row + offset) % length] += stencil_weight(offset)
    return matrix


def plane_weights(groups_y):
    slab = groups_y * HALF
    ring = ring_matrix(groups_y * SUB).reshape(groups_y, SUB, groups_y, SUB)
    blocks = []
    for shift in (-SUB, 0, SUB):
        along_x = np.array(
            [[stencil_weight(shift + i - o) for o in range(SUB)] for i in range(SUB)]
        )
        block = np.einsum("ab,io,jp->aijbop", np.eye(groups_y), along_x, np.eye(SUB))
        if shift == 0:
            block = block + np.einsum("ajbp,io->aijbop", ring, np.eye(SUB))
        blocks.append(block.reshape(slab, slab))
    high, low = split_terms(np.concatenate(blocks, axis=0))
    return np.concatenate([high, low], axis=0)


def depth_weights(groups_z):
    high, low = split_terms(ring_matrix(groups_z * LANE))
    return np.concatenate([high, low, high], axis=1)


def split_pair(value):
    high = value.astype(jnp.bfloat16)
    low = (value - high.astype(jnp.float32)).astype(jnp.bfloat16)
    return high, low


def mxu(left, right):
    return jnp.dot(left, right, preferred_element_type=jnp.float32)


def row_sums(values):
    row = lax.broadcasted_iota(jnp.int32, (SUB, LANE), 0)
    for stride in (1, 2, 4):
        keep = (row & stride) == 0
        values = [
            jnp.where(keep, one, two) + pltpu.roll(jnp.where(keep, two, one), stride, 0)
            for one, two in zip(values[0::2], values[1::2])
        ]
    return values[0]


SPARES = 1
TALL = 2 * SUB


def split_store(high_buf, low_buf, rows, cols, value):
    high, low = split_pair(value)
    high_buf[rows, cols] = high
    low_buf[rows, cols] = low


def slab_rows(slab_at, span):
    return pl.ds(pl.multiple_of(slab_at * span, span), span)


def plane_product(groups_x, span, high_buf, low_buf, plane, slabs):
    width = plane.shape[1]

    def around(buf, shift):
        parts = [
            buf[slab_rows(lax.rem(at + shift + groups_x, groups_x), span), :] for at in slabs
        ]
        return jnp.concatenate(parts, axis=0)

    high = [around(high_buf, shift) for shift in (-1, 0, 1)]
    low = [around(low_buf, shift) for shift in (-1, 0, 1)]
    left = jnp.concatenate(high + low + high, axis=1)
    right = jnp.concatenate([plane[: 3 * width], plane[: 3 * width], plane[3 * width :]], axis=0)
    return mxu(left, right)


def depth_product(span, high_buf, low_buf, depth, slab_at):
    high = high_buf[slab_rows(slab_at, span), :]
    low = low_buf[slab_rows(slab_at, span), :]
    return mxu(depth[...], jnp.concatenate([high, high, low], axis=0))


def lay_products(groups, high_buf, low_buf, plane, depth, slabs, near):
    groups_x, groups_y, groups_z = groups
    span = groups_z * LANE
    pairs_slab = groups_y // 2
    total = plane_product(groups_x, span, high_buf, low_buf, plane, slabs)
    for number, slab_at in enumerate(slabs):
        deep = depth_product(span, high_buf, low_buf, depth, slab_at)
        part = total[number * span : (number + 1) * span] + deep
        for tile in range(pairs_slab):
            cols = part[:, tile * LANE : (tile + 1) * LANE]
            near[slab_rows(slab_at * pairs_slab + tile, span), :] = cols


def chunk_of(groups_x):
    return 2 if groups_x % 2 == 0 else 1


def block_rows(groups_z, pair, parity, depth_at):
    return pl.ds(pl.multiple_of(((2 * pair + parity) * groups_z + depth_at) * HALF, HALF), HALF)


def first_kernel(groups, *refs):
    field_in, plane, depth, field, near, raw, high_buf, low_buf, sems = refs
    groups_x, groups_y, groups_z = groups
    span = groups_z * LANE
    pairs_slab = groups_y // 2
    load = pltpu.make_async_copy(field_in, raw, sems.at[0])
    load.start()
    load.wait()

    def lay_field(slab_at, carry):
        for tile in range(pairs_slab):
            pair = slab_at * pairs_slab + tile
            cols = slice(tile * LANE, (tile + 1) * LANE)
            for depth_at in range(groups_z):
                first = raw[block_rows(groups_z, pair, 0, depth_at), :]
                second = raw[block_rows(groups_z, pair, 1, depth_at), :]
                turned = jnp.concatenate([first, second], axis=0).T
                at = pl.multiple_of(pair * span + depth_at * LANE, LANE)
                field[pl.ds(at, LANE), :] = turned
                at = pl.multiple_of(slab_at * span + depth_at * LANE, LANE)
                split_store(high_buf, low_buf, pl.ds(at, LANE), cols, turned)
        return carry

    lax.fori_loop(0, groups_x, lay_field, 0)
    chunk = chunk_of(groups_x)

    def product(chunk_at, carry):
        slabs = [chunk_at * chunk + number for number in range(chunk)]
        lay_products(groups, high_buf, low_buf, plane, depth, slabs, near)
        return carry

    lax.fori_loop(0, groups_x // chunk, product, 0)


def filter_kernel(groups, atoms, place, half, my_place, *refs):
    groups_x, groups_y, groups_z = groups
    pieces = groups_y * groups_z
    field_a, near_a = refs[:2]
    packs_in = refs[2 : 2 + pieces]
    plane, depth, out = refs[2 + pieces : 5 + pieces]
    (
        field_b,
        field_c,
        turned_out,
        local,
        coeffs,
        high_buf,
        low_buf,
        near,
        packs,
        in_sems,
        pack_sems,
        out_sems,
    ) = refs[5 + pieces : 5 + pieces + 12]
    spares = refs[5 + pieces + 12 :]
    targets = (near,) + tuple(spares)
    columns = groups_x * groups_y
    domains = columns * groups_z
    pairs = columns // 2
    span = groups_z * LANE
    pairs_slab = groups_y // 2
    per_device = atoms // domains // SUB
    chunk = chunk_of(groups_x)
    half_width = (UPPER - CUTOFF) / 2.0
    middle = (UPPER + CUTOFF) / 2.0
    diagonal = -0.5 * 3.0 * STENCIL[0] / (SPACING * SPACING) - middle
    lane = lax.broadcasted_iota(jnp.int32, (SUB, LANE), 1)
    lower = lane < HALF
    side = lane // HALF
    f32 = jnp.float32

    loads = [pltpu.make_async_copy(near_a, near, in_sems.at[0])]
    pack_loads = []
    for hop_z in range(groups_z):
        for hop_y in range(groups_y):
            source = packs_in[hop_z * groups_y + hop_y]
            for hop_x in range(groups_x):
                from_x = lax.rem(my_place[0] + (groups_x - hop_x), groups_x)
                from_y = lax.rem(my_place[1] + (groups_y - hop_y), groups_y)
                from_z = lax.rem(my_place[2] + (groups_z - hop_z), groups_z)
                device = (from_x * groups_y + from_y) * groups_z + from_z
                number = (hop_z * groups_y + hop_y) * groups_x + hop_x
                pack_loads.append(
                    pltpu.make_async_copy(
                        source.at[hop_x], packs.at[device], pack_sems.at[number]
                    )
                )
    for load in pack_loads + loads:
        load.start()
    for spare in spares:
        spare[...] = jnp.zeros(spare.shape, f32)
    for load in pack_loads + loads:
        load.wait()

    def lay_potential(pair, carry):
        for depth_at in range(groups_z):
            for row in range(SUB):
                first = packs[2 * pair * groups_z + depth_at, row]
                second = packs[(2 * pair + 1) * groups_z + depth_at, row]
                at = pl.multiple_of(pair * span + depth_at * LANE + row * SUB, SUB)
                local[pl.ds(at, SUB), :] = diagonal + jnp.where(
                    lower, first, pltpu.roll(second, HALF, 1)
                )
                at = pl.multiple_of(at + HALF, SUB)
                local[pl.ds(at, SUB), :] = diagonal + jnp.where(
                    lower, pltpu.roll(first, HALF, 1), second
                )
        return carry

    lax.fori_loop(0, pairs, lay_potential, 0)

    ones = (
        (
            lax.broadcasted_iota(jnp.int32, (LANE, LANE), 0) // HALF
            == lax.broadcasted_iota(jnp.int32, (LANE, LANE), 1) // HALF
        )
        .astype(f32)
        .astype(jnp.bfloat16)
    )

    def part_groups(part, share):
        for number in range(share):
            for inner in range(per_device):
                yield part * share + number, inner

    def apply_step(cur, prev, new, alpha, beta, first, last):
        def project(part, carry):
            if not first:
                slabs = [part * chunk + number for number in range(chunk)]
                lay_products(groups, high_buf, low_buf, plane, depth, slabs, near)
            for device, inner in part_groups(part, domains // (groups_x // chunk)):
                group = device * per_device + inner
                terms = ([], [])
                for j in range(SUB):
                    atom = group * SUB + j
                    value = cur[pl.ds(place[atom], SUB), :]
                    both = jnp.where(side == half[atom], value, pltpu.roll(value, HALF, 1))
                    for kp in range(2):
                        at = SUB + (inner * 2 + kp) * SUB + j
                        terms[kp].append(both * packs[device, at])
                for kp in range(2):
                    at = pl.multiple_of((group * 2 + kp) * SUB, SUB)
                    coeffs[pl.ds(at, SUB), :] = row_sums(terms[kp])
            return carry

        lax.fori_loop(0, groups_x // chunk, project, 0)

        high, low = split_pair(coeffs[...])
        coeffs[...] = mxu(high, ones) + mxu(low, ones)

        def scatter(part, carry):
            for device, inner in part_groups(part, domains // groups_x):
                group = device * per_device + inner
                weights = [
                    coeffs[pl.ds(pl.multiple_of((group * 2 + kp) * SUB, SUB), SUB), :]
                    for kp in range(2)
                ]
                for j in range(SUB):
                    atom = group * SUB + j
                    parts = [
                        jnp.broadcast_to(weights[kp][j : j + 1], (SUB, LANE))
                        * packs[device, SUB + (inner * 2 + kp) * SUB + j]
                        for kp in range(2)
                    ]
                    value = parts[0] + parts[1]
                    value = value + pltpu.roll(value, HALF, 1)
                    value = jnp.where(side == half[atom], value, 0.0)
                    rows = pl.ds(place[atom], SUB)
                    target = targets[j % len(targets)]
                    target[rows, :] = target[rows, :] + value
            return carry

        lax.fori_loop(0, groups_x, scatter, 0)

        def combine(slab_at, carry):
            for tile in range(pairs_slab):
                pair = slab_at * pairs_slab + tile
                cols = slice(tile * LANE, (tile + 1) * LANE)
                for at_row in range(0, span, TALL):
                    rows = pl.ds(pl.multiple_of(pair * span + at_row, TALL), TALL)
                    slab_at_row = pl.ds(pl.multiple_of(slab_at * span + at_row, TALL), TALL)
                    total = local[rows, :] * cur[rows, :]
                    for target in targets:
                        total = total + target[rows, :]
                    if not last:
                        for target in targets[1:]:
                            target[rows, :] = jnp.zeros((TALL, LANE), f32)
                    total = total * alpha
                    if beta is not None:
                        total = total + beta * prev[rows, :]
                    new[rows, :] = total
                    if not last:
                        split_store(high_buf, low_buf, slab_at_row, cols, total)
                if last:
                    for depth_at in range(groups_z):
                        at = pl.multiple_of(pair * span + depth_at * LANE, LANE)
                        turned = new[pl.ds(at, LANE), :].T
                        turned_out[block_rows(groups_z, pair, 0, depth_at), :] = turned[:HALF]
                        turned_out[block_rows(groups_z, pair, 1, depth_at), :] = turned[HALF:]
                    rows = pl.ds(pl.multiple_of(pair * span, span), span)
                    pltpu.make_async_copy(
                        turned_out.at[rows], out.at[rows], out_sems.at[pair]
                    ).start()
            return carry

        lax.fori_loop(0, groups_x, combine, 0)

    sigma_one = half_width / (LOW_EDGE - middle)
    sigma_now = sigma_one
    apply_step(field_a, None, field_b, sigma_one / half_width, None, True, DEGREE == 1)
    prev, cur, new = field_a, field_b, field_c
    for degree_step in range(1, DEGREE):
        sigma_next = 1.0 / (2.0 / sigma_one - sigma_now)
        last = degree_step == DEGREE - 1
        target = prev if degree_step > 1 else new
        apply_step(
            cur,
            prev,
            target,
            2.0 * sigma_next / half_width,
            -sigma_now * sigma_next,
            False,
            last,
        )
        prev, cur = cur, target
        sigma_now = sigma_next

    def finish(pair, carry):
        rows = pl.ds(pl.multiple_of(pair * span, span), span)
        pltpu.make_async_copy(turned_out.at[rows], out.at[rows], out_sems.at[pair]).wait()
        return carry

    lax.fori_loop(0, pairs, finish, 0)


def pack_kernel(my_first, extent, coupling, potential, projectors, out):
    atoms = projectors.shape[0]
    f32, bf16 = jnp.float32, jnp.bfloat16
    lane = lax.broadcasted_iota(jnp.int32, (SUB, LANE), 1)
    row = lax.broadcasted_iota(jnp.int32, (SUB, LANE), 0)
    lower = lane < HALF

    flat = potential[...].reshape(HALF, LANE)
    turned = jnp.concatenate([flat, flat], axis=0).T
    low = lax.broadcasted_iota(jnp.int32, (HALF, LANE), 1) < HALF
    out[:SUB] = jnp.where(low, turned[:HALF], turned[HALF:]).reshape(SUB, SUB, LANE)

    cells = projectors.shape[2]
    own_row = lax.broadcasted_iota(jnp.int32, (SUB, cells), 1) % B
    own_row = own_row == lax.broadcasted_iota(jnp.int32, (SUB, cells), 0)
    sides = []
    for kh in range(2):
        parts = []
        for kp in range(2):
            for atom in range(atoms):
                line = projectors[atom, 2 * kp + kh : 2 * kp + kh + 1, :]
                parts.append(jnp.where(own_row, jnp.broadcast_to(line, (SUB, cells)), 0.0))
        sides.append(jnp.concatenate(parts, axis=0))
    value = jnp.concatenate(sides, axis=1)
    source = lax.broadcasted_iota(jnp.int32, (2 * cells, LANE), 0) // B
    hot = source == lax.broadcasted_iota(jnp.int32, (2 * cells, LANE), 1)
    hot = hot.astype(f32).astype(bf16)
    high = value.astype(bf16)
    rest = value - high.astype(f32)
    mid = rest.astype(bf16)
    small = (rest - mid.astype(f32)).astype(bf16)
    moved = (mxu(high, hot) + mxu(mid, hot)) + mxu(small, hot)

    reach = jnp.maximum(jnp.maximum((lane >> 3) & (B - 1), lane & (B - 1)), row)
    for kp in range(2):
        for atom in range(atoms):
            at = my_first[0] + atom
            scale = jnp.sqrt(
                jnp.where(lower, coupling[2 * kp, at], coupling[2 * kp + 1, at])
            )
            number = kp * atoms + atom
            part = moved[number * SUB : (number + 1) * SUB]
            group, j = atom // SUB, atom % SUB
            out[SUB + (group * 2 + kp) * SUB + j] = jnp.where(
                reach < extent[at], part * scale, 0.0
            )


def packed_inputs(my_first, extent, coupling, potential, projectors, interpret=False):
    vmem = pl.BlockSpec(memory_space=pltpu.VMEM)
    smem = pl.BlockSpec(memory_space=pltpu.SMEM)
    atoms = projectors.shape[0]
    return pl.pallas_call(
        pack_kernel,
        out_shape=jax.ShapeDtypeStruct((SUB + 2 * atoms, SUB, LANE), jnp.float32),
        in_specs=[smem] * 3 + [vmem] * 2,
        out_specs=vmem,
        compiler_params=pltpu.CompilerParams(vmem_limit_bytes=8 * 1024 * 1024),
        interpret=interpret,
    )(my_first, extent, coupling.T, potential, projectors)


def weights_kernel(plane_in, depth_in, plane, depth, sems):
    loads = [
        pltpu.make_async_copy(plane_in, plane, sems.at[0]),
        pltpu.make_async_copy(depth_in, depth, sems.at[1]),
    ]
    for load in loads:
        load.start()
    for load in loads:
        load.wait()


def weights_call(groups, interpret=False):
    plane = jnp.asarray(plane_weights(groups[1]))
    depth = jnp.asarray(depth_weights(groups[2]))
    return pl.pallas_call(
        weights_kernel,
        out_shape=[jax.ShapeDtypeStruct(part.shape, part.dtype) for part in (plane, depth)],
        in_specs=[pl.BlockSpec(memory_space=pl.ANY)] * 2,
        out_specs=[pl.BlockSpec(memory_space=pltpu.VMEM)] * 2,
        scratch_shapes=[pltpu.SemaphoreType.DMA((2,))],
        compiler_params=pltpu.CompilerParams(vmem_limit_bytes=4 * 1024 * 1024),
        interpret=interpret,
    )(plane, depth)


def box_places(groups, owner, anchor):
    groups_z = groups[2]
    column = owner // groups_z
    place = (column // 2 * groups_z + owner % groups_z) * LANE + anchor
    return place, column % 2


def first_call(groups, field, plane, depth, interpret=False):
    groups_x, groups_y, groups_z = groups
    span = groups_z * LANE
    cells = (groups_x * groups_y // 2 * span, LANE)
    slabs = (groups_x * span, groups_y * HALF)
    vmem = pl.BlockSpec(memory_space=pltpu.VMEM)
    anywhere = pl.BlockSpec(memory_space=pl.ANY)
    work = 2 * slabs[0] * slabs[1] * (9 * slabs[1] + 3 * span)
    return pl.pallas_call(
        functools.partial(first_kernel, groups),
        out_shape=[
            jax.ShapeDtypeStruct(cells, jnp.float32),
            jax.ShapeDtypeStruct(cells, jnp.float32),
        ],
        in_specs=[anywhere, vmem, vmem],
        out_specs=[vmem] * 2,
        scratch_shapes=[
            pltpu.VMEM(cells, jnp.float32),
            pltpu.VMEM(slabs, jnp.bfloat16),
            pltpu.VMEM(slabs, jnp.bfloat16),
            pltpu.SemaphoreType.DMA((1,)),
        ],
        compiler_params=pltpu.CompilerParams(vmem_limit_bytes=12 * 1024 * 1024),
        cost_estimate=pl.CostEstimate(
            flops=work, bytes_accessed=4 * field.size * 4, transcendentals=0
        ),
        interpret=interpret,
    )(field.reshape(cells), plane, depth)


def filter_call(
    groups, place, half, my_place, field, near, packs, plane, depth, interpret=False
):
    groups_x, groups_y, groups_z = groups
    columns = groups_x * groups_y
    atoms = place.shape[0]
    vmem = pl.BlockSpec(memory_space=pltpu.VMEM)
    anywhere = pl.BlockSpec(memory_space=pl.ANY)
    smem = pl.BlockSpec(memory_space=pltpu.SMEM)
    slabs = (groups_x * groups_z * LANE, groups_y * HALF)
    work = 2 * slabs[0] * slabs[1] * (9 * slabs[1] + 3 * groups_z * LANE)
    out = pl.pallas_call(
        functools.partial(filter_kernel, groups, atoms),
        out_shape=jax.ShapeDtypeStruct(field.shape, jnp.float32),
        in_specs=[smem] * 3 + [vmem] * 2 + [anywhere] * len(packs) + [vmem] * 2,
        out_specs=anywhere,
        scratch_shapes=[
            pltpu.VMEM(field.shape, jnp.float32),
            pltpu.VMEM(field.shape, jnp.float32),
            pltpu.VMEM(field.shape, jnp.float32),
            pltpu.VMEM(field.shape, jnp.float32),
            pltpu.VMEM((atoms * 2, LANE), jnp.float32),
            pltpu.VMEM(slabs, jnp.bfloat16),
            pltpu.VMEM(slabs, jnp.bfloat16),
            pltpu.VMEM(near.shape, jnp.float32),
            pltpu.VMEM((columns * groups_z,) + packs[0].shape[1:], jnp.float32),
            pltpu.SemaphoreType.DMA((1,)),
            pltpu.SemaphoreType.DMA((columns * groups_z,)),
            pltpu.SemaphoreType.DMA((columns // 2,)),
        ]
        + [pltpu.VMEM(field.shape, jnp.float32) for _ in range(SPARES)],
        compiler_params=pltpu.CompilerParams(vmem_limit_bytes=20 * 1024 * 1024),
        cost_estimate=pl.CostEstimate(
            flops=3 * work, bytes_accessed=8 * field.size * 4, transcendentals=0
        ),
        interpret=interpret,
    )(place, half, my_place, field, near, *packs, plane, depth)
    return out.reshape(columns * groups_z, SUB, SUB, LANE)


def hops(value, axis):
    count = lax.axis_size(axis)
    return [value] + [
        lax.ppermute(value, axis, [(i, (i + hop) % count) for i in range(count)])
        for hop in range(1, count)
    ]


def state_body(orbitals, potential, projectors, owner_rank, box_anchor, box_extent, coupling):
    axes = ("gx", "gy", "gz")
    groups = tuple(lax.axis_size(axis) for axis in axes)
    groups_z = groups[2]
    domains = groups[0] * groups[1] * groups_z
    atoms_own = projectors.shape[0]
    my_place = jnp.stack([lax.axis_index(axis) for axis in axes])
    me = (my_place[0] * groups[1] + my_place[1]) * groups_z + my_place[2]
    pack = packed_inputs((me * atoms_own)[None], box_extent, coupling, potential, projectors)
    line = jnp.stack(hops(pack, "gx"))
    place, half = box_places(groups, owner_rank, box_anchor[2])
    plane, depth = weights_call(groups)
    orbitals, line, place, half, plane, depth = lax.optimization_barrier(
        (orbitals, line, place, half, plane, depth)
    )
    crossed = [hops(piece, "gz") for piece in hops(line, "gy")]
    packs = [crossed[hop_y][hop_z] for hop_z in range(groups_z) for hop_y in range(groups[1])]
    field = lax.all_to_all(orbitals, axes, split_axis=0, concat_axis=0, tiled=True)
    field, near = first_call(groups, field, plane, depth)
    result = filter_call(groups, place, half, my_place, field, near, packs, plane, depth)
    filtered = lax.all_to_all(result, axes, split_axis=0, concat_axis=0, tiled=True)
    states = filtered.shape[0]
    flattened = filtered.reshape(states, -1)
    partial_value = jnp.dot(flattened, flattened.T, precision=lax.Precision.HIGHEST)
    quarter = partial_value.reshape(-1, SUB, states).transpose(1, 0, 2).reshape(SUB, -1)
    parts = lax.all_to_all(
        jnp.broadcast_to(quarter[None], (domains,) + quarter.shape),
        axes,
        split_axis=0,
        concat_axis=0,
        tiled=True,
    )
    summed = jnp.sum(parts, axis=0).reshape(SUB, -1, states).transpose(1, 0, 2)
    cells_total = orbitals.shape[1] * orbitals.shape[2] * orbitals.shape[3] * domains
    intersection = summed.reshape(states, states) / cells_total
    return (filtered, intersection)


def body(orbitals, potential, projectors, owner_rank, box_anchor, box_extent, coupling):
    domains = lax.axis_size("gx") * lax.axis_size("gy") * lax.axis_size("gz")
    whole_states = (
        orbitals.shape == (domains, SUB, SUB, LANE)
        and projectors.shape[0] % SUB == 0
        and projectors.shape[1] == NPROJ
        and lax.axis_size("gy") % 2 == 0
    )
    chosen = state_body if whole_states else domain_body
    return chosen(
        orbitals, potential, projectors, owner_rank, box_anchor, box_extent, coupling
    )


def solution(mesh):
    return jax.shard_map(
        body,
        mesh=mesh,
        in_specs=(
            P(None, "gx", "gy", "gz"),
            P("gx", "gy", "gz"),
            P(("gx", "gy", "gz"), None, None),
            P(),
            P(),
            P(),
            P(),
        ),
        out_specs=(P(None, "gx", "gy", "gz"), P()),
        check_vma=False,
    )
```

```python
import functools
import math
import jax
import jax.numpy as jnp
from jax import lax
from jax.experimental import pallas as pl
from jax.experimental.pallas import tpu as pltpu
import ml_dtypes
import numpy as np
from jax.sharding import PartitionSpec as P

B = 8
DEGREE = 4
ATOM_DEV = 8


STENCIL = (
    -5369.0 / 1800.0,
    12.0 / 7.0,
    -15.0 / 56.0,
    10.0 / 189.0,
    -1.0 / 112.0,
    2.0 / 1925.0,
    -1.0 / 16632.0,
)
SPACING = 0.5
LOW_EDGE = -2.5
CUTOFF = 4.0
UPPER = 60.0


def extended(cells, sides, width):
    for axis, dim in sides:
        count = lax.axis_size(axis)
        head = lax.slice_in_dim(cells, 0, width, axis=dim)
        tail = lax.slice_in_dim(cells, cells.shape[dim] - width, cells.shape[dim], axis=dim)
        cells = jnp.concatenate(
            [
                lax.ppermute(tail, axis, [(i, (i + 1) % count) for i in range(count)]),
                cells,
                lax.ppermute(head, axis, [((i + 1) % count, i) for i in range(count)]),
            ],
            axis=dim,
        )
    return cells


def laplace_padded(padded, shape):
    span_x, span_y, span_z = (shape[1], shape[2], shape[3])
    summed = 3.0 * STENCIL[0] * padded[:, 6 : 6 + span_x, 6 : 6 + span_y, 6 : 6 + span_z]
    for offset in range(1, 7):
        weight = STENCIL[offset]
        summed = summed + weight * (
            padded[:, 6 + offset : 6 + offset + span_x, 6 : 6 + span_y, 6 : 6 + span_z]
            + padded[:, 6 - offset : 6 - offset + span_x, 6 : 6 + span_y, 6 : 6 + span_z]
        )
        summed = summed + weight * (
            padded[:, 6 : 6 + span_x, 6 + offset : 6 + offset + span_y, 6 : 6 + span_z]
            + padded[:, 6 : 6 + span_x, 6 - offset : 6 - offset + span_y, 6 : 6 + span_z]
        )
        summed = summed + weight * (
            padded[:, 6 : 6 + span_x, 6 : 6 + span_y, 6 + offset : 6 + offset + span_z]
            + padded[:, 6 : 6 + span_x, 6 : 6 + span_y, 6 - offset : 6 - offset + span_z]
        )
    return summed / (SPACING * SPACING)


def collect_boxes(projectors, member, box_anchor, box_extent, coupling, capacity):
    member_int = member.astype(jnp.int32)
    slot_all = jnp.cumsum(member_int) - 1
    count = jnp.sum(member_int)
    slot_ids = jnp.arange(capacity, dtype=jnp.int32)
    onehot = ((slot_all[None, :] == slot_ids[:, None]) & member[None, :]).astype(jnp.float32)
    buffer = jnp.einsum(
        "cp,pkf->ckf",
        onehot,
        lax.all_gather(projectors, ("gx", "gy", "gz"), axis=0, tiled=True),
        precision=lax.Precision.HIGHEST,
    )
    hot_all = (slot_all[None, :] == slot_ids[:, None]) & member[None, :]
    slot_anchor = jnp.sum(jnp.where(hot_all[None, :, :], box_anchor[:, None, :], 0), axis=2)
    slot_extent = jnp.sum(jnp.where(hot_all, box_extent[None, :], 0), axis=1)
    slot_coupling = jnp.sum(jnp.where(hot_all[:, :, None], coupling[None, :, :], 0.0), axis=1)
    cell_offsets = jnp.arange(B, dtype=jnp.int32)
    limit = slot_extent[:, None, None, None]
    inside = (
        (cell_offsets[None, :, None, None] < limit)
        & (cell_offsets[None, None, :, None] < limit)
        & (cell_offsets[None, None, None, :] < limit)
    )
    buffer = buffer * inside.reshape(capacity, 1, B * B * B).astype(jnp.float32)
    return (buffer, slot_anchor, slot_coupling, count)


def nonlocal_term(field, buffer, slot_anchor, slot_coupling, count, domain_start):
    states = field.shape[0]

    def add_slot(slot_index, nonlocal_sum):
        corner = slot_anchor[:, slot_index] - domain_start
        start_cell = (0, corner[0], corner[1], corner[2])
        box_cells = lax.dynamic_slice(field, start_cell, (states, B, B, B)).reshape(
            states, B * B * B
        )
        proj_box = buffer[slot_index]
        coeffs = (
            jnp.dot(box_cells, proj_box.T, precision=lax.Precision.HIGHEST)
            * slot_coupling[slot_index][None, :]
        )
        addition = jnp.dot(coeffs, proj_box, precision=lax.Precision.HIGHEST).reshape(
            states, B, B, B
        )
        current = lax.dynamic_slice(nonlocal_sum, start_cell, (states, B, B, B))
        return lax.dynamic_update_slice(nonlocal_sum, current + addition, start_cell)

    return lax.fori_loop(0, count, add_slot, jnp.zeros_like(field))


def run_filter(field, apply_h):
    half_width = (UPPER - CUTOFF) / 2.0
    middle = (UPPER + CUTOFF) / 2.0
    sigma_one = half_width / (LOW_EDGE - middle)
    sigma_now = sigma_one
    result = (apply_h(field) - middle * field) * (sigma_one / half_width)
    previous = field
    for degree_step in range(1, DEGREE):
        sigma_next = 1.0 / (2.0 / sigma_one - sigma_now)
        next_state = (apply_h(result) - middle * result) * (
            2.0 * sigma_next / half_width
        ) - sigma_now * sigma_next * previous
        previous = result
        result = next_state
        sigma_now = sigma_next
    return result


def domain_body(orbitals, potential, projectors, owner_rank, box_anchor, box_extent, coupling):
    groups_y = lax.axis_size("gy")
    groups_z = lax.axis_size("gz")
    own_x = owner_rank // (groups_y * groups_z)
    own_y = owner_rank // groups_z % groups_y
    own_z = owner_rank % groups_z
    index_x = lax.axis_index("gx")
    index_y = lax.axis_index("gy")
    index_z = lax.axis_index("gz")
    span_x, span_y, span_z = (orbitals.shape[1], orbitals.shape[2], orbitals.shape[3])
    grid_anchor = jnp.stack([own_x * span_x, own_y * span_y, own_z * span_z]) + box_anchor
    member = (own_x == index_x) & (own_y == index_y) & (own_z == index_z)
    buffer, slot_anchor, slot_coupling, count = collect_boxes(
        projectors, member, grid_anchor, box_extent, coupling, 3 * ATOM_DEV
    )
    domain_start = jnp.stack([index_x * span_x, index_y * span_y, index_z * span_z])

    def apply_cube(field):
        padded = extended(field, (("gx", 1), ("gy", 2), ("gz", 3)), 6)
        return (
            -0.5 * laplace_padded(padded, field.shape)
            + potential[None] * field
            + nonlocal_term(field, buffer, slot_anchor, slot_coupling, count, domain_start)
        )

    filtered = run_filter(orbitals, apply_cube)
    flattened = filtered.reshape(filtered.shape[0], -1)
    partial_value = jnp.dot(flattened, flattened.T, precision=lax.Precision.HIGHEST)
    cells_total = span_x * span_y * span_z * lax.axis_size("gx") * groups_y * groups_z
    intersection = lax.psum(partial_value, ("gx", "gy", "gz")) / cells_total
    return (filtered, intersection)


SUB = 8
LANE = 128
HALF = LANE // 2
NPROJ = 4


def split_terms(matrix):
    high = matrix.astype(ml_dtypes.bfloat16)
    low = (matrix - high.astype(np.float64)).astype(ml_dtypes.bfloat16)
    return high, low


def stencil_weight(distance):
    if distance == 0 or abs(distance) > 6:
        return 0.0
    return -0.5 * STENCIL[abs(distance)] / (SPACING * SPACING)


def ring_matrix(length):
    matrix = np.zeros((length, length))
    for offset in range(-6, 7):
        for row in range(length):
            matrix[row, (row + offset) % length] += stencil_weight(offset)
    return matrix


def plane_weights(groups_y):
    slab = groups_y * HALF
    ring = ring_matrix(groups_y * SUB).reshape(groups_y, SUB, groups_y, SUB)
    blocks = []
    for shift in (-SUB, 0, SUB):
        along_x = np.array(
            [[stencil_weight(shift + i - o) for o in range(SUB)] for i in range(SUB)]
        )
        block = np.einsum("ab,io,jp->aijbop", np.eye(groups_y), along_x, np.eye(SUB))
        if shift == 0:
            block = block + np.einsum("ajbp,io->aijbop", ring, np.eye(SUB))
        blocks.append(block.reshape(slab, slab))
    high, low = split_terms(np.concatenate(blocks, axis=0))
    return np.concatenate([high, low], axis=0)


def depth_weights(groups_z):
    high, low = split_terms(ring_matrix(groups_z * LANE))
    return np.concatenate([high, low, high], axis=1)


def split_pair(value):
    high = value.astype(jnp.bfloat16)
    low = (value - high.astype(jnp.float32)).astype(jnp.bfloat16)
    return high, low


def mxu(left, right):
    return jnp.dot(left, right, preferred_element_type=jnp.float32)


def row_sums(values):
    row = lax.broadcasted_iota(jnp.int32, (SUB, LANE), 0)
    for stride in (1, 2, 4):
        keep = (row & stride) == 0
        values = [
            jnp.where(keep, one, two) + pltpu.roll(jnp.where(keep, two, one), stride, 0)
            for one, two in zip(values[0::2], values[1::2])
        ]
    return values[0]


SPARES = 1
TALL = 2 * SUB


def split_store(high_buf, low_buf, rows, cols, value):
    high, low = split_pair(value)
    high_buf[rows, cols] = high
    low_buf[rows, cols] = low


def slab_rows(slab_at, span):
    return pl.ds(pl.multiple_of(slab_at * span, span), span)


def plane_product(groups_x, span, high_buf, low_buf, plane, slabs):
    width = plane.shape[1]

    def around(buf, shift):
        parts = [
            buf[slab_rows(lax.rem(at + shift + groups_x, groups_x), span), :] for at in slabs
        ]
        return jnp.concatenate(parts, axis=0)

    high = [around(high_buf, shift) for shift in (-1, 0, 1)]
    low = [around(low_buf, shift) for shift in (-1, 0, 1)]
    left = jnp.concatenate(high + low + high, axis=1)
    right = jnp.concatenate([plane[: 3 * width], plane[: 3 * width], plane[3 * width :]], axis=0)
    return mxu(left, right)


def depth_product(span, high_buf, low_buf, depth, slab_at):
    high = high_buf[slab_rows(slab_at, span), :]
    low = low_buf[slab_rows(slab_at, span), :]
    return mxu(depth[...], jnp.concatenate([high, high, low], axis=0))


def lay_products(groups, high_buf, low_buf, plane, depth, slabs, near):
    groups_x, groups_y, groups_z = groups
    span = groups_z * LANE
    pairs_slab = groups_y // 2
    total = plane_product(groups_x, span, high_buf, low_buf, plane, slabs)
    for number, slab_at in enumerate(slabs):
        deep = depth_product(span, high_buf, low_buf, depth, slab_at)
        part = total[number * span : (number + 1) * span] + deep
        for tile in range(pairs_slab):
            cols = part[:, tile * LANE : (tile + 1) * LANE]
            near[slab_rows(slab_at * pairs_slab + tile, span), :] = cols


def chunk_of(groups_x):
    return 2 if groups_x % 2 == 0 else 1


def block_rows(groups_z, pair, parity, depth_at):
    return pl.ds(pl.multiple_of(((2 * pair + parity) * groups_z + depth_at) * HALF, HALF), HALF)


def first_kernel(groups, *refs):
    raw, plane, depth, field, near, high_buf, low_buf = refs
    groups_x, groups_y, groups_z = groups
    span = groups_z * LANE
    pairs_slab = groups_y // 2

    def lay_field(slab_at, carry):
        for tile in range(pairs_slab):
            pair = slab_at * pairs_slab + tile
            cols = slice(tile * LANE, (tile + 1) * LANE)
            for depth_at in range(groups_z):
                first = raw[block_rows(groups_z, pair, 0, depth_at), :]
                second = raw[block_rows(groups_z, pair, 1, depth_at), :]
                turned = jnp.concatenate([first, second], axis=0).T
                at = pl.multiple_of(pair * span + depth_at * LANE, LANE)
                field[pl.ds(at, LANE), :] = turned
                at = pl.multiple_of(slab_at * span + depth_at * LANE, LANE)
                split_store(high_buf, low_buf, pl.ds(at, LANE), cols, turned)
        return carry

    lax.fori_loop(0, groups_x, lay_field, 0)
    chunk = chunk_of(groups_x)

    def product(chunk_at, carry):
        slabs = [chunk_at * chunk + number for number in range(chunk)]
        lay_products(groups, high_buf, low_buf, plane, depth, slabs, near)
        return carry

    lax.fori_loop(0, groups_x // chunk, product, 0)


def filter_kernel(groups, atoms, place, half, my_place, *refs):
    groups_x, groups_y, groups_z = groups
    pieces = groups_y * groups_z
    field_a, near_a = refs[:2]
    packs_in = refs[2 : 2 + pieces]
    plane, depth, out = refs[2 + pieces : 5 + pieces]
    field_b, field_c, local, coeffs, high_buf, low_buf, near = refs[5 + pieces : 12 + pieces]
    spares = refs[12 + pieces :]
    targets = (near,) + tuple(spares)
    columns = groups_x * groups_y
    domains = columns * groups_z
    pairs = columns // 2
    span = groups_z * LANE
    pairs_slab = groups_y // 2
    per_device = atoms // domains // SUB
    chunk = chunk_of(groups_x)
    half_width = (UPPER - CUTOFF) / 2.0
    middle = (UPPER + CUTOFF) / 2.0
    diagonal = -0.5 * 3.0 * STENCIL[0] / (SPACING * SPACING) - middle
    lane = lax.broadcasted_iota(jnp.int32, (SUB, LANE), 1)
    lower = lane < HALF
    side = lane // HALF
    f32 = jnp.float32

    for target in targets:
        target[...] = jnp.zeros(target.shape, f32)

    def sources(hop_x):
        for hop_z in range(groups_z):
            for hop_y in range(groups_y):
                from_x = lax.rem(my_place[0] + (groups_x - hop_x), groups_x)
                from_y = lax.rem(my_place[1] + (groups_y - hop_y), groups_y)
                from_z = lax.rem(my_place[2] + (groups_z - hop_z), groups_z)
                yield packs_in[hop_z * groups_y + hop_y], from_x * groups_y + from_y, from_z

    def lay_potential(hop_x, carry):
        for piece, column, depth_at in sources(hop_x):
            mine = side == column % 2
            for tile in range(SUB):
                value = diagonal + piece[hop_x, tile]
                other = pltpu.roll(value, HALF, 1)
                for upper in range(2):
                    at = column // 2 * span + depth_at * LANE + upper * HALF + tile * SUB
                    rows = pl.ds(pl.multiple_of(at, SUB), SUB)
                    chosen = jnp.where(side == upper, value, other)
                    local[rows, :] = jnp.where(mine, chosen, local[rows, :])
        return carry

    lax.fori_loop(0, groups_x, lay_potential, 0)

    ones = (
        (
            lax.broadcasted_iota(jnp.int32, (LANE, LANE), 0) // HALF
            == lax.broadcasted_iota(jnp.int32, (LANE, LANE), 1) // HALF
        )
        .astype(f32)
        .astype(jnp.bfloat16)
    )

    def part_groups(part, share):
        for number in range(share):
            hop_x = part * share + number
            for at, (piece, column, depth_at) in enumerate(sources(hop_x)):
                for inner in range(per_device):
                    stored = (hop_x * pieces + at) * per_device + inner
                    atoms_at = ((column * groups_z + depth_at) * per_device + inner) * SUB
                    yield piece, hop_x, inner, stored, atoms_at

    def apply_step(cur, prev, new, alpha, beta, first, last):
        def project(part, carry):
            if not first:
                slabs = [part * chunk + number for number in range(chunk)]
                lay_products(groups, high_buf, low_buf, plane, depth, slabs, near)
            for piece, hop_x, inner, stored, atoms_at in part_groups(part, chunk):
                terms = ([], [])
                for j in range(SUB):
                    atom = atoms_at + j
                    value = cur[pl.ds(place[atom], SUB), :]
                    both = jnp.where(side == half[atom], value, pltpu.roll(value, HALF, 1))
                    for kp in range(2):
                        at = SUB + (inner * 2 + kp) * SUB + j
                        terms[kp].append(both * piece[hop_x, at])
                for kp in range(2):
                    at = pl.multiple_of((stored * 2 + kp) * SUB, SUB)
                    coeffs[pl.ds(at, SUB), :] = row_sums(terms[kp])
            return carry

        lax.fori_loop(0, groups_x // chunk, project, 0)

        high, low = split_pair(coeffs[...])
        coeffs[...] = mxu(high, ones) + mxu(low, ones)

        def scatter(part, carry):
            for piece, hop_x, inner, stored, atoms_at in part_groups(part, 1):
                weights = [
                    coeffs[pl.ds(pl.multiple_of((stored * 2 + kp) * SUB, SUB), SUB), :]
                    for kp in range(2)
                ]
                for j in range(SUB):
                    atom = atoms_at + j
                    parts = [
                        jnp.broadcast_to(weights[kp][j : j + 1], (SUB, LANE))
                        * piece[hop_x, SUB + (inner * 2 + kp) * SUB + j]
                        for kp in range(2)
                    ]
                    value = parts[0] + parts[1]
                    value = value + pltpu.roll(value, HALF, 1)
                    value = jnp.where(side == half[atom], value, 0.0)
                    rows = pl.ds(place[atom], SUB)
                    target = targets[j % len(targets)]
                    target[rows, :] = target[rows, :] + value
            return carry

        lax.fori_loop(0, groups_x, scatter, 0)

        def combine(slab_at, carry):
            for tile in range(pairs_slab):
                pair = slab_at * pairs_slab + tile
                cols = slice(tile * LANE, (tile + 1) * LANE)
                for at_row in range(0, span, TALL):
                    rows = pl.ds(pl.multiple_of(pair * span + at_row, TALL), TALL)
                    slab_at_row = pl.ds(pl.multiple_of(slab_at * span + at_row, TALL), TALL)
                    total = local[rows, :] * cur[rows, :]
                    if first:
                        total = total + near_a[rows, :]
                    for target in targets:
                        total = total + target[rows, :]
                    if not last:
                        for target in targets[1:]:
                            target[rows, :] = jnp.zeros((TALL, LANE), f32)
                    total = total * alpha
                    if beta is not None:
                        total = total + beta * prev[rows, :]
                    new[rows, :] = total
                    if not last:
                        split_store(high_buf, low_buf, slab_at_row, cols, total)
                if last:
                    for depth_at in range(groups_z):
                        at = pl.multiple_of(pair * span + depth_at * LANE, LANE)
                        turned = new[pl.ds(at, LANE), :].T
                        out[block_rows(groups_z, pair, 0, depth_at), :] = turned[:HALF]
                        out[block_rows(groups_z, pair, 1, depth_at), :] = turned[HALF:]
            return carry

        lax.fori_loop(0, groups_x, combine, 0)

    sigma_one = half_width / (LOW_EDGE - middle)
    sigma_now = sigma_one
    apply_step(field_a, None, field_b, sigma_one / half_width, None, True, DEGREE == 1)
    prev, cur, new = field_a, field_b, field_c
    for degree_step in range(1, DEGREE):
        sigma_next = 1.0 / (2.0 / sigma_one - sigma_now)
        last = degree_step == DEGREE - 1
        target = prev if degree_step > 1 else new
        apply_step(
            cur,
            prev,
            target,
            2.0 * sigma_next / half_width,
            -sigma_now * sigma_next,
            False,
            last,
        )
        prev, cur = cur, target
        sigma_now = sigma_next


def pack_kernel(my_first, extent, coupling, potential, projectors, out):
    atoms = projectors.shape[0]
    f32, bf16 = jnp.float32, jnp.bfloat16
    lane = lax.broadcasted_iota(jnp.int32, (SUB, LANE), 1)
    row = lax.broadcasted_iota(jnp.int32, (SUB, LANE), 0)
    lower = lane < HALF

    flat = potential[...].reshape(HALF, LANE)
    turned = jnp.concatenate([flat, flat], axis=0).T
    low = lax.broadcasted_iota(jnp.int32, (HALF, LANE), 1) < HALF
    out[:SUB] = jnp.where(low, turned[:HALF], turned[HALF:]).reshape(SUB, SUB, LANE)

    cells = projectors.shape[2]
    own_row = lax.broadcasted_iota(jnp.int32, (SUB, cells), 1) % B
    own_row = own_row == lax.broadcasted_iota(jnp.int32, (SUB, cells), 0)
    sides = []
    for kh in range(2):
        parts = []
        for kp in range(2):
            for atom in range(atoms):
                line = projectors[atom, 2 * kp + kh : 2 * kp + kh + 1, :]
                parts.append(jnp.where(own_row, jnp.broadcast_to(line, (SUB, cells)), 0.0))
        sides.append(jnp.concatenate(parts, axis=0))
    value = jnp.concatenate(sides, axis=1)
    source = lax.broadcasted_iota(jnp.int32, (2 * cells, LANE), 0) // B
    hot = source == lax.broadcasted_iota(jnp.int32, (2 * cells, LANE), 1)
    hot = hot.astype(f32).astype(bf16)
    high = value.astype(bf16)
    rest = value - high.astype(f32)
    mid = rest.astype(bf16)
    small = (rest - mid.astype(f32)).astype(bf16)
    moved = (mxu(high, hot) + mxu(mid, hot)) + mxu(small, hot)

    reach = jnp.maximum(jnp.maximum((lane >> 3) & (B - 1), lane & (B - 1)), row)
    for kp in range(2):
        for atom in range(atoms):
            at = my_first[0] + atom
            scale = jnp.sqrt(
                jnp.where(lower, coupling[2 * kp, at], coupling[2 * kp + 1, at])
            )
            number = kp * atoms + atom
            part = moved[number * SUB : (number + 1) * SUB]
            group, j = atom // SUB, atom % SUB
            out[SUB + (group * 2 + kp) * SUB + j] = jnp.where(
                reach < extent[at], part * scale, 0.0
            )


def packed_inputs(my_first, extent, coupling, potential, projectors, interpret=False):
    vmem = pl.BlockSpec(memory_space=pltpu.VMEM)
    smem = pl.BlockSpec(memory_space=pltpu.SMEM)
    atoms = projectors.shape[0]
    return pl.pallas_call(
        pack_kernel,
        out_shape=jax.ShapeDtypeStruct((SUB + 2 * atoms, SUB, LANE), jnp.float32),
        in_specs=[smem] * 3 + [vmem] * 2,
        out_specs=vmem,
        compiler_params=pltpu.CompilerParams(vmem_limit_bytes=8 * 1024 * 1024),
        interpret=interpret,
    )(my_first, extent, coupling.T, potential, projectors)


def weights_kernel(plane_in, depth_in, plane, depth, sems):
    loads = [
        pltpu.make_async_copy(plane_in, plane, sems.at[0]),
        pltpu.make_async_copy(depth_in, depth, sems.at[1]),
    ]
    for load in loads:
        load.start()
    for load in loads:
        load.wait()


def weights_call(groups, interpret=False):
    plane = jnp.asarray(plane_weights(groups[1]))
    depth = jnp.asarray(depth_weights(groups[2]))
    return pl.pallas_call(
        weights_kernel,
        out_shape=[jax.ShapeDtypeStruct(part.shape, part.dtype) for part in (plane, depth)],
        in_specs=[pl.BlockSpec(memory_space=pl.ANY)] * 2,
        out_specs=[pl.BlockSpec(memory_space=pltpu.VMEM)] * 2,
        scratch_shapes=[pltpu.SemaphoreType.DMA((2,))],
        compiler_params=pltpu.CompilerParams(vmem_limit_bytes=4 * 1024 * 1024),
        interpret=interpret,
    )(plane, depth)


def box_places(groups, owner, anchor):
    groups_z = groups[2]
    column = owner // groups_z
    place = (column // 2 * groups_z + owner % groups_z) * LANE + anchor
    return place, column % 2


def first_call(groups, field, plane, depth, interpret=False):
    groups_x, groups_y, groups_z = groups
    span = groups_z * LANE
    cells = (groups_x * groups_y // 2 * span, LANE)
    slabs = (groups_x * span, groups_y * HALF)
    vmem = pl.BlockSpec(memory_space=pltpu.VMEM)
    work = 2 * slabs[0] * slabs[1] * (9 * slabs[1] + 3 * span)
    return pl.pallas_call(
        functools.partial(first_kernel, groups),
        out_shape=[
            jax.ShapeDtypeStruct(cells, jnp.float32),
            jax.ShapeDtypeStruct(cells, jnp.float32),
        ],
        in_specs=[vmem] * 3,
        out_specs=[vmem] * 2,
        scratch_shapes=[
            pltpu.VMEM(slabs, jnp.bfloat16),
            pltpu.VMEM(slabs, jnp.bfloat16),
        ],
        compiler_params=pltpu.CompilerParams(vmem_limit_bytes=12 * 1024 * 1024),
        cost_estimate=pl.CostEstimate(
            flops=work, bytes_accessed=4 * field.size * 4, transcendentals=0
        ),
        interpret=interpret,
    )(field.reshape(cells), plane, depth)


def filter_call(
    groups, place, half, my_place, field, near, packs, plane, depth, interpret=False
):
    groups_x, groups_y, groups_z = groups
    columns = groups_x * groups_y
    atoms = place.shape[0]
    vmem = pl.BlockSpec(memory_space=pltpu.VMEM)
    smem = pl.BlockSpec(memory_space=pltpu.SMEM)
    slabs = (groups_x * groups_z * LANE, groups_y * HALF)
    work = 2 * slabs[0] * slabs[1] * (9 * slabs[1] + 3 * groups_z * LANE)
    out = pl.pallas_call(
        functools.partial(filter_kernel, groups, atoms),
        out_shape=jax.ShapeDtypeStruct(field.shape, jnp.float32),
        in_specs=[smem] * 3 + [vmem] * (len(packs) + 4),
        out_specs=vmem,
        scratch_shapes=[
            pltpu.VMEM(field.shape, jnp.float32),
            pltpu.VMEM(field.shape, jnp.float32),
            pltpu.VMEM(field.shape, jnp.float32),
            pltpu.VMEM((atoms * 2, LANE), jnp.float32),
            pltpu.VMEM(slabs, jnp.bfloat16),
            pltpu.VMEM(slabs, jnp.bfloat16),
        ]
        + [pltpu.VMEM(field.shape, jnp.float32) for _ in range(1 + SPARES)],
        compiler_params=pltpu.CompilerParams(vmem_limit_bytes=22 * 1024 * 1024),
        cost_estimate=pl.CostEstimate(
            flops=3 * work, bytes_accessed=8 * field.size * 4, transcendentals=0
        ),
        interpret=interpret,
    )(place, half, my_place, field, near, *packs, plane, depth)
    return out.reshape(columns * groups_z, SUB, SUB, LANE)


def hops(value, axis):
    count = lax.axis_size(axis)
    return [value] + [
        lax.ppermute(value, axis, [(i, (i + hop) % count) for i in range(count)])
        for hop in range(1, count)
    ]


def state_body(orbitals, potential, projectors, owner_rank, box_anchor, box_extent, coupling):
    axes = ("gx", "gy", "gz")
    groups = tuple(lax.axis_size(axis) for axis in axes)
    groups_z = groups[2]
    domains = groups[0] * groups[1] * groups_z
    atoms_own = projectors.shape[0]
    my_place = jnp.stack([lax.axis_index(axis) for axis in axes])
    me = (my_place[0] * groups[1] + my_place[1]) * groups_z + my_place[2]
    pack = packed_inputs((me * atoms_own)[None], box_extent, coupling, potential, projectors)
    line = jnp.stack(hops(pack, "gx"))
    place, half = box_places(groups, owner_rank, box_anchor[2])
    plane, depth = weights_call(groups)
    orbitals, line, place, half, plane, depth = lax.optimization_barrier(
        (orbitals, line, place, half, plane, depth)
    )
    crossed = [hops(piece, "gz") for piece in hops(line, "gy")]
    packs = [crossed[hop_y][hop_z] for hop_z in range(groups_z) for hop_y in range(groups[1])]
    field = lax.all_to_all(orbitals, axes, split_axis=0, concat_axis=0, tiled=True)
    field, near = first_call(groups, field, plane, depth)
    result = filter_call(groups, place, half, my_place, field, near, packs, plane, depth)
    filtered = lax.all_to_all(result, axes, split_axis=0, concat_axis=0, tiled=True)
    states = filtered.shape[0]
    flattened = filtered.reshape(states, -1)
    partial_value = jnp.dot(flattened, flattened.T, precision=lax.Precision.HIGHEST)
    quarter = partial_value.reshape(-1, SUB, states).transpose(1, 0, 2).reshape(SUB, -1)
    parts = lax.all_to_all(
        jnp.broadcast_to(quarter[None], (domains,) + quarter.shape),
        axes,
        split_axis=0,
        concat_axis=0,
        tiled=True,
    )
    summed = jnp.sum(parts, axis=0).reshape(SUB, -1, states).transpose(1, 0, 2)
    cells_total = orbitals.shape[1] * orbitals.shape[2] * orbitals.shape[3] * domains
    intersection = summed.reshape(states, states) / cells_total
    return (filtered, intersection)


def body(orbitals, potential, projectors, owner_rank, box_anchor, box_extent, coupling):
    domains = lax.axis_size("gx") * lax.axis_size("gy") * lax.axis_size("gz")
    whole_states = (
        orbitals.shape == (domains, SUB, SUB, LANE)
        and projectors.shape[0] % SUB == 0
        and projectors.shape[1] == NPROJ
        and lax.axis_size("gy") % 2 == 0
    )
    chosen = state_body if whole_states else domain_body
    return chosen(
        orbitals, potential, projectors, owner_rank, box_anchor, box_extent, coupling
    )


def solution(mesh):
    return jax.shard_map(
        body,
        mesh=mesh,
        in_specs=(
            P(None, "gx", "gy", "gz"),
            P("gx", "gy", "gz"),
            P(("gx", "gy", "gz"), None, None),
            P(),
            P(),
            P(),
            P(),
        ),
        out_specs=(P(None, "gx", "gy", "gz"), P()),
        check_vma=False,
    )
```

```python
import functools
import math
import jax
import jax.numpy as jnp
from jax import lax
from jax.experimental import pallas as pl
from jax.experimental.pallas import tpu as pltpu
import ml_dtypes
import numpy as np
from jax.sharding import PartitionSpec as P

B = 8
DEGREE = 4
ATOM_DEV = 8


STENCIL = (
    -5369.0 / 1800.0,
    12.0 / 7.0,
    -15.0 / 56.0,
    10.0 / 189.0,
    -1.0 / 112.0,
    2.0 / 1925.0,
    -1.0 / 16632.0,
)
SPACING = 0.5
LOW_EDGE = -2.5
CUTOFF = 4.0
UPPER = 60.0


def extended(cells, sides, width):
    for axis, dim in sides:
        count = lax.axis_size(axis)
        head = lax.slice_in_dim(cells, 0, width, axis=dim)
        tail = lax.slice_in_dim(cells, cells.shape[dim] - width, cells.shape[dim], axis=dim)
        cells = jnp.concatenate(
            [
                lax.ppermute(tail, axis, [(i, (i + 1) % count) for i in range(count)]),
                cells,
                lax.ppermute(head, axis, [((i + 1) % count, i) for i in range(count)]),
            ],
            axis=dim,
        )
    return cells


def laplace_padded(padded, shape):
    span_x, span_y, span_z = (shape[1], shape[2], shape[3])
    summed = 3.0 * STENCIL[0] * padded[:, 6 : 6 + span_x, 6 : 6 + span_y, 6 : 6 + span_z]
    for offset in range(1, 7):
        weight = STENCIL[offset]
        summed = summed + weight * (
            padded[:, 6 + offset : 6 + offset + span_x, 6 : 6 + span_y, 6 : 6 + span_z]
            + padded[:, 6 - offset : 6 - offset + span_x, 6 : 6 + span_y, 6 : 6 + span_z]
        )
        summed = summed + weight * (
            padded[:, 6 : 6 + span_x, 6 + offset : 6 + offset + span_y, 6 : 6 + span_z]
            + padded[:, 6 : 6 + span_x, 6 - offset : 6 - offset + span_y, 6 : 6 + span_z]
        )
        summed = summed + weight * (
            padded[:, 6 : 6 + span_x, 6 : 6 + span_y, 6 + offset : 6 + offset + span_z]
            + padded[:, 6 : 6 + span_x, 6 : 6 + span_y, 6 - offset : 6 - offset + span_z]
        )
    return summed / (SPACING * SPACING)


def collect_boxes(projectors, member, box_anchor, box_extent, coupling, capacity):
    member_int = member.astype(jnp.int32)
    slot_all = jnp.cumsum(member_int) - 1
    count = jnp.sum(member_int)
    slot_ids = jnp.arange(capacity, dtype=jnp.int32)
    onehot = ((slot_all[None, :] == slot_ids[:, None]) & member[None, :]).astype(jnp.float32)
    buffer = jnp.einsum(
        "cp,pkf->ckf",
        onehot,
        lax.all_gather(projectors, ("gx", "gy", "gz"), axis=0, tiled=True),
        precision=lax.Precision.HIGHEST,
    )
    hot_all = (slot_all[None, :] == slot_ids[:, None]) & member[None, :]
    slot_anchor = jnp.sum(jnp.where(hot_all[None, :, :], box_anchor[:, None, :], 0), axis=2)
    slot_extent = jnp.sum(jnp.where(hot_all, box_extent[None, :], 0), axis=1)
    slot_coupling = jnp.sum(jnp.where(hot_all[:, :, None], coupling[None, :, :], 0.0), axis=1)
    cell_offsets = jnp.arange(B, dtype=jnp.int32)
    limit = slot_extent[:, None, None, None]
    inside = (
        (cell_offsets[None, :, None, None] < limit)
        & (cell_offsets[None, None, :, None] < limit)
        & (cell_offsets[None, None, None, :] < limit)
    )
    buffer = buffer * inside.reshape(capacity, 1, B * B * B).astype(jnp.float32)
    return (buffer, slot_anchor, slot_coupling, count)


def nonlocal_term(field, buffer, slot_anchor, slot_coupling, count, domain_start):
    states = field.shape[0]

    def add_slot(slot_index, nonlocal_sum):
        corner = slot_anchor[:, slot_index] - domain_start
        start_cell = (0, corner[0], corner[1], corner[2])
        box_cells = lax.dynamic_slice(field, start_cell, (states, B, B, B)).reshape(
            states, B * B * B
        )
        proj_box = buffer[slot_index]
        coeffs = (
            jnp.dot(box_cells, proj_box.T, precision=lax.Precision.HIGHEST)
            * slot_coupling[slot_index][None, :]
        )
        addition = jnp.dot(coeffs, proj_box, precision=lax.Precision.HIGHEST).reshape(
            states, B, B, B
        )
        current = lax.dynamic_slice(nonlocal_sum, start_cell, (states, B, B, B))
        return lax.dynamic_update_slice(nonlocal_sum, current + addition, start_cell)

    return lax.fori_loop(0, count, add_slot, jnp.zeros_like(field))


def run_filter(field, apply_h):
    half_width = (UPPER - CUTOFF) / 2.0
    middle = (UPPER + CUTOFF) / 2.0
    sigma_one = half_width / (LOW_EDGE - middle)
    sigma_now = sigma_one
    result = (apply_h(field) - middle * field) * (sigma_one / half_width)
    previous = field
    for degree_step in range(1, DEGREE):
        sigma_next = 1.0 / (2.0 / sigma_one - sigma_now)
        next_state = (apply_h(result) - middle * result) * (
            2.0 * sigma_next / half_width
        ) - sigma_now * sigma_next * previous
        previous = result
        result = next_state
        sigma_now = sigma_next
    return result


def domain_body(orbitals, potential, projectors, owner_rank, box_anchor, box_extent, coupling):
    groups_y = lax.axis_size("gy")
    groups_z = lax.axis_size("gz")
    own_x = owner_rank // (groups_y * groups_z)
    own_y = owner_rank // groups_z % groups_y
    own_z = owner_rank % groups_z
    index_x = lax.axis_index("gx")
    index_y = lax.axis_index("gy")
    index_z = lax.axis_index("gz")
    span_x, span_y, span_z = (orbitals.shape[1], orbitals.shape[2], orbitals.shape[3])
    grid_anchor = jnp.stack([own_x * span_x, own_y * span_y, own_z * span_z]) + box_anchor
    member = (own_x == index_x) & (own_y == index_y) & (own_z == index_z)
    buffer, slot_anchor, slot_coupling, count = collect_boxes(
        projectors, member, grid_anchor, box_extent, coupling, 3 * ATOM_DEV
    )
    domain_start = jnp.stack([index_x * span_x, index_y * span_y, index_z * span_z])

    def apply_cube(field):
        padded = extended(field, (("gx", 1), ("gy", 2), ("gz", 3)), 6)
        return (
            -0.5 * laplace_padded(padded, field.shape)
            + potential[None] * field
            + nonlocal_term(field, buffer, slot_anchor, slot_coupling, count, domain_start)
        )

    filtered = run_filter(orbitals, apply_cube)
    flattened = filtered.reshape(filtered.shape[0], -1)
    partial_value = jnp.dot(flattened, flattened.T, precision=lax.Precision.HIGHEST)
    cells_total = span_x * span_y * span_z * lax.axis_size("gx") * groups_y * groups_z
    intersection = lax.psum(partial_value, ("gx", "gy", "gz")) / cells_total
    return (filtered, intersection)


SUB = 8
LANE = 128
HALF = LANE // 2
NPROJ = 4


def split_terms(matrix):
    high = matrix.astype(ml_dtypes.bfloat16)
    low = (matrix - high.astype(np.float64)).astype(ml_dtypes.bfloat16)
    return high, low


def stencil_weight(distance):
    if distance == 0 or abs(distance) > 6:
        return 0.0
    return -0.5 * STENCIL[abs(distance)] / (SPACING * SPACING)


def ring_matrix(length):
    matrix = np.zeros((length, length))
    for offset in range(-6, 7):
        for row in range(length):
            matrix[row, (row + offset) % length] += stencil_weight(offset)
    return matrix


def plane_weights(groups_y):
    slab = groups_y * HALF
    ring = ring_matrix(groups_y * SUB).reshape(groups_y, SUB, groups_y, SUB)
    blocks = []
    for shift in (-SUB, 0, SUB):
        along_x = np.array(
            [[stencil_weight(shift + i - o) for o in range(SUB)] for i in range(SUB)]
        )
        block = np.einsum("ab,io,jp->aijbop", np.eye(groups_y), along_x, np.eye(SUB))
        if shift == 0:
            block = block + np.einsum("ajbp,io->aijbop", ring, np.eye(SUB))
        blocks.append(block.reshape(slab, slab))
    high, low = split_terms(np.concatenate(blocks, axis=0))
    return np.concatenate([high, low], axis=0)


def depth_weights(groups_z):
    high, low = split_terms(ring_matrix(groups_z * LANE))
    return np.concatenate([high, low, high], axis=1)


def split_pair(value):
    high = value.astype(jnp.bfloat16)
    low = (value - high.astype(jnp.float32)).astype(jnp.bfloat16)
    return high, low


def mxu(left, right):
    return jnp.dot(left, right, preferred_element_type=jnp.float32)


def row_sums(values):
    row = lax.broadcasted_iota(jnp.int32, (SUB, LANE), 0)
    for stride in (1, 2, 4):
        keep = (row & stride) == 0
        values = [
            jnp.where(keep, one, two) + pltpu.roll(jnp.where(keep, two, one), stride, 0)
            for one, two in zip(values[0::2], values[1::2])
        ]
    return values[0]


SPARES = 1
TALL = 2 * SUB


def split_store(high_buf, low_buf, rows, cols, value):
    high, low = split_pair(value)
    high_buf[rows, cols] = high
    low_buf[rows, cols] = low


def slab_rows(slab_at, span):
    return pl.ds(pl.multiple_of(slab_at * span, span), span)


def plane_product(groups_x, span, high_buf, low_buf, plane, slabs):
    width = plane.shape[1]

    def around(buf, shift):
        parts = [
            buf[slab_rows(lax.rem(at + shift + groups_x, groups_x), span), :] for at in slabs
        ]
        return jnp.concatenate(parts, axis=0)

    high = [around(high_buf, shift) for shift in (-1, 0, 1)]
    low = [around(low_buf, shift) for shift in (-1, 0, 1)]
    left = jnp.concatenate(high + low + high, axis=1)
    right = jnp.concatenate([plane[: 3 * width], plane[: 3 * width], plane[3 * width :]], axis=0)
    return mxu(left, right)


def depth_product(span, high_buf, low_buf, depth, slab_at):
    high = high_buf[slab_rows(slab_at, span), :]
    low = low_buf[slab_rows(slab_at, span), :]
    return mxu(depth[...], jnp.concatenate([high, high, low], axis=0))


def lay_products(groups, high_buf, low_buf, plane, depth, slabs, near):
    groups_x, groups_y, groups_z = groups
    span = groups_z * LANE
    pairs_slab = groups_y // 2
    total = plane_product(groups_x, span, high_buf, low_buf, plane, slabs)
    for number, slab_at in enumerate(slabs):
        deep = depth_product(span, high_buf, low_buf, depth, slab_at)
        part = total[number * span : (number + 1) * span] + deep
        for tile in range(pairs_slab):
            cols = part[:, tile * LANE : (tile + 1) * LANE]
            near[slab_rows(slab_at * pairs_slab + tile, span), :] = cols


def chunk_of(groups_x):
    return 2 if groups_x % 2 == 0 else 1


def block_rows(groups_z, pair, parity, depth_at):
    return pl.ds(pl.multiple_of(((2 * pair + parity) * groups_z + depth_at) * HALF, HALF), HALF)


def first_kernel(groups, *refs):
    raw, plane, depth, field, near, high_buf, low_buf = refs
    groups_x, groups_y, groups_z = groups
    span = groups_z * LANE
    pairs_slab = groups_y // 2

    def lay_field(slab_at, carry):
        for tile in range(pairs_slab):
            pair = slab_at * pairs_slab + tile
            cols = slice(tile * LANE, (tile + 1) * LANE)
            for depth_at in range(groups_z):
                first = raw[block_rows(groups_z, pair, 0, depth_at), :]
                second = raw[block_rows(groups_z, pair, 1, depth_at), :]
                turned = jnp.concatenate([first, second], axis=0).T
                at = pl.multiple_of(pair * span + depth_at * LANE, LANE)
                field[pl.ds(at, LANE), :] = turned
                at = pl.multiple_of(slab_at * span + depth_at * LANE, LANE)
                split_store(high_buf, low_buf, pl.ds(at, LANE), cols, turned)
        return carry

    lax.fori_loop(0, groups_x, lay_field, 0)
    chunk = chunk_of(groups_x)

    def product(chunk_at, carry):
        slabs = [chunk_at * chunk + number for number in range(chunk)]
        lay_products(groups, high_buf, low_buf, plane, depth, slabs, near)
        return carry

    lax.fori_loop(0, groups_x // chunk, product, 0)


def pieces_from(groups, my_place, packs_in, hop_x):
    groups_x, groups_y, groups_z = groups
    for hop_z in range(groups_z):
        for hop_y in range(groups_y):
            from_x = lax.rem(my_place[0] + (groups_x - hop_x), groups_x)
            from_y = lax.rem(my_place[1] + (groups_y - hop_y), groups_y)
            from_z = lax.rem(my_place[2] + (groups_z - hop_z), groups_z)
            yield packs_in[hop_z * groups_y + hop_y], from_x * groups_y + from_y, from_z


def potential_kernel(groups, my_place, *refs):
    packs_in, local = refs[:-1], refs[-1]
    span = groups[2] * LANE
    side = lax.broadcasted_iota(jnp.int32, (SUB, LANE), 1) // HALF
    middle = (UPPER + CUTOFF) / 2.0
    diagonal = -0.5 * 3.0 * STENCIL[0] / (SPACING * SPACING) - middle

    def lay_potential(hop_x, carry):
        for piece, column, depth_at in pieces_from(groups, my_place, packs_in, hop_x):
            mine = side == column % 2
            for tile in range(SUB):
                value = diagonal + piece[hop_x, tile]
                other = pltpu.roll(value, HALF, 1)
                for upper in range(2):
                    at = column // 2 * span + depth_at * LANE + upper * HALF + tile * SUB
                    rows = pl.ds(pl.multiple_of(at, SUB), SUB)
                    chosen = jnp.where(side == upper, value, other)
                    local[rows, :] = jnp.where(mine, chosen, local[rows, :])
        return carry

    lax.fori_loop(0, groups[0], lay_potential, 0)


def filter_kernel(groups, atoms, place, half, my_place, *refs):
    groups_x, groups_y, groups_z = groups
    pieces = groups_y * groups_z
    field_a, near_a, local = refs[:3]
    packs_in = refs[3 : 3 + pieces]
    plane, depth, out = refs[3 + pieces : 6 + pieces]
    field_b, field_c, coeffs, high_buf, low_buf, near = refs[6 + pieces : 12 + pieces]
    spares = refs[12 + pieces :]
    targets = (near,) + tuple(spares)
    columns = groups_x * groups_y
    domains = columns * groups_z
    pairs = columns // 2
    span = groups_z * LANE
    pairs_slab = groups_y // 2
    per_device = atoms // domains // SUB
    chunk = chunk_of(groups_x)
    half_width = (UPPER - CUTOFF) / 2.0
    middle = (UPPER + CUTOFF) / 2.0
    diagonal = -0.5 * 3.0 * STENCIL[0] / (SPACING * SPACING) - middle
    lane = lax.broadcasted_iota(jnp.int32, (SUB, LANE), 1)
    lower = lane < HALF
    side = lane // HALF
    f32 = jnp.float32

    for target in targets:
        target[...] = jnp.zeros(target.shape, f32)

    def sources(hop_x):
        return pieces_from(groups, my_place, packs_in, hop_x)

    ones = (
        (
            lax.broadcasted_iota(jnp.int32, (LANE, LANE), 0) // HALF
            == lax.broadcasted_iota(jnp.int32, (LANE, LANE), 1) // HALF
        )
        .astype(f32)
        .astype(jnp.bfloat16)
    )

    def part_groups(part, share):
        for number in range(share):
            hop_x = part * share + number
            for at, (piece, column, depth_at) in enumerate(sources(hop_x)):
                for inner in range(per_device):
                    stored = (hop_x * pieces + at) * per_device + inner
                    atoms_at = ((column * groups_z + depth_at) * per_device + inner) * SUB
                    yield piece, hop_x, inner, stored, atoms_at

    def apply_step(cur, prev, new, alpha, beta, first, last):
        def project(part, carry):
            if not first:
                slabs = [part * chunk + number for number in range(chunk)]
                lay_products(groups, high_buf, low_buf, plane, depth, slabs, near)
            sums = []
            for piece, hop_x, inner, stored, atoms_at in part_groups(part, chunk):
                terms = ([], [])
                for j in range(SUB):
                    atom = atoms_at + j
                    value = cur[pl.ds(place[atom], SUB), :]
                    both = jnp.where(side == half[atom], value, pltpu.roll(value, HALF, 1))
                    for kp in range(2):
                        at = SUB + (inner * 2 + kp) * SUB + j
                        terms[kp].append(both * piece[hop_x, at])
                sums += [row_sums(terms[0]), row_sums(terms[1])]
            high, low = split_pair(jnp.concatenate(sums, axis=0))
            rows = len(sums) * SUB
            at = pl.multiple_of(part * rows, rows)
            coeffs[pl.ds(at, rows), :] = mxu(high, ones) + mxu(low, ones)
            return carry

        lax.fori_loop(0, groups_x // chunk, project, 0)

        def scatter(part, carry):
            for piece, hop_x, inner, stored, atoms_at in part_groups(part, 1):
                weights = [
                    coeffs[pl.ds(pl.multiple_of((stored * 2 + kp) * SUB, SUB), SUB), :]
                    for kp in range(2)
                ]
                for j in range(SUB):
                    atom = atoms_at + j
                    parts = [
                        jnp.broadcast_to(weights[kp][j : j + 1], (SUB, LANE))
                        * piece[hop_x, SUB + (inner * 2 + kp) * SUB + j]
                        for kp in range(2)
                    ]
                    value = parts[0] + parts[1]
                    value = value + pltpu.roll(value, HALF, 1)
                    value = jnp.where(side == half[atom], value, 0.0)
                    rows = pl.ds(place[atom], SUB)
                    target = targets[j % len(targets)]
                    target[rows, :] = target[rows, :] + value
            return carry

        lax.fori_loop(0, groups_x, scatter, 0)

        def combine(slab_at, carry):
            for tile in range(pairs_slab):
                pair = slab_at * pairs_slab + tile
                cols = slice(tile * LANE, (tile + 1) * LANE)
                for at_row in range(0, span, TALL):
                    rows = pl.ds(pl.multiple_of(pair * span + at_row, TALL), TALL)
                    slab_at_row = pl.ds(pl.multiple_of(slab_at * span + at_row, TALL), TALL)
                    total = local[rows, :] * cur[rows, :]
                    if first:
                        total = total + near_a[rows, :]
                    for target in targets:
                        total = total + target[rows, :]
                    if not last:
                        for target in targets[1:]:
                            target[rows, :] = jnp.zeros((TALL, LANE), f32)
                    total = total * alpha
                    if beta is not None:
                        total = total + beta * prev[rows, :]
                    new[rows, :] = total
                    if not last:
                        split_store(high_buf, low_buf, slab_at_row, cols, total)
                if last:
                    for depth_at in range(groups_z):
                        at = pl.multiple_of(pair * span + depth_at * LANE, LANE)
                        turned = new[pl.ds(at, LANE), :].T
                        out[block_rows(groups_z, pair, 0, depth_at), :] = turned[:HALF]
                        out[block_rows(groups_z, pair, 1, depth_at), :] = turned[HALF:]
            return carry

        lax.fori_loop(0, groups_x, combine, 0)

    sigma_one = half_width / (LOW_EDGE - middle)
    sigma_now = sigma_one
    apply_step(field_a, None, field_b, sigma_one / half_width, None, True, DEGREE == 1)
    prev, cur, new = field_a, field_b, field_c
    for degree_step in range(1, DEGREE):
        sigma_next = 1.0 / (2.0 / sigma_one - sigma_now)
        last = degree_step == DEGREE - 1
        target = prev if degree_step > 1 else new
        apply_step(
            cur,
            prev,
            target,
            2.0 * sigma_next / half_width,
            -sigma_now * sigma_next,
            False,
            last,
        )
        prev, cur = cur, target
        sigma_now = sigma_next


def pack_kernel(my_first, extent, coupling, potential, projectors, out):
    atoms = projectors.shape[0]
    f32, bf16 = jnp.float32, jnp.bfloat16
    lane = lax.broadcasted_iota(jnp.int32, (SUB, LANE), 1)
    row = lax.broadcasted_iota(jnp.int32, (SUB, LANE), 0)
    lower = lane < HALF

    flat = potential[...].reshape(HALF, LANE)
    turned = jnp.concatenate([flat, flat], axis=0).T
    low = lax.broadcasted_iota(jnp.int32, (HALF, LANE), 1) < HALF
    out[:SUB] = jnp.where(low, turned[:HALF], turned[HALF:]).reshape(SUB, SUB, LANE)

    cells = projectors.shape[2]
    own_row = lax.broadcasted_iota(jnp.int32, (SUB, cells), 1) % B
    own_row = own_row == lax.broadcasted_iota(jnp.int32, (SUB, cells), 0)
    sides = []
    for kh in range(2):
        parts = []
        for kp in range(2):
            for atom in range(atoms):
                line = projectors[atom, 2 * kp + kh : 2 * kp + kh + 1, :]
                parts.append(jnp.where(own_row, jnp.broadcast_to(line, (SUB, cells)), 0.0))
        sides.append(jnp.concatenate(parts, axis=0))
    value = jnp.concatenate(sides, axis=1)
    source = lax.broadcasted_iota(jnp.int32, (2 * cells, LANE), 0) // B
    hot = source == lax.broadcasted_iota(jnp.int32, (2 * cells, LANE), 1)
    hot = hot.astype(f32).astype(bf16)
    high = value.astype(bf16)
    rest = value - high.astype(f32)
    mid = rest.astype(bf16)
    small = (rest - mid.astype(f32)).astype(bf16)
    moved = (mxu(high, hot) + mxu(mid, hot)) + mxu(small, hot)

    reach = jnp.maximum(jnp.maximum((lane >> 3) & (B - 1), lane & (B - 1)), row)
    for kp in range(2):
        for atom in range(atoms):
            at = my_first[0] + atom
            scale = jnp.sqrt(
                jnp.where(lower, coupling[2 * kp, at], coupling[2 * kp + 1, at])
            )
            number = kp * atoms + atom
            part = moved[number * SUB : (number + 1) * SUB]
            group, j = atom // SUB, atom % SUB
            out[SUB + (group * 2 + kp) * SUB + j] = jnp.where(
                reach < extent[at], part * scale, 0.0
            )


def packed_inputs(my_first, extent, coupling, potential, projectors, interpret=False):
    vmem = pl.BlockSpec(memory_space=pltpu.VMEM)
    smem = pl.BlockSpec(memory_space=pltpu.SMEM)
    atoms = projectors.shape[0]
    return pl.pallas_call(
        pack_kernel,
        out_shape=jax.ShapeDtypeStruct((SUB + 2 * atoms, SUB, LANE), jnp.float32),
        in_specs=[smem] * 3 + [vmem] * 2,
        out_specs=vmem,
        compiler_params=pltpu.CompilerParams(vmem_limit_bytes=8 * 1024 * 1024),
        interpret=interpret,
    )(my_first, extent, coupling.T, potential, projectors)


def weights_kernel(plane_in, depth_in, plane, depth, sems):
    loads = [
        pltpu.make_async_copy(plane_in, plane, sems.at[0]),
        pltpu.make_async_copy(depth_in, depth, sems.at[1]),
    ]
    for load in loads:
        load.start()
    for load in loads:
        load.wait()


def weights_call(groups, interpret=False):
    plane = jnp.asarray(plane_weights(groups[1]))
    depth = jnp.asarray(depth_weights(groups[2]))
    return pl.pallas_call(
        weights_kernel,
        out_shape=[jax.ShapeDtypeStruct(part.shape, part.dtype) for part in (plane, depth)],
        in_specs=[pl.BlockSpec(memory_space=pl.ANY)] * 2,
        out_specs=[pl.BlockSpec(memory_space=pltpu.VMEM)] * 2,
        scratch_shapes=[pltpu.SemaphoreType.DMA((2,))],
        compiler_params=pltpu.CompilerParams(vmem_limit_bytes=4 * 1024 * 1024),
        interpret=interpret,
    )(plane, depth)


def box_places(groups, owner, anchor):
    groups_z = groups[2]
    column = owner // groups_z
    place = (column // 2 * groups_z + owner % groups_z) * LANE + anchor
    return place, column % 2


def first_call(groups, field, plane, depth, interpret=False):
    groups_x, groups_y, groups_z = groups
    span = groups_z * LANE
    cells = (groups_x * groups_y // 2 * span, LANE)
    slabs = (groups_x * span, groups_y * HALF)
    vmem = pl.BlockSpec(memory_space=pltpu.VMEM)
    work = 2 * slabs[0] * slabs[1] * (9 * slabs[1] + 3 * span)
    return pl.pallas_call(
        functools.partial(first_kernel, groups),
        out_shape=[
            jax.ShapeDtypeStruct(cells, jnp.float32),
            jax.ShapeDtypeStruct(cells, jnp.float32),
        ],
        in_specs=[vmem] * 3,
        out_specs=[vmem] * 2,
        scratch_shapes=[
            pltpu.VMEM(slabs, jnp.bfloat16),
            pltpu.VMEM(slabs, jnp.bfloat16),
        ],
        compiler_params=pltpu.CompilerParams(vmem_limit_bytes=12 * 1024 * 1024),
        cost_estimate=pl.CostEstimate(
            flops=work, bytes_accessed=4 * field.size * 4, transcendentals=0
        ),
        interpret=interpret,
    )(field.reshape(cells), plane, depth)


def potential_call(groups, my_place, packs, interpret=False):
    groups_x, groups_y, groups_z = groups
    cells = (groups_x * groups_y // 2 * groups_z * LANE, LANE)
    vmem = pl.BlockSpec(memory_space=pltpu.VMEM)
    return pl.pallas_call(
        functools.partial(potential_kernel, groups),
        out_shape=jax.ShapeDtypeStruct(cells, jnp.float32),
        in_specs=[pl.BlockSpec(memory_space=pltpu.SMEM)] + [vmem] * len(packs),
        out_specs=vmem,
        compiler_params=pltpu.CompilerParams(vmem_limit_bytes=8 * 1024 * 1024),
        cost_estimate=pl.CostEstimate(
            flops=0, bytes_accessed=160 * cells[0] * LANE, transcendentals=0
        ),
        interpret=interpret,
    )(my_place, *packs)


def filter_call(
    groups, place, half, my_place, field, near, local, packs, plane, depth, interpret=False
):
    groups_x, groups_y, groups_z = groups
    columns = groups_x * groups_y
    atoms = place.shape[0]
    vmem = pl.BlockSpec(memory_space=pltpu.VMEM)
    smem = pl.BlockSpec(memory_space=pltpu.SMEM)
    slabs = (groups_x * groups_z * LANE, groups_y * HALF)
    work = 2 * slabs[0] * slabs[1] * (9 * slabs[1] + 3 * groups_z * LANE)
    out = pl.pallas_call(
        functools.partial(filter_kernel, groups, atoms),
        out_shape=jax.ShapeDtypeStruct(field.shape, jnp.float32),
        in_specs=[smem] * 3 + [vmem] * (len(packs) + 5),
        out_specs=vmem,
        scratch_shapes=[
            pltpu.VMEM(field.shape, jnp.float32),
            pltpu.VMEM(field.shape, jnp.float32),
            pltpu.VMEM((atoms * 2, LANE), jnp.float32),
            pltpu.VMEM(slabs, jnp.bfloat16),
            pltpu.VMEM(slabs, jnp.bfloat16),
        ]
        + [pltpu.VMEM(field.shape, jnp.float32) for _ in range(1 + SPARES)],
        compiler_params=pltpu.CompilerParams(vmem_limit_bytes=22 * 1024 * 1024),
        cost_estimate=pl.CostEstimate(
            flops=3 * work, bytes_accessed=8 * field.size * 4, transcendentals=0
        ),
        interpret=interpret,
    )(place, half, my_place, field, near, local, *packs, plane, depth)
    return out.reshape(columns * groups_z, SUB, SUB, LANE)


def hops(value, axis):
    count = lax.axis_size(axis)
    return [value] + [
        lax.ppermute(value, axis, [(i, (i + hop) % count) for i in range(count)])
        for hop in range(1, count)
    ]


def state_body(orbitals, potential, projectors, owner_rank, box_anchor, box_extent, coupling):
    axes = ("gx", "gy", "gz")
    groups = tuple(lax.axis_size(axis) for axis in axes)
    groups_z = groups[2]
    domains = groups[0] * groups[1] * groups_z
    atoms_own = projectors.shape[0]
    my_place = jnp.stack([lax.axis_index(axis) for axis in axes])
    me = (my_place[0] * groups[1] + my_place[1]) * groups_z + my_place[2]
    pack = packed_inputs((me * atoms_own)[None], box_extent, coupling, potential, projectors)
    line = jnp.stack(hops(pack, "gx"))
    place, half = box_places(groups, owner_rank, box_anchor[2])
    plane, depth = weights_call(groups)
    orbitals, line, place, half, plane, depth = lax.optimization_barrier(
        (orbitals, line, place, half, plane, depth)
    )
    crossed = [hops(piece, "gz") for piece in hops(line, "gy")]
    packs = [crossed[hop_y][hop_z] for hop_z in range(groups_z) for hop_y in range(groups[1])]
    field = lax.all_to_all(orbitals, axes, split_axis=0, concat_axis=0, tiled=True)
    field, near = first_call(groups, field, plane, depth)
    local = potential_call(groups, my_place, packs)
    result = filter_call(groups, place, half, my_place, field, near, local, packs, plane, depth)
    filtered = lax.all_to_all(result, axes, split_axis=0, concat_axis=0, tiled=True)
    states = filtered.shape[0]
    flattened = filtered.reshape(states, -1)
    partial_value = jnp.dot(flattened, flattened.T, precision=lax.Precision.HIGHEST)
    quarter = partial_value.reshape(-1, SUB, states).transpose(1, 0, 2).reshape(SUB, -1)
    parts = lax.all_to_all(
        jnp.broadcast_to(quarter[None], (domains,) + quarter.shape),
        axes,
        split_axis=0,
        concat_axis=0,
        tiled=True,
    )
    summed = jnp.sum(parts, axis=0).reshape(SUB, -1, states).transpose(1, 0, 2)
    cells_total = orbitals.shape[1] * orbitals.shape[2] * orbitals.shape[3] * domains
    intersection = summed.reshape(states, states) / cells_total
    return (filtered, intersection)


def body(orbitals, potential, projectors, owner_rank, box_anchor, box_extent, coupling):
    domains = lax.axis_size("gx") * lax.axis_size("gy") * lax.axis_size("gz")
    whole_states = (
        orbitals.shape == (domains, SUB, SUB, LANE)
        and projectors.shape[0] % SUB == 0
        and projectors.shape[1] == NPROJ
        and lax.axis_size("gy") % 2 == 0
    )
    chosen = state_body if whole_states else domain_body
    return chosen(
        orbitals, potential, projectors, owner_rank, box_anchor, box_extent, coupling
    )


def solution(mesh):
    return jax.shard_map(
        body,
        mesh=mesh,
        in_specs=(
            P(None, "gx", "gy", "gz"),
            P("gx", "gy", "gz"),
            P(("gx", "gy", "gz"), None, None),
            P(),
            P(),
            P(),
            P(),
        ),
        out_specs=(P(None, "gx", "gy", "gz"), P()),
        check_vma=False,
    )
```

```python
import functools
import math
import jax
import jax.numpy as jnp
from jax import lax
from jax.experimental import pallas as pl
from jax.experimental.pallas import tpu as pltpu
import ml_dtypes
import numpy as np
from jax.sharding import PartitionSpec as P

B = 8
DEGREE = 4
ATOM_DEV = 8


STENCIL = (
    -5369.0 / 1800.0,
    12.0 / 7.0,
    -15.0 / 56.0,
    10.0 / 189.0,
    -1.0 / 112.0,
    2.0 / 1925.0,
    -1.0 / 16632.0,
)
SPACING = 0.5
LOW_EDGE = -2.5
CUTOFF = 4.0
UPPER = 60.0


def extended(cells, sides, width):
    for axis, dim in sides:
        count = lax.axis_size(axis)
        head = lax.slice_in_dim(cells, 0, width, axis=dim)
        tail = lax.slice_in_dim(cells, cells.shape[dim] - width, cells.shape[dim], axis=dim)
        cells = jnp.concatenate(
            [
                lax.ppermute(tail, axis, [(i, (i + 1) % count) for i in range(count)]),
                cells,
                lax.ppermute(head, axis, [((i + 1) % count, i) for i in range(count)]),
            ],
            axis=dim,
        )
    return cells


def laplace_padded(padded, shape):
    span_x, span_y, span_z = (shape[1], shape[2], shape[3])
    summed = 3.0 * STENCIL[0] * padded[:, 6 : 6 + span_x, 6 : 6 + span_y, 6 : 6 + span_z]
    for offset in range(1, 7):
        weight = STENCIL[offset]
        summed = summed + weight * (
            padded[:, 6 + offset : 6 + offset + span_x, 6 : 6 + span_y, 6 : 6 + span_z]
            + padded[:, 6 - offset : 6 - offset + span_x, 6 : 6 + span_y, 6 : 6 + span_z]
        )
        summed = summed + weight * (
            padded[:, 6 : 6 + span_x, 6 + offset : 6 + offset + span_y, 6 : 6 + span_z]
            + padded[:, 6 : 6 + span_x, 6 - offset : 6 - offset + span_y, 6 : 6 + span_z]
        )
        summed = summed + weight * (
            padded[:, 6 : 6 + span_x, 6 : 6 + span_y, 6 + offset : 6 + offset + span_z]
            + padded[:, 6 : 6 + span_x, 6 : 6 + span_y, 6 - offset : 6 - offset + span_z]
        )
    return summed / (SPACING * SPACING)


def collect_boxes(projectors, member, box_anchor, box_extent, coupling, capacity):
    member_int = member.astype(jnp.int32)
    slot_all = jnp.cumsum(member_int) - 1
    count = jnp.sum(member_int)
    slot_ids = jnp.arange(capacity, dtype=jnp.int32)
    onehot = ((slot_all[None, :] == slot_ids[:, None]) & member[None, :]).astype(jnp.float32)
    buffer = jnp.einsum(
        "cp,pkf->ckf",
        onehot,
        lax.all_gather(projectors, ("gx", "gy", "gz"), axis=0, tiled=True),
        precision=lax.Precision.HIGHEST,
    )
    hot_all = (slot_all[None, :] == slot_ids[:, None]) & member[None, :]
    slot_anchor = jnp.sum(jnp.where(hot_all[None, :, :], box_anchor[:, None, :], 0), axis=2)
    slot_extent = jnp.sum(jnp.where(hot_all, box_extent[None, :], 0), axis=1)
    slot_coupling = jnp.sum(jnp.where(hot_all[:, :, None], coupling[None, :, :], 0.0), axis=1)
    cell_offsets = jnp.arange(B, dtype=jnp.int32)
    limit = slot_extent[:, None, None, None]
    inside = (
        (cell_offsets[None, :, None, None] < limit)
        & (cell_offsets[None, None, :, None] < limit)
        & (cell_offsets[None, None, None, :] < limit)
    )
    buffer = buffer * inside.reshape(capacity, 1, B * B * B).astype(jnp.float32)
    return (buffer, slot_anchor, slot_coupling, count)


def nonlocal_term(field, buffer, slot_anchor, slot_coupling, count, domain_start):
    states = field.shape[0]

    def add_slot(slot_index, nonlocal_sum):
        corner = slot_anchor[:, slot_index] - domain_start
        start_cell = (0, corner[0], corner[1], corner[2])
        box_cells = lax.dynamic_slice(field, start_cell, (states, B, B, B)).reshape(
            states, B * B * B
        )
        proj_box = buffer[slot_index]
        coeffs = (
            jnp.dot(box_cells, proj_box.T, precision=lax.Precision.HIGHEST)
            * slot_coupling[slot_index][None, :]
        )
        addition = jnp.dot(coeffs, proj_box, precision=lax.Precision.HIGHEST).reshape(
            states, B, B, B
        )
        current = lax.dynamic_slice(nonlocal_sum, start_cell, (states, B, B, B))
        return lax.dynamic_update_slice(nonlocal_sum, current + addition, start_cell)

    return lax.fori_loop(0, count, add_slot, jnp.zeros_like(field))


def run_filter(field, apply_h):
    half_width = (UPPER - CUTOFF) / 2.0
    middle = (UPPER + CUTOFF) / 2.0
    sigma_one = half_width / (LOW_EDGE - middle)
    sigma_now = sigma_one
    result = (apply_h(field) - middle * field) * (sigma_one / half_width)
    previous = field
    for degree_step in range(1, DEGREE):
        sigma_next = 1.0 / (2.0 / sigma_one - sigma_now)
        next_state = (apply_h(result) - middle * result) * (
            2.0 * sigma_next / half_width
        ) - sigma_now * sigma_next * previous
        previous = result
        result = next_state
        sigma_now = sigma_next
    return result


def domain_body(orbitals, potential, projectors, owner_rank, box_anchor, box_extent, coupling):
    groups_y = lax.axis_size("gy")
    groups_z = lax.axis_size("gz")
    own_x = owner_rank // (groups_y * groups_z)
    own_y = owner_rank // groups_z % groups_y
    own_z = owner_rank % groups_z
    index_x = lax.axis_index("gx")
    index_y = lax.axis_index("gy")
    index_z = lax.axis_index("gz")
    span_x, span_y, span_z = (orbitals.shape[1], orbitals.shape[2], orbitals.shape[3])
    grid_anchor = jnp.stack([own_x * span_x, own_y * span_y, own_z * span_z]) + box_anchor
    member = (own_x == index_x) & (own_y == index_y) & (own_z == index_z)
    buffer, slot_anchor, slot_coupling, count = collect_boxes(
        projectors, member, grid_anchor, box_extent, coupling, 3 * ATOM_DEV
    )
    domain_start = jnp.stack([index_x * span_x, index_y * span_y, index_z * span_z])

    def apply_cube(field):
        padded = extended(field, (("gx", 1), ("gy", 2), ("gz", 3)), 6)
        return (
            -0.5 * laplace_padded(padded, field.shape)
            + potential[None] * field
            + nonlocal_term(field, buffer, slot_anchor, slot_coupling, count, domain_start)
        )

    filtered = run_filter(orbitals, apply_cube)
    flattened = filtered.reshape(filtered.shape[0], -1)
    partial_value = jnp.dot(flattened, flattened.T, precision=lax.Precision.HIGHEST)
    cells_total = span_x * span_y * span_z * lax.axis_size("gx") * groups_y * groups_z
    intersection = lax.psum(partial_value, ("gx", "gy", "gz")) / cells_total
    return (filtered, intersection)


SUB = 8
LANE = 128
HALF = LANE // 2
NPROJ = 4


def split_terms(matrix):
    high = matrix.astype(ml_dtypes.bfloat16)
    low = (matrix - high.astype(np.float64)).astype(ml_dtypes.bfloat16)
    return high, low


def stencil_weight(distance):
    if distance == 0 or abs(distance) > 6:
        return 0.0
    return -0.5 * STENCIL[abs(distance)] / (SPACING * SPACING)


def ring_matrix(length):
    matrix = np.zeros((length, length))
    for offset in range(-6, 7):
        for row in range(length):
            matrix[row, (row + offset) % length] += stencil_weight(offset)
    return matrix


def plane_weights(groups_y):
    slab = groups_y * HALF
    ring = ring_matrix(groups_y * SUB).reshape(groups_y, SUB, groups_y, SUB)
    blocks = []
    for shift in (-SUB, 0, SUB):
        along_x = np.array(
            [[stencil_weight(shift + i - o) for o in range(SUB)] for i in range(SUB)]
        )
        block = np.einsum("ab,io,jp->aijbop", np.eye(groups_y), along_x, np.eye(SUB))
        if shift == 0:
            block = block + np.einsum("ajbp,io->aijbop", ring, np.eye(SUB))
        blocks.append(block.reshape(slab, slab))
    high, low = split_terms(np.concatenate(blocks, axis=0))
    return np.concatenate([high, low], axis=0)


def depth_weights(groups_z):
    high, low = split_terms(ring_matrix(groups_z * LANE))
    return np.concatenate([high, low, high], axis=1)


def split_pair(value):
    high = value.astype(jnp.bfloat16)
    low = (value - high.astype(jnp.float32)).astype(jnp.bfloat16)
    return high, low


def mxu(left, right):
    return jnp.dot(left, right, preferred_element_type=jnp.float32)


def row_sums(values):
    row = lax.broadcasted_iota(jnp.int32, (SUB, LANE), 0)
    for stride in (1, 2, 4):
        keep = (row & stride) == 0
        values = [
            jnp.where(keep, one, two) + pltpu.roll(jnp.where(keep, two, one), stride, 0)
            for one, two in zip(values[0::2], values[1::2])
        ]
    return values[0]


SPARES = 1
TALL = 2 * SUB


def split_store(high_buf, low_buf, rows, cols, value):
    high, low = split_pair(value)
    high_buf[rows, cols] = high
    low_buf[rows, cols] = low


def slab_rows(slab_at, span):
    return pl.ds(pl.multiple_of(slab_at * span, span), span)


def plane_product(groups_x, span, high_buf, low_buf, plane, slabs):
    width = plane.shape[1]

    def around(buf, shift):
        parts = [
            buf[slab_rows(lax.rem(at + shift + groups_x, groups_x), span), :] for at in slabs
        ]
        return jnp.concatenate(parts, axis=0)

    high = [around(high_buf, shift) for shift in (-1, 0, 1)]
    low = [around(low_buf, shift) for shift in (-1, 0, 1)]
    left = jnp.concatenate(high + low + high, axis=1)
    right = jnp.concatenate([plane[: 3 * width], plane[: 3 * width], plane[3 * width :]], axis=0)
    return mxu(left, right)


def depth_product(span, high_buf, low_buf, depth, slab_at):
    high = high_buf[slab_rows(slab_at, span), :]
    low = low_buf[slab_rows(slab_at, span), :]
    return mxu(depth[...], jnp.concatenate([high, high, low], axis=0))


def lay_products(groups, high_buf, low_buf, plane, depth, slabs, near):
    groups_x, groups_y, groups_z = groups
    span = groups_z * LANE
    pairs_slab = groups_y // 2
    total = plane_product(groups_x, span, high_buf, low_buf, plane, slabs)
    for number, slab_at in enumerate(slabs):
        deep = depth_product(span, high_buf, low_buf, depth, slab_at)
        part = total[number * span : (number + 1) * span] + deep
        for tile in range(pairs_slab):
            cols = part[:, tile * LANE : (tile + 1) * LANE]
            near[slab_rows(slab_at * pairs_slab + tile, span), :] = cols


def chunk_of(groups_x):
    return 2 if groups_x % 2 == 0 else 1


def block_rows(groups_z, pair, parity, depth_at):
    return pl.ds(pl.multiple_of(((2 * pair + parity) * groups_z + depth_at) * HALF, HALF), HALF)


def first_kernel(groups, *refs):
    raw, plane, depth, field, near, high_buf, low_buf = refs
    groups_x, groups_y, groups_z = groups
    span = groups_z * LANE
    pairs_slab = groups_y // 2

    def lay_field(slab_at, carry):
        for tile in range(pairs_slab):
            pair = slab_at * pairs_slab + tile
            cols = slice(tile * LANE, (tile + 1) * LANE)
            for depth_at in range(groups_z):
                first = raw[block_rows(groups_z, pair, 0, depth_at), :]
                second = raw[block_rows(groups_z, pair, 1, depth_at), :]
                turned = jnp.concatenate([first, second], axis=0).T
                at = pl.multiple_of(pair * span + depth_at * LANE, LANE)
                field[pl.ds(at, LANE), :] = turned
                at = pl.multiple_of(slab_at * span + depth_at * LANE, LANE)
                split_store(high_buf, low_buf, pl.ds(at, LANE), cols, turned)
        return carry

    lax.fori_loop(0, groups_x, lay_field, 0)
    chunk = chunk_of(groups_x)

    def product(chunk_at, carry):
        slabs = [chunk_at * chunk + number for number in range(chunk)]
        lay_products(groups, high_buf, low_buf, plane, depth, slabs, near)
        return carry

    lax.fori_loop(0, groups_x // chunk, product, 0)


def filter_kernel(groups, atoms, place, half, my_place, *refs):
    groups_x, groups_y, groups_z = groups
    pieces = groups_y * groups_z
    field_a, near_a = refs[:2]
    packs_in = refs[2 : 2 + pieces]
    plane, depth, out = refs[2 + pieces : 5 + pieces]
    field_b, field_c, local, coeffs, high_buf, low_buf, near = refs[5 + pieces : 12 + pieces]
    spares = refs[12 + pieces :]
    targets = (near,) + tuple(spares)
    columns = groups_x * groups_y
    domains = columns * groups_z
    pairs = columns // 2
    span = groups_z * LANE
    pairs_slab = groups_y // 2
    per_device = atoms // domains // SUB
    chunk = chunk_of(groups_x)
    half_width = (UPPER - CUTOFF) / 2.0
    middle = (UPPER + CUTOFF) / 2.0
    diagonal = -0.5 * 3.0 * STENCIL[0] / (SPACING * SPACING) - middle
    lane = lax.broadcasted_iota(jnp.int32, (SUB, LANE), 1)
    lower = lane < HALF
    side = lane // HALF
    f32 = jnp.float32

    for target in targets:
        target[...] = jnp.zeros(target.shape, f32)

    def sources(hop_x):
        for hop_z in range(groups_z):
            for hop_y in range(groups_y):
                from_x = lax.rem(my_place[0] + (groups_x - hop_x), groups_x)
                from_y = lax.rem(my_place[1] + (groups_y - hop_y), groups_y)
                from_z = lax.rem(my_place[2] + (groups_z - hop_z), groups_z)
                yield packs_in[hop_z * groups_y + hop_y], from_x * groups_y + from_y, from_z

    def lay_potential(hop_x, carry):
        for piece, column, depth_at in sources(hop_x):
            mine = side == column % 2
            for tile in range(SUB):
                value = diagonal + piece[hop_x, tile]
                other = pltpu.roll(value, HALF, 1)
                for upper in range(2):
                    at = column // 2 * span + depth_at * LANE + upper * HALF + tile * SUB
                    rows = pl.ds(pl.multiple_of(at, SUB), SUB)
                    chosen = jnp.where(side == upper, value, other)
                    local[rows, :] = jnp.where(mine, chosen, local[rows, :])
        return carry

    lax.fori_loop(0, groups_x, lay_potential, 0)

    ones = (
        (
            lax.broadcasted_iota(jnp.int32, (LANE, LANE), 0) // HALF
            == lax.broadcasted_iota(jnp.int32, (LANE, LANE), 1) // HALF
        )
        .astype(f32)
        .astype(jnp.bfloat16)
    )

    def part_groups(part, share):
        for number in range(share):
            hop_x = part * share + number
            for at, (piece, column, depth_at) in enumerate(sources(hop_x)):
                for inner in range(per_device):
                    stored = (hop_x * pieces + at) * per_device + inner
                    atoms_at = ((column * groups_z + depth_at) * per_device + inner) * SUB
                    yield piece, hop_x, inner, stored, atoms_at

    def apply_step(cur, prev, new, alpha, beta, first, last):
        def project(part, carry):
            if not first:
                slabs = [part * chunk + number for number in range(chunk)]
                lay_products(groups, high_buf, low_buf, plane, depth, slabs, near)
            sums = []
            for piece, hop_x, inner, stored, atoms_at in part_groups(part, chunk):
                terms = ([], [])
                for j in range(SUB):
                    atom = atoms_at + j
                    value = cur[pl.ds(place[atom], SUB), :]
                    both = jnp.where(side == half[atom], value, pltpu.roll(value, HALF, 1))
                    for kp in range(2):
                        at = SUB + (inner * 2 + kp) * SUB + j
                        terms[kp].append(both * piece[hop_x, at])
                sums += [row_sums(terms[0]), row_sums(terms[1])]
            high, low = split_pair(jnp.concatenate(sums, axis=0))
            rows = len(sums) * SUB
            at = pl.multiple_of(part * rows, rows)
            coeffs[pl.ds(at, rows), :] = mxu(high, ones) + mxu(low, ones)
            return carry

        lax.fori_loop(0, groups_x // chunk, project, 0)

        def scatter(part, carry):
            for piece, hop_x, inner, stored, atoms_at in part_groups(part, 1):
                weights = [
                    coeffs[pl.ds(pl.multiple_of((stored * 2 + kp) * SUB, SUB), SUB), :]
                    for kp in range(2)
                ]
                for j in range(SUB):
                    atom = atoms_at + j
                    parts = [
                        jnp.broadcast_to(weights[kp][j : j + 1], (SUB, LANE))
                        * piece[hop_x, SUB + (inner * 2 + kp) * SUB + j]
                        for kp in range(2)
                    ]
                    value = parts[0] + parts[1]
                    value = value + pltpu.roll(value, HALF, 1)
                    value = jnp.where(side == half[atom], value, 0.0)
                    rows = pl.ds(place[atom], SUB)
                    target = targets[j % len(targets)]
                    target[rows, :] = target[rows, :] + value
            return carry

        lax.fori_loop(0, groups_x, scatter, 0)

        def combine(slab_at, carry):
            for tile in range(pairs_slab):
                pair = slab_at * pairs_slab + tile
                cols = slice(tile * LANE, (tile + 1) * LANE)
                for at_row in range(0, span, TALL):
                    rows = pl.ds(pl.multiple_of(pair * span + at_row, TALL), TALL)
                    slab_at_row = pl.ds(pl.multiple_of(slab_at * span + at_row, TALL), TALL)
                    total = local[rows, :] * cur[rows, :]
                    if first:
                        total = total + near_a[rows, :]
                    for target in targets:
                        total = total + target[rows, :]
                    if not last:
                        for target in targets[1:]:
                            target[rows, :] = jnp.zeros((TALL, LANE), f32)
                    total = total * alpha
                    if beta is not None:
                        total = total + beta * prev[rows, :]
                    new[rows, :] = total
                    if not last:
                        split_store(high_buf, low_buf, slab_at_row, cols, total)
                if last:
                    for depth_at in range(groups_z):
                        at = pl.multiple_of(pair * span + depth_at * LANE, LANE)
                        turned = new[pl.ds(at, LANE), :].T
                        out[block_rows(groups_z, pair, 0, depth_at), :] = turned[:HALF]
                        out[block_rows(groups_z, pair, 1, depth_at), :] = turned[HALF:]
            return carry

        lax.fori_loop(0, groups_x, combine, 0)

    sigma_one = half_width / (LOW_EDGE - middle)
    sigma_now = sigma_one
    apply_step(field_a, None, field_b, sigma_one / half_width, None, True, DEGREE == 1)
    prev, cur, new = field_a, field_b, field_c
    for degree_step in range(1, DEGREE):
        sigma_next = 1.0 / (2.0 / sigma_one - sigma_now)
        last = degree_step == DEGREE - 1
        target = prev if degree_step > 1 else new
        apply_step(
            cur,
            prev,
            target,
            2.0 * sigma_next / half_width,
            -sigma_now * sigma_next,
            False,
            last,
        )
        prev, cur = cur, target
        sigma_now = sigma_next


def pack_kernel(my_first, extent, coupling, potential, projectors, out):
    atoms = projectors.shape[0]
    f32, bf16 = jnp.float32, jnp.bfloat16
    lane = lax.broadcasted_iota(jnp.int32, (SUB, LANE), 1)
    row = lax.broadcasted_iota(jnp.int32, (SUB, LANE), 0)
    lower = lane < HALF

    flat = potential[...].reshape(HALF, LANE)
    turned = jnp.concatenate([flat, flat], axis=0).T
    low = lax.broadcasted_iota(jnp.int32, (HALF, LANE), 1) < HALF
    out[:SUB] = jnp.where(low, turned[:HALF], turned[HALF:]).reshape(SUB, SUB, LANE)

    cells = projectors.shape[2]
    own_row = lax.broadcasted_iota(jnp.int32, (SUB, cells), 1) % B
    own_row = own_row == lax.broadcasted_iota(jnp.int32, (SUB, cells), 0)
    sides = []
    for kh in range(2):
        parts = []
        for kp in range(2):
            for atom in range(atoms):
                line = projectors[atom, 2 * kp + kh : 2 * kp + kh + 1, :]
                parts.append(jnp.where(own_row, jnp.broadcast_to(line, (SUB, cells)), 0.0))
        sides.append(jnp.concatenate(parts, axis=0))
    value = jnp.concatenate(sides, axis=1)
    source = lax.broadcasted_iota(jnp.int32, (2 * cells, LANE), 0) // B
    hot = source == lax.broadcasted_iota(jnp.int32, (2 * cells, LANE), 1)
    hot = hot.astype(f32).astype(bf16)
    high = value.astype(bf16)
    rest = value - high.astype(f32)
    mid = rest.astype(bf16)
    small = (rest - mid.astype(f32)).astype(bf16)
    moved = (mxu(high, hot) + mxu(mid, hot)) + mxu(small, hot)

    reach = jnp.maximum(jnp.maximum((lane >> 3) & (B - 1), lane & (B - 1)), row)
    for kp in range(2):
        for atom in range(atoms):
            at = my_first[0] + atom
            scale = jnp.sqrt(
                jnp.where(lower, coupling[2 * kp, at], coupling[2 * kp + 1, at])
            )
            number = kp * atoms + atom
            part = moved[number * SUB : (number + 1) * SUB]
            group, j = atom // SUB, atom % SUB
            out[SUB + (group * 2 + kp) * SUB + j] = jnp.where(
                reach < extent[at], part * scale, 0.0
            )


def packed_inputs(my_first, extent, coupling, potential, projectors, interpret=False):
    vmem = pl.BlockSpec(memory_space=pltpu.VMEM)
    smem = pl.BlockSpec(memory_space=pltpu.SMEM)
    atoms = projectors.shape[0]
    return pl.pallas_call(
        pack_kernel,
        out_shape=jax.ShapeDtypeStruct((SUB + 2 * atoms, SUB, LANE), jnp.float32),
        in_specs=[smem] * 3 + [vmem] * 2,
        out_specs=vmem,
        compiler_params=pltpu.CompilerParams(vmem_limit_bytes=8 * 1024 * 1024),
        interpret=interpret,
    )(my_first, extent, coupling.T, potential, projectors)


def weights_kernel(plane_in, depth_in, plane, depth, sems):
    loads = [
        pltpu.make_async_copy(plane_in, plane, sems.at[0]),
        pltpu.make_async_copy(depth_in, depth, sems.at[1]),
    ]
    for load in loads:
        load.start()
    for load in loads:
        load.wait()


def weights_call(groups, interpret=False):
    plane = jnp.asarray(plane_weights(groups[1]))
    depth = jnp.asarray(depth_weights(groups[2]))
    return pl.pallas_call(
        weights_kernel,
        out_shape=[jax.ShapeDtypeStruct(part.shape, part.dtype) for part in (plane, depth)],
        in_specs=[pl.BlockSpec(memory_space=pl.ANY)] * 2,
        out_specs=[pl.BlockSpec(memory_space=pltpu.VMEM)] * 2,
        scratch_shapes=[pltpu.SemaphoreType.DMA((2,))],
        compiler_params=pltpu.CompilerParams(vmem_limit_bytes=4 * 1024 * 1024),
        interpret=interpret,
    )(plane, depth)


def box_places(groups, owner, anchor):
    groups_z = groups[2]
    column = owner // groups_z
    place = (column // 2 * groups_z + owner % groups_z) * LANE + anchor
    return place, column % 2


def first_call(groups, field, plane, depth, interpret=False):
    groups_x, groups_y, groups_z = groups
    span = groups_z * LANE
    cells = (groups_x * groups_y // 2 * span, LANE)
    slabs = (groups_x * span, groups_y * HALF)
    vmem = pl.BlockSpec(memory_space=pltpu.VMEM)
    work = 2 * slabs[0] * slabs[1] * (9 * slabs[1] + 3 * span)
    return pl.pallas_call(
        functools.partial(first_kernel, groups),
        out_shape=[
            jax.ShapeDtypeStruct(cells, jnp.float32),
            jax.ShapeDtypeStruct(cells, jnp.float32),
        ],
        in_specs=[vmem] * 3,
        out_specs=[vmem] * 2,
        scratch_shapes=[
            pltpu.VMEM(slabs, jnp.bfloat16),
            pltpu.VMEM(slabs, jnp.bfloat16),
        ],
        compiler_params=pltpu.CompilerParams(vmem_limit_bytes=12 * 1024 * 1024),
        cost_estimate=pl.CostEstimate(
            flops=work, bytes_accessed=4 * field.size * 4, transcendentals=0
        ),
        interpret=interpret,
    )(field.reshape(cells), plane, depth)


def filter_call(
    groups, place, half, my_place, field, near, packs, plane, depth, interpret=False
):
    groups_x, groups_y, groups_z = groups
    columns = groups_x * groups_y
    atoms = place.shape[0]
    vmem = pl.BlockSpec(memory_space=pltpu.VMEM)
    smem = pl.BlockSpec(memory_space=pltpu.SMEM)
    slabs = (groups_x * groups_z * LANE, groups_y * HALF)
    work = 2 * slabs[0] * slabs[1] * (9 * slabs[1] + 3 * groups_z * LANE)
    out = pl.pallas_call(
        functools.partial(filter_kernel, groups, atoms),
        out_shape=jax.ShapeDtypeStruct(field.shape, jnp.float32),
        in_specs=[smem] * 3 + [vmem] * (len(packs) + 4),
        out_specs=vmem,
        scratch_shapes=[
            pltpu.VMEM(field.shape, jnp.float32),
            pltpu.VMEM(field.shape, jnp.float32),
            pltpu.VMEM(field.shape, jnp.float32),
            pltpu.VMEM((atoms * 2, LANE), jnp.float32),
            pltpu.VMEM(slabs, jnp.bfloat16),
            pltpu.VMEM(slabs, jnp.bfloat16),
        ]
        + [pltpu.VMEM(field.shape, jnp.float32) for _ in range(1 + SPARES)],
        compiler_params=pltpu.CompilerParams(vmem_limit_bytes=22 * 1024 * 1024),
        cost_estimate=pl.CostEstimate(
            flops=3 * work, bytes_accessed=8 * field.size * 4, transcendentals=0
        ),
        interpret=interpret,
    )(place, half, my_place, field, near, *packs, plane, depth)
    return out.reshape(columns * groups_z, SUB, SUB, LANE)


def hops(value, axis):
    count = lax.axis_size(axis)
    return [value] + [
        lax.ppermute(value, axis, [(i, (i + hop) % count) for i in range(count)])
        for hop in range(1, count)
    ]


def state_body(orbitals, potential, projectors, owner_rank, box_anchor, box_extent, coupling):
    axes = ("gx", "gy", "gz")
    groups = tuple(lax.axis_size(axis) for axis in axes)
    groups_z = groups[2]
    domains = groups[0] * groups[1] * groups_z
    atoms_own = projectors.shape[0]
    my_place = jnp.stack([lax.axis_index(axis) for axis in axes])
    me = (my_place[0] * groups[1] + my_place[1]) * groups_z + my_place[2]
    pack = packed_inputs((me * atoms_own)[None], box_extent, coupling, potential, projectors)
    line = jnp.stack(hops(pack, "gx"))
    place, half = box_places(groups, owner_rank, box_anchor[2])
    plane, depth = weights_call(groups)
    orbitals, line, place, half, plane, depth = lax.optimization_barrier(
        (orbitals, line, place, half, plane, depth)
    )
    crossed = [hops(piece, "gz") for piece in hops(line, "gy")]
    packs = [crossed[hop_y][hop_z] for hop_z in range(groups_z) for hop_y in range(groups[1])]
    field = lax.all_to_all(orbitals, axes, split_axis=0, concat_axis=0, tiled=True)
    field, near = first_call(groups, field, plane, depth)
    result = filter_call(groups, place, half, my_place, field, near, packs, plane, depth)
    filtered = lax.all_to_all(result, axes, split_axis=0, concat_axis=0, tiled=True)
    states = filtered.shape[0]
    flattened = filtered.reshape(states, -1)
    partial_value = jnp.dot(flattened, flattened.T, precision=lax.Precision.HIGHEST)
    quarter = partial_value.reshape(-1, SUB, states).transpose(1, 0, 2).reshape(SUB, -1)
    parts = lax.all_to_all(
        jnp.broadcast_to(quarter[None], (domains,) + quarter.shape),
        axes,
        split_axis=0,
        concat_axis=0,
        tiled=True,
    )
    summed = jnp.sum(parts, axis=0).reshape(SUB, -1, states).transpose(1, 0, 2)
    cells_total = orbitals.shape[1] * orbitals.shape[2] * orbitals.shape[3] * domains
    intersection = summed.reshape(states, states) / cells_total
    return (filtered, intersection)


def body(orbitals, potential, projectors, owner_rank, box_anchor, box_extent, coupling):
    domains = lax.axis_size("gx") * lax.axis_size("gy") * lax.axis_size("gz")
    whole_states = (
        orbitals.shape == (domains, SUB, SUB, LANE)
        and projectors.shape[0] % SUB == 0
        and projectors.shape[1] == NPROJ
        and lax.axis_size("gy") % 2 == 0
    )
    chosen = state_body if whole_states else domain_body
    return chosen(
        orbitals, potential, projectors, owner_rank, box_anchor, box_extent, coupling
    )


def solution(mesh):
    return jax.shard_map(
        body,
        mesh=mesh,
        in_specs=(
            P(None, "gx", "gy", "gz"),
            P("gx", "gy", "gz"),
            P(("gx", "gy", "gz"), None, None),
            P(),
            P(),
            P(),
            P(),
        ),
        out_specs=(P(None, "gx", "gy", "gz"), P()),
        check_vma=False,
    )
```

```python
import functools
import math
import jax
import jax.numpy as jnp
from jax import lax
from jax.experimental import pallas as pl
from jax.experimental.pallas import tpu as pltpu
import ml_dtypes
import numpy as np
from jax.sharding import PartitionSpec as P

B = 8
DEGREE = 4
ATOM_DEV = 8


STENCIL = (
    -5369.0 / 1800.0,
    12.0 / 7.0,
    -15.0 / 56.0,
    10.0 / 189.0,
    -1.0 / 112.0,
    2.0 / 1925.0,
    -1.0 / 16632.0,
)
SPACING = 0.5
LOW_EDGE = -2.5
CUTOFF = 4.0
UPPER = 60.0


def extended(cells, sides, width):
    for axis, dim in sides:
        count = lax.axis_size(axis)
        head = lax.slice_in_dim(cells, 0, width, axis=dim)
        tail = lax.slice_in_dim(cells, cells.shape[dim] - width, cells.shape[dim], axis=dim)
        cells = jnp.concatenate(
            [
                lax.ppermute(tail, axis, [(i, (i + 1) % count) for i in range(count)]),
                cells,
                lax.ppermute(head, axis, [((i + 1) % count, i) for i in range(count)]),
            ],
            axis=dim,
        )
    return cells


def laplace_padded(padded, shape):
    span_x, span_y, span_z = (shape[1], shape[2], shape[3])
    summed = 3.0 * STENCIL[0] * padded[:, 6 : 6 + span_x, 6 : 6 + span_y, 6 : 6 + span_z]
    for offset in range(1, 7):
        weight = STENCIL[offset]
        summed = summed + weight * (
            padded[:, 6 + offset : 6 + offset + span_x, 6 : 6 + span_y, 6 : 6 + span_z]
            + padded[:, 6 - offset : 6 - offset + span_x, 6 : 6 + span_y, 6 : 6 + span_z]
        )
        summed = summed + weight * (
            padded[:, 6 : 6 + span_x, 6 + offset : 6 + offset + span_y, 6 : 6 + span_z]
            + padded[:, 6 : 6 + span_x, 6 - offset : 6 - offset + span_y, 6 : 6 + span_z]
        )
        summed = summed + weight * (
            padded[:, 6 : 6 + span_x, 6 : 6 + span_y, 6 + offset : 6 + offset + span_z]
            + padded[:, 6 : 6 + span_x, 6 : 6 + span_y, 6 - offset : 6 - offset + span_z]
        )
    return summed / (SPACING * SPACING)


def collect_boxes(projectors, member, box_anchor, box_extent, coupling, capacity):
    member_int = member.astype(jnp.int32)
    slot_all = jnp.cumsum(member_int) - 1
    count = jnp.sum(member_int)
    slot_ids = jnp.arange(capacity, dtype=jnp.int32)
    onehot = ((slot_all[None, :] == slot_ids[:, None]) & member[None, :]).astype(jnp.float32)
    buffer = jnp.einsum(
        "cp,pkf->ckf",
        onehot,
        lax.all_gather(projectors, ("gx", "gy", "gz"), axis=0, tiled=True),
        precision=lax.Precision.HIGHEST,
    )
    hot_all = (slot_all[None, :] == slot_ids[:, None]) & member[None, :]
    slot_anchor = jnp.sum(jnp.where(hot_all[None, :, :], box_anchor[:, None, :], 0), axis=2)
    slot_extent = jnp.sum(jnp.where(hot_all, box_extent[None, :], 0), axis=1)
    slot_coupling = jnp.sum(jnp.where(hot_all[:, :, None], coupling[None, :, :], 0.0), axis=1)
    cell_offsets = jnp.arange(B, dtype=jnp.int32)
    limit = slot_extent[:, None, None, None]
    inside = (
        (cell_offsets[None, :, None, None] < limit)
        & (cell_offsets[None, None, :, None] < limit)
        & (cell_offsets[None, None, None, :] < limit)
    )
    buffer = buffer * inside.reshape(capacity, 1, B * B * B).astype(jnp.float32)
    return (buffer, slot_anchor, slot_coupling, count)


def nonlocal_term(field, buffer, slot_anchor, slot_coupling, count, domain_start):
    states = field.shape[0]

    def add_slot(slot_index, nonlocal_sum):
        corner = slot_anchor[:, slot_index] - domain_start
        start_cell = (0, corner[0], corner[1], corner[2])
        box_cells = lax.dynamic_slice(field, start_cell, (states, B, B, B)).reshape(
            states, B * B * B
        )
        proj_box = buffer[slot_index]
        coeffs = (
            jnp.dot(box_cells, proj_box.T, precision=lax.Precision.HIGHEST)
            * slot_coupling[slot_index][None, :]
        )
        addition = jnp.dot(coeffs, proj_box, precision=lax.Precision.HIGHEST).reshape(
            states, B, B, B
        )
        current = lax.dynamic_slice(nonlocal_sum, start_cell, (states, B, B, B))
        return lax.dynamic_update_slice(nonlocal_sum, current + addition, start_cell)

    return lax.fori_loop(0, count, add_slot, jnp.zeros_like(field))


def run_filter(field, apply_h):
    half_width = (UPPER - CUTOFF) / 2.0
    middle = (UPPER + CUTOFF) / 2.0
    sigma_one = half_width / (LOW_EDGE - middle)
    sigma_now = sigma_one
    result = (apply_h(field) - middle * field) * (sigma_one / half_width)
    previous = field
    for degree_step in range(1, DEGREE):
        sigma_next = 1.0 / (2.0 / sigma_one - sigma_now)
        next_state = (apply_h(result) - middle * result) * (
            2.0 * sigma_next / half_width
        ) - sigma_now * sigma_next * previous
        previous = result
        result = next_state
        sigma_now = sigma_next
    return result


def domain_body(orbitals, potential, projectors, owner_rank, box_anchor, box_extent, coupling):
    groups_y = lax.axis_size("gy")
    groups_z = lax.axis_size("gz")
    own_x = owner_rank // (groups_y * groups_z)
    own_y = owner_rank // groups_z % groups_y
    own_z = owner_rank % groups_z
    index_x = lax.axis_index("gx")
    index_y = lax.axis_index("gy")
    index_z = lax.axis_index("gz")
    span_x, span_y, span_z = (orbitals.shape[1], orbitals.shape[2], orbitals.shape[3])
    grid_anchor = jnp.stack([own_x * span_x, own_y * span_y, own_z * span_z]) + box_anchor
    member = (own_x == index_x) & (own_y == index_y) & (own_z == index_z)
    buffer, slot_anchor, slot_coupling, count = collect_boxes(
        projectors, member, grid_anchor, box_extent, coupling, 3 * ATOM_DEV
    )
    domain_start = jnp.stack([index_x * span_x, index_y * span_y, index_z * span_z])

    def apply_cube(field):
        padded = extended(field, (("gx", 1), ("gy", 2), ("gz", 3)), 6)
        return (
            -0.5 * laplace_padded(padded, field.shape)
            + potential[None] * field
            + nonlocal_term(field, buffer, slot_anchor, slot_coupling, count, domain_start)
        )

    filtered = run_filter(orbitals, apply_cube)
    flattened = filtered.reshape(filtered.shape[0], -1)
    partial_value = jnp.dot(flattened, flattened.T, precision=lax.Precision.HIGHEST)
    cells_total = span_x * span_y * span_z * lax.axis_size("gx") * groups_y * groups_z
    intersection = lax.psum(partial_value, ("gx", "gy", "gz")) / cells_total
    return (filtered, intersection)


SUB = 8
LANE = 128
HALF = LANE // 2
NPROJ = 4


def split_terms(matrix):
    high = matrix.astype(ml_dtypes.bfloat16)
    low = (matrix - high.astype(np.float64)).astype(ml_dtypes.bfloat16)
    return high, low


def stencil_weight(distance):
    if distance == 0 or abs(distance) > 6:
        return 0.0
    return -0.5 * STENCIL[abs(distance)] / (SPACING * SPACING)


def ring_matrix(length):
    matrix = np.zeros((length, length))
    for offset in range(-6, 7):
        for row in range(length):
            matrix[row, (row + offset) % length] += stencil_weight(offset)
    return matrix


def plane_weights(groups_y):
    slab = groups_y * HALF
    ring = ring_matrix(groups_y * SUB).reshape(groups_y, SUB, groups_y, SUB)
    blocks = []
    for shift in (-SUB, 0, SUB):
        along_x = np.array(
            [[stencil_weight(shift + i - o) for o in range(SUB)] for i in range(SUB)]
        )
        block = np.einsum("ab,io,jp->aijbop", np.eye(groups_y), along_x, np.eye(SUB))
        if shift == 0:
            block = block + np.einsum("ajbp,io->aijbop", ring, np.eye(SUB))
        blocks.append(block.reshape(slab, slab))
    high, low = split_terms(np.concatenate(blocks, axis=0))
    return np.concatenate([high, low], axis=0)


def depth_weights(groups_z):
    high, low = split_terms(ring_matrix(groups_z * LANE))
    return np.concatenate([high, low, high], axis=1)


def split_pair(value):
    high = value.astype(jnp.bfloat16)
    low = (value - high.astype(jnp.float32)).astype(jnp.bfloat16)
    return high, low


def mxu(left, right):
    return jnp.dot(left, right, preferred_element_type=jnp.float32)


def row_sums(values):
    row = lax.broadcasted_iota(jnp.int32, (SUB, LANE), 0)
    for stride in (1, 2, 4):
        keep = (row & stride) == 0
        values = [
            jnp.where(keep, one, two) + pltpu.roll(jnp.where(keep, two, one), stride, 0)
            for one, two in zip(values[0::2], values[1::2])
        ]
    return values[0]


SPARES = 1
TALL = 2 * SUB


def split_store(high_buf, low_buf, rows, cols, value):
    high, low = split_pair(value)
    high_buf[rows, cols] = high
    low_buf[rows, cols] = low


def slab_rows(slab_at, span):
    return pl.ds(pl.multiple_of(slab_at * span, span), span)


def plane_product(groups_x, span, high_buf, low_buf, plane, slabs):
    width = plane.shape[1]

    def around(buf, shift):
        parts = [
            buf[slab_rows(lax.rem(at + shift + groups_x, groups_x), span), :] for at in slabs
        ]
        return jnp.concatenate(parts, axis=0)

    high = [around(high_buf, shift) for shift in (-1, 0, 1)]
    low = [around(low_buf, shift) for shift in (-1, 0, 1)]
    left = jnp.concatenate(high + low + high, axis=1)
    right = jnp.concatenate([plane[: 3 * width], plane[: 3 * width], plane[3 * width :]], axis=0)
    return mxu(left, right)


def depth_product(span, high_buf, low_buf, depth, slab_at):
    high = high_buf[slab_rows(slab_at, span), :]
    low = low_buf[slab_rows(slab_at, span), :]
    return mxu(depth[...], jnp.concatenate([high, high, low], axis=0))


def lay_products(groups, high_buf, low_buf, plane, depth, slabs, near):
    groups_x, groups_y, groups_z = groups
    span = groups_z * LANE
    pairs_slab = groups_y // 2
    total = plane_product(groups_x, span, high_buf, low_buf, plane, slabs)
    for number, slab_at in enumerate(slabs):
        deep = depth_product(span, high_buf, low_buf, depth, slab_at)
        part = total[number * span : (number + 1) * span] + deep
        for tile in range(pairs_slab):
            cols = part[:, tile * LANE : (tile + 1) * LANE]
            near[slab_rows(slab_at * pairs_slab + tile, span), :] = cols


def chunk_of(groups_x):
    return 2 if groups_x % 2 == 0 else 1


def block_rows(groups_z, pair, parity, depth_at):
    return pl.ds(pl.multiple_of(((2 * pair + parity) * groups_z + depth_at) * HALF, HALF), HALF)


def first_kernel(groups, *refs):
    raw, plane, depth, field, near, high_buf, low_buf = refs
    groups_x, groups_y, groups_z = groups
    span = groups_z * LANE
    pairs_slab = groups_y // 2

    def lay_field(slab_at, carry):
        for tile in range(pairs_slab):
            pair = slab_at * pairs_slab + tile
            cols = slice(tile * LANE, (tile + 1) * LANE)
            for depth_at in range(groups_z):
                first = raw[block_rows(groups_z, pair, 0, depth_at), :]
                second = raw[block_rows(groups_z, pair, 1, depth_at), :]
                turned = jnp.concatenate([first, second], axis=0).T
                at = pl.multiple_of(pair * span + depth_at * LANE, LANE)
                field[pl.ds(at, LANE), :] = turned
                at = pl.multiple_of(slab_at * span + depth_at * LANE, LANE)
                split_store(high_buf, low_buf, pl.ds(at, LANE), cols, turned)
        return carry

    lax.fori_loop(0, groups_x, lay_field, 0)
    chunk = chunk_of(groups_x)

    def product(chunk_at, carry):
        slabs = [chunk_at * chunk + number for number in range(chunk)]
        lay_products(groups, high_buf, low_buf, plane, depth, slabs, near)
        return carry

    lax.fori_loop(0, groups_x // chunk, product, 0)


def hops_apart(count):
    near = sorted({0, 1 % count, count - 1})
    return near, [hop for hop in range(count) if hop not in near]


def filter_kernel(groups, atoms, place, half, my_place, *refs):
    groups_x, groups_y, groups_z = groups
    pieces = groups_y * groups_z
    field_a, near_a = refs[:2]
    kinds = hops_apart(groups_x)
    arrays = pieces * sum(1 for hops_of in kinds if hops_of)
    packs_in = refs[2 : 2 + arrays]
    plane, depth, out = refs[2 + arrays : 5 + arrays]
    field_b, field_c, local, coeffs, high_buf, low_buf, near = refs[5 + arrays : 12 + arrays]
    spares = refs[12 + arrays :]
    targets = (near,) + tuple(spares)
    columns = groups_x * groups_y
    domains = columns * groups_z
    pairs = columns // 2
    span = groups_z * LANE
    pairs_slab = groups_y // 2
    per_device = atoms // domains // SUB
    chunk = chunk_of(groups_x)
    half_width = (UPPER - CUTOFF) / 2.0
    middle = (UPPER + CUTOFF) / 2.0
    diagonal = -0.5 * 3.0 * STENCIL[0] / (SPACING * SPACING) - middle
    lane = lax.broadcasted_iota(jnp.int32, (SUB, LANE), 1)
    lower = lane < HALF
    side = lane // HALF
    f32 = jnp.float32

    for target in targets:
        target[...] = jnp.zeros(target.shape, f32)

    def sources(kind, index):
        hop_x = index + 2 if kind else jnp.where(index < 2, index, groups_x - 1)
        for hop_z in range(groups_z):
            for hop_y in range(groups_y):
                from_x = lax.rem(my_place[0] + (groups_x - hop_x), groups_x)
                from_y = lax.rem(my_place[1] + (groups_y - hop_y), groups_y)
                from_z = lax.rem(my_place[2] + (groups_z - hop_z), groups_z)
                piece = packs_in[kind * pieces + hop_z * groups_y + hop_y]
                yield piece, from_x * groups_y + from_y, from_z

    def each_hop(visit):
        for kind, hops_of in enumerate(kinds):
            if hops_of:

                def step(index, carry, kind=kind):
                    visit(kind, index)
                    return carry

                lax.fori_loop(0, len(hops_of), step, 0)

    def lay_potential(kind, hop_x):
        for piece, column, depth_at in sources(kind, hop_x):
            mine = side == column % 2
            for tile in range(SUB):
                value = diagonal + piece[hop_x, tile]
                other = pltpu.roll(value, HALF, 1)
                for upper in range(2):
                    at = column // 2 * span + depth_at * LANE + upper * HALF + tile * SUB
                    rows = pl.ds(pl.multiple_of(at, SUB), SUB)
                    chosen = jnp.where(side == upper, value, other)
                    local[rows, :] = jnp.where(mine, chosen, local[rows, :])

    each_hop(lay_potential)

    ones = (
        (
            lax.broadcasted_iota(jnp.int32, (LANE, LANE), 0) // HALF
            == lax.broadcasted_iota(jnp.int32, (LANE, LANE), 1) // HALF
        )
        .astype(f32)
        .astype(jnp.bfloat16)
    )

    blocks = [(kind, index) for kind, hops_of in enumerate(kinds) for index in range(len(hops_of))]

    def hop_groups(kind, index):
        block = index + kind * len(kinds[0])
        for at, (piece, column, depth_at) in enumerate(sources(kind, index)):
            for inner in range(per_device):
                stored = (block * pieces + at) * per_device + inner
                atoms_at = ((column * groups_z + depth_at) * per_device + inner) * SUB
                yield piece, index, inner, stored, atoms_at

    def apply_step(cur, prev, new, alpha, beta, first, last):
        def project(part):
            if not first:
                slabs = [part * chunk + number for number in range(chunk)]
                lay_products(groups, high_buf, low_buf, plane, depth, slabs, near)
            sums = []
            held = [
                group
                for kind, index in blocks[part * chunk : (part + 1) * chunk]
                for group in hop_groups(kind, index)
            ]
            for piece, hop_x, inner, stored, atoms_at in held:
                terms = ([], [])
                for j in range(SUB):
                    atom = atoms_at + j
                    value = cur[pl.ds(place[atom], SUB), :]
                    both = jnp.where(side == half[atom], value, pltpu.roll(value, HALF, 1))
                    for kp in range(2):
                        at = SUB + (inner * 2 + kp) * SUB + j
                        terms[kp].append(both * piece[hop_x, at])
                sums += [row_sums(terms[0]), row_sums(terms[1])]
            high, low = split_pair(jnp.concatenate(sums, axis=0))
            rows = len(sums) * SUB
            coeffs[part * rows : (part + 1) * rows, :] = mxu(high, ones) + mxu(low, ones)

        for part in range(groups_x // chunk):
            project(part)

        def scatter(kind, index):
            for piece, hop_x, inner, stored, atoms_at in hop_groups(kind, index):
                weights = [
                    coeffs[pl.ds(pl.multiple_of((stored * 2 + kp) * SUB, SUB), SUB), :]
                    for kp in range(2)
                ]
                for j in range(SUB):
                    atom = atoms_at + j
                    parts = [
                        jnp.broadcast_to(weights[kp][j : j + 1], (SUB, LANE))
                        * piece[hop_x, SUB + (inner * 2 + kp) * SUB + j]
                        for kp in range(2)
                    ]
                    value = parts[0] + parts[1]
                    value = value + pltpu.roll(value, HALF, 1)
                    value = jnp.where(side == half[atom], value, 0.0)
                    rows = pl.ds(place[atom], SUB)
                    target = targets[j % len(targets)]
                    target[rows, :] = target[rows, :] + value

        each_hop(scatter)

        def combine(slab_at, carry):
            for tile in range(pairs_slab):
                pair = slab_at * pairs_slab + tile
                cols = slice(tile * LANE, (tile + 1) * LANE)
                for at_row in range(0, span, TALL):
                    rows = pl.ds(pl.multiple_of(pair * span + at_row, TALL), TALL)
                    slab_at_row = pl.ds(pl.multiple_of(slab_at * span + at_row, TALL), TALL)
                    total = local[rows, :] * cur[rows, :]
                    if first:
                        total = total + near_a[rows, :]
                    for target in targets:
                        total = total + target[rows, :]
                    if not last:
                        for target in targets[1:]:
                            target[rows, :] = jnp.zeros((TALL, LANE), f32)
                    total = total * alpha
                    if beta is not None:
                        total = total + beta * prev[rows, :]
                    new[rows, :] = total
                    if not last:
                        split_store(high_buf, low_buf, slab_at_row, cols, total)
                if last:
                    for depth_at in range(groups_z):
                        at = pl.multiple_of(pair * span + depth_at * LANE, LANE)
                        turned = new[pl.ds(at, LANE), :].T
                        out[block_rows(groups_z, pair, 0, depth_at), :] = turned[:HALF]
                        out[block_rows(groups_z, pair, 1, depth_at), :] = turned[HALF:]
            return carry

        lax.fori_loop(0, groups_x, combine, 0)

    sigma_one = half_width / (LOW_EDGE - middle)
    sigma_now = sigma_one
    apply_step(field_a, None, field_b, sigma_one / half_width, None, True, DEGREE == 1)
    prev, cur, new = field_a, field_b, field_c
    for degree_step in range(1, DEGREE):
        sigma_next = 1.0 / (2.0 / sigma_one - sigma_now)
        last = degree_step == DEGREE - 1
        target = prev if degree_step > 1 else new
        apply_step(
            cur,
            prev,
            target,
            2.0 * sigma_next / half_width,
            -sigma_now * sigma_next,
            False,
            last,
        )
        prev, cur = cur, target
        sigma_now = sigma_next


def pack_kernel(my_first, extent, coupling, potential, projectors, out):
    atoms = projectors.shape[0]
    f32, bf16 = jnp.float32, jnp.bfloat16
    lane = lax.broadcasted_iota(jnp.int32, (SUB, LANE), 1)
    row = lax.broadcasted_iota(jnp.int32, (SUB, LANE), 0)
    lower = lane < HALF

    flat = potential[...].reshape(HALF, LANE)
    turned = jnp.concatenate([flat, flat], axis=0).T
    low = lax.broadcasted_iota(jnp.int32, (HALF, LANE), 1) < HALF
    out[:SUB] = jnp.where(low, turned[:HALF], turned[HALF:]).reshape(SUB, SUB, LANE)

    cells = projectors.shape[2]
    own_row = lax.broadcasted_iota(jnp.int32, (SUB, cells), 1) % B
    own_row = own_row == lax.broadcasted_iota(jnp.int32, (SUB, cells), 0)
    sides = []
    for kh in range(2):
        parts = []
        for kp in range(2):
            for atom in range(atoms):
                line = projectors[atom, 2 * kp + kh : 2 * kp + kh + 1, :]
                parts.append(jnp.where(own_row, jnp.broadcast_to(line, (SUB, cells)), 0.0))
        sides.append(jnp.concatenate(parts, axis=0))
    value = jnp.concatenate(sides, axis=1)
    source = lax.broadcasted_iota(jnp.int32, (2 * cells, LANE), 0) // B
    hot = source == lax.broadcasted_iota(jnp.int32, (2 * cells, LANE), 1)
    hot = hot.astype(f32).astype(bf16)
    high = value.astype(bf16)
    rest = value - high.astype(f32)
    mid = rest.astype(bf16)
    small = (rest - mid.astype(f32)).astype(bf16)
    moved = (mxu(high, hot) + mxu(mid, hot)) + mxu(small, hot)

    reach = jnp.maximum(jnp.maximum((lane >> 3) & (B - 1), lane & (B - 1)), row)
    for kp in range(2):
        for atom in range(atoms):
            at = my_first[0] + atom
            scale = jnp.sqrt(
                jnp.where(lower, coupling[2 * kp, at], coupling[2 * kp + 1, at])
            )
            number = kp * atoms + atom
            part = moved[number * SUB : (number + 1) * SUB]
            group, j = atom // SUB, atom % SUB
            out[SUB + (group * 2 + kp) * SUB + j] = jnp.where(
                reach < extent[at], part * scale, 0.0
            )


def packed_inputs(my_first, extent, coupling, potential, projectors, interpret=False):
    vmem = pl.BlockSpec(memory_space=pltpu.VMEM)
    smem = pl.BlockSpec(memory_space=pltpu.SMEM)
    atoms = projectors.shape[0]
    return pl.pallas_call(
        pack_kernel,
        out_shape=jax.ShapeDtypeStruct((SUB + 2 * atoms, SUB, LANE), jnp.float32),
        in_specs=[smem] * 3 + [vmem] * 2,
        out_specs=vmem,
        compiler_params=pltpu.CompilerParams(vmem_limit_bytes=8 * 1024 * 1024),
        interpret=interpret,
    )(my_first, extent, coupling.T, potential, projectors)


def weights_kernel(plane_in, depth_in, plane, depth, sems):
    loads = [
        pltpu.make_async_copy(plane_in, plane, sems.at[0]),
        pltpu.make_async_copy(depth_in, depth, sems.at[1]),
    ]
    for load in loads:
        load.start()
    for load in loads:
        load.wait()


def weights_call(groups, interpret=False):
    plane = jnp.asarray(plane_weights(groups[1]))
    depth = jnp.asarray(depth_weights(groups[2]))
    return pl.pallas_call(
        weights_kernel,
        out_shape=[jax.ShapeDtypeStruct(part.shape, part.dtype) for part in (plane, depth)],
        in_specs=[pl.BlockSpec(memory_space=pl.ANY)] * 2,
        out_specs=[pl.BlockSpec(memory_space=pltpu.VMEM)] * 2,
        scratch_shapes=[pltpu.SemaphoreType.DMA((2,))],
        compiler_params=pltpu.CompilerParams(vmem_limit_bytes=4 * 1024 * 1024),
        interpret=interpret,
    )(plane, depth)


def box_places(groups, owner, anchor):
    groups_z = groups[2]
    column = owner // groups_z
    place = (column // 2 * groups_z + owner % groups_z) * LANE + anchor
    return place, column % 2


def first_call(groups, field, plane, depth, interpret=False):
    groups_x, groups_y, groups_z = groups
    span = groups_z * LANE
    cells = (groups_x * groups_y // 2 * span, LANE)
    slabs = (groups_x * span, groups_y * HALF)
    vmem = pl.BlockSpec(memory_space=pltpu.VMEM)
    work = 2 * slabs[0] * slabs[1] * (9 * slabs[1] + 3 * span)
    return pl.pallas_call(
        functools.partial(first_kernel, groups),
        out_shape=[
            jax.ShapeDtypeStruct(cells, jnp.float32),
            jax.ShapeDtypeStruct(cells, jnp.float32),
        ],
        in_specs=[vmem] * 3,
        out_specs=[vmem] * 2,
        scratch_shapes=[
            pltpu.VMEM(slabs, jnp.bfloat16),
            pltpu.VMEM(slabs, jnp.bfloat16),
        ],
        compiler_params=pltpu.CompilerParams(vmem_limit_bytes=12 * 1024 * 1024),
        cost_estimate=pl.CostEstimate(
            flops=work, bytes_accessed=4 * field.size * 4, transcendentals=0
        ),
        interpret=interpret,
    )(field.reshape(cells), plane, depth)


def filter_call(
    groups, place, half, my_place, field, near, packs, plane, depth, interpret=False
):
    groups_x, groups_y, groups_z = groups
    columns = groups_x * groups_y
    atoms = place.shape[0]
    vmem = pl.BlockSpec(memory_space=pltpu.VMEM)
    smem = pl.BlockSpec(memory_space=pltpu.SMEM)
    slabs = (groups_x * groups_z * LANE, groups_y * HALF)
    work = 2 * slabs[0] * slabs[1] * (9 * slabs[1] + 3 * groups_z * LANE)
    out = pl.pallas_call(
        functools.partial(filter_kernel, groups, atoms),
        out_shape=jax.ShapeDtypeStruct(field.shape, jnp.float32),
        in_specs=[smem] * 3 + [vmem] * (len(packs) + 4),
        out_specs=vmem,
        scratch_shapes=[
            pltpu.VMEM(field.shape, jnp.float32),
            pltpu.VMEM(field.shape, jnp.float32),
            pltpu.VMEM(field.shape, jnp.float32),
            pltpu.VMEM((atoms * 2, LANE), jnp.float32),
            pltpu.VMEM(slabs, jnp.bfloat16),
            pltpu.VMEM(slabs, jnp.bfloat16),
        ]
        + [pltpu.VMEM(field.shape, jnp.float32) for _ in range(1 + SPARES)],
        compiler_params=pltpu.CompilerParams(vmem_limit_bytes=22 * 1024 * 1024),
        cost_estimate=pl.CostEstimate(
            flops=3 * work, bytes_accessed=8 * field.size * 4, transcendentals=0
        ),
        interpret=interpret,
    )(place, half, my_place, field, near, *packs, plane, depth)
    return out.reshape(columns * groups_z, SUB, SUB, LANE)


def moved(value, axis, hop):
    count = lax.axis_size(axis)
    if hop == 0:
        return value
    return lax.ppermute(value, axis, [(i, (i + hop) % count) for i in range(count)])


def hops(value, axis):
    return [moved(value, axis, hop) for hop in range(lax.axis_size(axis))]


def state_body(orbitals, potential, projectors, owner_rank, box_anchor, box_extent, coupling):
    axes = ("gx", "gy", "gz")
    groups = tuple(lax.axis_size(axis) for axis in axes)
    groups_z = groups[2]
    domains = groups[0] * groups[1] * groups_z
    atoms_own = projectors.shape[0]
    my_place = jnp.stack([lax.axis_index(axis) for axis in axes])
    me = (my_place[0] * groups[1] + my_place[1]) * groups_z + my_place[2]
    pack = packed_inputs((me * atoms_own)[None], box_extent, coupling, potential, projectors)
    near_hops, far_hops = hops_apart(groups[0])
    near_line = jnp.stack([moved(pack, "gx", hop) for hop in near_hops])
    place, half = box_places(groups, owner_rank, box_anchor[2])
    plane, depth = weights_call(groups)
    orbitals, near_line, place, half, plane, depth = lax.optimization_barrier(
        (orbitals, near_line, place, half, plane, depth)
    )
    lines = [near_line]
    if far_hops:
        lines.append(jnp.stack([moved(pack, "gx", hop) for hop in far_hops]))
    packs = []
    for line in lines:
        crossed = [hops(piece, "gz") for piece in hops(line, "gy")]
        packs += [crossed[hop_y][hop_z] for hop_z in range(groups_z) for hop_y in range(groups[1])]
    field = lax.all_to_all(orbitals, axes, split_axis=0, concat_axis=0, tiled=True)
    field, near = first_call(groups, field, plane, depth)
    result = filter_call(groups, place, half, my_place, field, near, packs, plane, depth)
    filtered = lax.all_to_all(result, axes, split_axis=0, concat_axis=0, tiled=True)
    states = filtered.shape[0]
    flattened = filtered.reshape(states, -1)
    partial_value = jnp.dot(flattened, flattened.T, precision=lax.Precision.HIGHEST)
    quarter = partial_value.reshape(-1, SUB, states).transpose(1, 0, 2).reshape(SUB, -1)
    parts = lax.all_to_all(
        jnp.broadcast_to(quarter[None], (domains,) + quarter.shape),
        axes,
        split_axis=0,
        concat_axis=0,
        tiled=True,
    )
    summed = jnp.sum(parts, axis=0).reshape(SUB, -1, states).transpose(1, 0, 2)
    cells_total = orbitals.shape[1] * orbitals.shape[2] * orbitals.shape[3] * domains
    intersection = summed.reshape(states, states) / cells_total
    return (filtered, intersection)


def body(orbitals, potential, projectors, owner_rank, box_anchor, box_extent, coupling):
    domains = lax.axis_size("gx") * lax.axis_size("gy") * lax.axis_size("gz")
    whole_states = (
        orbitals.shape == (domains, SUB, SUB, LANE)
        and projectors.shape[0] % SUB == 0
        and projectors.shape[1] == NPROJ
        and lax.axis_size("gy") % 2 == 0
    )
    chosen = state_body if whole_states else domain_body
    return chosen(
        orbitals, potential, projectors, owner_rank, box_anchor, box_extent, coupling
    )


def solution(mesh):
    return jax.shard_map(
        body,
        mesh=mesh,
        in_specs=(
            P(None, "gx", "gy", "gz"),
            P("gx", "gy", "gz"),
            P(("gx", "gy", "gz"), None, None),
            P(),
            P(),
            P(),
            P(),
        ),
        out_specs=(P(None, "gx", "gy", "gz"), P()),
        check_vma=False,
    )
```

```python
import functools
import math
import jax
import jax.numpy as jnp
from jax import lax
from jax.experimental import pallas as pl
from jax.experimental.pallas import tpu as pltpu
import ml_dtypes
import numpy as np
from jax.sharding import PartitionSpec as P

B = 8
DEGREE = 4
ATOM_DEV = 8


STENCIL = (
    -5369.0 / 1800.0,
    12.0 / 7.0,
    -15.0 / 56.0,
    10.0 / 189.0,
    -1.0 / 112.0,
    2.0 / 1925.0,
    -1.0 / 16632.0,
)
SPACING = 0.5
LOW_EDGE = -2.5
CUTOFF = 4.0
UPPER = 60.0


def extended(cells, sides, width):
    for axis, dim in sides:
        count = lax.axis_size(axis)
        head = lax.slice_in_dim(cells, 0, width, axis=dim)
        tail = lax.slice_in_dim(cells, cells.shape[dim] - width, cells.shape[dim], axis=dim)
        cells = jnp.concatenate(
            [
                lax.ppermute(tail, axis, [(i, (i + 1) % count) for i in range(count)]),
                cells,
                lax.ppermute(head, axis, [((i + 1) % count, i) for i in range(count)]),
            ],
            axis=dim,
        )
    return cells


def laplace_padded(padded, shape):
    span_x, span_y, span_z = (shape[1], shape[2], shape[3])
    summed = 3.0 * STENCIL[0] * padded[:, 6 : 6 + span_x, 6 : 6 + span_y, 6 : 6 + span_z]
    for offset in range(1, 7):
        weight = STENCIL[offset]
        summed = summed + weight * (
            padded[:, 6 + offset : 6 + offset + span_x, 6 : 6 + span_y, 6 : 6 + span_z]
            + padded[:, 6 - offset : 6 - offset + span_x, 6 : 6 + span_y, 6 : 6 + span_z]
        )
        summed = summed + weight * (
            padded[:, 6 : 6 + span_x, 6 + offset : 6 + offset + span_y, 6 : 6 + span_z]
            + padded[:, 6 : 6 + span_x, 6 - offset : 6 - offset + span_y, 6 : 6 + span_z]
        )
        summed = summed + weight * (
            padded[:, 6 : 6 + span_x, 6 : 6 + span_y, 6 + offset : 6 + offset + span_z]
            + padded[:, 6 : 6 + span_x, 6 : 6 + span_y, 6 - offset : 6 - offset + span_z]
        )
    return summed / (SPACING * SPACING)


def collect_boxes(projectors, member, box_anchor, box_extent, coupling, capacity):
    member_int = member.astype(jnp.int32)
    slot_all = jnp.cumsum(member_int) - 1
    count = jnp.sum(member_int)
    slot_ids = jnp.arange(capacity, dtype=jnp.int32)
    onehot = ((slot_all[None, :] == slot_ids[:, None]) & member[None, :]).astype(jnp.float32)
    buffer = jnp.einsum(
        "cp,pkf->ckf",
        onehot,
        lax.all_gather(projectors, ("gx", "gy", "gz"), axis=0, tiled=True),
        precision=lax.Precision.HIGHEST,
    )
    hot_all = (slot_all[None, :] == slot_ids[:, None]) & member[None, :]
    slot_anchor = jnp.sum(jnp.where(hot_all[None, :, :], box_anchor[:, None, :], 0), axis=2)
    slot_extent = jnp.sum(jnp.where(hot_all, box_extent[None, :], 0), axis=1)
    slot_coupling = jnp.sum(jnp.where(hot_all[:, :, None], coupling[None, :, :], 0.0), axis=1)
    cell_offsets = jnp.arange(B, dtype=jnp.int32)
    limit = slot_extent[:, None, None, None]
    inside = (
        (cell_offsets[None, :, None, None] < limit)
        & (cell_offsets[None, None, :, None] < limit)
        & (cell_offsets[None, None, None, :] < limit)
    )
    buffer = buffer * inside.reshape(capacity, 1, B * B * B).astype(jnp.float32)
    return (buffer, slot_anchor, slot_coupling, count)


def nonlocal_term(field, buffer, slot_anchor, slot_coupling, count, domain_start):
    states = field.shape[0]

    def add_slot(slot_index, nonlocal_sum):
        corner = slot_anchor[:, slot_index] - domain_start
        start_cell = (0, corner[0], corner[1], corner[2])
        box_cells = lax.dynamic_slice(field, start_cell, (states, B, B, B)).reshape(
            states, B * B * B
        )
        proj_box = buffer[slot_index]
        coeffs = (
            jnp.dot(box_cells, proj_box.T, precision=lax.Precision.HIGHEST)
            * slot_coupling[slot_index][None, :]
        )
        addition = jnp.dot(coeffs, proj_box, precision=lax.Precision.HIGHEST).reshape(
            states, B, B, B
        )
        current = lax.dynamic_slice(nonlocal_sum, start_cell, (states, B, B, B))
        return lax.dynamic_update_slice(nonlocal_sum, current + addition, start_cell)

    return lax.fori_loop(0, count, add_slot, jnp.zeros_like(field))


def run_filter(field, apply_h):
    half_width = (UPPER - CUTOFF) / 2.0
    middle = (UPPER + CUTOFF) / 2.0
    sigma_one = half_width / (LOW_EDGE - middle)
    sigma_now = sigma_one
    result = (apply_h(field) - middle * field) * (sigma_one / half_width)
    previous = field
    for degree_step in range(1, DEGREE):
        sigma_next = 1.0 / (2.0 / sigma_one - sigma_now)
        next_state = (apply_h(result) - middle * result) * (
            2.0 * sigma_next / half_width
        ) - sigma_now * sigma_next * previous
        previous = result
        result = next_state
        sigma_now = sigma_next
    return result


def domain_body(orbitals, potential, projectors, owner_rank, box_anchor, box_extent, coupling):
    groups_y = lax.axis_size("gy")
    groups_z = lax.axis_size("gz")
    own_x = owner_rank // (groups_y * groups_z)
    own_y = owner_rank // groups_z % groups_y
    own_z = owner_rank % groups_z
    index_x = lax.axis_index("gx")
    index_y = lax.axis_index("gy")
    index_z = lax.axis_index("gz")
    span_x, span_y, span_z = (orbitals.shape[1], orbitals.shape[2], orbitals.shape[3])
    grid_anchor = jnp.stack([own_x * span_x, own_y * span_y, own_z * span_z]) + box_anchor
    member = (own_x == index_x) & (own_y == index_y) & (own_z == index_z)
    buffer, slot_anchor, slot_coupling, count = collect_boxes(
        projectors, member, grid_anchor, box_extent, coupling, 3 * ATOM_DEV
    )
    domain_start = jnp.stack([index_x * span_x, index_y * span_y, index_z * span_z])

    def apply_cube(field):
        padded = extended(field, (("gx", 1), ("gy", 2), ("gz", 3)), 6)
        return (
            -0.5 * laplace_padded(padded, field.shape)
            + potential[None] * field
            + nonlocal_term(field, buffer, slot_anchor, slot_coupling, count, domain_start)
        )

    filtered = run_filter(orbitals, apply_cube)
    flattened = filtered.reshape(filtered.shape[0], -1)
    partial_value = jnp.dot(flattened, flattened.T, precision=lax.Precision.HIGHEST)
    cells_total = span_x * span_y * span_z * lax.axis_size("gx") * groups_y * groups_z
    intersection = lax.psum(partial_value, ("gx", "gy", "gz")) / cells_total
    return (filtered, intersection)


SUB = 8
LANE = 128
HALF = LANE // 2
NPROJ = 4


def split_terms(matrix):
    high = matrix.astype(ml_dtypes.bfloat16)
    low = (matrix - high.astype(np.float64)).astype(ml_dtypes.bfloat16)
    return high, low


def stencil_weight(distance):
    if distance == 0 or abs(distance) > 6:
        return 0.0
    return -0.5 * STENCIL[abs(distance)] / (SPACING * SPACING)


def ring_matrix(length):
    matrix = np.zeros((length, length))
    for offset in range(-6, 7):
        for row in range(length):
            matrix[row, (row + offset) % length] += stencil_weight(offset)
    return matrix


def plane_weights(groups_y):
    slab = groups_y * HALF
    ring = ring_matrix(groups_y * SUB).reshape(groups_y, SUB, groups_y, SUB)
    blocks = []
    for shift in (-SUB, 0, SUB):
        along_x = np.array(
            [[stencil_weight(shift + i - o) for o in range(SUB)] for i in range(SUB)]
        )
        block = np.einsum("ab,io,jp->aijbop", np.eye(groups_y), along_x, np.eye(SUB))
        if shift == 0:
            block = block + np.einsum("ajbp,io->aijbop", ring, np.eye(SUB))
        blocks.append(block.reshape(slab, slab))
    high, low = split_terms(np.concatenate(blocks, axis=0))
    return np.concatenate([high, low], axis=0)


def depth_weights(groups_z):
    high, low = split_terms(ring_matrix(groups_z * LANE))
    return np.concatenate([high, low, high], axis=1)


def split_pair(value):
    high = value.astype(jnp.bfloat16)
    low = (value - high.astype(jnp.float32)).astype(jnp.bfloat16)
    return high, low


def mxu(left, right):
    return jnp.dot(left, right, preferred_element_type=jnp.float32)


def row_sums(values):
    row = lax.broadcasted_iota(jnp.int32, (SUB, LANE), 0)
    for stride in (1, 2, 4):
        keep = (row & stride) == 0
        values = [
            jnp.where(keep, one, two) + pltpu.roll(jnp.where(keep, two, one), stride, 0)
            for one, two in zip(values[0::2], values[1::2])
        ]
    return values[0]


SPARES = 1
TALL = 2 * SUB


def split_store(high_buf, low_buf, rows, cols, value):
    high, low = split_pair(value)
    high_buf[rows, cols] = high
    low_buf[rows, cols] = low


def slab_rows(slab_at, span):
    return pl.ds(pl.multiple_of(slab_at * span, span), span)


def plane_product(groups_x, span, high_buf, low_buf, plane, slabs):
    width = plane.shape[1]

    def around(buf, shift):
        parts = [
            buf[slab_rows(lax.rem(at + shift + groups_x, groups_x), span), :] for at in slabs
        ]
        return jnp.concatenate(parts, axis=0)

    high = [around(high_buf, shift) for shift in (-1, 0, 1)]
    low = [around(low_buf, shift) for shift in (-1, 0, 1)]
    left = jnp.concatenate(high + low + high, axis=1)
    right = jnp.concatenate([plane[: 3 * width], plane[: 3 * width], plane[3 * width :]], axis=0)
    return mxu(left, right)


def depth_product(span, high_buf, low_buf, depth, slab_at):
    high = high_buf[slab_rows(slab_at, span), :]
    low = low_buf[slab_rows(slab_at, span), :]
    return mxu(depth[...], jnp.concatenate([high, high, low], axis=0))


def lay_products(groups, high_buf, low_buf, plane, depth, slabs, near):
    groups_x, groups_y, groups_z = groups
    span = groups_z * LANE
    pairs_slab = groups_y // 2
    total = plane_product(groups_x, span, high_buf, low_buf, plane, slabs)
    for number, slab_at in enumerate(slabs):
        deep = depth_product(span, high_buf, low_buf, depth, slab_at)
        part = total[number * span : (number + 1) * span] + deep
        for tile in range(pairs_slab):
            cols = part[:, tile * LANE : (tile + 1) * LANE]
            near[slab_rows(slab_at * pairs_slab + tile, span), :] = cols


def chunk_of(groups_x):
    return 2 if groups_x % 2 == 0 else 1


def block_rows(groups_z, pair, parity, depth_at):
    return pl.ds(pl.multiple_of(((2 * pair + parity) * groups_z + depth_at) * HALF, HALF), HALF)


def first_kernel(groups, *refs):
    raw, plane, depth, field, near, high_buf, low_buf = refs
    groups_x, groups_y, groups_z = groups
    span = groups_z * LANE
    pairs_slab = groups_y // 2

    def lay_field(slab_at, carry):
        for tile in range(pairs_slab):
            pair = slab_at * pairs_slab + tile
            cols = slice(tile * LANE, (tile + 1) * LANE)
            for depth_at in range(groups_z):
                first = raw[block_rows(groups_z, pair, 0, depth_at), :]
                second = raw[block_rows(groups_z, pair, 1, depth_at), :]
                turned = jnp.concatenate([first, second], axis=0).T
                at = pl.multiple_of(pair * span + depth_at * LANE, LANE)
                field[pl.ds(at, LANE), :] = turned
                at = pl.multiple_of(slab_at * span + depth_at * LANE, LANE)
                split_store(high_buf, low_buf, pl.ds(at, LANE), cols, turned)
        return carry

    lax.fori_loop(0, groups_x, lay_field, 0)
    chunk = chunk_of(groups_x)

    def product(chunk_at, carry):
        slabs = [chunk_at * chunk + number for number in range(chunk)]
        lay_products(groups, high_buf, low_buf, plane, depth, slabs, near)
        return carry

    lax.fori_loop(0, groups_x // chunk, product, 0)


def filter_kernel(groups, atoms, place, half, my_place, *refs):
    groups_x, groups_y, groups_z = groups
    pieces = groups_y * groups_z
    field_a, near_a = refs[:2]
    packs_in = refs[2 : 2 + pieces]
    plane, depth, out = refs[2 + pieces : 5 + pieces]
    field_b, field_c, local, coeffs, high_buf, low_buf, near = refs[5 + pieces : 12 + pieces]
    spares = refs[12 + pieces :]
    targets = (near,) + tuple(spares)
    columns = groups_x * groups_y
    domains = columns * groups_z
    pairs = columns // 2
    span = groups_z * LANE
    pairs_slab = groups_y // 2
    per_device = atoms // domains // SUB
    chunk = chunk_of(groups_x)
    half_width = (UPPER - CUTOFF) / 2.0
    middle = (UPPER + CUTOFF) / 2.0
    diagonal = -0.5 * 3.0 * STENCIL[0] / (SPACING * SPACING) - middle
    lane = lax.broadcasted_iota(jnp.int32, (SUB, LANE), 1)
    lower = lane < HALF
    side = lane // HALF
    f32 = jnp.float32

    for target in targets:
        target[...] = jnp.zeros(target.shape, f32)

    def sources(hop_x):
        for hop_z in range(groups_z):
            for hop_y in range(groups_y):
                from_x = lax.rem(my_place[0] + (groups_x - hop_x), groups_x)
                from_y = lax.rem(my_place[1] + (groups_y - hop_y), groups_y)
                from_z = lax.rem(my_place[2] + (groups_z - hop_z), groups_z)
                yield packs_in[hop_z * groups_y + hop_y], from_x * groups_y + from_y, from_z

    def lay_potential(hop_x, carry):
        for piece, column, depth_at in sources(hop_x):
            mine = side == column % 2
            for tile in range(SUB):
                value = diagonal + piece[hop_x, tile]
                other = pltpu.roll(value, HALF, 1)
                for upper in range(2):
                    at = column // 2 * span + depth_at * LANE + upper * HALF + tile * SUB
                    rows = pl.ds(pl.multiple_of(at, SUB), SUB)
                    chosen = jnp.where(side == upper, value, other)
                    local[rows, :] = jnp.where(mine, chosen, local[rows, :])
        return carry

    lax.fori_loop(0, groups_x, lay_potential, 0)

    ones = (
        (
            lax.broadcasted_iota(jnp.int32, (LANE, LANE), 0) // HALF
            == lax.broadcasted_iota(jnp.int32, (LANE, LANE), 1) // HALF
        )
        .astype(f32)
        .astype(jnp.bfloat16)
    )

    def part_groups(part, share):
        for number in range(share):
            hop_x = part * share + number
            for at, (piece, column, depth_at) in enumerate(sources(hop_x)):
                for inner in range(per_device):
                    stored = (hop_x * pieces + at) * per_device + inner
                    atoms_at = ((column * groups_z + depth_at) * per_device + inner) * SUB
                    yield piece, hop_x, inner, stored, atoms_at

    def apply_step(cur, prev, new, alpha, beta, first, last):
        def project(part, carry):
            if not first:
                slabs = [part * chunk + number for number in range(chunk)]
                lay_products(groups, high_buf, low_buf, plane, depth, slabs, near)
            sums = []
            for piece, hop_x, inner, stored, atoms_at in part_groups(part, chunk):
                terms = ([], [])
                for j in range(SUB):
                    atom = atoms_at + j
                    value = cur[pl.ds(place[atom], SUB), :]
                    both = jnp.where(side == half[atom], value, pltpu.roll(value, HALF, 1))
                    for kp in range(2):
                        at = SUB + (inner * 2 + kp) * SUB + j
                        terms[kp].append(both * piece[hop_x, at])
                sums += [row_sums(terms[0]), row_sums(terms[1])]
            high, low = split_pair(jnp.concatenate(sums, axis=0))
            rows = len(sums) * SUB
            at = pl.multiple_of(part * rows, rows)
            coeffs[pl.ds(at, rows), :] = mxu(high, ones) + mxu(low, ones)
            return carry

        lax.fori_loop(0, groups_x // chunk, project, 0)

        def scatter(part, carry):
            for piece, hop_x, inner, stored, atoms_at in part_groups(part, chunk):
                weights = [
                    coeffs[pl.ds(pl.multiple_of((stored * 2 + kp) * SUB, SUB), SUB), :]
                    for kp in range(2)
                ]
                for j in range(SUB):
                    atom = atoms_at + j
                    parts = [
                        jnp.broadcast_to(weights[kp][j : j + 1], (SUB, LANE))
                        * piece[hop_x, SUB + (inner * 2 + kp) * SUB + j]
                        for kp in range(2)
                    ]
                    value = parts[0] + parts[1]
                    value = value + pltpu.roll(value, HALF, 1)
                    value = jnp.where(side == half[atom], value, 0.0)
                    rows = pl.ds(place[atom], SUB)
                    target = targets[j % len(targets)]
                    target[rows, :] = target[rows, :] + value
            return carry

        lax.fori_loop(0, groups_x // chunk, scatter, 0)

        def combine(slab_at, carry):
            for tile in range(pairs_slab):
                pair = slab_at * pairs_slab + tile
                cols = slice(tile * LANE, (tile + 1) * LANE)
                for at_row in range(0, span, TALL):
                    rows = pl.ds(pl.multiple_of(pair * span + at_row, TALL), TALL)
                    slab_at_row = pl.ds(pl.multiple_of(slab_at * span + at_row, TALL), TALL)
                    total = local[rows, :] * cur[rows, :]
                    if first:
                        total = total + near_a[rows, :]
                    for target in targets:
                        total = total + target[rows, :]
                    if not last:
                        for target in targets[1:]:
                            target[rows, :] = jnp.zeros((TALL, LANE), f32)
                    total = total * alpha
                    if beta is not None:
                        total = total + beta * prev[rows, :]
                    new[rows, :] = total
                    if not last:
                        split_store(high_buf, low_buf, slab_at_row, cols, total)
                if last:
                    for depth_at in range(groups_z):
                        at = pl.multiple_of(pair * span + depth_at * LANE, LANE)
                        turned = new[pl.ds(at, LANE), :].T
                        out[block_rows(groups_z, pair, 0, depth_at), :] = turned[:HALF]
                        out[block_rows(groups_z, pair, 1, depth_at), :] = turned[HALF:]
            return carry

        lax.fori_loop(0, groups_x, combine, 0)

    sigma_one = half_width / (LOW_EDGE - middle)
    sigma_now = sigma_one
    apply_step(field_a, None, field_b, sigma_one / half_width, None, True, DEGREE == 1)
    prev, cur, new = field_a, field_b, field_c
    for degree_step in range(1, DEGREE):
        sigma_next = 1.0 / (2.0 / sigma_one - sigma_now)
        last = degree_step == DEGREE - 1
        target = prev if degree_step > 1 else new
        apply_step(
            cur,
            prev,
            target,
            2.0 * sigma_next / half_width,
            -sigma_now * sigma_next,
            False,
            last,
        )
        prev, cur = cur, target
        sigma_now = sigma_next


def pack_kernel(my_first, extent, coupling, potential, projectors, out):
    atoms = projectors.shape[0]
    f32, bf16 = jnp.float32, jnp.bfloat16
    lane = lax.broadcasted_iota(jnp.int32, (SUB, LANE), 1)
    row = lax.broadcasted_iota(jnp.int32, (SUB, LANE), 0)
    lower = lane < HALF

    flat = potential[...].reshape(HALF, LANE)
    turned = jnp.concatenate([flat, flat], axis=0).T
    low = lax.broadcasted_iota(jnp.int32, (HALF, LANE), 1) < HALF
    out[:SUB] = jnp.where(low, turned[:HALF], turned[HALF:]).reshape(SUB, SUB, LANE)

    cells = projectors.shape[2]
    own_row = lax.broadcasted_iota(jnp.int32, (SUB, cells), 1) % B
    own_row = own_row == lax.broadcasted_iota(jnp.int32, (SUB, cells), 0)
    sides = []
    for kh in range(2):
        parts = []
        for kp in range(2):
            for atom in range(atoms):
                line = projectors[atom, 2 * kp + kh : 2 * kp + kh + 1, :]
                parts.append(jnp.where(own_row, jnp.broadcast_to(line, (SUB, cells)), 0.0))
        sides.append(jnp.concatenate(parts, axis=0))
    value = jnp.concatenate(sides, axis=1)
    source = lax.broadcasted_iota(jnp.int32, (2 * cells, LANE), 0) // B
    hot = source == lax.broadcasted_iota(jnp.int32, (2 * cells, LANE), 1)
    hot = hot.astype(f32).astype(bf16)
    high = value.astype(bf16)
    rest = value - high.astype(f32)
    mid = rest.astype(bf16)
    small = (rest - mid.astype(f32)).astype(bf16)
    moved = (mxu(high, hot) + mxu(mid, hot)) + mxu(small, hot)

    reach = jnp.maximum(jnp.maximum((lane >> 3) & (B - 1), lane & (B - 1)), row)
    for kp in range(2):
        for atom in range(atoms):
            at = my_first[0] + atom
            scale = jnp.sqrt(
                jnp.where(lower, coupling[2 * kp, at], coupling[2 * kp + 1, at])
            )
            number = kp * atoms + atom
            part = moved[number * SUB : (number + 1) * SUB]
            group, j = atom // SUB, atom % SUB
            out[SUB + (group * 2 + kp) * SUB + j] = jnp.where(
                reach < extent[at], part * scale, 0.0
            )


def packed_inputs(my_first, extent, coupling, potential, projectors, interpret=False):
    vmem = pl.BlockSpec(memory_space=pltpu.VMEM)
    smem = pl.BlockSpec(memory_space=pltpu.SMEM)
    atoms = projectors.shape[0]
    return pl.pallas_call(
        pack_kernel,
        out_shape=jax.ShapeDtypeStruct((SUB + 2 * atoms, SUB, LANE), jnp.float32),
        in_specs=[smem] * 3 + [vmem] * 2,
        out_specs=vmem,
        compiler_params=pltpu.CompilerParams(vmem_limit_bytes=8 * 1024 * 1024),
        interpret=interpret,
    )(my_first, extent, coupling.T, potential, projectors)


def weights_kernel(plane_in, depth_in, plane, depth, sems):
    loads = [
        pltpu.make_async_copy(plane_in, plane, sems.at[0]),
        pltpu.make_async_copy(depth_in, depth, sems.at[1]),
    ]
    for load in loads:
        load.start()
    for load in loads:
        load.wait()


def weights_call(groups, interpret=False):
    plane = jnp.asarray(plane_weights(groups[1]))
    depth = jnp.asarray(depth_weights(groups[2]))
    return pl.pallas_call(
        weights_kernel,
        out_shape=[jax.ShapeDtypeStruct(part.shape, part.dtype) for part in (plane, depth)],
        in_specs=[pl.BlockSpec(memory_space=pl.ANY)] * 2,
        out_specs=[pl.BlockSpec(memory_space=pltpu.VMEM)] * 2,
        scratch_shapes=[pltpu.SemaphoreType.DMA((2,))],
        compiler_params=pltpu.CompilerParams(vmem_limit_bytes=4 * 1024 * 1024),
        interpret=interpret,
    )(plane, depth)


def box_places(groups, owner, anchor):
    groups_z = groups[2]
    column = owner // groups_z
    place = (column // 2 * groups_z + owner % groups_z) * LANE + anchor
    return place, column % 2


def first_call(groups, field, plane, depth, interpret=False):
    groups_x, groups_y, groups_z = groups
    span = groups_z * LANE
    cells = (groups_x * groups_y // 2 * span, LANE)
    slabs = (groups_x * span, groups_y * HALF)
    vmem = pl.BlockSpec(memory_space=pltpu.VMEM)
    work = 2 * slabs[0] * slabs[1] * (9 * slabs[1] + 3 * span)
    return pl.pallas_call(
        functools.partial(first_kernel, groups),
        out_shape=[
            jax.ShapeDtypeStruct(cells, jnp.float32),
            jax.ShapeDtypeStruct(cells, jnp.float32),
        ],
        in_specs=[vmem] * 3,
        out_specs=[vmem] * 2,
        scratch_shapes=[
            pltpu.VMEM(slabs, jnp.bfloat16),
            pltpu.VMEM(slabs, jnp.bfloat16),
        ],
        compiler_params=pltpu.CompilerParams(vmem_limit_bytes=12 * 1024 * 1024),
        cost_estimate=pl.CostEstimate(
            flops=work, bytes_accessed=4 * field.size * 4, transcendentals=0
        ),
        interpret=interpret,
    )(field.reshape(cells), plane, depth)


def filter_call(
    groups, place, half, my_place, field, near, packs, plane, depth, interpret=False
):
    groups_x, groups_y, groups_z = groups
    columns = groups_x * groups_y
    atoms = place.shape[0]
    vmem = pl.BlockSpec(memory_space=pltpu.VMEM)
    smem = pl.BlockSpec(memory_space=pltpu.SMEM)
    slabs = (groups_x * groups_z * LANE, groups_y * HALF)
    work = 2 * slabs[0] * slabs[1] * (9 * slabs[1] + 3 * groups_z * LANE)
    out = pl.pallas_call(
        functools.partial(filter_kernel, groups, atoms),
        out_shape=jax.ShapeDtypeStruct(field.shape, jnp.float32),
        in_specs=[smem] * 3 + [vmem] * (len(packs) + 4),
        out_specs=vmem,
        scratch_shapes=[
            pltpu.VMEM(field.shape, jnp.float32),
            pltpu.VMEM(field.shape, jnp.float32),
            pltpu.VMEM(field.shape, jnp.float32),
            pltpu.VMEM((atoms * 2, LANE), jnp.float32),
            pltpu.VMEM(slabs, jnp.bfloat16),
            pltpu.VMEM(slabs, jnp.bfloat16),
        ]
        + [pltpu.VMEM(field.shape, jnp.float32) for _ in range(1 + SPARES)],
        compiler_params=pltpu.CompilerParams(vmem_limit_bytes=22 * 1024 * 1024),
        cost_estimate=pl.CostEstimate(
            flops=3 * work, bytes_accessed=8 * field.size * 4, transcendentals=0
        ),
        interpret=interpret,
    )(place, half, my_place, field, near, *packs, plane, depth)
    return out.reshape(columns * groups_z, SUB, SUB, LANE)


def hops(value, axis):
    count = lax.axis_size(axis)
    return [value] + [
        lax.ppermute(value, axis, [(i, (i + hop) % count) for i in range(count)])
        for hop in range(1, count)
    ]


def state_body(orbitals, potential, projectors, owner_rank, box_anchor, box_extent, coupling):
    axes = ("gx", "gy", "gz")
    groups = tuple(lax.axis_size(axis) for axis in axes)
    groups_z = groups[2]
    domains = groups[0] * groups[1] * groups_z
    atoms_own = projectors.shape[0]
    my_place = jnp.stack([lax.axis_index(axis) for axis in axes])
    me = (my_place[0] * groups[1] + my_place[1]) * groups_z + my_place[2]
    pack = packed_inputs((me * atoms_own)[None], box_extent, coupling, potential, projectors)
    line = jnp.stack(hops(pack, "gx"))
    place, half = box_places(groups, owner_rank, box_anchor[2])
    plane, depth = weights_call(groups)
    orbitals, line, place, half, plane, depth = lax.optimization_barrier(
        (orbitals, line, place, half, plane, depth)
    )
    crossed = [hops(piece, "gz") for piece in hops(line, "gy")]
    packs = [crossed[hop_y][hop_z] for hop_z in range(groups_z) for hop_y in range(groups[1])]
    field = lax.all_to_all(orbitals, axes, split_axis=0, concat_axis=0, tiled=True)
    field, near = first_call(groups, field, plane, depth)
    result = filter_call(groups, place, half, my_place, field, near, packs, plane, depth)
    filtered = lax.all_to_all(result, axes, split_axis=0, concat_axis=0, tiled=True)
    states = filtered.shape[0]
    flattened = filtered.reshape(states, -1)
    partial_value = jnp.dot(flattened, flattened.T, precision=lax.Precision.HIGHEST)
    quarter = partial_value.reshape(-1, SUB, states).transpose(1, 0, 2).reshape(SUB, -1)
    parts = lax.all_to_all(
        jnp.broadcast_to(quarter[None], (domains,) + quarter.shape),
        axes,
        split_axis=0,
        concat_axis=0,
        tiled=True,
    )
    summed = jnp.sum(parts, axis=0).reshape(SUB, -1, states).transpose(1, 0, 2)
    cells_total = orbitals.shape[1] * orbitals.shape[2] * orbitals.shape[3] * domains
    intersection = summed.reshape(states, states) / cells_total
    return (filtered, intersection)


def body(orbitals, potential, projectors, owner_rank, box_anchor, box_extent, coupling):
    domains = lax.axis_size("gx") * lax.axis_size("gy") * lax.axis_size("gz")
    whole_states = (
        orbitals.shape == (domains, SUB, SUB, LANE)
        and projectors.shape[0] % SUB == 0
        and projectors.shape[1] == NPROJ
        and lax.axis_size("gy") % 2 == 0
    )
    chosen = state_body if whole_states else domain_body
    return chosen(
        orbitals, potential, projectors, owner_rank, box_anchor, box_extent, coupling
    )


def solution(mesh):
    return jax.shard_map(
        body,
        mesh=mesh,
        in_specs=(
            P(None, "gx", "gy", "gz"),
            P("gx", "gy", "gz"),
            P(("gx", "gy", "gz"), None, None),
            P(),
            P(),
            P(),
            P(),
        ),
        out_specs=(P(None, "gx", "gy", "gz"), P()),
        check_vma=False,
    )
```
